32 devices in a mesh: ctx: 8 (over z, y), fsdp: 4 (over x, core).
Axes of the slice: x: 2, y: 2, z: 4, core: 2. Of those that a mesh axis runs over, the one named last changes fastest.
Arguments:
- sig_raw: bfloat16 [1024, 8192], P('ctx', 'fsdp'), may hold values from -6 to 6
- map_raw: bfloat16 [1024, 2048], P('ctx'), may hold values from -1.796875 to 1.796875
- step_size_logits: float32 [1024, 128], P('ctx', 'fsdp'), may hold values from -5.4 to 21.5
- d_out: bfloat16 [1024, 8192], P('ctx', 'fsdp'), may hold values from -6 to 6
- sig_taps: float32 [4, 8192], P(None, 'fsdp'), may hold values from -3 to 3
- map_taps: float32 [4, 2048], P(None, 'fsdp'), may hold values from -3 to 3
- sig_bias: float32 [8192], P('fsdp'), may hold values from -3 to 3
- map_bias: float32 [2048], P('fsdp'), may hold values from -0.6 to 0.6
- a_log: float32 [128], P('fsdp'), as said below
- dt_bias: float32 [128], P('fsdp'), may hold values from -5 to -4.2
- skip_gain: float32 [128], P('fsdp'), may hold values from 0.1 to 3
Outputs:
- d_sig: float32 [1024, 8192], P('ctx', 'fsdp')
- d_map: float32 [1024, 2048], P('ctx', 'fsdp')
- d_dt: float32 [1024, 128], P('ctx', 'fsdp')
- d_sig_taps: float32 [4, 8192], P(None, 'fsdp')
- d_map_taps: float32 [4, 2048], P(None, 'fsdp')
- d_sig_bias: float32 [8192], P('fsdp')
- d_map_bias: float32 [2048], P('fsdp')
- d_a_log: float32 [128], P('fsdp')
- scaled_timestep_shift_grad: float32 [128], P('fsdp')
- d_skip: float32 [128], P('fsdp')
The draws below stay inside these ranges and needn't reach their ends.
Inputs may be any that keep to these rules, and one draw needn't show every extreme that they name: Each head's rate exp(a_log) lies either between 2 and 4 or between 30 / 1024 and 200 / 1024.
All inputs are finite; a program needn't handle non-finite values.
Results may differ from the reference program's by a relative error of at most 0.0066.
Values may be sent and summed in bfloat16 or wider, within the bound.
No kernel may reach another device: no remote copies, remote signals or barrier semaphores. Data moves between devices by JAX's collectives and lax.ppermute only.
A program may use at most 128 MiB of HBM per device.

```python
import math
import jax
import jax.numpy as jnp
import numpy as np
from jax import lax

HEADS = 128
HDIM = 64
STATE = 128
GROUPS = 8
KSIZE = 4
BLK = 64
TOKEN_COUNT = 1024
CH = 10240
N_CTX = 8


def draw_a_log(key, part):
    kind_key, slow_key, quick_key = jax.random.split(key, 3)
    quick = jax.random.randint(kind_key, (HEADS,), 0, 2) == 0
    span = 0.01 * TOKEN_COUNT
    slow_log = jax.random.uniform(slow_key, (HEADS,), jnp.float32, jnp.log(0.3 / span), jnp.log(2.0 / span))
    quick_log = jax.random.uniform(quick_key, (HEADS,), jnp.float32, jnp.log(2.0), jnp.log(4.0))
    return jnp.where(quick, quick_log, slow_log)


def draw_step_size_logits(key, part):
    base_key, place_lookup, height_key = jax.random.split(key, 3)
    starting_shift = jnp.clip(0.5 * jax.random.normal(base_key, (TOKEN_COUNT, HEADS), jnp.float32), -1.5, 1.5)
    spike_place = jax.random.randint(place_lookup, (TOKEN_COUNT, HEADS), 0, 1024) == 0
    raised_by = jax.random.uniform(height_key, (TOKEN_COUNT, HEADS), jnp.float32, 10.0, 20.0)
    return starting_shift + jnp.where(spike_place, raised_by, 0.0)


def block_scale(own_key, shape, cuts, low, top_value):
    def one(dim, blocks):
        steps = jax.random.uniform(jax.random.fold_in(jax.random.fold_in(own_key, 6), dim), (blocks,), jnp.float32, low / len(cuts), top_value / len(cuts))
        return jnp.repeat(jnp.exp(steps), shape[dim] // blocks).reshape((-1,) + (1,) * (len(shape) - dim - 1))

    factor_of = one(*cuts[0])
    for cut in cuts[1:]:
        factor_of = factor_of * one(*cut)
    return factor_of


def gaussian(own_key, shape, deviation, bound, cuts=(), kind=jnp.bfloat16):
    drawn = deviation * jax.random.normal(own_key, shape, jnp.float32)
    if cuts:
        drawn = drawn * block_scale(own_key, shape, cuts, -0.22, 0.18)
    return jnp.clip(drawn, -bound, bound).astype(kind)


def setup_inputs(seed: int = 0) -> dict:
    key_list = jax.random.split(jax.random.key(seed), 12)
    sig_raw = gaussian(key_list[0], (TOKEN_COUNT, HEADS * HDIM), 1.0, 6.0, ((0, 8), (1, 4)))
    map_raw = gaussian(key_list[1], (TOKEN_COUNT, 2 * GROUPS * STATE), 0.3, 1.796875, ((0, 8),))
    step_size_logits = draw_step_size_logits(jax.random.fold_in(key_list[11], 71), 0)
    d_out = gaussian(key_list[3], (TOKEN_COUNT, HEADS * HDIM), 1.0, 6.0, ((0, 8), (1, 4)))
    sig_taps = gaussian(key_list[4], (KSIZE, HEADS * HDIM), KSIZE ** -0.5, 3.0, ((1, 4),), jnp.float32)
    map_taps = gaussian(key_list[5], (KSIZE, 2 * GROUPS * STATE), KSIZE ** -0.5, 3.0, ((1, 4),), jnp.float32)
    sig_bias = gaussian(key_list[6], (HEADS * HDIM,), 0.5, 3.0, ((0, 4),), jnp.float32)
    map_bias = gaussian(key_list[7], (2 * GROUPS * STATE,), 0.1, 0.6, ((0, 4),), jnp.float32)
    a_log = draw_a_log(jax.random.fold_in(key_list[11], 71), 0)
    dt_bias = jnp.clip(-5.0 + 0.8000002 * jax.random.uniform(key_list[9], (HEADS,), jnp.float32) ** block_scale(key_list[9], (HEADS,), ((0, 4),), -0.2, 0.2), -5.0, -4.2)
    skip_gain = jnp.clip(jnp.exp(math.log(3.0) - 3.4011974 * jax.random.uniform(key_list[10], (HEADS,), jnp.float32) ** block_scale(key_list[10], (HEADS,), ((0, 4),), -0.2, 0.2)), 0.1, 3.0)
    return {"sig_raw": sig_raw, "map_raw": map_raw, "step_size_logits": step_size_logits, "d_out": d_out, "sig_taps": sig_taps, "map_taps": map_taps, "sig_bias": sig_bias, "map_bias": map_bias, "a_log": a_log, "dt_bias": dt_bias, "skip_gain": skip_gain}


def ein(form, left, right):
    return jnp.einsum(form, left.astype(jnp.float32), right.astype(jnp.float32))

def silu_slope(value):
    sig = jax.nn.sigmoid(value)
    return sig * (1.0 + value * (1.0 - sig))

def block_parts(activated, dt_rows, a_log, dt_bias, groups):
    length = activated.shape[0]
    heads = dt_rows.shape[1]
    inner = heads * HDIM
    shared = groups * STATE
    ratio = heads // groups
    signal = activated[:, :inner].reshape(length, heads, HDIM)
    input_map = activated[:, inner:inner + shared].reshape(length, groups, STATE)
    output_map = activated[:, inner + shared:].reshape(length, groups, STATE)
    input_heads = jnp.repeat(input_map, ratio, axis=1)
    output_heads = jnp.repeat(output_map, ratio, axis=1)
    step = jax.nn.softplus(dt_rows + dt_bias)
    rate = -jnp.exp(a_log)
    row_ids = lax.broadcasted_iota(jnp.int32, (length, length), 0)
    col_ids = lax.broadcasted_iota(jnp.int32, (length, length), 1)
    lower = (row_ids >= col_ids).astype(jnp.float32)
    decay_sum = jnp.dot(lower, step * rate, precision=lax.Precision.HIGHEST)
    to_end = jnp.exp(decay_sum[-1][None, :] - decay_sum)
    scaled = (signal.astype(jnp.float32) * step[:, :, None]).astype(jnp.bfloat16)
    weighted = (scaled.astype(jnp.float32) * to_end[:, :, None]).astype(jnp.bfloat16)
    local = ein('qhp,qhn->hpn', weighted, input_heads)
    return (signal, input_map, output_map, input_heads, output_heads, step, rate, lower, decay_sum, scaled, to_end, weighted, local)

def entry_grad(parts, d_rows):
    decay_sum = parts[8]
    output_heads = parts[4]
    scaled_grad = (d_rows.astype(jnp.float32) * jnp.exp(decay_sum)[:, :, None]).astype(jnp.bfloat16)
    return (scaled_grad, ein('thp,thn->hpn', scaled_grad, output_heads))

def block_grads(parts, d_rows, scaled_grad, h_in, carried, skip_gain, dt_rows, dt_bias):
    signal, input_map, output_map, input_heads, output_heads, step, rate, lower, decay_sum, scaled, to_end, weighted, local = parts
    length = d_rows.shape[0]
    heads = d_rows.shape[1]
    groups = input_map.shape[1]
    width_state = input_map.shape[2]
    ratio = heads // groups
    grad_f = d_rows.astype(jnp.float32)
    signal_f = signal.astype(jnp.float32)
    grad_skip = lax.optimization_barrier(jnp.sum(grad_f * signal_f, axis=(0, 2)))
    h_low = h_in.astype(jnp.bfloat16)
    carried_low = carried.astype(jnp.bfloat16)
    offset = jnp.exp(decay_sum)[:, :, None] * ein('thn,hpn->thp', output_heads, h_low)
    grad_sum = lax.optimization_barrier(jnp.sum(grad_f * offset, axis=2))
    out_heads_grad = ein('thp,hpn->thn', scaled_grad, h_low)
    grad_weighted = ein('shn,hpn->shp', input_heads, carried_low)
    in_heads_grad = ein('shp,hpn->shn', weighted, carried_low)
    back = lax.optimization_barrier(jnp.sum(grad_weighted * scaled.astype(jnp.float32), axis=2)) * to_end
    end_term = jnp.exp(decay_sum[-1]) * lax.optimization_barrier(jnp.sum(h_in * carried, axis=(1, 2)))
    last_row = (lax.broadcasted_iota(jnp.int32, (length, 1), 0) == length - 1).astype(jnp.float32)
    grad_sum = grad_sum - back + last_row * (lax.optimization_barrier(jnp.sum(back, axis=0)) + end_term)[None, :]
    spread = decay_sum.T[:, :, None] - decay_sum.T[:, None, :]
    decay = jnp.where(lower[None] > 0, jnp.exp(jnp.minimum(spread, 0.0)), 0.0)
    score = ein('tgn,sgn->gts', output_map, input_map)
    mix = jnp.repeat(score, ratio, axis=0) * decay
    grad_mix = ein('thp,shp->hts', d_rows, scaled)
    grad_scaled = grad_weighted * to_end[:, :, None] + ein('hts,thp->shp', mix.astype(jnp.bfloat16), d_rows)
    product = grad_mix * mix
    grad_sum = grad_sum + (lax.optimization_barrier(jnp.sum(product, axis=2)) - lax.optimization_barrier(jnp.sum(product, axis=1))).T
    grad_score = lax.optimization_barrier(jnp.sum((grad_mix * decay).reshape(groups, ratio, length, length), axis=1)).astype(jnp.bfloat16)
    grad_outmap = ein('gts,sgn->tgn', grad_score, input_map) + lax.optimization_barrier(jnp.sum(out_heads_grad.reshape(length, groups, ratio, width_state), axis=2))
    grad_in = ein('gts,tgn->sgn', grad_score, output_map) + lax.optimization_barrier(jnp.sum(in_heads_grad.reshape(length, groups, ratio, width_state), axis=2))
    grad_log = jnp.dot(lower.T, grad_sum, precision=lax.Precision.HIGHEST)
    descent_increment = grad_log * rate + lax.optimization_barrier(jnp.sum(grad_scaled * signal_f, axis=2))
    grad_signal = skip_gain[None, :, None] * grad_f + grad_scaled * step[:, :, None]
    grad_dt = descent_increment * jax.nn.sigmoid(dt_rows + dt_bias)
    decay_log_gradient = lax.optimization_barrier(jnp.sum(grad_log * step, axis=0)) * rate
    grad_act = jnp.concatenate([grad_signal.reshape(length, heads * HDIM), grad_in.reshape(length, groups * width_state), grad_outmap.reshape(length, groups * width_state)], axis=1)
    return (grad_act, grad_dt, decay_log_gradient, lax.optimization_barrier(jnp.sum(grad_dt, axis=0)), grad_skip)

def reference(sig_raw, map_raw, step_size_logits, d_out, sig_taps, map_taps, sig_bias, map_bias, a_log, dt_bias, skip_gain):
    blocks = 2 * N_CTX
    order = np.array([2 * p if p < N_CTX else 2 * (blocks - 1 - p) + 1 for p in range(blocks)], dtype=np.int32)
    back_order = np.argsort(order).astype(np.int32)

    def unzig(array):
        return array.reshape((blocks, BLK) + array.shape[1:])[order].reshape(array.shape)

    def rezig(array):
        return array.reshape((blocks, BLK) + array.shape[1:])[back_order].reshape(array.shape)
    sig_width = HEADS * HDIM
    raw_rows = jnp.concatenate([unzig(sig_raw), unzig(map_raw)], axis=1)
    conv_weight = jnp.concatenate([sig_taps, map_taps], axis=1)
    conv_bias = jnp.concatenate([sig_bias, map_bias], axis=0)
    dt_rows = unzig(step_size_logits)
    grad_rows = unzig(d_out)
    padded = jnp.concatenate([jnp.zeros((KSIZE - 1, CH), jnp.float32), raw_rows.astype(jnp.float32)], axis=0)
    preact = conv_bias[None, :] + jnp.zeros((TOKEN_COUNT, CH), jnp.float32)
    for tap in range(KSIZE):
        preact = preact + conv_weight[tap][None, :] * padded[tap:tap + TOKEN_COUNT]
    activated = jax.nn.silu(preact).astype(jnp.bfloat16)
    act_blocks = activated.reshape(blocks, BLK, CH)
    step_size_blocks = dt_rows.reshape(blocks, BLK, HEADS)
    grad_blocks = grad_rows.reshape(blocks, BLK, HEADS, HDIM)

    def first_pass(entry):
        parts = block_parts(entry[0], entry[1], a_log, dt_bias, GROUPS)
        scaled_grad, state_grad = entry_grad(parts, entry[2])
        return (parts[8][-1], parts[12], state_grad)
    ends, locals_all, state_grads = lax.map(first_pass, (act_blocks, step_size_blocks, grad_blocks))
    zero_state = jnp.zeros((HEADS, HDIM, STATE), jnp.float32)

    def forward_link(state, entry):
        return (jnp.exp(entry[0])[:, None, None] * state + entry[1], state)
    _, h_ins = lax.scan(forward_link, zero_state, (ends, locals_all))

    def backward_link(state, entry):
        return (entry[1] + jnp.exp(entry[0])[:, None, None] * state, state)
    _, carried = lax.scan(backward_link, zero_state, (ends, state_grads), reverse=True)

    def second_pass(entry):
        parts = block_parts(entry[0], entry[1], a_log, dt_bias, GROUPS)
        scaled_grad, state_grad = entry_grad(parts, entry[2])
        return block_grads(parts, entry[2], scaled_grad, entry[3], entry[4], skip_gain, entry[1], dt_bias)
    grad_act, grad_dt, decay_log_gradient, grad_dtb, grad_skip = lax.map(second_pass, (act_blocks, step_size_blocks, grad_blocks, h_ins, carried))
    grad_pre = grad_act.reshape(TOKEN_COUNT, CH) * silu_slope(preact)
    padded_next = jnp.concatenate([grad_pre, jnp.zeros((KSIZE - 1, CH), jnp.float32)], axis=0)
    grad_raw = jnp.zeros((TOKEN_COUNT, CH), jnp.float32)
    for tap in range(KSIZE):
        grad_raw = grad_raw + conv_weight[tap][None, :] * padded_next[KSIZE - 1 - tap:KSIZE - 1 - tap + TOKEN_COUNT]
    grad_taps = jnp.stack([lax.optimization_barrier(jnp.sum(grad_pre * padded[tap:tap + TOKEN_COUNT], axis=0)) for tap in range(KSIZE)])
    bias_grad = lax.optimization_barrier(jnp.sum(grad_pre, axis=0))
    stored = rezig(grad_raw)
    scale = 1.0 / np.sqrt(float(TOKEN_COUNT))
    return (stored[:, :sig_width], stored[:, sig_width:], rezig(grad_dt.reshape(TOKEN_COUNT, HEADS)), grad_taps[:, :sig_width] * scale, grad_taps[:, sig_width:] * scale, bias_grad[:sig_width] * scale, bias_grad[sig_width:] * scale, lax.optimization_barrier(jnp.sum(decay_log_gradient, axis=0)) * scale, lax.optimization_barrier(jnp.sum(grad_dtb, axis=0)) * scale, lax.optimization_barrier(jnp.sum(grad_skip, axis=0)) * scale)
```

```python
import functools
import math

import jax
import jax.numpy as jnp
from jax import lax
from jax.experimental import pallas as pl
from jax.experimental.pallas import tpu as pltpu
from jax.sharding import PartitionSpec as P

HEADS = 128
HDIM = 64
STATE = 128
GROUPS = 8


def prefix(part, axis, combine, identity, reverse):
    count = lax.axis_size(axis)
    place = lax.axis_index(axis)
    ahead = count - 1 - place if reverse else place
    gathered = jax.tree.map(lambda a: lax.all_gather(a, axis), part)
    state = jax.tree.map(lambda a, e: jnp.zeros_like(a) + jnp.asarray(e, a.dtype), part, identity)

    def one(lap, state):
        source = count - 1 - lap if reverse else lap
        return combine(
            state, jax.tree.map(lambda a: lax.dynamic_index_in_dim(a, source, 0, False), gathered)
        )

    return lax.fori_loop(0, ahead, one, state)


def broadcast(x, axis, root):
    mine = lax.axis_index(axis) == root
    return lax.psum(jnp.where(mine, x, jnp.zeros_like(x)), axis)


def extended(block, sides, width):
    for axis, dim in sides:
        count = lax.axis_size(axis)
        forward = [(i, i + 1) for i in range(count - 1)]
        backward = [(target, source) for source, target in forward]
        low = lax.ppermute(
            lax.slice_in_dim(block, block.shape[dim] - width, None, axis=dim), axis, forward
        )
        high = lax.ppermute(lax.slice_in_dim(block, 0, width, axis=dim), axis, backward)
        block = jnp.concatenate([low, block, high], axis=dim)
    return block


def ein(form, left, right):
    return jnp.einsum(form, left, right, preferred_element_type=jnp.float32)


def silu_slope(value):
    sig = jax.nn.sigmoid(value)
    return sig * (1.0 + value * (1.0 - sig))


def block_parts(activated, dt_rows, a_log, dt_bias, groups):
    length = activated.shape[0]
    heads = dt_rows.shape[1]
    inner = heads * HDIM
    shared = groups * STATE
    ratio = heads // groups
    signal = activated[:, :inner].reshape(length, heads, HDIM)
    input_map = activated[:, inner : inner + shared].reshape(length, groups, STATE)
    output_map = activated[:, inner + shared :].reshape(length, groups, STATE)
    input_heads = jnp.repeat(input_map, ratio, axis=1)
    output_heads = jnp.repeat(output_map, ratio, axis=1)
    step = jax.nn.softplus(dt_rows + dt_bias)
    rate = -jnp.exp(a_log)
    row_ids = lax.broadcasted_iota(jnp.int32, (length, length), 0)
    col_ids = lax.broadcasted_iota(jnp.int32, (length, length), 1)
    lower = (row_ids >= col_ids).astype(jnp.float32)
    decay_sum = jnp.dot(lower, step * rate, precision=lax.Precision.HIGHEST)
    to_end = jnp.exp(decay_sum[-1][None, :] - decay_sum)
    scaled = (signal.astype(jnp.float32) * step[:, :, None]).astype(jnp.bfloat16)
    weighted = (scaled.astype(jnp.float32) * to_end[:, :, None]).astype(jnp.bfloat16)
    local = ein("qhp,qhn->hpn", weighted, input_heads)
    return (
        signal,
        input_map,
        output_map,
        input_heads,
        output_heads,
        step,
        rate,
        lower,
        decay_sum,
        scaled,
        to_end,
        weighted,
        local,
    )


def entry_grad(parts, d_rows):
    decay_sum = parts[8]
    output_heads = parts[4]
    scaled_grad = (d_rows.astype(jnp.float32) * jnp.exp(decay_sum)[:, :, None]).astype(jnp.bfloat16)
    return (scaled_grad, ein("thp,thn->hpn", scaled_grad, output_heads))


def block_grads(parts, d_rows, scaled_grad, h_in, carried, skip_gain, dt_rows, dt_bias):
    (
        signal,
        input_map,
        output_map,
        input_heads,
        output_heads,
        step,
        rate,
        lower,
        decay_sum,
        scaled,
        to_end,
        weighted,
        local,
    ) = parts
    length = d_rows.shape[0]
    heads = d_rows.shape[1]
    groups = input_map.shape[1]
    width_state = input_map.shape[2]
    ratio = heads // groups
    grad_f = d_rows.astype(jnp.float32)
    signal_f = signal.astype(jnp.float32)
    grad_skip = jnp.sum(grad_f * signal_f, axis=(0, 2))
    h_low = h_in.astype(jnp.bfloat16)
    carried_low = carried.astype(jnp.bfloat16)
    offset = jnp.exp(decay_sum)[:, :, None] * ein("thn,hpn->thp", output_heads, h_low)
    grad_sum = jnp.sum(grad_f * offset, axis=2)
    out_heads_grad = ein("thp,hpn->thn", scaled_grad, h_low)
    grad_weighted = ein("shn,hpn->shp", input_heads, carried_low)
    in_heads_grad = ein("shp,hpn->shn", weighted, carried_low)
    back = jnp.sum(grad_weighted * scaled.astype(jnp.float32), axis=2) * to_end
    end_term = jnp.exp(decay_sum[-1]) * jnp.sum(h_in * carried, axis=(1, 2))
    last_row = (lax.broadcasted_iota(jnp.int32, (length, 1), 0) == length - 1).astype(jnp.float32)
    grad_sum = grad_sum - back + last_row * (jnp.sum(back, axis=0) + end_term)[None, :]
    spread = decay_sum.T[:, :, None] - decay_sum.T[:, None, :]
    decay = jnp.where(lower[None] > 0, jnp.exp(jnp.minimum(spread, 0.0)), 0.0)
    score = ein("tgn,sgn->gts", output_map, input_map)
    mix = jnp.repeat(score, ratio, axis=0) * decay
    grad_mix = ein("thp,shp->hts", d_rows, scaled)
    grad_scaled = grad_weighted * to_end[:, :, None] + ein(
        "hts,thp->shp", mix.astype(jnp.bfloat16), d_rows
    )
    product = grad_mix * mix
    grad_sum = grad_sum + (jnp.sum(product, axis=2) - jnp.sum(product, axis=1)).T
    grad_score = jnp.sum((grad_mix * decay).reshape(groups, ratio, length, length), axis=1).astype(
        jnp.bfloat16
    )
    grad_outmap = ein("gts,sgn->tgn", grad_score, input_map) + jnp.sum(
        out_heads_grad.reshape(length, groups, ratio, width_state), axis=2
    )
    grad_in = ein("gts,tgn->sgn", grad_score, output_map) + jnp.sum(
        in_heads_grad.reshape(length, groups, ratio, width_state), axis=2
    )
    grad_log = jnp.dot(lower.T, grad_sum, precision=lax.Precision.HIGHEST)
    descent_increment = grad_log * rate + jnp.sum(grad_scaled * signal_f, axis=2)
    grad_signal = skip_gain[None, :, None] * grad_f + grad_scaled * step[:, :, None]
    grad_dt = descent_increment * jax.nn.sigmoid(dt_rows + dt_bias)
    decay_log_gradient = jnp.sum(grad_log * step, axis=0) * rate
    grad_act = jnp.concatenate(
        [
            grad_signal.reshape(length, heads * HDIM),
            grad_in.reshape(length, groups * width_state),
            grad_outmap.reshape(length, groups * width_state),
        ],
        axis=1,
    )
    return (grad_act, grad_dt, decay_log_gradient, jnp.sum(grad_dt, axis=0), grad_skip)


def link(earlier, later):
    return (earlier[0] + later[0], jnp.exp(later[0])[:, None, None] * earlier[1] + later[1])


def link_blocks(lower_pair, upper_pair):
    zero_rate = jnp.zeros_like(lower_pair[0])
    zero_state = jnp.zeros_like(lower_pair[1])
    below = prefix(lower_pair, "ctx", link, (zero_rate, zero_state), False)
    beyond = prefix(upper_pair, "ctx", link, (zero_rate, zero_state), True)
    total = jax.tree.map(
        lambda part: broadcast(part, "ctx", lax.axis_size("ctx") - 1), link(below, lower_pair)
    )
    return jnp.stack([below[1], link(total, beyond)[1]])


def conv_back(grad_pre, wide_grad, kernel_taps, padded, at_end, length):
    rim = kernel_taps.shape[0] - 1
    after = jnp.stack(
        [jnp.where(at_end, grad_pre[1, :rim], wide_grad[3 * rim : 4 * rim]), wide_grad[0:rim]]
    )
    padded_next = jnp.concatenate([grad_pre, after], axis=1)
    grad_raw = jnp.zeros(grad_pre.shape, jnp.float32)
    for tap in range(rim + 1):
        grad_raw = (
            grad_raw
            + kernel_taps[tap][None, None, :] * padded_next[:, rim - tap : rim - tap + length]
        )
    tap_grads = jnp.stack(
        [jnp.sum(grad_pre * padded[:, tap : tap + length], axis=(0, 1)) for tap in range(rim + 1)]
    )
    return (grad_raw, tap_grads, jnp.sum(grad_pre, axis=(0, 1)))


def first_rows(grad_pre, rim):
    return jnp.concatenate([grad_pre[0, :rim], grad_pre[1, :rim]], axis=0)


def shards_chain(
    sig_raw,
    map_raw,
    step_size_logits,
    d_out,
    sig_taps,
    map_taps,
    sig_bias,
    map_bias,
    a_log,
    dt_bias,
    skip_gain,
):
    all_map_taps, all_map_bias = (
        lax.all_gather(map_taps, "fsdp", axis=1, tiled=True),
        lax.all_gather(map_bias, "fsdp", axis=0, tiled=True),
    )
    kernel_taps = jnp.concatenate([sig_taps, all_map_taps], axis=1)
    kernel_bias = jnp.concatenate([sig_bias, all_map_bias], axis=0)
    kernel = kernel_taps.shape[0]
    rim = kernel - 1
    length = sig_raw.shape[0] // 2
    sig_width = sig_raw.shape[1]
    map_width = map_raw.shape[1]
    width = sig_width + map_width
    heads_here = step_size_logits.shape[1]
    ratio = HEADS // GROUPS
    group_count = max(1, heads_here // ratio)
    first_group = lax.axis_index("fsdp") * heads_here // ratio
    fsdp_count = lax.axis_size("fsdp")
    owned = map_width // fsdp_count
    map_start = lax.axis_index("fsdp") * owned
    raw_rows = jnp.concatenate([sig_raw, map_raw], axis=1).reshape(2, length, width)
    tails = jnp.concatenate([raw_rows[1, length - rim :], raw_rows[0, length - rim :]], axis=0)
    wide = extended(tails, (("ctx", 0),), rim)
    at_end = lax.axis_index("ctx") == lax.axis_size("ctx") - 1
    before = jnp.stack(
        [wide[0:rim], jnp.where(at_end, raw_rows[0, length - rim :], wide[3 * rim : 4 * rim])]
    )
    padded = jnp.concatenate([before, raw_rows], axis=1).astype(jnp.float32)
    preact = kernel_bias[None, None, :] + jnp.zeros((2, length, width), jnp.float32)
    for tap in range(kernel):
        preact = preact + kernel_taps[tap][None, None, :] * padded[:, tap : tap + length]
    activated = jax.nn.silu(preact).astype(jnp.bfloat16)
    maps_all = activated[:, :, sig_width:].reshape(2, length, 2, GROUPS, STATE)
    maps_mine = lax.dynamic_slice_in_dim(maps_all, first_group, group_count, 3)
    local_act = jnp.concatenate(
        [activated[:, :, :sig_width], maps_mine.reshape(2, length, 2 * group_count * STATE)], axis=2
    )
    dt_rows = step_size_logits.reshape(2, length, heads_here)
    grad_rows = d_out.reshape(2, length, heads_here, HDIM)

    def parts_of(act_block, dt_block):
        return block_parts(act_block, dt_block, a_log, dt_bias, group_count)

    parts = jax.vmap(parts_of)(local_act, dt_rows)
    scaled_grad, state_grad = jax.vmap(entry_grad)(parts, grad_rows)
    ends = parts[8][:, -1]
    h_ins = link_blocks((ends[0], parts[12][0]), (ends[1], parts[12][1]))
    carried_pair = link_blocks((ends[1], state_grad[1]), (ends[0], state_grad[0]))
    carried = jnp.stack([carried_pair[1], carried_pair[0]])
    grad_act, grad_dt, decay_log_gradient, grad_dtb, grad_skip = jax.vmap(
        block_grads, in_axes=(0, 0, 0, 0, 0, None, 0, None)
    )(parts, grad_rows, scaled_grad, h_ins, carried, skip_gain, dt_rows, dt_bias)
    slope = silu_slope(preact)
    grad_pre_sig = grad_act[:, :, :sig_width] * slope[:, :, :sig_width]
    grad_mine = grad_act[:, :, sig_width:].reshape(2, length, 2, group_count, STATE)
    zero_index = jnp.zeros((), jnp.int32)
    placed = lax.dynamic_update_slice(
        jnp.zeros((2, length, 2, GROUPS, STATE), jnp.float32),
        grad_mine,
        (zero_index, zero_index, zero_index, first_group, zero_index),
    )
    map_term = placed.reshape(2, length, map_width)
    map_owned = lax.psum_scatter(map_term, "fsdp", scatter_dimension=2, tiled=True)
    map_slope = lax.dynamic_slice_in_dim(slope[:, :, sig_width:], map_start, owned, 2)
    grad_pre = jnp.concatenate([grad_pre_sig, map_owned * map_slope], axis=2)
    own_taps = jnp.concatenate([sig_taps, map_taps], axis=1)
    own_padded = jnp.concatenate(
        [
            padded[:, :, :sig_width],
            lax.dynamic_slice_in_dim(padded[:, :, sig_width:], map_start, owned, 2),
        ],
        axis=2,
    )
    wide_grad = extended(first_rows(grad_pre, rim), (("ctx", 0),), rim)
    grad_raw, tap_grads, bias_grads = conv_back(
        grad_pre, wide_grad, own_taps, own_padded, at_end, length
    )
    map_raw_grad = grad_raw[:, :, sig_width:]
    map_tap_grad = tap_grads[:, sig_width:]
    map_bias_grad = bias_grads[sig_width:]
    sig_raw_grad = grad_raw[:, :, :sig_width]
    sig_tap_grad = tap_grads[:, :sig_width]
    sig_bias_grad = bias_grads[:sig_width]
    reduced = lax.psum(
        (
            sig_tap_grad,
            map_tap_grad,
            sig_bias_grad,
            map_bias_grad,
            jnp.sum(decay_log_gradient, axis=0),
            jnp.sum(grad_dtb, axis=0),
            jnp.sum(grad_skip, axis=0),
        ),
        "ctx",
    )
    scale = 1.0 / math.sqrt(float(lax.axis_size("ctx") * 2 * length))
    final = jax.tree.map(lambda grad_part: grad_part * scale, reduced)
    return (
        sig_raw_grad.reshape(2 * length, sig_width),
        map_raw_grad.reshape(2 * length, owned),
        grad_dt.reshape(2 * length, heads_here),
        final[0],
        final[1],
        final[2],
        final[3],
        final[4],
        final[5],
        final[6],
    )


TILE = 128
NT = (((1,), (1,)), ((), ()))
TN = (((0,), (0,)), ((), ()))
NN = (((1,), (0,)), ((), ()))
BF = jnp.bfloat16
F32 = jnp.float32


def mm(a, b, dims=NN):
    return lax.dot_general(a, b, dims, preferred_element_type=F32)


def mm_f32(a, b, dims=NN):
    return lax.dot_general(a, b, dims, precision=lax.Precision.HIGHEST, preferred_element_type=F32)


def split3(x):
    hi = x.astype(BF)
    rest = x - hi.astype(F32)
    mid = rest.astype(BF)
    return hi, mid, (rest - mid.astype(F32)).astype(BF)


def ids(shape, dim):
    return lax.broadcasted_iota(jnp.int32, shape, dim)


def pack_kernel(ctx, rows, sig_ref, map_ref, dt_ref, dy_ref, out_ref, dt_rows):
    heads = dt_ref.shape[1]
    mine = heads // ctx
    fsdp_place = lax.axis_index("fsdp")
    half = map_ref.shape[1] // 2
    padded = jnp.concatenate([dt_ref[...], jnp.zeros((rows, TILE - heads), F32)], axis=1)
    dt_rows[0:TILE, :] = jnp.transpose(padded)
    low = ids((8, TILE), 0) < mine
    for c in range(ctx):
        for j in range(2):
            cols = slice(c * 2 * TILE + j * TILE, c * 2 * TILE + (j + 1) * TILE)
            out_ref[c, j * TILE : (j + 1) * TILE, :] = sig_ref[:, cols]
            out_ref[c, (2 + j) * TILE : (3 + j) * TILE, :] = dy_ref[:, cols]
            first = (2 * fsdp_place + c // 4) * TILE + j * half
            out_ref[c, (4 + j) * TILE : (5 + j) * TILE, :] = map_ref[
                :, pl.ds(pl.multiple_of(first, TILE), TILE)
            ]
        hi, mid, lo = split3(dt_rows[c * mine : c * mine + 8, :])
        both = jnp.where(low, hi.astype(F32), pltpu.roll(mid.astype(F32), mine, 0))
        out_ref[c, 6 * TILE : 6 * TILE + 16, :] = jnp.concatenate(
            [both, lo.astype(F32)], axis=0
        ).astype(BF)


def core_kernel(
    scale,
    x_ref,
    taps_ref,
    bias_ref,
    mtaps_ref,
    alog_ref,
    dtb_ref,
    skip_ref,
    out_ref,
    xp,
    dp,
    act,
    slope,
    gp,
    scaled_s,
    weighted_s,
    sgrad_s,
    step_e,
    toend_e,
    exp_e,
    h_s,
    sg_s,
    carry,
    step_r,
    ds_r,
    sig_r,
    ddt_r,
    tap_acc,
    skip_acc,
    alog_acc,
    ddt_acc,
    after,
):
    ctx_place = lax.axis_index("ctx")
    fsdp_place = lax.axis_index("fsdp")
    chunks = 8
    heads = 4
    half_lane = ids((TILE, TILE), 1) < TILE // 2
    lane_row = ids((1, TILE), 1)
    row8 = ids((8, TILE), 0)
    lane8 = ids((8, TILE), 1)
    used8 = row8 < heads

    def blocks_of(chunk):
        found = []
        for e in range(2):
            b = 2 * chunk + e
            found.append((b, 0) if b < 8 else (15 - b, TILE // 2))
        return found

    xp[0:8, :] = jnp.zeros((8, 4 * TILE), F32)
    after[...] = jnp.zeros_like(after)
    rate8 = jnp.zeros((8, TILE), F32)
    bias8 = jnp.zeros((8, TILE), F32)
    skip_row = []
    for h in range(heads):
        at = ctx_place * heads + h
        rate8 = jnp.where(row8 == h, alog_ref[at], rate8)
        bias8 = jnp.where(row8 == h, dtb_ref[at], bias8)
    rate8 = -jnp.exp(rate8)
    for j in range(2):
        at = ctx_place * heads + 2 * j
        skip_row.append(jnp.where(lane_row < TILE // 2, skip_ref[at], skip_ref[at + 1]))
    dts = []
    for s in range(8):
        packed = x_ref[s, 6 * TILE : 6 * TILE + 16, :].astype(F32)
        top = packed[0:8]
        value = top + pltpu.roll(top, 4, 0) + packed[8:16]
        dts.append(jnp.where(used8, value, 0.0))
    for i in range(chunks):
        (s0, o0), (s1, o1) = blocks_of(i)
        for e, (s, o) in enumerate(((s0, o0), (s1, o1))):
            r = i * TILE + e * 64
            for j in range(2):
                xp[8 + r : 8 + r + 64, j * TILE : (j + 1) * TILE] = x_ref[
                    s, j * TILE + o : j * TILE + o + 64, :
                ].astype(F32)
                xp[8 + r : 8 + r + 64, (2 + j) * TILE : (3 + j) * TILE] = x_ref[
                    s, (4 + j) * TILE + o : (4 + j) * TILE + o + 64, :
                ].astype(F32)
                dp[r : r + 64, j * TILE : (j + 1) * TILE] = x_ref[
                    s, (2 + j) * TILE + o : (2 + j) * TILE + o + 64, :
                ]
        a = dts[s0] if o0 == 0 else pltpu.roll(dts[s0], 64, 1)
        b = dts[s1] if o1 != 0 else pltpu.roll(dts[s1], 64, 1)
        logits = jnp.where(lane8 < 64, a, b) + bias8
        small = jnp.exp(-jnp.abs(logits))
        step = jnp.maximum(logits, 0.0) + jnp.log1p(small)
        step_r[8 * i : 8 * i + 8, :] = jnp.where(used8, step, 0.0)
        sig_r[8 * i : 8 * i + 8, :] = jnp.where(logits >= 0, 1.0, small) / (1.0 + small)
        ds_r[8 * i : 8 * i + 8, :] = jnp.where(used8, step * rate8, 0.0)
    row_q = ids((TILE, TILE), 0)
    col_q = ids((TILE, TILE), 1)
    upto = (row_q <= col_q).astype(F32)
    ds_r[...] = mm_f32(ds_r[...], upto)
    tail_sums = jnp.concatenate(
        [(row_q >= col_q).astype(F32), (row_q < col_q).astype(F32)], axis=0
    )
    seen = row_q <= col_q

    def weights(j):
        if j < 2:
            at = pl.ds(pl.multiple_of(ctx_place * 2 * TILE + j * TILE, TILE), TILE)
            return [taps_ref[k : k + 1, at] for k in range(4)], bias_ref[0:1, at]
        group = 2 * fsdp_place + ctx_place // 4
        owner = 2 * (j - 2) + fsdp_place // 2
        at = pl.ds(pl.multiple_of((group % 4) * TILE, TILE), TILE)
        return [mtaps_ref[owner, k : k + 1, at] for k in range(4)], mtaps_ref[owner, 4:5, at]

    def shifted(block, k):
        return block[8:] if k == 3 else pltpu.roll(block, 3 - k, 0)[8:]

    def columns(i):
        both = jnp.concatenate(
            [
                step_r[pl.ds(pl.multiple_of(8 * i, 8), 8), :],
                ds_r[pl.ds(pl.multiple_of(8 * i, 8), 8), :],
            ],
            axis=0,
        )
        full = jnp.concatenate([both, jnp.zeros((TILE - 16, TILE), F32)], axis=0)
        return jnp.transpose(full)

    carry[...] = jnp.zeros_like(carry)

    def forward(i, _):
        r0 = pl.multiple_of(i * TILE, TILE)
        rows = pl.ds(r0, TILE)
        for j in range(4):
            lanes = slice(j * TILE, (j + 1) * TILE)
            block = xp[pl.ds(r0, TILE + 8), lanes]
            taps, bias = weights(j)
            pre = bias + taps[0] * shifted(block, 0)
            for k in range(1, 4):
                pre = pre + taps[k] * shifted(block, k)
            sig = 1.0 / (1.0 + jnp.exp(-pre))
            act[rows, lanes] = (pre * sig).astype(BF)
            slope[rows, lanes] = sig * (1.0 + pre * (1.0 - sig))
        cols = columns(i)
        end = []
        for j in range(2):
            lanes = slice(j * TILE, (j + 1) * TILE)
            step = jnp.where(half_lane, cols[:, 2 * j : 2 * j + 1], cols[:, 2 * j + 1 : 2 * j + 2])
            ds = jnp.where(half_lane, cols[:, 8 + 2 * j : 9 + 2 * j], cols[:, 9 + 2 * j : 10 + 2 * j])
            last = ds[TILE - 1 : TILE, :]
            grow = jnp.exp(ds)
            toend = jnp.exp(last - ds)
            step_e[rows, lanes] = step
            toend_e[rows, lanes] = toend
            exp_e[rows, lanes] = grow
            end.append(jnp.exp(last))
            scaled = (act[rows, lanes].astype(F32) * step).astype(BF)
            scaled_s[rows, lanes] = scaled
            weighted_s[rows, lanes] = (scaled.astype(F32) * toend).astype(BF)
            sgrad_s[rows, lanes] = (dp[rows, lanes].astype(F32) * grow).astype(BF)
        in_map = act[rows, 2 * TILE : 3 * TILE]
        out_map = act[rows, 3 * TILE : 4 * TILE]
        local = mm(in_map, weighted_s[rows, :], TN)
        sg_s[i] = mm(out_map, sgrad_s[rows, :], TN)
        h_s[i] = carry[...]
        carry[...] = carry[...] * jnp.concatenate(end, axis=1) + local
        return 0

    lax.fori_loop(0, chunks, forward, 0)

    carry[...] = jnp.zeros_like(carry)
    tap_acc[...] = jnp.zeros_like(tap_acc)
    skip_acc[...] = jnp.zeros_like(skip_acc)
    alog_acc[...] = jnp.zeros_like(alog_acc)
    ddt_acc[...] = jnp.zeros_like(ddt_acc)

    def head_sums(x, j):
        pick = (row8 == 2 * j + lane8 // 64).astype(BF)
        hi = x.astype(BF)
        lo = (x - hi.astype(F32)).astype(BF)
        return mm(pick, hi, NT) + mm(pick, lo, NT)

    def eights(x):
        return jnp.sum(x.reshape(x.shape[0] // 8, 8, x.shape[1]), axis=0)

    def backward(n, _):
        i = chunks - 1 - n
        r0 = pl.multiple_of(i * TILE, TILE)
        rows = pl.ds(r0, TILE)
        at8 = pl.ds(pl.multiple_of(8 * i, 8), 8)
        in_map = act[rows, 2 * TILE : 3 * TILE]
        out_map = act[rows, 3 * TILE : 4 * TILE]
        h_in = h_s[i]
        carried = carry[...]
        h_low = h_in.astype(BF)
        c_low = carried.astype(BF)
        off = mm(out_map, h_low)
        gw = mm(in_map, c_low)
        out_grad = mm(sgrad_s[rows, :], h_low, NT)
        in_grad = mm(weighted_s[rows, :], c_low, NT)
        score = mm(in_map, out_map, NT)
        end = exp_e[pl.ds(r0 + TILE - 8, 8), :][7:8, :]
        ends = jnp.sum(h_in * carried, axis=0, keepdims=True) * end
        carry[...] = sg_s[i] + carried * end
        cols = columns(i)
        ds8 = ds_r[at8, :]
        grad_score = jnp.zeros((TILE, TILE), F32)
        gsum = jnp.zeros((8, TILE), F32)
        back = jnp.zeros((8, TILE), F32)
        stepsum = jnp.zeros((8, TILE), F32)
        end_sum = jnp.zeros((8, TILE), F32)
        rcol = jnp.zeros((TILE, TILE), F32)
        for j in range(2):
            lanes = slice(j * TILE, (j + 1) * TILE)
            sc = scaled_s[rows, lanes]
            dy = dp[rows, lanes]
            diag = jnp.zeros((TILE, TILE), F32)
            for e in range(2):
                h = 2 * j + e
                part = half_lane if e == 0 else jnp.logical_not(half_lane)
                gm = mm(jnp.where(part, sc, jnp.zeros_like(sc)), dy, NT)
                spread = ds8[h : h + 1, :] - cols[:, 8 + h : 9 + h]
                decay = jnp.exp(jnp.where(seen, spread, -1e30))
                gd = gm * decay
                grad_score = grad_score + gd
                both = gd * score
                rcol = jnp.where(col_q == h, jnp.sum(both, axis=1, keepdims=True), rcol)
                gsum = gsum + jnp.where(row8 == h, jnp.sum(both, axis=0, keepdims=True), 0.0)
                mix = (score * decay).astype(BF)
                diag = diag + mm(mix, jnp.where(part, dy, jnp.zeros_like(dy)))
            dyf = dy.astype(F32)
            scf = sc.astype(F32)
            sigf = act[rows, lanes].astype(F32)
            gwe = gw[:, lanes] * toend_e[rows, lanes]
            grad_scaled = gwe + diag
            gsum = gsum + head_sums(dyf * exp_e[rows, lanes] * off[:, lanes], j)
            back = back + head_sums(gwe * scf, j)
            stepsum = stepsum + head_sums(grad_scaled * sigf, j)
            end_sum = end_sum + head_sums(jnp.broadcast_to(ends[:, lanes], (TILE, TILE)), j)
            skip_acc[:, lanes] += eights(dyf * sigf)
            grad_sig = skip_row[j] * dyf + grad_scaled * step_e[rows, lanes]
            gp[rows, lanes] = grad_sig * slope[rows, lanes]
        gs = grad_score.astype(BF)
        gp[rows, 2 * TILE : 3 * TILE] = (in_grad + mm(gs, out_map)) * slope[rows, 2 * TILE : 3 * TILE]
        gp[rows, 3 * TILE : 4 * TILE] = (out_grad + mm(gs, in_map, TN)) * slope[
            rows, 3 * TILE : 4 * TILE
        ]
        gsum = gsum - jnp.transpose(rcol)[0:8, :]
        grad_log = mm_f32(jnp.concatenate([gsum, back], axis=1), tail_sums) + end_sum
        step8 = step_r[at8, :]
        ddt = jnp.where(used8, (grad_log * rate8 + stepsum) * sig_r[at8, :], 0.0)
        ddt_r[at8, :] = ddt
        ddt_acc[...] += ddt
        alog_acc[...] += grad_log * step8
        for j in range(4):
            lanes = slice(j * TILE, (j + 1) * TILE)
            grads = jnp.concatenate([gp[rows, lanes], after[:, lanes]], axis=0)
            block = xp[pl.ds(r0, TILE + 8), lanes]
            taps, bias = weights(j)
            here = grads[0:TILE]
            after[:, lanes] = here[0:8]
            raw = taps[3] * here
            for k in range(3):
                raw = raw + taps[k] * pltpu.roll(grads, 5 + k, 0)[8:]
            for k in range(4):
                tap_acc[k, :, lanes] += eights(here * shifted(block, k))
            tap_acc[4, :, lanes] += eights(here)
            out = raw.astype(BF)
            for e in range(2):
                b = 2 * i + e
                s = jnp.where(b < 8, b, 15 - b)
                o = jnp.where(b < 8, 0, 64)
                out_ref[s, pl.ds(pl.multiple_of(j * TILE + o, 64), 64), :] = out[
                    e * 64 : (e + 1) * 64
                ]
        return 0

    lax.fori_loop(0, chunks, backward, 0)

    rows = []
    for j in range(4):
        lanes = slice(j * TILE, (j + 1) * TILE)
        for k in range(5):
            rows.append(jnp.sum(tap_acc[k, :, lanes], axis=0, keepdims=True))
    alog = jnp.sum(alog_acc[...] * rate8, axis=1, keepdims=True)
    ddtb = jnp.sum(ddt_acc[...], axis=1, keepdims=True)
    skips = jnp.zeros((8, TILE), F32)
    for j in range(2):
        total = jnp.sum(skip_acc[:, j * TILE : (j + 1) * TILE], axis=0, keepdims=True)
        for e in range(2):
            part = jnp.sum(jnp.where(lane_row // 64 == e, total, 0.0), axis=1, keepdims=True)
            skips = jnp.where(row8 == 2 * j + e, part, skips)
    trio = jnp.where(lane8 == 0, alog, jnp.where(lane8 == 1, ddtb, skips))
    trio = jnp.where(lane8 < 3, trio, 0.0)
    params = jnp.concatenate(rows + [jnp.zeros((4, TILE), F32), trio], axis=0) * scale
    p_hi, p_lo, _ = split3(params)
    param_rows = jnp.concatenate([p_hi, p_lo], axis=0)
    for s in range(8):
        low = ddt_r[8 * (s // 2) : 8 * (s // 2) + 8, :]
        up_chunk = (15 - s) // 2
        high = ddt_r[8 * up_chunk : 8 * up_chunk + 8, :]
        if s % 2 == 1:
            low = pltpu.roll(low, 64, 1)
        if (15 - s) % 2 == 0:
            high = pltpu.roll(high, 64, 1)
        here = jnp.where(lane8 < 64, low, high)
        hi, mid, lo = split3(here)
        both = hi.astype(F32) + pltpu.roll(mid.astype(F32), 4, 0)
        out_ref[s, 4 * TILE : 4 * TILE + 16, :] = jnp.concatenate(
            [both, lo.astype(F32)], axis=0
        ).astype(BF)
        out_ref[s, 4 * TILE + 16 : 4 * TILE + 80, :] = param_rows


def unpack_kernel(y_ref, dsig_ref, ddt_ref, taps_ref, bias_ref, trio_ref, one_ref, two_ref):
    fsdp_place = lax.axis_index("fsdp")
    even = lax.rem(fsdp_place, 2) == 0
    row8 = ids((8, TILE), 0)
    dt_rows = []
    trios = []
    for c in range(8):
        for j in range(2):
            lanes = slice((2 * c + j) * TILE, (2 * c + j + 1) * TILE)
            dsig_ref[:, lanes] = y_ref[c, j * TILE : (j + 1) * TILE, :].astype(F32)
        packed = y_ref[c, 4 * TILE : 4 * TILE + 16, :].astype(F32)
        top = packed[0:8]
        value = jnp.where(row8 < 4, top + pltpu.roll(top, 4, 0) + packed[8:16], 0.0)
        if c % 2 == 0:
            dt_rows.append(value)
        else:
            dt_rows[-1] = dt_rows[-1] + pltpu.roll(value, 4, 0)
        params = y_ref[c, 4 * TILE + 16 : 4 * TILE + 48, :].astype(F32) + y_ref[
            c, 4 * TILE + 48 : 4 * TILE + 80, :
        ].astype(F32)
        for j in range(2):
            lanes = slice((2 * c + j) * TILE, (2 * c + j + 1) * TILE)
            taps_ref[0:4, lanes] = params[5 * j : 5 * j + 4]
            bias_ref[0:1, lanes] = params[5 * j + 4 : 5 * j + 5]
        trio = params[24:32]
        if c % 2 == 0:
            trios.append(jnp.where(row8 < 4, trio, 0.0))
        else:
            trios[-1] = trios[-1] + jnp.where(row8 >= 4, pltpu.roll(trio, 4, 0), 0.0)
    full = jnp.concatenate(dt_rows + [jnp.zeros((TILE - 32, TILE), F32)], axis=0)
    ddt_ref[...] = jnp.transpose(full)[:, 0:32]
    full = jnp.concatenate(trios + [jnp.zeros((TILE - 32, TILE), F32)], axis=0)
    trio_ref[...] = jnp.transpose(full)[0:8, :]
    for g in range(2):
        lanes = slice(g * TILE, (g + 1) * TILE)
        sums = []
        for j in range(2):
            main = jnp.zeros((TILE, TILE), F32)
            param = jnp.zeros((32, TILE), F32)
            for c in range(4 * g, 4 * g + 4):
                main = main + y_ref[c, (2 + j) * TILE : (3 + j) * TILE, :].astype(F32)
                param = (
                    param
                    + y_ref[c, 4 * TILE + 16 : 4 * TILE + 48, :].astype(F32)
                    + y_ref[c, 4 * TILE + 48 : 4 * TILE + 80, :].astype(F32)
                )
            five = jnp.zeros((8, TILE), F32)
            for k in range(5):
                five = jnp.where(row8 == k, param[10 + 5 * j + k : 11 + 5 * j + k], five)
            sums.append((main, five))
        one_ref[0:TILE, lanes] = jnp.where(even, sums[0][0], sums[1][0])
        one_ref[TILE : TILE + 8, lanes] = jnp.where(even, sums[0][1], sums[1][1])
        two_ref[0:TILE, lanes] = jnp.where(even, sums[1][0], sums[0][0])
        two_ref[TILE : TILE + 8, lanes] = jnp.where(even, sums[1][1], sums[0][1])


ROUTE_ONE = [(0, 0), (2, 1), (1, 2), (3, 3)]
ROUTE_TWO = [(0, 2), (2, 3), (1, 0), (3, 1)]


def shards_whole(
    sig_raw,
    map_raw,
    step_size_logits,
    d_out,
    sig_taps,
    map_taps,
    sig_bias,
    map_bias,
    a_log,
    dt_bias,
    skip_gain,
):
    ctx = lax.axis_size("ctx")
    fsdp = lax.axis_size("fsdp")
    rows, sig_width = sig_raw.shape
    owned = map_taps.shape[1]
    params = pltpu.CompilerParams(vmem_limit_bytes=48 * 1024 * 1024)
    vmem = pl.BlockSpec(memory_space=pltpu.VMEM)
    smem = pl.BlockSpec(memory_space=pltpu.SMEM)
    map_params = lax.all_gather(
        jnp.concatenate([map_taps, map_bias[None, :]], axis=0), "fsdp", axis=0
    )
    packed = pl.pallas_call(
        functools.partial(pack_kernel, ctx, rows),
        out_shape=jax.ShapeDtypeStruct((ctx, 6 * TILE + 16, TILE), BF),
        in_specs=[vmem] * 4,
        out_specs=vmem,
        scratch_shapes=[pltpu.VMEM((TILE + 8, TILE), F32)],
        compiler_params=params,
    )(sig_raw, map_raw, step_size_logits, d_out)
    got = lax.all_to_all(packed, "ctx", 0, 0, tiled=True)
    scale = 1.0 / math.sqrt(float(ctx * rows))
    total = ctx * rows
    wide = pltpu.VMEM((total, 2 * TILE), F32)
    narrow = pltpu.VMEM((total, 2 * TILE), BF)
    row64 = pltpu.VMEM((64, TILE), F32)
    done = pl.pallas_call(
        functools.partial(core_kernel, scale),
        out_shape=jax.ShapeDtypeStruct((ctx, 4 * TILE + 80, TILE), BF),
        in_specs=[vmem] * 4 + [smem] * 3,
        out_specs=vmem,
        scratch_shapes=[
            pltpu.VMEM((total + 8, 4 * TILE), F32),
            narrow,
            pltpu.VMEM((total, 4 * TILE), BF),
            pltpu.VMEM((total, 4 * TILE), F32),
            pltpu.VMEM((total + 8, 4 * TILE), F32),
            narrow,
            narrow,
            narrow,
            wide,
            wide,
            wide,
            pltpu.VMEM((8, TILE, 2 * TILE), F32),
            pltpu.VMEM((8, TILE, 2 * TILE), F32),
            pltpu.VMEM((TILE, 2 * TILE), F32),
            row64,
            row64,
            row64,
            row64,
            pltpu.VMEM((5, 8, 4 * TILE), F32),
            pltpu.VMEM((8, 2 * TILE), F32),
            pltpu.VMEM((8, TILE), F32),
            pltpu.VMEM((8, TILE), F32),
            pltpu.VMEM((8, 4 * TILE), F32),
        ],
        compiler_params=params,
    )(got, sig_taps, sig_bias[None, :], map_params, a_log, dt_bias, skip_gain)
    back = lax.all_to_all(done, "ctx", 0, 0, tiled=True)
    d_sig, d_dt, taps, bias, trio, one, two = pl.pallas_call(
        unpack_kernel,
        out_shape=(
            jax.ShapeDtypeStruct((rows, sig_width), F32),
            jax.ShapeDtypeStruct((rows, 32), F32),
            jax.ShapeDtypeStruct((4, sig_width), F32),
            jax.ShapeDtypeStruct((1, sig_width), F32),
            jax.ShapeDtypeStruct((8, TILE), F32),
            jax.ShapeDtypeStruct((TILE + 8, 2 * TILE), F32),
            jax.ShapeDtypeStruct((TILE + 8, 2 * TILE), F32),
        ),
        in_specs=[vmem],
        out_specs=(vmem,) * 7,
        compiler_params=params,
    )(back)
    one = lax.ppermute(one, "fsdp", ROUTE_ONE)
    two = lax.ppermute(two, "fsdp", ROUTE_TWO)
    swap = lax.axis_index("fsdp") >= fsdp // 2
    d_map = jnp.concatenate([jnp.where(swap, two, one), jnp.where(swap, one, two)], axis=1)
    return (
        d_sig,
        d_map[:rows],
        d_dt,
        taps,
        d_map[rows : rows + 4],
        bias[0],
        d_map[rows + 4],
        trio[0, :32],
        trio[1, :32],
        trio[2, :32],
    )


def shards(*args):
    sig_raw, map_raw, step_size_logits = args[:3]
    ctx = lax.axis_size("ctx")
    fsdp = lax.axis_size("fsdp")
    fits = (
        ctx == 8
        and fsdp == 4
        and sig_raw.shape == (TILE, 2048)
        and map_raw.shape == (TILE, 2 * GROUPS * STATE)
        and step_size_logits.shape[1] == 32
    )
    return shards_whole(*args) if fits else shards_chain(*args)


def solution(mesh):
    return jax.shard_map(
        shards,
        mesh=mesh,
        in_specs=(
            P("ctx", "fsdp"),
            P("ctx", None),
            P("ctx", "fsdp"),
            P("ctx", "fsdp"),
            P(None, "fsdp"),
            P(None, "fsdp"),
            P("fsdp"),
            P("fsdp"),
            P("fsdp"),
            P("fsdp"),
            P("fsdp"),
        ),
        out_specs=(
            P("ctx", "fsdp"),
            P("ctx", "fsdp"),
            P("ctx", "fsdp"),
            P(None, "fsdp"),
            P(None, "fsdp"),
            P("fsdp"),
            P("fsdp"),
            P("fsdp"),
            P("fsdp"),
            P("fsdp"),
        ),
        check_vma=False,
    )
```

```python
import functools
import math

import jax
import jax.numpy as jnp
from jax import lax
from jax.experimental import pallas as pl
from jax.experimental.pallas import tpu as pltpu
from jax.sharding import PartitionSpec as P

HEADS = 128
HDIM = 64
STATE = 128
GROUPS = 8


def prefix(part, axis, combine, identity, reverse):
    count = lax.axis_size(axis)
    place = lax.axis_index(axis)
    ahead = count - 1 - place if reverse else place
    gathered = jax.tree.map(lambda a: lax.all_gather(a, axis), part)
    state = jax.tree.map(lambda a, e: jnp.zeros_like(a) + jnp.asarray(e, a.dtype), part, identity)

    def one(lap, state):
        source = count - 1 - lap if reverse else lap
        return combine(
            state, jax.tree.map(lambda a: lax.dynamic_index_in_dim(a, source, 0, False), gathered)
        )

    return lax.fori_loop(0, ahead, one, state)


def broadcast(x, axis, root):
    mine = lax.axis_index(axis) == root
    return lax.psum(jnp.where(mine, x, jnp.zeros_like(x)), axis)


def extended(block, sides, width):
    for axis, dim in sides:
        count = lax.axis_size(axis)
        forward = [(i, i + 1) for i in range(count - 1)]
        backward = [(target, source) for source, target in forward]
        low = lax.ppermute(
            lax.slice_in_dim(block, block.shape[dim] - width, None, axis=dim), axis, forward
        )
        high = lax.ppermute(lax.slice_in_dim(block, 0, width, axis=dim), axis, backward)
        block = jnp.concatenate([low, block, high], axis=dim)
    return block


def ein(form, left, right):
    return jnp.einsum(form, left, right, preferred_element_type=jnp.float32)


def silu_slope(value):
    sig = jax.nn.sigmoid(value)
    return sig * (1.0 + value * (1.0 - sig))


def block_parts(activated, dt_rows, a_log, dt_bias, groups):
    length = activated.shape[0]
    heads = dt_rows.shape[1]
    inner = heads * HDIM
    shared = groups * STATE
    ratio = heads // groups
    signal = activated[:, :inner].reshape(length, heads, HDIM)
    input_map = activated[:, inner : inner + shared].reshape(length, groups, STATE)
    output_map = activated[:, inner + shared :].reshape(length, groups, STATE)
    input_heads = jnp.repeat(input_map, ratio, axis=1)
    output_heads = jnp.repeat(output_map, ratio, axis=1)
    step = jax.nn.softplus(dt_rows + dt_bias)
    rate = -jnp.exp(a_log)
    row_ids = lax.broadcasted_iota(jnp.int32, (length, length), 0)
    col_ids = lax.broadcasted_iota(jnp.int32, (length, length), 1)
    lower = (row_ids >= col_ids).astype(jnp.float32)
    decay_sum = jnp.dot(lower, step * rate, precision=lax.Precision.HIGHEST)
    to_end = jnp.exp(decay_sum[-1][None, :] - decay_sum)
    scaled = (signal.astype(jnp.float32) * step[:, :, None]).astype(jnp.bfloat16)
    weighted = (scaled.astype(jnp.float32) * to_end[:, :, None]).astype(jnp.bfloat16)
    local = ein("qhp,qhn->hpn", weighted, input_heads)
    return (
        signal,
        input_map,
        output_map,
        input_heads,
        output_heads,
        step,
        rate,
        lower,
        decay_sum,
        scaled,
        to_end,
        weighted,
        local,
    )


def entry_grad(parts, d_rows):
    decay_sum = parts[8]
    output_heads = parts[4]
    scaled_grad = (d_rows.astype(jnp.float32) * jnp.exp(decay_sum)[:, :, None]).astype(jnp.bfloat16)
    return (scaled_grad, ein("thp,thn->hpn", scaled_grad, output_heads))


def block_grads(parts, d_rows, scaled_grad, h_in, carried, skip_gain, dt_rows, dt_bias):
    (
        signal,
        input_map,
        output_map,
        input_heads,
        output_heads,
        step,
        rate,
        lower,
        decay_sum,
        scaled,
        to_end,
        weighted,
        local,
    ) = parts
    length = d_rows.shape[0]
    heads = d_rows.shape[1]
    groups = input_map.shape[1]
    width_state = input_map.shape[2]
    ratio = heads // groups
    grad_f = d_rows.astype(jnp.float32)
    signal_f = signal.astype(jnp.float32)
    grad_skip = jnp.sum(grad_f * signal_f, axis=(0, 2))
    h_low = h_in.astype(jnp.bfloat16)
    carried_low = carried.astype(jnp.bfloat16)
    offset = jnp.exp(decay_sum)[:, :, None] * ein("thn,hpn->thp", output_heads, h_low)
    grad_sum = jnp.sum(grad_f * offset, axis=2)
    out_heads_grad = ein("thp,hpn->thn", scaled_grad, h_low)
    grad_weighted = ein("shn,hpn->shp", input_heads, carried_low)
    in_heads_grad = ein("shp,hpn->shn", weighted, carried_low)
    back = jnp.sum(grad_weighted * scaled.astype(jnp.float32), axis=2) * to_end
    end_term = jnp.exp(decay_sum[-1]) * jnp.sum(h_in * carried, axis=(1, 2))
    last_row = (lax.broadcasted_iota(jnp.int32, (length, 1), 0) == length - 1).astype(jnp.float32)
    grad_sum = grad_sum - back + last_row * (jnp.sum(back, axis=0) + end_term)[None, :]
    spread = decay_sum.T[:, :, None] - decay_sum.T[:, None, :]
    decay = jnp.where(lower[None] > 0, jnp.exp(jnp.minimum(spread, 0.0)), 0.0)
    score = ein("tgn,sgn->gts", output_map, input_map)
    mix = jnp.repeat(score, ratio, axis=0) * decay
    grad_mix = ein("thp,shp->hts", d_rows, scaled)
    grad_scaled = grad_weighted * to_end[:, :, None] + ein(
        "hts,thp->shp", mix.astype(jnp.bfloat16), d_rows
    )
    product = grad_mix * mix
    grad_sum = grad_sum + (jnp.sum(product, axis=2) - jnp.sum(product, axis=1)).T
    grad_score = jnp.sum((grad_mix * decay).reshape(groups, ratio, length, length), axis=1).astype(
        jnp.bfloat16
    )
    grad_outmap = ein("gts,sgn->tgn", grad_score, input_map) + jnp.sum(
        out_heads_grad.reshape(length, groups, ratio, width_state), axis=2
    )
    grad_in = ein("gts,tgn->sgn", grad_score, output_map) + jnp.sum(
        in_heads_grad.reshape(length, groups, ratio, width_state), axis=2
    )
    grad_log = jnp.dot(lower.T, grad_sum, precision=lax.Precision.HIGHEST)
    descent_increment = grad_log * rate + jnp.sum(grad_scaled * signal_f, axis=2)
    grad_signal = skip_gain[None, :, None] * grad_f + grad_scaled * step[:, :, None]
    grad_dt = descent_increment * jax.nn.sigmoid(dt_rows + dt_bias)
    decay_log_gradient = jnp.sum(grad_log * step, axis=0) * rate
    grad_act = jnp.concatenate(
        [
            grad_signal.reshape(length, heads * HDIM),
            grad_in.reshape(length, groups * width_state),
            grad_outmap.reshape(length, groups * width_state),
        ],
        axis=1,
    )
    return (grad_act, grad_dt, decay_log_gradient, jnp.sum(grad_dt, axis=0), grad_skip)


def link(earlier, later):
    return (earlier[0] + later[0], jnp.exp(later[0])[:, None, None] * earlier[1] + later[1])


def link_blocks(lower_pair, upper_pair):
    zero_rate = jnp.zeros_like(lower_pair[0])
    zero_state = jnp.zeros_like(lower_pair[1])
    below = prefix(lower_pair, "ctx", link, (zero_rate, zero_state), False)
    beyond = prefix(upper_pair, "ctx", link, (zero_rate, zero_state), True)
    total = jax.tree.map(
        lambda part: broadcast(part, "ctx", lax.axis_size("ctx") - 1), link(below, lower_pair)
    )
    return jnp.stack([below[1], link(total, beyond)[1]])


def conv_back(grad_pre, wide_grad, kernel_taps, padded, at_end, length):
    rim = kernel_taps.shape[0] - 1
    after = jnp.stack(
        [jnp.where(at_end, grad_pre[1, :rim], wide_grad[3 * rim : 4 * rim]), wide_grad[0:rim]]
    )
    padded_next = jnp.concatenate([grad_pre, after], axis=1)
    grad_raw = jnp.zeros(grad_pre.shape, jnp.float32)
    for tap in range(rim + 1):
        grad_raw = (
            grad_raw
            + kernel_taps[tap][None, None, :] * padded_next[:, rim - tap : rim - tap + length]
        )
    tap_grads = jnp.stack(
        [jnp.sum(grad_pre * padded[:, tap : tap + length], axis=(0, 1)) for tap in range(rim + 1)]
    )
    return (grad_raw, tap_grads, jnp.sum(grad_pre, axis=(0, 1)))


def first_rows(grad_pre, rim):
    return jnp.concatenate([grad_pre[0, :rim], grad_pre[1, :rim]], axis=0)


def shards_chain(
    sig_raw,
    map_raw,
    step_size_logits,
    d_out,
    sig_taps,
    map_taps,
    sig_bias,
    map_bias,
    a_log,
    dt_bias,
    skip_gain,
):
    all_map_taps, all_map_bias = (
        lax.all_gather(map_taps, "fsdp", axis=1, tiled=True),
        lax.all_gather(map_bias, "fsdp", axis=0, tiled=True),
    )
    kernel_taps = jnp.concatenate([sig_taps, all_map_taps], axis=1)
    kernel_bias = jnp.concatenate([sig_bias, all_map_bias], axis=0)
    kernel = kernel_taps.shape[0]
    rim = kernel - 1
    length = sig_raw.shape[0] // 2
    sig_width = sig_raw.shape[1]
    map_width = map_raw.shape[1]
    width = sig_width + map_width
    heads_here = step_size_logits.shape[1]
    ratio = HEADS // GROUPS
    group_count = max(1, heads_here // ratio)
    first_group = lax.axis_index("fsdp") * heads_here // ratio
    fsdp_count = lax.axis_size("fsdp")
    owned = map_width // fsdp_count
    map_start = lax.axis_index("fsdp") * owned
    raw_rows = jnp.concatenate([sig_raw, map_raw], axis=1).reshape(2, length, width)
    tails = jnp.concatenate([raw_rows[1, length - rim :], raw_rows[0, length - rim :]], axis=0)
    wide = extended(tails, (("ctx", 0),), rim)
    at_end = lax.axis_index("ctx") == lax.axis_size("ctx") - 1
    before = jnp.stack(
        [wide[0:rim], jnp.where(at_end, raw_rows[0, length - rim :], wide[3 * rim : 4 * rim])]
    )
    padded = jnp.concatenate([before, raw_rows], axis=1).astype(jnp.float32)
    preact = kernel_bias[None, None, :] + jnp.zeros((2, length, width), jnp.float32)
    for tap in range(kernel):
        preact = preact + kernel_taps[tap][None, None, :] * padded[:, tap : tap + length]
    activated = jax.nn.silu(preact).astype(jnp.bfloat16)
    maps_all = activated[:, :, sig_width:].reshape(2, length, 2, GROUPS, STATE)
    maps_mine = lax.dynamic_slice_in_dim(maps_all, first_group, group_count, 3)
    local_act = jnp.concatenate(
        [activated[:, :, :sig_width], maps_mine.reshape(2, length, 2 * group_count * STATE)], axis=2
    )
    dt_rows = step_size_logits.reshape(2, length, heads_here)
    grad_rows = d_out.reshape(2, length, heads_here, HDIM)

    def parts_of(act_block, dt_block):
        return block_parts(act_block, dt_block, a_log, dt_bias, group_count)

    parts = jax.vmap(parts_of)(local_act, dt_rows)
    scaled_grad, state_grad = jax.vmap(entry_grad)(parts, grad_rows)
    ends = parts[8][:, -1]
    h_ins = link_blocks((ends[0], parts[12][0]), (ends[1], parts[12][1]))
    carried_pair = link_blocks((ends[1], state_grad[1]), (ends[0], state_grad[0]))
    carried = jnp.stack([carried_pair[1], carried_pair[0]])
    grad_act, grad_dt, decay_log_gradient, grad_dtb, grad_skip = jax.vmap(
        block_grads, in_axes=(0, 0, 0, 0, 0, None, 0, None)
    )(parts, grad_rows, scaled_grad, h_ins, carried, skip_gain, dt_rows, dt_bias)
    slope = silu_slope(preact)
    grad_pre_sig = grad_act[:, :, :sig_width] * slope[:, :, :sig_width]
    grad_mine = grad_act[:, :, sig_width:].reshape(2, length, 2, group_count, STATE)
    zero_index = jnp.zeros((), jnp.int32)
    placed = lax.dynamic_update_slice(
        jnp.zeros((2, length, 2, GROUPS, STATE), jnp.float32),
        grad_mine,
        (zero_index, zero_index, zero_index, first_group, zero_index),
    )
    map_term = placed.reshape(2, length, map_width)
    map_owned = lax.psum_scatter(map_term, "fsdp", scatter_dimension=2, tiled=True)
    map_slope = lax.dynamic_slice_in_dim(slope[:, :, sig_width:], map_start, owned, 2)
    grad_pre = jnp.concatenate([grad_pre_sig, map_owned * map_slope], axis=2)
    own_taps = jnp.concatenate([sig_taps, map_taps], axis=1)
    own_padded = jnp.concatenate(
        [
            padded[:, :, :sig_width],
            lax.dynamic_slice_in_dim(padded[:, :, sig_width:], map_start, owned, 2),
        ],
        axis=2,
    )
    wide_grad = extended(first_rows(grad_pre, rim), (("ctx", 0),), rim)
    grad_raw, tap_grads, bias_grads = conv_back(
        grad_pre, wide_grad, own_taps, own_padded, at_end, length
    )
    map_raw_grad = grad_raw[:, :, sig_width:]
    map_tap_grad = tap_grads[:, sig_width:]
    map_bias_grad = bias_grads[sig_width:]
    sig_raw_grad = grad_raw[:, :, :sig_width]
    sig_tap_grad = tap_grads[:, :sig_width]
    sig_bias_grad = bias_grads[:sig_width]
    reduced = lax.psum(
        (
            sig_tap_grad,
            map_tap_grad,
            sig_bias_grad,
            map_bias_grad,
            jnp.sum(decay_log_gradient, axis=0),
            jnp.sum(grad_dtb, axis=0),
            jnp.sum(grad_skip, axis=0),
        ),
        "ctx",
    )
    scale = 1.0 / math.sqrt(float(lax.axis_size("ctx") * 2 * length))
    final = jax.tree.map(lambda grad_part: grad_part * scale, reduced)
    return (
        sig_raw_grad.reshape(2 * length, sig_width),
        map_raw_grad.reshape(2 * length, owned),
        grad_dt.reshape(2 * length, heads_here),
        final[0],
        final[1],
        final[2],
        final[3],
        final[4],
        final[5],
        final[6],
    )


TILE = 128
HALF = 64
NT = (((1,), (1,)), ((), ()))
TN = (((0,), (0,)), ((), ()))
NN = (((1,), (0,)), ((), ()))
BF = jnp.bfloat16
F32 = jnp.float32


def mm(a, b, dims=NN):
    return lax.dot_general(a, b, dims, preferred_element_type=F32)


def mm_f32(a, b, dims=NN):
    return lax.dot_general(a, b, dims, precision=lax.Precision.HIGHEST, preferred_element_type=F32)


def split3(x):
    hi = x.astype(BF)
    rest = x - hi.astype(F32)
    mid = rest.astype(BF)
    return hi, mid, (rest - mid.astype(F32)).astype(BF)


def ids(shape, dim):
    return lax.broadcasted_iota(jnp.int32, shape, dim)


def lanes_of(j):
    return slice(j * TILE, (j + 1) * TILE)


def place():
    ctx_place = lax.axis_index("ctx")
    quad = lax.div(ctx_place, 4)
    return quad, lax.rem(ctx_place, 4), lax.axis_index("fsdp")


def at_tile(start, width=TILE):
    return pl.ds(pl.multiple_of(start, TILE), width)


def pack_kernel(sig_ref, map_ref, dt_ref, dy_ref, *rest):
    x_refs, halo_refs, (dt_rows, sems) = rest[:4], rest[4:8], rest[8:]
    quad, r, f = place()
    copies = []

    def send(source, target):
        copy = pltpu.make_async_copy(source, target, sems.at[len(copies)])
        copy.start()
        copies.append(copy)

    half = map_ref.shape[1] // 2
    for k in (1, 2, 3, 0):
        dest = lax.bitwise_xor(r, k)
        x = x_refs[k]
        cols = at_tile(dest * 4 * TILE, 4 * TILE)
        send(sig_ref.at[:, cols], x.at[0:TILE, :])
        send(dy_ref.at[:, cols], x.at[TILE : 2 * TILE, :])
        group = (2 * f + lax.div(dest, 2)) * TILE
        for j in range(2):
            for e in range(2):
                send(
                    map_ref.at[e * HALF : (e + 1) * HALF, at_tile(group + j * half)],
                    x.at[2 * TILE : 2 * TILE + HALF, lanes_of(2 * j + e)],
                )
    for m in range(4):
        dest = jnp.where(quad == 0, m, 3 - m)
        rows = pl.ds(pl.multiple_of(jnp.where(quad == 0, HALF - 16, TILE - 16), 16), 16)
        send(sig_ref.at[rows, at_tile(dest * 4 * TILE, 4 * TILE)], halo_refs[m].at[:, 0 : 4 * TILE])
        group = (2 * f + lax.div(dest, 2)) * TILE
        for j in range(2):
            send(map_ref.at[rows, at_tile(group + j * half)], halo_refs[m].at[:, lanes_of(4 + j)])
    for k in range(4):
        dest = lax.bitwise_xor(r, k)
        hi, mid, lo = split3(dt_ref[pl.ds(pl.multiple_of(8 * dest, 8), 8), :])
        zero = jnp.zeros((8, TILE), F32)
        dt_rows[k, :, 0:TILE] = jnp.concatenate([hi.astype(F32), mid.astype(F32)], axis=0).astype(BF)
        dt_rows[k, :, TILE : 2 * TILE] = jnp.concatenate([lo.astype(F32), zero], axis=0).astype(BF)
        dt_rows[k, :, 2 * TILE : 4 * TILE] = jnp.zeros((16, 2 * TILE), BF)
        send(dt_rows.at[k], x_refs[k].at[2 * TILE + HALF : 2 * TILE + HALF + 16, :])
    for copy in copies:
        copy.wait()


def tap_rows(j, taps_ref, bias_ref, mtaps_ref):
    quad, r, f = place()
    if j < 4:
        at = at_tile((4 * r + j) * TILE)
        return [taps_ref[k : k + 1, at] for k in range(4)], bias_ref[0:1, at]
    group = 2 * f + lax.div(r, 2)
    owner = 2 * (j - 4) + lax.div(f, 2)
    at = at_tile(lax.rem(group, 4) * TILE)
    return [mtaps_ref[owner, k : k + 1, at] for k in range(4)], mtaps_ref[owner, 4:5, at]


def shifted(block, k):
    return block[8:] if k == 3 else pltpu.roll(block, 3 - k, 0)[8:]


def columns(*rows8):
    total = 8 * len(rows8)
    full = jnp.concatenate(list(rows8) + [jnp.zeros((TILE - total, TILE), F32)], axis=0)
    return jnp.transpose(full)


def head_row(ref, r):
    row8 = ids((8, TILE), 0)
    out = jnp.zeros((8, TILE), F32)
    for h in range(8):
        out = jnp.where(row8 == h, ref[8 * r + h], out)
    return out


def first_kernel(
    x0,
    x1,
    x2,
    x3,
    b0,
    b1,
    b2,
    b3,
    taps_ref,
    bias_ref,
    mtaps_ref,
    alog_ref,
    dtb_ref,
    mid_ref,
    xp,
    dp,
    act,
    slope,
    scaled_s,
    weighted_s,
    sgrad_s,
    step_e,
    toend_e,
    exp_e,
    s_s,
    t_s,
    step_r,
    ds_r,
    sig_r,
    dt_src,
):
    quad, r, f = place()
    high = quad == 1
    half_lane = ids((TILE, TILE), 1) < HALF
    lane8 = ids((8, TILE), 1)
    for k, x in enumerate((x0, x1, x2, x3)):
        s = lax.bitwise_xor(r, k)
        low_at = pl.multiple_of(HALF * s, HALF)
        up_at = pl.multiple_of(HALF * (3 - s), HALF)
        for e, at in ((0, low_at), (1, up_at)):
            here = slice(e * HALF, (e + 1) * HALF)
            rows = pl.ds(pl.multiple_of(8 + at, 8), HALF)
            xp[e, rows, 0 : 4 * TILE] = x[here, :].astype(F32)
            for j in range(2):
                xp[e, rows, lanes_of(4 + j)] = x[
                    2 * TILE : 2 * TILE + HALF, lanes_of(2 * j + e)
                ].astype(F32)
            dp[pl.ds(pl.multiple_of(2 * TILE * e + at, HALF), HALF), :] = x[
                TILE + e * HALF : TILE + (e + 1) * HALF, :
            ]
        packed = x[2 * TILE + HALF : 2 * TILE + HALF + 16, 0 : 2 * TILE].astype(F32)
        dt_src[s] = packed[0:8, 0:TILE] + packed[8:16, 0:TILE] + packed[0:8, TILE : 2 * TILE]
    edge = jnp.zeros((8, 6 * TILE), F32)
    for b in (b0, b1, b2, b3):
        edge = edge + b[...].astype(F32)[8:16]
    xp[0, 0:8, :] = jnp.where(high, edge, 0.0)
    xp[1, 0:8, :] = jnp.where(high, xp[0, 2 * TILE : 2 * TILE + 8, :], edge)

    rate8 = -jnp.exp(head_row(alog_ref, r))
    bias8 = head_row(dtb_ref, r)
    for i in range(4):
        if i < 2:
            a, b = dt_src[2 * i], pltpu.roll(dt_src[2 * i + 1], HALF, 1)
        else:
            a, b = pltpu.roll(dt_src[7 - 2 * i], HALF, 1), dt_src[6 - 2 * i]
        logits = jnp.where(lane8 < HALF, a, b) + bias8
        small = jnp.exp(-jnp.abs(logits))
        step = jnp.maximum(logits, 0.0) + jnp.log1p(small)
        at8 = slice(8 * i, 8 * i + 8)
        step_r[at8, :] = step
        sig_r[at8, :] = jnp.where(logits >= 0, 1.0, small) / (1.0 + small)
        ds_r[at8, :] = step * rate8
    upto = (ids((TILE, TILE), 0) <= ids((TILE, TILE), 1)).astype(F32)
    ds_r[...] = mm_f32(ds_r[...], upto)

    ends = []
    for i in range(4):
        rows = slice(i * TILE, (i + 1) * TILE)
        base = (i % 2) * TILE
        for j in range(6):
            lanes = lanes_of(j)
            block = xp[i // 2, base : base + TILE + 8, lanes]
            taps, bias = tap_rows(j, taps_ref, bias_ref, mtaps_ref)
            pre = bias + taps[0] * shifted(block, 0)
            for k in range(1, 4):
                pre = pre + taps[k] * shifted(block, k)
            sig = 1.0 / (1.0 + jnp.exp(-pre))
            act[rows, lanes] = (pre * sig).astype(BF)
            slope[rows, lanes] = sig * (1.0 + pre * (1.0 - sig))
        cols = columns(step_r[8 * i : 8 * i + 8, :], ds_r[8 * i : 8 * i + 8, :])
        end = []
        for j in range(4):
            lanes = lanes_of(j)
            step = jnp.where(half_lane, cols[:, 2 * j : 2 * j + 1], cols[:, 2 * j + 1 : 2 * j + 2])
            ds = jnp.where(
                half_lane, cols[:, 8 + 2 * j : 9 + 2 * j], cols[:, 9 + 2 * j : 10 + 2 * j]
            )
            last = ds[TILE - 1 : TILE, :]
            grow = jnp.exp(ds)
            toend = jnp.exp(last - ds)
            step_e[rows, lanes] = step
            toend_e[rows, lanes] = toend
            exp_e[rows, lanes] = grow
            end.append(jnp.exp(last))
            scaled = (act[rows, lanes].astype(F32) * step).astype(BF)
            scaled_s[rows, lanes] = scaled
            weighted_s[rows, lanes] = (scaled.astype(F32) * toend).astype(BF)
            sgrad_s[rows, lanes] = (dp[rows, lanes].astype(F32) * grow).astype(BF)
        ends.append(jnp.concatenate(end, axis=1))
        s_s[i] = mm(act[rows, lanes_of(4)], weighted_s[rows, :], TN)
        t_s[i] = mm(act[rows, lanes_of(5)], sgrad_s[rows, :], TN)
    f_a = ends[1] * s_s[0] + s_s[1]
    f_b = ends[3] * s_s[2] + s_s[3]
    g_a = t_s[0] + ends[0] * t_s[1]
    g_b = t_s[2] + ends[2] * t_s[3]
    d_a = ends[0] * ends[1]
    d_b = ends[2] * ends[3]
    mid_ref[0:TILE, :] = jnp.where(high, d_b * f_a + f_b, f_a).astype(BF)
    mid_ref[TILE : 2 * TILE, :] = jnp.where(high, g_a + d_a * g_b, g_b).astype(BF)
    hi, mid, lo = split3(jnp.broadcast_to(d_a * d_b, (16, 4 * TILE)))
    row16 = ids((16, 4 * TILE), 0)
    parts = jnp.where(
        row16 == 0,
        hi.astype(F32),
        jnp.where(row16 == 1, mid.astype(F32), jnp.where(row16 == 2, lo.astype(F32), 0.0)),
    )
    mid_ref[2 * TILE : 2 * TILE + 16, :] = parts.astype(BF)


def second_kernel(dp, act, scaled_s, ds_r, diag_ref, gmap_ref, gsum_ref):
    half_lane = ids((TILE, TILE), 1) < HALF
    row8 = ids((8, TILE), 0)
    col_q = ids((TILE, TILE), 1)
    seen = ids((TILE, TILE), 0) <= col_q
    for i in range(4):
        rows = slice(i * TILE, (i + 1) * TILE)
        in_map = act[rows, lanes_of(4)]
        out_map = act[rows, lanes_of(5)]
        score = mm(in_map, out_map, NT)
        ds8 = ds_r[8 * i : 8 * i + 8, :]
        cols = columns(ds8)
        grad_score = jnp.zeros((TILE, TILE), F32)
        gsum = jnp.zeros((8, TILE), F32)
        rcol = jnp.zeros((TILE, TILE), F32)
        for j in range(4):
            sc = scaled_s[rows, lanes_of(j)]
            dy = dp[rows, lanes_of(j)]
            diag = jnp.zeros((TILE, TILE), F32)
            for e in range(2):
                h = 2 * j + e
                part = half_lane if e == 0 else jnp.logical_not(half_lane)
                gm = mm(jnp.where(part, sc, jnp.zeros_like(sc)), dy, NT)
                spread = ds8[h : h + 1, :] - cols[:, h : h + 1]
                decay = jnp.exp(jnp.where(seen, spread, -1e30))
                gd = gm * decay
                grad_score = grad_score + gd
                both = gd * score
                rcol = jnp.where(col_q == h, jnp.sum(both, axis=1, keepdims=True), rcol)
                gsum = gsum + jnp.where(row8 == h, jnp.sum(both, axis=0, keepdims=True), 0.0)
                mix = (score * decay).astype(BF)
                diag = diag + mm(mix, jnp.where(part, dy, jnp.zeros_like(dy)))
            diag_ref[rows, lanes_of(j)] = diag
        gs = grad_score.astype(BF)
        gmap_ref[rows, lanes_of(0)] = mm(gs, out_map)
        gmap_ref[rows, lanes_of(1)] = mm(gs, in_map, TN)
        gsum_ref[8 * i : 8 * i + 8, :] = gsum - jnp.transpose(rcol)[0:8, :]


def eights(x):
    return jnp.sum(x.reshape(x.shape[0] // 8, 8, x.shape[1]), axis=0)


def third_kernel(
    scale,
    mid_ref,
    xp,
    dp,
    act,
    slope,
    scaled_s,
    weighted_s,
    sgrad_s,
    step_e,
    toend_e,
    exp_e,
    s_s,
    t_s,
    step_r,
    ds_r,
    sig_r,
    diag_ref,
    gmap_ref,
    gsum_ref,
    taps_ref,
    bias_ref,
    mtaps_ref,
    alog_ref,
    skip_ref,
    y0,
    y1,
    y2,
    y3,
    cross_ref,
    h_s,
    c_s,
    gp,
    dx,
    blk,
):
    quad, r, f = place()
    high = quad == 1
    lane_row = ids((1, TILE), 1)
    row8 = ids((8, TILE), 0)
    lane8 = ids((8, TILE), 1)
    rate8 = -jnp.exp(head_row(alog_ref, r))
    ends = [exp_e[(i + 1) * TILE - 8 : (i + 1) * TILE, :][7:8, :] for i in range(4)]
    f_in = mid_ref[0:TILE, :].astype(F32)
    g_in = mid_ref[TILE : 2 * TILE, :].astype(F32)
    across = jnp.sum(mid_ref[2 * TILE : 2 * TILE + 16, :].astype(F32), axis=0, keepdims=True)
    f_a = ends[1] * s_s[0] + s_s[1]
    h_s[0] = jnp.where(high, f_in, 0.0)
    h_s[1] = ends[0] * h_s[0] + s_s[0]
    h_s[2] = jnp.where(high, ends[1] * h_s[1] + s_s[1], across * f_a + f_in)
    h_s[3] = ends[2] * h_s[2] + s_s[2]
    g_b = t_s[2] + ends[2] * t_s[3]
    c_s[3] = jnp.where(high, g_in, 0.0)
    c_s[2] = t_s[3] + ends[3] * c_s[3]
    c_s[1] = jnp.where(high, t_s[2] + ends[2] * c_s[2], g_in + across * g_b)
    c_s[0] = t_s[1] + ends[1] * c_s[1]

    row_q = ids((TILE, TILE), 0)
    col_q = ids((TILE, TILE), 1)
    tail_sums = jnp.concatenate(
        [(row_q >= col_q).astype(F32), (row_q < col_q).astype(F32)], axis=0
    )
    skip_row = []
    for j in range(4):
        at = 8 * r + 2 * j
        skip_row.append(jnp.where(lane_row < HALF, skip_ref[at], skip_ref[at + 1]))

    def head_sums(x, j):
        pick = (row8 == 2 * j + lane8 // HALF).astype(BF)
        hi = x.astype(BF)
        lo = (x - hi.astype(F32)).astype(BF)
        return mm(pick, hi, NT) + mm(pick, lo, NT)

    taps_of = [tap_rows(j, taps_ref, bias_ref, mtaps_ref)[0] for j in range(6)]
    after = [jnp.zeros((8, TILE), F32) for _ in range(6)]
    tap_acc = [[jnp.zeros((8, TILE), F32) for _ in range(5)] for _ in range(6)]
    skip_acc = [jnp.zeros((8, TILE), F32) for _ in range(4)]
    alog_acc = jnp.zeros((8, TILE), F32)
    ddt_acc = jnp.zeros((8, TILE), F32)
    first_low = None
    for i in (3, 2, 1, 0):
        rows = slice(i * TILE, (i + 1) * TILE)
        at8 = slice(8 * i, 8 * i + 8)
        in_map = act[rows, lanes_of(4)]
        out_map = act[rows, lanes_of(5)]
        h_low = h_s[i].astype(BF)
        c_low = c_s[i].astype(BF)
        off = mm(out_map, h_low)
        gw = mm(in_map, c_low)
        out_grad = mm(sgrad_s[rows, :], h_low, NT)
        in_grad = mm(weighted_s[rows, :], c_low, NT)
        end_row = jnp.sum(h_s[i] * c_s[i], axis=0, keepdims=True) * ends[i]
        gsum = gsum_ref[at8, :]
        back = jnp.zeros((8, TILE), F32)
        stepsum = jnp.zeros((8, TILE), F32)
        end_sum = jnp.zeros((8, TILE), F32)
        for j in range(4):
            lanes = lanes_of(j)
            dyf = dp[rows, lanes].astype(F32)
            scf = scaled_s[rows, lanes].astype(F32)
            sigf = act[rows, lanes].astype(F32)
            gwe = gw[:, lanes] * toend_e[rows, lanes]
            grad_scaled = gwe + diag_ref[rows, lanes]
            gsum = gsum + head_sums(dyf * exp_e[rows, lanes] * off[:, lanes], j)
            back = back + head_sums(gwe * scf, j)
            stepsum = stepsum + head_sums(grad_scaled * sigf, j)
            end_sum = end_sum + jnp.where(row8 == 2 * j + lane8 // HALF, end_row[:, lanes], 0.0)
            skip_acc[j] = skip_acc[j] + eights(dyf * sigf)
            grad_sig = skip_row[j] * dyf + grad_scaled * step_e[rows, lanes]
            gp[:, lanes] = grad_sig * slope[rows, lanes]
        gp[:, lanes_of(4)] = (in_grad + gmap_ref[rows, lanes_of(0)]) * slope[rows, lanes_of(4)]
        gp[:, lanes_of(5)] = (out_grad + gmap_ref[rows, lanes_of(1)]) * slope[rows, lanes_of(5)]
        grad_log = mm_f32(jnp.concatenate([gsum, back], axis=1), tail_sums) + jnp.sum(
            end_sum, axis=1, keepdims=True
        )
        ddt = (grad_log * rate8 + stepsum) * sig_r[at8, :]
        blk[2 * i] = ddt
        blk[2 * i + 1] = pltpu.roll(ddt, HALF, 1)
        ddt_acc = ddt_acc + ddt
        alog_acc = alog_acc + grad_log * step_r[at8, :]
        base = (i % 2) * TILE
        starts = []
        for j in range(6):
            lanes = lanes_of(j)
            here = gp[:, lanes]
            grads = jnp.concatenate([here, after[j]], axis=0)
            block = xp[i // 2, base : base + TILE + 8, lanes]
            taps = taps_of[j]
            raw = taps[3] * here
            for k in range(3):
                raw = raw + taps[k] * pltpu.roll(grads, 5 + k, 0)[8:]
            for k in range(4):
                tap_acc[j][k] = tap_acc[j][k] + eights(here * shifted(block, k))
            tap_acc[j][4] = tap_acc[j][4] + eights(here)
            dx[rows, lanes] = raw.astype(BF)
            starts.append(here[0:8])
            after[j] = jnp.where(high, starts[j], 0.0) if i == 2 else starts[j]
        if i == 2:
            first_low = starts
        if i == 0:
            first_high = starts

    for j in range(6):
        first = jnp.where(high, first_high[j], first_low[j])
        grads = jnp.concatenate([jnp.zeros((8, TILE), F32), first], axis=0)
        spill = jnp.zeros((8, TILE), F32)
        for k in range(3):
            spill = spill + taps_of[j][k] * pltpu.roll(grads, 5 + k, 0)[8:]
        starts[j] = spill
    zero8 = jnp.zeros((8, TILE), F32)
    cross_ref[0:16, :] = jnp.concatenate(
        [
            jnp.concatenate(starts[0:4], axis=1),
            jnp.concatenate([starts[4], starts[5], zero8, zero8], axis=1),
        ],
        axis=0,
    ).astype(BF)
    rows = []
    for j in range(6):
        for k in range(5):
            rows.append(jnp.sum(tap_acc[j][k], axis=0, keepdims=True))
    trio = jnp.zeros((TILE, TILE), F32)
    alog = jnp.sum(alog_acc * rate8, axis=1, keepdims=True)
    ddtb = jnp.sum(ddt_acc, axis=1, keepdims=True)
    skips = jnp.zeros((8, TILE), F32)
    for j in range(4):
        total = jnp.sum(skip_acc[j], axis=0, keepdims=True)
        skips = skips + jnp.where(row8 == 2 * j + lane8 // HALF, total, 0.0)
    skips = jnp.sum(skips, axis=1, keepdims=True)
    three = jnp.where(lane8 == 0, alog, jnp.where(lane8 == 1, ddtb, skips))
    flat = columns(jnp.where(lane8 < 3, three, 0.0))
    trio = flat[0:1] + pltpu.roll(flat[0:8], 32, 1)[1:2] + pltpu.roll(flat[0:8], 64, 1)[2:3]
    trio = pltpu.roll(jnp.broadcast_to(trio, (8, TILE)), 8 * r, 1)[0:1]
    params = jnp.concatenate(rows + [trio, jnp.zeros((1, TILE), F32)], axis=0) * scale
    p_hi, p_lo, _ = split3(params)
    param_rows = jnp.concatenate([p_hi[0:16], p_hi[16:32], p_lo[0:16], p_lo[16:32]], axis=1)
    cross_ref[16:32, :] = param_rows
    for k, y in enumerate((y0, y1, y2, y3)):
        s = lax.bitwise_xor(r, k)
        low_rows = pl.ds(pl.multiple_of(HALF * s, HALF), HALF)
        up_rows = pl.ds(pl.multiple_of(2 * TILE + HALF * (3 - s), HALF), HALF)
        y[0:HALF, :] = dx[low_rows, 0 : 4 * TILE]
        y[HALF:TILE, :] = dx[up_rows, 0 : 4 * TILE]
        for j in range(2):
            y[TILE : TILE + HALF, lanes_of(2 * j)] = dx[low_rows, lanes_of(4 + j)]
            y[TILE : TILE + HALF, lanes_of(2 * j + 1)] = dx[up_rows, lanes_of(4 + j)]
        here = jnp.where(lane8 < HALF, blk[s], pltpu.roll(blk[7 - s], HALF, 1))
        hi, mid, lo = split3(here)
        top = jnp.concatenate([hi.astype(F32), mid.astype(F32)], axis=0)
        low = jnp.concatenate([lo.astype(F32), zero8], axis=0)
        y[TILE + HALF : TILE + HALF + 16, :] = jnp.concatenate(
            [top, low, jnp.zeros((16, 2 * TILE), F32)], axis=1
        ).astype(BF)
        y[TILE + HALF + 16 : TILE + HALF + 32, :] = param_rows


def whole_params(ref, start):
    value = ref[start : start + 16, :].astype(F32)
    return jnp.concatenate(
        [
            value[:, lanes_of(0)] + value[:, lanes_of(2)],
            value[:, lanes_of(1)] + value[:, lanes_of(3)],
        ],
        axis=0,
    )


PARAMS_AT = TILE + HALF + 16


def maps_kernel(y0, y1, y2, y3, z0, z1, z2, z3, one_ref, two_ref):
    quad, r, f = place()
    ys, zs = (y0, y1, y2, y3), (z0, z1, z2, z3)
    even = lax.rem(f, 2) == 0
    own = lax.div(r, 2)
    row8 = ids((8, TILE), 0)
    third = jnp.logical_and(quad == 0, r == 3)
    fourth = jnp.logical_and(quad == 1, r == 0)
    for pair in range(2):
        group = own if pair == 0 else 1 - own
        lanes = at_tile(group * TILE)
        sums = []
        for j in range(2):
            halves = []
            for e in range(2):
                total = jnp.zeros((HALF, TILE), F32)
                spill = jnp.zeros((8, TILE), F32)
                for k in (2 * pair, 2 * pair + 1):
                    total = total + ys[k][TILE : TILE + HALF, lanes_of(2 * j + e)].astype(F32)
                    spill = spill + zs[k][0:16, lanes_of(j)].astype(F32)[8:16]
                here = third if e == 0 else fourth
                spill = jnp.where(here, spill, 0.0)
                halves += [total[0 : HALF - 8], total[HALF - 8 : HALF] + spill]
            five = jnp.zeros((8, TILE), F32)
            for k in (2 * pair, 2 * pair + 1):
                for ref, start in ((ys[k], PARAMS_AT), (zs[k], 16)):
                    param = whole_params(ref, start)
                    for t in range(5):
                        five = five + jnp.where(row8 == t, param[20 + 5 * j + t : 21 + 5 * j + t], 0.0)
            sums.append(jnp.concatenate(halves + [five], axis=0))
        one_ref[:, lanes] = jnp.where(even, sums[0], sums[1])
        two_ref[:, lanes] = jnp.where(even, sums[1], sums[0])


def rows_kernel(y0, y1, y2, y3, z0, z1, z2, z3, dsig_ref, ddt_ref, taps_ref, bias_ref, trio_ref):
    quad, r, f = place()
    third = jnp.logical_and(quad == 0, r == 3)
    fourth = jnp.logical_and(quad == 1, r == 0)
    trio = jnp.zeros((1, TILE), F32)
    for k, (y, z) in enumerate(((y0, z0), (y1, z1), (y2, z2), (y3, z3))):
        s = lax.bitwise_xor(r, k)
        cols = at_tile(s * 4 * TILE, 4 * TILE)
        dsig_ref[:, cols] = y[0:TILE, :].astype(F32)
        spill = z[0:16, :].astype(F32)[0:8]
        dsig_ref[HALF - 8 : HALF, cols] += jnp.where(third, spill, 0.0)
        dsig_ref[TILE - 8 : TILE, cols] += jnp.where(fourth, spill, 0.0)
        packed = y[TILE + HALF : TILE + HALF + 16, 0 : 2 * TILE].astype(F32)
        ddt_ref[pl.ds(pl.multiple_of(8 * s, 8), 8), :] = (
            packed[0:8, 0:TILE] + packed[8:16, 0:TILE] + packed[0:8, TILE : 2 * TILE]
        )
        params = whole_params(y, PARAMS_AT) + whole_params(z, 16)
        for j in range(4):
            lanes = at_tile((4 * s + j) * TILE)
            taps_ref[0:4, lanes] = params[5 * j : 5 * j + 4]
            bias_ref[0:1, lanes] = params[5 * j + 4 : 5 * j + 5]
        trio = trio + params[30:31]
    trio_ref[...] = jnp.broadcast_to(trio, (8, TILE))


ROUTE_ONE = [(0, 0), (2, 1), (1, 2), (3, 3)]
ROUTE_TWO = [(0, 2), (2, 3), (1, 0), (3, 1)]


def shards_quad(
    sig_raw,
    map_raw,
    step_size_logits,
    d_out,
    sig_taps,
    map_taps,
    sig_bias,
    map_bias,
    a_log,
    dt_bias,
    skip_gain,
):
    ctx = lax.axis_size("ctx")
    fsdp = lax.axis_size("fsdp")
    rows, sig_width = sig_raw.shape
    vmem = pl.BlockSpec(memory_space=pltpu.VMEM)
    smem = pl.BlockSpec(memory_space=pltpu.SMEM)
    any_space = pl.BlockSpec(memory_space=pl.ANY)

    def call(kernel, out_shape, in_specs, out_specs, scratch, mib, cost):
        return pl.pallas_call(
            kernel,
            out_shape=out_shape,
            in_specs=in_specs,
            out_specs=out_specs,
            scratch_shapes=scratch,
            compiler_params=pltpu.CompilerParams(vmem_limit_bytes=mib * 1024 * 1024),
            cost_estimate=pl.CostEstimate(flops=cost, bytes_accessed=cost // 100, transcendentals=0),
        )

    def shape(*dims, kind=F32):
        return jax.ShapeDtypeStruct(dims, kind)

    inside = [[(c, c ^ k) for c in range(ctx)] for k in range(4)]
    over = [[(c, c ^ 4 ^ k) for c in range(ctx)] for k in range(4)]
    x_rows = 2 * TILE + HALF + 16
    packed = call(
        pack_kernel,
        (shape(x_rows, 4 * TILE, kind=BF),) * 4 + (shape(16, 6 * TILE, kind=BF),) * 4,
        [any_space, any_space, vmem, any_space],
        (any_space,) * 8,
        [pltpu.VMEM((4, 16, 4 * TILE), BF), pltpu.SemaphoreType.DMA((40,))],
        16,
        10**6,
    )(sig_raw, map_raw, step_size_logits.T, d_out)
    xs = [packed[0]] + [lax.ppermute(packed[k], "ctx", inside[k]) for k in (1, 2, 3)]
    halos = [lax.ppermute(packed[4 + m], "ctx", [(3, 4 + m), (4, 3 - m)]) for m in range(4)]
    map_params = lax.all_gather(
        jnp.concatenate([map_taps, map_bias[None, :]], axis=0), "fsdp", axis=0
    )
    total = 4 * TILE
    mid, *kept = call(
        first_kernel,
        (
            shape(2 * TILE + 16, 4 * TILE, kind=BF),
            shape(2, 2 * TILE + 8, 6 * TILE),
            shape(total, 4 * TILE, kind=BF),
            shape(total, 6 * TILE, kind=BF),
            shape(total, 6 * TILE),
            shape(total, 4 * TILE, kind=BF),
            shape(total, 4 * TILE, kind=BF),
            shape(total, 4 * TILE, kind=BF),
            shape(total, 4 * TILE),
            shape(total, 4 * TILE),
            shape(total, 4 * TILE),
            shape(4, TILE, 4 * TILE),
            shape(4, TILE, 4 * TILE),
            shape(32, TILE),
            shape(32, TILE),
            shape(32, TILE),
        ),
        [vmem] * 11 + [smem] * 2,
        (vmem,) * 16,
        [pltpu.VMEM((4, 8, TILE), F32)],
        24,
        10**9,
    )(*xs, *halos, sig_taps, sig_bias[None, :], map_params, a_log, dt_bias)
    xp, dp, act, slope, scaled, weighted, sgrad, step_e, toend_e, exp_e, s_s, t_s = kept[:12]
    step_r, ds_r, sig_r = kept[12:]
    mid = lax.ppermute(mid, "ctx", over[0])
    diag, gmap, gsum = call(
        second_kernel,
        (shape(total, 4 * TILE), shape(total, 2 * TILE), shape(32, TILE)),
        [vmem] * 4,
        (vmem,) * 3,
        [],
        16,
        10**9,
    )(dp, act, scaled, ds_r)
    scale = 1.0 / math.sqrt(float(ctx * rows))
    y_rows = TILE + HALF + 32
    *ys, cross = call(
        functools.partial(third_kernel, scale),
        (shape(y_rows, 4 * TILE, kind=BF),) * 4 + (shape(32, 4 * TILE, kind=BF),),
        [vmem] * 22 + [smem] * 2,
        (vmem,) * 5,
        [
            pltpu.VMEM((4, TILE, 4 * TILE), F32),
            pltpu.VMEM((4, TILE, 4 * TILE), F32),
            pltpu.VMEM((TILE, 6 * TILE), F32),
            pltpu.VMEM((total, 6 * TILE), BF),
            pltpu.VMEM((8, 8, TILE), F32),
        ],
        32,
        10**9,
    )(
        mid,
        *kept,
        diag,
        gmap,
        gsum,
        sig_taps,
        sig_bias[None, :],
        map_params,
        a_log,
        skip_gain,
    )
    ys = [ys[0]] + [lax.ppermute(ys[k], "ctx", inside[k]) for k in (1, 2, 3)]
    zs = [lax.ppermute(cross, "ctx", over[k]) for k in range(4)]
    one, two = call(
        maps_kernel,
        (shape(TILE + 8, 2 * TILE), shape(TILE + 8, 2 * TILE)),
        [vmem] * 8,
        (vmem,) * 2,
        [],
        16,
        10**6,
    )(*ys, *zs)
    one = lax.ppermute(one, "fsdp", ROUTE_ONE)
    two = lax.ppermute(two, "fsdp", ROUTE_TWO)
    d_sig, d_dt, taps, bias, trio = call(
        rows_kernel,
        (
            shape(rows, sig_width),
            shape(32, TILE),
            shape(4, sig_width),
            shape(1, sig_width),
            shape(8, TILE),
        ),
        [vmem] * 8,
        (vmem,) * 5,
        [],
        16,
        10**8,
    )(*ys, *zs)
    swap = lax.axis_index("fsdp") >= fsdp // 2
    d_map = jnp.concatenate([jnp.where(swap, two, one), jnp.where(swap, one, two)], axis=1)
    return (
        d_sig,
        d_map[:rows],
        d_dt.T,
        taps,
        d_map[rows : rows + 4],
        bias[0],
        d_map[rows + 4],
        trio[0, 0:32],
        trio[0, 32:64],
        trio[0, 64:96],
    )


def shards(*args):
    sig_raw, map_raw, step_size_logits = args[:3]
    ctx = lax.axis_size("ctx")
    fsdp = lax.axis_size("fsdp")
    fits = (
        ctx == 8
        and fsdp == 4
        and sig_raw.shape == (TILE, 2048)
        and map_raw.shape == (TILE, 2 * GROUPS * STATE)
        and step_size_logits.shape[1] == 32
    )
    return shards_quad(*args) if fits else shards_chain(*args)


def solution(mesh):
    return jax.shard_map(
        shards,
        mesh=mesh,
        in_specs=(
            P("ctx", "fsdp"),
            P("ctx", None),
            P("ctx", "fsdp"),
            P("ctx", "fsdp"),
            P(None, "fsdp"),
            P(None, "fsdp"),
            P("fsdp"),
            P("fsdp"),
            P("fsdp"),
            P("fsdp"),
            P("fsdp"),
        ),
        out_specs=(
            P("ctx", "fsdp"),
            P("ctx", "fsdp"),
            P("ctx", "fsdp"),
            P(None, "fsdp"),
            P(None, "fsdp"),
            P("fsdp"),
            P("fsdp"),
            P("fsdp"),
            P("fsdp"),
            P("fsdp"),
        ),
        check_vma=False,
    )
```

```python
import functools
import math

import jax
import jax.numpy as jnp
from jax import lax
from jax.experimental import pallas as pl
from jax.experimental.pallas import tpu as pltpu
from jax.sharding import PartitionSpec as P

HEADS = 128
HDIM = 64
STATE = 128
GROUPS = 8


def prefix(part, axis, combine, identity, reverse):
    count = lax.axis_size(axis)
    place = lax.axis_index(axis)
    ahead = count - 1 - place if reverse else place
    gathered = jax.tree.map(lambda a: lax.all_gather(a, axis), part)
    state = jax.tree.map(lambda a, e: jnp.zeros_like(a) + jnp.asarray(e, a.dtype), part, identity)

    def one(lap, state):
        source = count - 1 - lap if reverse else lap
        return combine(
            state, jax.tree.map(lambda a: lax.dynamic_index_in_dim(a, source, 0, False), gathered)
        )

    return lax.fori_loop(0, ahead, one, state)


def broadcast(x, axis, root):
    mine = lax.axis_index(axis) == root
    return lax.psum(jnp.where(mine, x, jnp.zeros_like(x)), axis)


def extended(block, sides, width):
    for axis, dim in sides:
        count = lax.axis_size(axis)
        forward = [(i, i + 1) for i in range(count - 1)]
        backward = [(target, source) for source, target in forward]
        low = lax.ppermute(
            lax.slice_in_dim(block, block.shape[dim] - width, None, axis=dim), axis, forward
        )
        high = lax.ppermute(lax.slice_in_dim(block, 0, width, axis=dim), axis, backward)
        block = jnp.concatenate([low, block, high], axis=dim)
    return block


def ein(form, left, right):
    return jnp.einsum(form, left, right, preferred_element_type=jnp.float32)


def silu_slope(value):
    sig = jax.nn.sigmoid(value)
    return sig * (1.0 + value * (1.0 - sig))


def block_parts(activated, dt_rows, a_log, dt_bias, groups):
    length = activated.shape[0]
    heads = dt_rows.shape[1]
    inner = heads * HDIM
    shared = groups * STATE
    ratio = heads // groups
    signal = activated[:, :inner].reshape(length, heads, HDIM)
    input_map = activated[:, inner : inner + shared].reshape(length, groups, STATE)
    output_map = activated[:, inner + shared :].reshape(length, groups, STATE)
    input_heads = jnp.repeat(input_map, ratio, axis=1)
    output_heads = jnp.repeat(output_map, ratio, axis=1)
    step = jax.nn.softplus(dt_rows + dt_bias)
    rate = -jnp.exp(a_log)
    row_ids = lax.broadcasted_iota(jnp.int32, (length, length), 0)
    col_ids = lax.broadcasted_iota(jnp.int32, (length, length), 1)
    lower = (row_ids >= col_ids).astype(jnp.float32)
    decay_sum = jnp.dot(lower, step * rate, precision=lax.Precision.HIGHEST)
    to_end = jnp.exp(decay_sum[-1][None, :] - decay_sum)
    scaled = (signal.astype(jnp.float32) * step[:, :, None]).astype(jnp.bfloat16)
    weighted = (scaled.astype(jnp.float32) * to_end[:, :, None]).astype(jnp.bfloat16)
    local = ein("qhp,qhn->hpn", weighted, input_heads)
    return (
        signal,
        input_map,
        output_map,
        input_heads,
        output_heads,
        step,
        rate,
        lower,
        decay_sum,
        scaled,
        to_end,
        weighted,
        local,
    )


def entry_grad(parts, d_rows):
    decay_sum = parts[8]
    output_heads = parts[4]
    scaled_grad = (d_rows.astype(jnp.float32) * jnp.exp(decay_sum)[:, :, None]).astype(jnp.bfloat16)
    return (scaled_grad, ein("thp,thn->hpn", scaled_grad, output_heads))


def block_grads(parts, d_rows, scaled_grad, h_in, carried, skip_gain, dt_rows, dt_bias):
    (
        signal,
        input_map,
        output_map,
        input_heads,
        output_heads,
        step,
        rate,
        lower,
        decay_sum,
        scaled,
        to_end,
        weighted,
        local,
    ) = parts
    length = d_rows.shape[0]
    heads = d_rows.shape[1]
    groups = input_map.shape[1]
    width_state = input_map.shape[2]
    ratio = heads // groups
    grad_f = d_rows.astype(jnp.float32)
    signal_f = signal.astype(jnp.float32)
    grad_skip = jnp.sum(grad_f * signal_f, axis=(0, 2))
    h_low = h_in.astype(jnp.bfloat16)
    carried_low = carried.astype(jnp.bfloat16)
    offset = jnp.exp(decay_sum)[:, :, None] * ein("thn,hpn->thp", output_heads, h_low)
    grad_sum = jnp.sum(grad_f * offset, axis=2)
    out_heads_grad = ein("thp,hpn->thn", scaled_grad, h_low)
    grad_weighted = ein("shn,hpn->shp", input_heads, carried_low)
    in_heads_grad = ein("shp,hpn->shn", weighted, carried_low)
    back = jnp.sum(grad_weighted * scaled.astype(jnp.float32), axis=2) * to_end
    end_term = jnp.exp(decay_sum[-1]) * jnp.sum(h_in * carried, axis=(1, 2))
    last_row = (lax.broadcasted_iota(jnp.int32, (length, 1), 0) == length - 1).astype(jnp.float32)
    grad_sum = grad_sum - back + last_row * (jnp.sum(back, axis=0) + end_term)[None, :]
    spread = decay_sum.T[:, :, None] - decay_sum.T[:, None, :]
    decay = jnp.where(lower[None] > 0, jnp.exp(jnp.minimum(spread, 0.0)), 0.0)
    score = ein("tgn,sgn->gts", output_map, input_map)
    mix = jnp.repeat(score, ratio, axis=0) * decay
    grad_mix = ein("thp,shp->hts", d_rows, scaled)
    grad_scaled = grad_weighted * to_end[:, :, None] + ein(
        "hts,thp->shp", mix.astype(jnp.bfloat16), d_rows
    )
    product = grad_mix * mix
    grad_sum = grad_sum + (jnp.sum(product, axis=2) - jnp.sum(product, axis=1)).T
    grad_score = jnp.sum((grad_mix * decay).reshape(groups, ratio, length, length), axis=1).astype(
        jnp.bfloat16
    )
    grad_outmap = ein("gts,sgn->tgn", grad_score, input_map) + jnp.sum(
        out_heads_grad.reshape(length, groups, ratio, width_state), axis=2
    )
    grad_in = ein("gts,tgn->sgn", grad_score, output_map) + jnp.sum(
        in_heads_grad.reshape(length, groups, ratio, width_state), axis=2
    )
    grad_log = jnp.dot(lower.T, grad_sum, precision=lax.Precision.HIGHEST)
    descent_increment = grad_log * rate + jnp.sum(grad_scaled * signal_f, axis=2)
    grad_signal = skip_gain[None, :, None] * grad_f + grad_scaled * step[:, :, None]
    grad_dt = descent_increment * jax.nn.sigmoid(dt_rows + dt_bias)
    decay_log_gradient = jnp.sum(grad_log * step, axis=0) * rate
    grad_act = jnp.concatenate(
        [
            grad_signal.reshape(length, heads * HDIM),
            grad_in.reshape(length, groups * width_state),
            grad_outmap.reshape(length, groups * width_state),
        ],
        axis=1,
    )
    return (grad_act, grad_dt, decay_log_gradient, jnp.sum(grad_dt, axis=0), grad_skip)


def link(earlier, later):
    return (earlier[0] + later[0], jnp.exp(later[0])[:, None, None] * earlier[1] + later[1])


def link_blocks(lower_pair, upper_pair):
    zero_rate = jnp.zeros_like(lower_pair[0])
    zero_state = jnp.zeros_like(lower_pair[1])
    below = prefix(lower_pair, "ctx", link, (zero_rate, zero_state), False)
    beyond = prefix(upper_pair, "ctx", link, (zero_rate, zero_state), True)
    total = jax.tree.map(
        lambda part: broadcast(part, "ctx", lax.axis_size("ctx") - 1), link(below, lower_pair)
    )
    return jnp.stack([below[1], link(total, beyond)[1]])


def conv_back(grad_pre, wide_grad, kernel_taps, padded, at_end, length):
    rim = kernel_taps.shape[0] - 1
    after = jnp.stack(
        [jnp.where(at_end, grad_pre[1, :rim], wide_grad[3 * rim : 4 * rim]), wide_grad[0:rim]]
    )
    padded_next = jnp.concatenate([grad_pre, after], axis=1)
    grad_raw = jnp.zeros(grad_pre.shape, jnp.float32)
    for tap in range(rim + 1):
        grad_raw = (
            grad_raw
            + kernel_taps[tap][None, None, :] * padded_next[:, rim - tap : rim - tap + length]
        )
    tap_grads = jnp.stack(
        [jnp.sum(grad_pre * padded[:, tap : tap + length], axis=(0, 1)) for tap in range(rim + 1)]
    )
    return (grad_raw, tap_grads, jnp.sum(grad_pre, axis=(0, 1)))


def first_rows(grad_pre, rim):
    return jnp.concatenate([grad_pre[0, :rim], grad_pre[1, :rim]], axis=0)


def shards_chain(
    sig_raw,
    map_raw,
    step_size_logits,
    d_out,
    sig_taps,
    map_taps,
    sig_bias,
    map_bias,
    a_log,
    dt_bias,
    skip_gain,
):
    all_map_taps, all_map_bias = (
        lax.all_gather(map_taps, "fsdp", axis=1, tiled=True),
        lax.all_gather(map_bias, "fsdp", axis=0, tiled=True),
    )
    kernel_taps = jnp.concatenate([sig_taps, all_map_taps], axis=1)
    kernel_bias = jnp.concatenate([sig_bias, all_map_bias], axis=0)
    kernel = kernel_taps.shape[0]
    rim = kernel - 1
    length = sig_raw.shape[0] // 2
    sig_width = sig_raw.shape[1]
    map_width = map_raw.shape[1]
    width = sig_width + map_width
    heads_here = step_size_logits.shape[1]
    ratio = HEADS // GROUPS
    group_count = max(1, heads_here // ratio)
    first_group = lax.axis_index("fsdp") * heads_here // ratio
    fsdp_count = lax.axis_size("fsdp")
    owned = map_width // fsdp_count
    map_start = lax.axis_index("fsdp") * owned
    raw_rows = jnp.concatenate([sig_raw, map_raw], axis=1).reshape(2, length, width)
    tails = jnp.concatenate([raw_rows[1, length - rim :], raw_rows[0, length - rim :]], axis=0)
    wide = extended(tails, (("ctx", 0),), rim)
    at_end = lax.axis_index("ctx") == lax.axis_size("ctx") - 1
    before = jnp.stack(
        [wide[0:rim], jnp.where(at_end, raw_rows[0, length - rim :], wide[3 * rim : 4 * rim])]
    )
    padded = jnp.concatenate([before, raw_rows], axis=1).astype(jnp.float32)
    preact = kernel_bias[None, None, :] + jnp.zeros((2, length, width), jnp.float32)
    for tap in range(kernel):
        preact = preact + kernel_taps[tap][None, None, :] * padded[:, tap : tap + length]
    activated = jax.nn.silu(preact).astype(jnp.bfloat16)
    maps_all = activated[:, :, sig_width:].reshape(2, length, 2, GROUPS, STATE)
    maps_mine = lax.dynamic_slice_in_dim(maps_all, first_group, group_count, 3)
    local_act = jnp.concatenate(
        [activated[:, :, :sig_width], maps_mine.reshape(2, length, 2 * group_count * STATE)], axis=2
    )
    dt_rows = step_size_logits.reshape(2, length, heads_here)
    grad_rows = d_out.reshape(2, length, heads_here, HDIM)

    def parts_of(act_block, dt_block):
        return block_parts(act_block, dt_block, a_log, dt_bias, group_count)

    parts = jax.vmap(parts_of)(local_act, dt_rows)
    scaled_grad, state_grad = jax.vmap(entry_grad)(parts, grad_rows)
    ends = parts[8][:, -1]
    h_ins = link_blocks((ends[0], parts[12][0]), (ends[1], parts[12][1]))
    carried_pair = link_blocks((ends[1], state_grad[1]), (ends[0], state_grad[0]))
    carried = jnp.stack([carried_pair[1], carried_pair[0]])
    grad_act, grad_dt, decay_log_gradient, grad_dtb, grad_skip = jax.vmap(
        block_grads, in_axes=(0, 0, 0, 0, 0, None, 0, None)
    )(parts, grad_rows, scaled_grad, h_ins, carried, skip_gain, dt_rows, dt_bias)
    slope = silu_slope(preact)
    grad_pre_sig = grad_act[:, :, :sig_width] * slope[:, :, :sig_width]
    grad_mine = grad_act[:, :, sig_width:].reshape(2, length, 2, group_count, STATE)
    zero_index = jnp.zeros((), jnp.int32)
    placed = lax.dynamic_update_slice(
        jnp.zeros((2, length, 2, GROUPS, STATE), jnp.float32),
        grad_mine,
        (zero_index, zero_index, zero_index, first_group, zero_index),
    )
    map_term = placed.reshape(2, length, map_width)
    map_owned = lax.psum_scatter(map_term, "fsdp", scatter_dimension=2, tiled=True)
    map_slope = lax.dynamic_slice_in_dim(slope[:, :, sig_width:], map_start, owned, 2)
    grad_pre = jnp.concatenate([grad_pre_sig, map_owned * map_slope], axis=2)
    own_taps = jnp.concatenate([sig_taps, map_taps], axis=1)
    own_padded = jnp.concatenate(
        [
            padded[:, :, :sig_width],
            lax.dynamic_slice_in_dim(padded[:, :, sig_width:], map_start, owned, 2),
        ],
        axis=2,
    )
    wide_grad = extended(first_rows(grad_pre, rim), (("ctx", 0),), rim)
    grad_raw, tap_grads, bias_grads = conv_back(
        grad_pre, wide_grad, own_taps, own_padded, at_end, length
    )
    map_raw_grad = grad_raw[:, :, sig_width:]
    map_tap_grad = tap_grads[:, sig_width:]
    map_bias_grad = bias_grads[sig_width:]
    sig_raw_grad = grad_raw[:, :, :sig_width]
    sig_tap_grad = tap_grads[:, :sig_width]
    sig_bias_grad = bias_grads[:sig_width]
    reduced = lax.psum(
        (
            sig_tap_grad,
            map_tap_grad,
            sig_bias_grad,
            map_bias_grad,
            jnp.sum(decay_log_gradient, axis=0),
            jnp.sum(grad_dtb, axis=0),
            jnp.sum(grad_skip, axis=0),
        ),
        "ctx",
    )
    scale = 1.0 / math.sqrt(float(lax.axis_size("ctx") * 2 * length))
    final = jax.tree.map(lambda grad_part: grad_part * scale, reduced)
    return (
        sig_raw_grad.reshape(2 * length, sig_width),
        map_raw_grad.reshape(2 * length, owned),
        grad_dt.reshape(2 * length, heads_here),
        final[0],
        final[1],
        final[2],
        final[3],
        final[4],
        final[5],
        final[6],
    )


TILE = 128
HALF = 64
NT = (((1,), (1,)), ((), ()))
TN = (((0,), (0,)), ((), ()))
NN = (((1,), (0,)), ((), ()))
BF = jnp.bfloat16
F32 = jnp.float32


def mm(a, b, dims=NN):
    return lax.dot_general(a, b, dims, preferred_element_type=F32)


def mm_f32(a, b, dims=NN):
    return lax.dot_general(a, b, dims, precision=lax.Precision.HIGHEST, preferred_element_type=F32)


def split3(x):
    hi = x.astype(BF)
    rest = x - hi.astype(F32)
    mid = rest.astype(BF)
    return hi, mid, (rest - mid.astype(F32)).astype(BF)


def ids(shape, dim):
    return lax.broadcasted_iota(jnp.int32, shape, dim)


def lanes_of(j):
    return slice(j * TILE, (j + 1) * TILE)


def place():
    ctx_place = lax.axis_index("ctx")
    quad = lax.div(ctx_place, 4)
    return quad, lax.rem(ctx_place, 4), lax.axis_index("fsdp")


def at_tile(start, width=TILE):
    return pl.ds(pl.multiple_of(start, TILE), width)


def pack_kernel(sig_ref, map_ref, dt_ref, dy_ref, mtaps_ref, mbias_ref, *rest):
    x_refs, halo_refs, tap_ref, (dt_in, sems) = rest[:4], rest[4:8], rest[8], rest[9:]
    quad, r, f = place()
    copies = []
    dt_copy = pltpu.make_async_copy(dt_ref, dt_in, sems.at[36])
    dt_copy.start()

    def send(source, target):
        copy = pltpu.make_async_copy(source, target, sems.at[len(copies)])
        copy.start()
        copies.append(copy)

    half = map_ref.shape[1] // 2
    for k in (1, 2, 3, 0):
        dest = lax.bitwise_xor(r, k)
        x = x_refs[k]
        cols = at_tile(dest * 4 * TILE, 4 * TILE)
        send(sig_ref.at[:, cols], x.at[0:TILE, :])
        send(dy_ref.at[:, cols], x.at[TILE : 2 * TILE, :])
        group = (2 * f + lax.div(dest, 2)) * TILE
        for j in range(2):
            for e in range(2):
                send(
                    map_ref.at[e * HALF : (e + 1) * HALF, at_tile(group + j * half)],
                    x.at[2 * TILE : 2 * TILE + HALF, lanes_of(2 * j + e)],
                )
    for m in range(4):
        dest = jnp.where(quad == 0, m, 3 - m)
        rows = pl.ds(pl.multiple_of(jnp.where(quad == 0, HALF - 16, TILE - 16), 16), 16)
        send(sig_ref.at[rows, at_tile(dest * 4 * TILE, 4 * TILE)], halo_refs[m].at[:, 0 : 4 * TILE])
        group = (2 * f + lax.div(dest, 2)) * TILE
        for j in range(2):
            send(map_ref.at[rows, at_tile(group + j * half)], halo_refs[m].at[:, lanes_of(4 + j)])
    tap_ref[0:4, :] = mtaps_ref[...]
    tap_ref[4:5, :] = mbias_ref[...]
    tap_ref[5:8, :] = jnp.zeros_like(tap_ref[5:8, :])
    dt_copy.wait()
    zero = jnp.zeros((8, TILE), F32)
    for k in range(4):
        dest = lax.bitwise_xor(r, k)
        hi, mid, lo = split3(dt_in[pl.ds(pl.multiple_of(8 * dest, 8), 8), :])
        top = jnp.concatenate([hi.astype(F32), mid.astype(F32)], axis=0)
        low = jnp.concatenate([lo.astype(F32), zero], axis=0)
        x_refs[k][2 * TILE + HALF : 2 * TILE + HALF + 16, :] = jnp.concatenate(
            [top, low, jnp.zeros((16, 2 * TILE), F32)], axis=1
        ).astype(BF)
    for copy in copies:
        copy.wait()


def tap_rows(j, taps_ref, bias_ref, mtaps_ref):
    quad, r, f = place()
    if j < 4:
        at = at_tile((4 * r + j) * TILE)
        return [taps_ref[k : k + 1, at] for k in range(4)], bias_ref[0:1, at]
    group = 2 * f + lax.div(r, 2)
    owner = 2 * (j - 4) + lax.div(f, 2)
    at = at_tile(lax.rem(group, 4) * TILE)
    return [mtaps_ref[owner, k : k + 1, at] for k in range(4)], mtaps_ref[owner, 4:5, at]


def shifted(block, k):
    return block[8:] if k == 3 else pltpu.roll(block, 3 - k, 0)[8:]


def columns(*rows8):
    total = 8 * len(rows8)
    full = jnp.concatenate(list(rows8) + [jnp.zeros((TILE - total, TILE), F32)], axis=0)
    return jnp.transpose(full)


def head_row(ref, r):
    row8 = ids((8, TILE), 0)
    out = jnp.zeros((8, TILE), F32)
    for h in range(8):
        out = jnp.where(row8 == h, ref[8 * r + h], out)
    return out


def first_kernel(
    x0,
    x1,
    x2,
    x3,
    b0,
    b1,
    b2,
    b3,
    taps_ref,
    bias_ref,
    mtaps_ref,
    alog_ref,
    dtb_ref,
    mid_ref,
    xp,
    dp,
    act,
    slope,
    scaled_s,
    weighted_s,
    sgrad_s,
    step_e,
    toend_e,
    exp_e,
    s_s,
    t_s,
    step_r,
    ds_r,
    sig_r,
    dt_src,
):
    quad, r, f = place()
    high = quad == 1
    half_lane = ids((TILE, TILE), 1) < HALF
    lane8 = ids((8, TILE), 1)
    for k, x in enumerate((x0, x1, x2, x3)):
        s = lax.bitwise_xor(r, k)
        low_at = pl.multiple_of(HALF * s, HALF)
        up_at = pl.multiple_of(HALF * (3 - s), HALF)
        for e, at in ((0, low_at), (1, up_at)):
            here = slice(e * HALF, (e + 1) * HALF)
            rows = pl.ds(pl.multiple_of(8 + at, 8), HALF)
            xp[e, rows, 0 : 4 * TILE] = x[here, :].astype(F32)
            for j in range(2):
                xp[e, rows, lanes_of(4 + j)] = x[
                    2 * TILE : 2 * TILE + HALF, lanes_of(2 * j + e)
                ].astype(F32)
            dp[pl.ds(pl.multiple_of(2 * TILE * e + at, HALF), HALF), :] = x[
                TILE + e * HALF : TILE + (e + 1) * HALF, :
            ]
        packed = x[2 * TILE + HALF : 2 * TILE + HALF + 16, 0 : 2 * TILE].astype(F32)
        dt_src[s] = packed[0:8, 0:TILE] + packed[8:16, 0:TILE] + packed[0:8, TILE : 2 * TILE]
    edge = jnp.zeros((8, 6 * TILE), F32)
    for b in (b0, b1, b2, b3):
        edge = edge + b[...].astype(F32)[8:16]
    xp[0, 0:8, :] = jnp.where(high, edge, 0.0)
    xp[1, 0:8, :] = jnp.where(high, xp[0, 2 * TILE : 2 * TILE + 8, :], edge)

    rate8 = -jnp.exp(head_row(alog_ref, r))
    bias8 = head_row(dtb_ref, r)
    for i in range(4):
        if i < 2:
            a, b = dt_src[2 * i], pltpu.roll(dt_src[2 * i + 1], HALF, 1)
        else:
            a, b = pltpu.roll(dt_src[7 - 2 * i], HALF, 1), dt_src[6 - 2 * i]
        logits = jnp.where(lane8 < HALF, a, b) + bias8
        small = jnp.exp(-jnp.abs(logits))
        step = jnp.maximum(logits, 0.0) + jnp.log1p(small)
        at8 = slice(8 * i, 8 * i + 8)
        step_r[at8, :] = step
        sig_r[at8, :] = jnp.where(logits >= 0, 1.0, small) / (1.0 + small)
        ds_r[at8, :] = step * rate8
    upto = (ids((TILE, TILE), 0) <= ids((TILE, TILE), 1)).astype(F32)
    ds_r[...] = mm_f32(ds_r[...], upto)

    ends = []
    for i in range(4):
        rows = slice(i * TILE, (i + 1) * TILE)
        base = (i % 2) * TILE
        for j in range(6):
            lanes = lanes_of(j)
            block = xp[i // 2, base : base + TILE + 8, lanes]
            taps, bias = tap_rows(j, taps_ref, bias_ref, mtaps_ref)
            pre = bias + taps[0] * shifted(block, 0)
            for k in range(1, 4):
                pre = pre + taps[k] * shifted(block, k)
            sig = 1.0 / (1.0 + jnp.exp(-pre))
            act[rows, lanes] = (pre * sig).astype(BF)
            slope[rows, lanes] = sig * (1.0 + pre * (1.0 - sig))
        cols = columns(step_r[8 * i : 8 * i + 8, :], ds_r[8 * i : 8 * i + 8, :])
        end = []
        for j in range(4):
            lanes = lanes_of(j)
            step = jnp.where(half_lane, cols[:, 2 * j : 2 * j + 1], cols[:, 2 * j + 1 : 2 * j + 2])
            ds = jnp.where(
                half_lane, cols[:, 8 + 2 * j : 9 + 2 * j], cols[:, 9 + 2 * j : 10 + 2 * j]
            )
            last = ds[TILE - 1 : TILE, :]
            grow = jnp.exp(ds)
            toend = jnp.exp(last - ds)
            step_e[rows, lanes] = step
            toend_e[rows, lanes] = toend
            exp_e[rows, lanes] = grow
            end.append(jnp.exp(last))
            scaled = (act[rows, lanes].astype(F32) * step).astype(BF)
            scaled_s[rows, lanes] = scaled
            weighted_s[rows, lanes] = (scaled.astype(F32) * toend).astype(BF)
            sgrad_s[rows, lanes] = (dp[rows, lanes].astype(F32) * grow).astype(BF)
        ends.append(jnp.concatenate(end, axis=1))
        s_s[i] = mm(act[rows, lanes_of(4)], weighted_s[rows, :], TN)
        t_s[i] = mm(act[rows, lanes_of(5)], sgrad_s[rows, :], TN)
    f_a = ends[1] * s_s[0] + s_s[1]
    f_b = ends[3] * s_s[2] + s_s[3]
    g_a = t_s[0] + ends[0] * t_s[1]
    g_b = t_s[2] + ends[2] * t_s[3]
    d_a = ends[0] * ends[1]
    d_b = ends[2] * ends[3]
    mid_ref[0:TILE, :] = jnp.where(high, d_b * f_a + f_b, f_a).astype(BF)
    mid_ref[TILE : 2 * TILE, :] = jnp.where(high, g_a + d_a * g_b, g_b).astype(BF)
    hi, mid, lo = split3(jnp.broadcast_to(d_a * d_b, (16, 4 * TILE)))
    row16 = ids((16, 4 * TILE), 0)
    parts = jnp.where(
        row16 == 0,
        hi.astype(F32),
        jnp.where(row16 == 1, mid.astype(F32), jnp.where(row16 == 2, lo.astype(F32), 0.0)),
    )
    mid_ref[2 * TILE : 2 * TILE + 16, :] = parts.astype(BF)


def second_kernel(dp, act, scaled_s, ds_r, diag_ref, gmap_ref, gsum_ref):
    half_lane = ids((TILE, TILE), 1) < HALF
    row8 = ids((8, TILE), 0)
    col_q = ids((TILE, TILE), 1)
    seen = ids((TILE, TILE), 0) <= col_q
    for i in range(4):
        rows = slice(i * TILE, (i + 1) * TILE)
        in_map = act[rows, lanes_of(4)]
        out_map = act[rows, lanes_of(5)]
        score = mm(in_map, out_map, NT)
        ds8 = ds_r[8 * i : 8 * i + 8, :]
        cols = columns(ds8)
        grad_score = jnp.zeros((TILE, TILE), F32)
        gsum = jnp.zeros((8, TILE), F32)
        rcol = jnp.zeros((TILE, TILE), F32)
        for j in range(4):
            sc = scaled_s[rows, lanes_of(j)]
            dy = dp[rows, lanes_of(j)]
            diag = jnp.zeros((TILE, TILE), F32)
            for e in range(2):
                h = 2 * j + e
                part = half_lane if e == 0 else jnp.logical_not(half_lane)
                gm = mm(jnp.where(part, sc, jnp.zeros_like(sc)), dy, NT)
                spread = ds8[h : h + 1, :] - cols[:, h : h + 1]
                decay = jnp.exp(jnp.where(seen, spread, -1e30))
                gd = gm * decay
                grad_score = grad_score + gd
                both = gd * score
                rcol = jnp.where(col_q == h, jnp.sum(both, axis=1, keepdims=True), rcol)
                gsum = gsum + jnp.where(row8 == h, jnp.sum(both, axis=0, keepdims=True), 0.0)
                mix = (score * decay).astype(BF)
                diag = diag + mm(mix, jnp.where(part, dy, jnp.zeros_like(dy)))
            diag_ref[rows, lanes_of(j)] = diag
        gs = grad_score.astype(BF)
        gmap_ref[rows, lanes_of(0)] = mm(gs, out_map)
        gmap_ref[rows, lanes_of(1)] = mm(gs, in_map, TN)
        gsum_ref[8 * i : 8 * i + 8, :] = gsum - jnp.transpose(rcol)[0:8, :]


def eights(x):
    return jnp.sum(x.reshape(x.shape[0] // 8, 8, x.shape[1]), axis=0)


def end_rows_of(exp_e):
    return [exp_e[(i + 1) * TILE - 8 : (i + 1) * TILE, :][7:8, :] for i in range(4)]


def taps_back(here, after, taps):
    grads = jnp.concatenate([here, after], axis=0)
    raw = taps[3] * here
    for k in range(3):
        raw = raw + taps[k] * pltpu.roll(grads, 5 + k, 0)[8:]
    return raw


def spill_of(first, taps):
    grads = jnp.concatenate([jnp.zeros((8, TILE), F32), first], axis=0)
    spill = jnp.zeros((8, TILE), F32)
    for k in range(3):
        spill = spill + taps[k] * pltpu.roll(grads, 5 + k, 0)[8:]
    return spill


def tap_sums(here, block, sums):
    for k in range(4):
        sums[k] = sums[k] + eights(here * shifted(block, k))
    sums[4] = sums[4] + eights(here)


def maps_kernel(
    mid_ref,
    s_s,
    t_s,
    exp_e,
    act,
    slope,
    weighted_s,
    sgrad_s,
    gmap_ref,
    xp,
    taps_ref,
    bias_ref,
    mtaps_ref,
    one_ref,
    two_ref,
    hlow_ref,
    clow_ref,
    endrow_ref,
    h_s,
    c_s,
):
    quad, r, f = place()
    high = quad == 1
    even = lax.rem(f, 2) == 0
    ends = end_rows_of(exp_e)
    f_in = mid_ref[0:TILE, :].astype(F32)
    g_in = mid_ref[TILE : 2 * TILE, :].astype(F32)
    across = jnp.sum(mid_ref[2 * TILE : 2 * TILE + 16, :].astype(F32), axis=0, keepdims=True)
    f_a = ends[1] * s_s[0] + s_s[1]
    h_s[0] = jnp.where(high, f_in, 0.0)
    h_s[1] = ends[0] * h_s[0] + s_s[0]
    h_s[2] = jnp.where(high, ends[1] * h_s[1] + s_s[1], across * f_a + f_in)
    h_s[3] = ends[2] * h_s[2] + s_s[2]
    g_b = t_s[2] + ends[2] * t_s[3]
    c_s[3] = jnp.where(high, g_in, 0.0)
    c_s[2] = t_s[3] + ends[3] * c_s[3]
    c_s[1] = jnp.where(high, t_s[2] + ends[2] * c_s[2], g_in + across * g_b)
    c_s[0] = t_s[1] + ends[1] * c_s[1]
    taps_of = [tap_rows(4 + j, taps_ref, bias_ref, mtaps_ref)[0] for j in range(2)]
    after = [jnp.zeros((8, TILE), F32) for _ in range(2)]
    sums = [[jnp.zeros((8, TILE), F32) for _ in range(5)] for _ in range(2)]
    first = [None, None]
    end_rows = [None] * 4
    for i in (3, 2, 1, 0):
        rows = slice(i * TILE, (i + 1) * TILE)
        hlow_ref[i] = h_s[i].astype(BF)
        clow_ref[i] = c_s[i].astype(BF)
        end_rows[i] = jnp.sum(h_s[i] * c_s[i], axis=0, keepdims=True) * ends[i]
        grads = (
            mm(weighted_s[rows, :], clow_ref[i], NT) + gmap_ref[rows, lanes_of(0)],
            mm(sgrad_s[rows, :], hlow_ref[i], NT) + gmap_ref[rows, lanes_of(1)],
        )
        base = (i % 2) * TILE
        raws = []
        for j in range(2):
            here = grads[j] * slope[rows, lanes_of(4 + j)]
            raws.append(taps_back(here, after[j], taps_of[j]))
            tap_sums(here, xp[i // 2, base : base + TILE + 8, lanes_of(4 + j)], sums[j])
            start = here[0:8]
            after[j] = jnp.where(high, start, 0.0) if i == 2 else start
            if i == 2:
                first[j] = start
            if i == 0:
                first[j] = jnp.where(high, start, first[j])
        one_ref[rows, :] = jnp.where(even, raws[0], raws[1]).astype(BF)
        two_ref[rows, :] = jnp.where(even, raws[1], raws[0]).astype(BF)
    endrow_ref[...] = jnp.concatenate(end_rows + [jnp.zeros((4, 4 * TILE), F32)], axis=0)
    row8 = ids((8, TILE), 0)
    tails = []
    for j in range(2):
        five = jnp.zeros((8, TILE), F32)
        for t in range(5):
            five = jnp.where(row8 == t, jnp.sum(sums[j][t], axis=0, keepdims=True), five)
        hi, lo, _ = split3(five)
        zero8 = jnp.zeros((8, TILE), F32)
        tails.append(
            jnp.concatenate(
                [spill_of(first[j], taps_of[j]), zero8, hi.astype(F32), lo.astype(F32)], axis=0
            )
        )
    one_ref[4 * TILE : 4 * TILE + 32, :] = jnp.where(even, tails[0], tails[1]).astype(BF)
    two_ref[4 * TILE : 4 * TILE + 32, :] = jnp.where(even, tails[1], tails[0]).astype(BF)


def third_kernel(
    hlow_ref,
    clow_ref,
    endrow_ref,
    xp,
    dp,
    act,
    slope,
    scaled_s,
    step_e,
    toend_e,
    exp_e,
    step_r,
    sig_r,
    diag_ref,
    gsum_ref,
    taps_ref,
    alog_ref,
    skip_ref,
    gp,
    blk,
    spill_ref,
    params_ref,
):
    quad, r, f = place()
    high = quad == 1
    lane_row = ids((1, TILE), 1)
    row8 = ids((8, TILE), 0)
    lane8 = ids((8, TILE), 1)
    rate8 = -jnp.exp(head_row(alog_ref, r))
    row_q = ids((TILE, TILE), 0)
    col_q = ids((TILE, TILE), 1)
    tail_sums = jnp.concatenate(
        [(row_q >= col_q).astype(F32), (row_q < col_q).astype(F32)], axis=0
    )
    skip_row = []
    for j in range(4):
        at = 8 * r + 2 * j
        skip_row.append(jnp.where(lane_row < HALF, skip_ref[at], skip_ref[at + 1]))

    def head_sums(x, j):
        pick = (row8 == 2 * j + lane8 // HALF).astype(BF)
        hi = x.astype(BF)
        lo = (x - hi.astype(F32)).astype(BF)
        return mm(pick, hi, NT) + mm(pick, lo, NT)

    sums = [[jnp.zeros((8, TILE), F32) for _ in range(5)] for _ in range(4)]
    skip_acc = [jnp.zeros((8, TILE), F32) for _ in range(4)]
    alog_acc = jnp.zeros((8, TILE), F32)
    ddt_acc = jnp.zeros((8, TILE), F32)
    for i in range(4):
        rows = slice(i * TILE, (i + 1) * TILE)
        at8 = slice(8 * i, 8 * i + 8)
        base = (i % 2) * TILE
        off = mm(act[rows, lanes_of(5)], hlow_ref[i])
        gw = mm(act[rows, lanes_of(4)], clow_ref[i])
        end_row = endrow_ref[i : i + 1, :]
        gsum = gsum_ref[at8, :]
        back = jnp.zeros((8, TILE), F32)
        stepsum = jnp.zeros((8, TILE), F32)
        end_sum = jnp.zeros((8, TILE), F32)
        for j in range(4):
            lanes = lanes_of(j)
            dyf = dp[rows, lanes].astype(F32)
            scf = scaled_s[rows, lanes].astype(F32)
            sigf = act[rows, lanes].astype(F32)
            gwe = gw[:, lanes] * toend_e[rows, lanes]
            grad_scaled = gwe + diag_ref[rows, lanes]
            gsum = gsum + head_sums(dyf * exp_e[rows, lanes] * off[:, lanes], j)
            back = back + head_sums(gwe * scf, j)
            stepsum = stepsum + head_sums(grad_scaled * sigf, j)
            end_sum = end_sum + jnp.where(row8 == 2 * j + lane8 // HALF, end_row[:, lanes], 0.0)
            skip_acc[j] = skip_acc[j] + eights(dyf * sigf)
            grad_sig = skip_row[j] * dyf + grad_scaled * step_e[rows, lanes]
            here = grad_sig * slope[rows, lanes]
            gp[rows, lanes] = here
            tap_sums(here, xp[i // 2, base : base + TILE + 8, lanes], sums[j])
        grad_log = mm_f32(jnp.concatenate([gsum, back], axis=1), tail_sums) + jnp.sum(
            end_sum, axis=1, keepdims=True
        )
        ddt = (grad_log * rate8 + stepsum) * sig_r[at8, :]
        blk[2 * i] = ddt
        blk[2 * i + 1] = pltpu.roll(ddt, HALF, 1)
        ddt_acc = ddt_acc + ddt
        alog_acc = alog_acc + grad_log * step_r[at8, :]
    rows = []
    for j in range(4):
        taps = [taps_ref[k : k + 1, at_tile((4 * r + j) * TILE)] for k in range(4)]
        first = jnp.where(high, gp[0:8, lanes_of(j)], gp[2 * TILE : 2 * TILE + 8, lanes_of(j)])
        spill_ref[:, lanes_of(j)] = spill_of(first, taps)
        for t in range(5):
            rows.append(jnp.sum(sums[j][t], axis=0, keepdims=True))
    alog = jnp.sum(alog_acc * rate8, axis=1, keepdims=True)
    ddtb = jnp.sum(ddt_acc, axis=1, keepdims=True)
    skips = jnp.zeros((8, TILE), F32)
    for j in range(4):
        total = jnp.sum(skip_acc[j], axis=0, keepdims=True)
        skips = skips + jnp.where(row8 == 2 * j + lane8 // HALF, total, 0.0)
    skips = jnp.sum(skips, axis=1, keepdims=True)
    three = jnp.where(lane8 == 0, alog, jnp.where(lane8 == 1, ddtb, skips))
    flat = columns(jnp.where(lane8 < 3, three, 0.0))
    trio = flat[0:1] + pltpu.roll(flat[0:8], 32, 1)[1:2] + pltpu.roll(flat[0:8], 64, 1)[2:3]
    trio = pltpu.roll(jnp.broadcast_to(trio, (8, TILE)), 8 * r, 1)[0:1]
    params_ref[...] = jnp.concatenate(rows + [trio, jnp.zeros((3, TILE), F32)], axis=0)


def split_params(params):
    hi, lo, _ = split3(params)
    return jnp.concatenate([hi[0:16], hi[16:32], lo[0:16], lo[16:32]], axis=1)


def whole_params(value):
    value = value.astype(F32)
    return jnp.concatenate(
        [
            value[:, lanes_of(0)] + value[:, lanes_of(2)],
            value[:, lanes_of(1)] + value[:, lanes_of(3)],
        ],
        axis=0,
    )


def cross_kernel(scale, params_ref, spill_ref, one_ref, two_ref, cross_ref):
    tails = [ref[4 * TILE : 4 * TILE + 32, :].astype(F32) for ref in (one_ref, two_ref)]
    fives = [tail[16:24] + tail[24:32] for tail in tails]
    params = jnp.concatenate(
        [
            params_ref[0:20],
            fives[0][0:5],
            fives[1][0:5],
            params_ref[20:21],
            jnp.zeros((1, TILE), F32),
        ],
        axis=0,
    )
    maps = jnp.concatenate([tails[0][0:8], tails[1][0:8], jnp.zeros((8, 2 * TILE), F32)], axis=1)
    cross_ref[0:16, :] = jnp.concatenate([spill_ref[...], maps], axis=0).astype(BF)
    cross_ref[16:32, :] = split_params(params * scale)


def send_kernel(gp, taps_ref, y0, y1, y2, y3, dx):
    quad, r, f = place()
    high = quad == 1
    for j in range(4):
        lanes = lanes_of(j)
        taps = [taps_ref[k : k + 1, at_tile((4 * r + j) * TILE)] for k in range(4)]
        for i in range(4):
            rows = slice(i * TILE, (i + 1) * TILE)
            if i == 3:
                after = jnp.zeros((8, TILE), F32)
            else:
                after = gp[(i + 1) * TILE : (i + 1) * TILE + 8, lanes]
            if i == 1:
                after = jnp.where(high, after, 0.0)
            dx[rows, lanes] = taps_back(gp[rows, lanes], after, taps).astype(BF)
    for k, y in enumerate((y0, y1, y2, y3)):
        s = lax.bitwise_xor(r, k)
        for e, at in ((0, HALF * s), (1, 2 * TILE + HALF * (3 - s))):
            y[e * HALF : (e + 1) * HALF, :] = dx[pl.ds(pl.multiple_of(at, HALF), HALF), :]


def merge_kernel(own_ref, other_ref, one_ref, two_ref, blk, w0, w1, w2, w3):
    quad, r, f = place()
    lane8 = ids((8, TILE), 1)
    param_rows = split_params(
        whole_params(own_ref[16:32, :]) + whole_params(other_ref[16:32, :])
    )
    for k, w in enumerate((w0, w1, w2, w3)):
        s = lax.bitwise_xor(r, k)
        for e, at in ((0, HALF * s), (1, 2 * TILE + HALF * (3 - s))):
            rows = pl.ds(pl.multiple_of(at, HALF), HALF)
            w[0:HALF, lanes_of(e)] = one_ref[rows, :]
            w[0:HALF, lanes_of(2 + e)] = two_ref[rows, :]
        here = jnp.where(lane8 < HALF, blk[s], pltpu.roll(blk[7 - s], HALF, 1))
        hi, mid, lo = split3(here)
        top = jnp.concatenate([hi.astype(F32), mid.astype(F32)], axis=0)
        low = jnp.concatenate([lo.astype(F32), jnp.zeros((8, TILE), F32)], axis=0)
        w[HALF : HALF + 16, :] = jnp.concatenate(
            [top, low, jnp.zeros((16, 2 * TILE), F32)], axis=1
        ).astype(BF)
        w[HALF + 16 : HALF + 32, :] = other_ref[0:16, :]
        w[HALF + 32 : HALF + 48, :] = param_rows


def last_kernel(
    y0, y1, y2, y3, w0, w1, w2, w3, dsig_ref, dmap_ref, ddt_ref, taps_ref, mtaps_ref, bias_ref, mbias_ref, *trio_refs
):
    quad, r, f = place()
    ys = (y0, y1, y2, y3)
    ws = (w0, w1, w2, w3)
    third = jnp.logical_and(quad == 0, r == 3)
    fourth = jnp.logical_and(quad == 1, r == 0)
    params = []
    trio = jnp.zeros((1, TILE), F32)
    for k, y in enumerate(ys):
        s = lax.bitwise_xor(r, k)
        cols = at_tile(s * 4 * TILE, 4 * TILE)
        dsig_ref[:, cols] = y[0:TILE, :].astype(F32)
        spill = ws[k][HALF + 16 : HALF + 32, :].astype(F32)[0:8]
        dsig_ref[HALF - 8 : HALF, cols] += jnp.where(third, spill, 0.0)
        dsig_ref[TILE - 8 : TILE, cols] += jnp.where(fourth, spill, 0.0)
        packed = ws[k][HALF : HALF + 16, 0 : 2 * TILE].astype(F32)
        ddt_ref[pl.ds(pl.multiple_of(8 * s, 8), 8), :] = (
            packed[0:8, 0:TILE] + packed[8:16, 0:TILE] + packed[0:8, TILE : 2 * TILE]
        )
        param = whole_params(ws[k][HALF + 32 : HALF + 48, :])
        params.append(param)
        for j in range(4):
            lanes = at_tile((4 * s + j) * TILE)
            taps_ref[0:4, lanes] = param[5 * j : 5 * j + 4]
            bias_ref[0:1, lanes] = param[5 * j + 4 : 5 * j + 5]
        trio = trio + param[30:31]
    trio = jnp.broadcast_to(trio, (8, TILE))
    for t, ref in enumerate(trio_refs):
        moved = trio if t == 0 else pltpu.roll(trio, TILE - 32 * t, 1)
        ref[...] = moved[0:1, 0:32]
    own = lax.div(r, 2)
    swap = f >= 2
    for pair in range(2):
        group = own if pair == 0 else 1 - own
        a, b = 2 * pair, 2 * pair + 1
        for j in range(2):
            where = jnp.where(swap, 1 - j, j)
            lanes = at_tile((2 * where + group) * TILE)
            for e in range(2):
                dmap_ref[e * HALF : (e + 1) * HALF, lanes] = ws[a][
                    0:HALF, lanes_of(2 * j + e)
                ].astype(F32) + ws[b][0:HALF, lanes_of(2 * j + e)].astype(F32)
            spill = (
                ws[a][HALF + 16 : HALF + 32, lanes_of(j)].astype(F32)[8:16]
                + ws[b][HALF + 16 : HALF + 32, lanes_of(j)].astype(F32)[8:16]
            )
            dmap_ref[HALF - 8 : HALF, lanes] += jnp.where(third, spill, 0.0)
            dmap_ref[TILE - 8 : TILE, lanes] += jnp.where(fourth, spill, 0.0)
            five = params[a][20 + 5 * j : 25 + 5 * j] + params[b][20 + 5 * j : 25 + 5 * j]
            mtaps_ref[0:4, lanes] = five[0:4]
            mbias_ref[0:1, lanes] = five[4:5]


ROUTE_ONE = [(0, 0), (2, 1), (1, 2), (3, 3)]
ROUTE_TWO = [(0, 2), (2, 3), (1, 0), (3, 1)]


def shards_quad(
    sig_raw,
    map_raw,
    step_size_logits,
    d_out,
    sig_taps,
    map_taps,
    sig_bias,
    map_bias,
    a_log,
    dt_bias,
    skip_gain,
):
    ctx = lax.axis_size("ctx")
    rows, sig_width = sig_raw.shape
    vmem = pl.BlockSpec(memory_space=pltpu.VMEM)
    smem = pl.BlockSpec(memory_space=pltpu.SMEM)
    hbm = pl.BlockSpec(memory_space=pltpu.HBM)

    def call(kernel, out_shape, in_specs, out_specs, scratch, mib, cost):
        return pl.pallas_call(
            kernel,
            out_shape=out_shape,
            in_specs=in_specs,
            out_specs=out_specs,
            scratch_shapes=scratch,
            compiler_params=pltpu.CompilerParams(vmem_limit_bytes=mib * 1024 * 1024),
            cost_estimate=pl.CostEstimate(flops=cost, bytes_accessed=cost // 100, transcendentals=0),
        )

    def shape(*dims, kind=F32):
        return jax.ShapeDtypeStruct(dims, kind)

    inside = [[(c, c ^ k) for c in range(ctx)] for k in range(4)]
    over = [(c, c ^ 4) for c in range(ctx)]
    total = 4 * TILE
    wide, narrow = 6 * TILE, 4 * TILE
    owned = map_taps.shape[1]
    sig_bias_row = sig_bias[None, :]
    packed = call(
        pack_kernel,
        (shape(2 * TILE + HALF + 16, narrow, kind=BF),) * 4
        + (shape(16, wide, kind=BF),) * 4
        + (shape(8, owned),),
        [hbm, hbm, hbm, hbm, vmem, vmem],
        (vmem,) * 9,
        [pltpu.VMEM((32, TILE), F32), pltpu.SemaphoreType.DMA((37,))],
        60,
        10**6,
    )(sig_raw, map_raw, step_size_logits.T, d_out, map_taps, map_bias[None, :])
    xs = [packed[0]] + [lax.ppermute(packed[k], "ctx", inside[k]) for k in (1, 2, 3)]
    halos = [lax.ppermute(packed[4 + m], "ctx", [(3, 4 + m), (4, 3 - m)]) for m in range(4)]
    map_params = lax.all_gather(packed[8], "fsdp", axis=0)
    own_taps = (sig_taps, sig_bias_row, map_params)
    mid, *kept = call(
        first_kernel,
        (
            shape(2 * TILE + 16, narrow, kind=BF),
            shape(2, 2 * TILE + 8, wide),
            shape(total, narrow, kind=BF),
            shape(total, wide, kind=BF),
            shape(total, wide),
            shape(total, narrow, kind=BF),
            shape(total, narrow, kind=BF),
            shape(total, narrow, kind=BF),
            shape(total, narrow),
            shape(total, narrow),
            shape(total, narrow),
            shape(4, TILE, narrow),
            shape(4, TILE, narrow),
            shape(32, TILE),
            shape(32, TILE),
            shape(32, TILE),
        ),
        [vmem] * 11 + [smem] * 2,
        (vmem,) * 16,
        [pltpu.VMEM((4, 8, TILE), F32)],
        24,
        4 * 10**9,
    )(*xs, *halos, *own_taps, a_log, dt_bias)
    xp, dp, act, slope, scaled, weighted, sgrad, step_e, toend_e, exp_e, s_s, t_s = kept[:12]
    step_r, ds_r, sig_r = kept[12:]
    mid = lax.ppermute(mid, "ctx", over)
    diag, gmap, gsum = call(
        second_kernel,
        (shape(total, narrow), shape(total, 2 * TILE), shape(32, TILE)),
        [vmem] * 4,
        (vmem,) * 3,
        [],
        16,
        4 * 10**9,
    )(dp, act, scaled, ds_r)
    one, two, hlow, clow, endrow = call(
        maps_kernel,
        (
            shape(total + 32, TILE, kind=BF),
            shape(total + 32, TILE, kind=BF),
            shape(4, TILE, narrow, kind=BF),
            shape(4, TILE, narrow, kind=BF),
            shape(8, narrow),
        ),
        [vmem] * 13,
        (vmem,) * 5,
        [pltpu.VMEM((4, TILE, narrow), F32), pltpu.VMEM((4, TILE, narrow), F32)],
        24,
        2 * 10**9,
    )(mid, s_s, t_s, exp_e, act, slope, weighted, sgrad, gmap, xp, *own_taps)
    one = lax.ppermute(one, "fsdp", ROUTE_ONE)
    two = lax.ppermute(two, "fsdp", ROUTE_TWO)
    gp, blk, spill, params = call(
        third_kernel,
        (shape(total, narrow), shape(8, 8, TILE), shape(8, narrow), shape(24, TILE)),
        [vmem] * 16 + [smem] * 2,
        (vmem,) * 4,
        [],
        24,
        3 * 10**9,
    )(
        hlow,
        clow,
        endrow,
        xp,
        dp,
        act,
        slope,
        scaled,
        step_e,
        toend_e,
        exp_e,
        step_r,
        sig_r,
        diag,
        gsum,
        sig_taps,
        a_log,
        skip_gain,
    )
    scale = 1.0 / math.sqrt(float(ctx * rows))
    cross = call(
        functools.partial(cross_kernel, scale),
        shape(32, narrow, kind=BF),
        [vmem] * 4,
        vmem,
        [],
        16,
        10**6,
    )(params, spill, one, two)
    other = lax.ppermute(cross, "ctx", over)
    ys = call(
        send_kernel,
        (shape(TILE, narrow, kind=BF),) * 4,
        [vmem] * 2,
        (vmem,) * 4,
        [pltpu.VMEM((total, narrow), BF)],
        16,
        10**9,
    )(gp, sig_taps)
    ys = [ys[0]] + [lax.ppermute(ys[k], "ctx", inside[k]) for k in (1, 2, 3)]
    ws = call(
        merge_kernel,
        (shape(HALF + 48, narrow, kind=BF),) * 4,
        [vmem] * 5,
        (vmem,) * 4,
        [],
        16,
        10**6,
    )(cross, other, one, two, blk)
    ws = [ws[0]] + [lax.ppermute(ws[k], "ctx", inside[k]) for k in (1, 2, 3)]
    d_sig, d_map, d_dt, taps, map_taps_grad, bias, map_bias_grad, *trio = call(
        last_kernel,
        (
            shape(rows, sig_width),
            shape(rows, owned),
            shape(32, TILE),
            shape(4, sig_width),
            shape(4, owned),
            shape(1, sig_width),
            shape(1, owned),
        )
        + (shape(1, 32),) * 3,
        [vmem] * 8,
        (vmem,) * 10,
        [],
        16,
        10**6,
    )(*ys, *ws)
    return (
        d_sig,
        d_map,
        d_dt.T,
        taps,
        map_taps_grad,
        bias[0],
        map_bias_grad[0],
        *(t[0] for t in trio),
    )


def shards(*args):
    sig_raw, map_raw, step_size_logits = args[:3]
    ctx = lax.axis_size("ctx")
    fsdp = lax.axis_size("fsdp")
    fits = (
        ctx == 8
        and fsdp == 4
        and sig_raw.shape == (TILE, 2048)
        and map_raw.shape == (TILE, 2 * GROUPS * STATE)
        and step_size_logits.shape[1] == 32
    )
    return shards_quad(*args) if fits else shards_chain(*args)


def solution(mesh):
    return jax.shard_map(
        shards,
        mesh=mesh,
        in_specs=(
            P("ctx", "fsdp"),
            P("ctx", None),
            P("ctx", "fsdp"),
            P("ctx", "fsdp"),
            P(None, "fsdp"),
            P(None, "fsdp"),
            P("fsdp"),
            P("fsdp"),
            P("fsdp"),
            P("fsdp"),
            P("fsdp"),
        ),
        out_specs=(
            P("ctx", "fsdp"),
            P("ctx", "fsdp"),
            P("ctx", "fsdp"),
            P(None, "fsdp"),
            P(None, "fsdp"),
            P("fsdp"),
            P("fsdp"),
            P("fsdp"),
            P("fsdp"),
            P("fsdp"),
        ),
        check_vma=False,
    )
```

```python
import functools
import math

import jax
import jax.numpy as jnp
from jax import lax
from jax.experimental import pallas as pl
from jax.experimental.pallas import tpu as pltpu
from jax.sharding import PartitionSpec as P

HEADS = 128
HDIM = 64
STATE = 128
GROUPS = 8


def prefix(part, axis, combine, identity, reverse):
    count = lax.axis_size(axis)
    place = lax.axis_index(axis)
    ahead = count - 1 - place if reverse else place
    gathered = jax.tree.map(lambda a: lax.all_gather(a, axis), part)
    state = jax.tree.map(lambda a, e: jnp.zeros_like(a) + jnp.asarray(e, a.dtype), part, identity)

    def one(lap, state):
        source = count - 1 - lap if reverse else lap
        return combine(
            state, jax.tree.map(lambda a: lax.dynamic_index_in_dim(a, source, 0, False), gathered)
        )

    return lax.fori_loop(0, ahead, one, state)


def broadcast(x, axis, root):
    mine = lax.axis_index(axis) == root
    return lax.psum(jnp.where(mine, x, jnp.zeros_like(x)), axis)


def extended(block, sides, width):
    for axis, dim in sides:
        count = lax.axis_size(axis)
        forward = [(i, i + 1) for i in range(count - 1)]
        backward = [(target, source) for source, target in forward]
        low = lax.ppermute(
            lax.slice_in_dim(block, block.shape[dim] - width, None, axis=dim), axis, forward
        )
        high = lax.ppermute(lax.slice_in_dim(block, 0, width, axis=dim), axis, backward)
        block = jnp.concatenate([low, block, high], axis=dim)
    return block


def ein(form, left, right):
    return jnp.einsum(form, left, right, preferred_element_type=jnp.float32)


def silu_slope(value):
    sig = jax.nn.sigmoid(value)
    return sig * (1.0 + value * (1.0 - sig))


def block_parts(activated, dt_rows, a_log, dt_bias, groups):
    length = activated.shape[0]
    heads = dt_rows.shape[1]
    inner = heads * HDIM
    shared = groups * STATE
    ratio = heads // groups
    signal = activated[:, :inner].reshape(length, heads, HDIM)
    input_map = activated[:, inner : inner + shared].reshape(length, groups, STATE)
    output_map = activated[:, inner + shared :].reshape(length, groups, STATE)
    input_heads = jnp.repeat(input_map, ratio, axis=1)
    output_heads = jnp.repeat(output_map, ratio, axis=1)
    step = jax.nn.softplus(dt_rows + dt_bias)
    rate = -jnp.exp(a_log)
    row_ids = lax.broadcasted_iota(jnp.int32, (length, length), 0)
    col_ids = lax.broadcasted_iota(jnp.int32, (length, length), 1)
    lower = (row_ids >= col_ids).astype(jnp.float32)
    decay_sum = jnp.dot(lower, step * rate, precision=lax.Precision.HIGHEST)
    to_end = jnp.exp(decay_sum[-1][None, :] - decay_sum)
    scaled = (signal.astype(jnp.float32) * step[:, :, None]).astype(jnp.bfloat16)
    weighted = (scaled.astype(jnp.float32) * to_end[:, :, None]).astype(jnp.bfloat16)
    local = ein("qhp,qhn->hpn", weighted, input_heads)
    return (
        signal,
        input_map,
        output_map,
        input_heads,
        output_heads,
        step,
        rate,
        lower,
        decay_sum,
        scaled,
        to_end,
        weighted,
        local,
    )


def entry_grad(parts, d_rows):
    decay_sum = parts[8]
    output_heads = parts[4]
    scaled_grad = (d_rows.astype(jnp.float32) * jnp.exp(decay_sum)[:, :, None]).astype(jnp.bfloat16)
    return (scaled_grad, ein("thp,thn->hpn", scaled_grad, output_heads))


def block_grads(parts, d_rows, scaled_grad, h_in, carried, skip_gain, dt_rows, dt_bias):
    (
        signal,
        input_map,
        output_map,
        input_heads,
        output_heads,
        step,
        rate,
        lower,
        decay_sum,
        scaled,
        to_end,
        weighted,
        local,
    ) = parts
    length = d_rows.shape[0]
    heads = d_rows.shape[1]
    groups = input_map.shape[1]
    width_state = input_map.shape[2]
    ratio = heads // groups
    grad_f = d_rows.astype(jnp.float32)
    signal_f = signal.astype(jnp.float32)
    grad_skip = jnp.sum(grad_f * signal_f, axis=(0, 2))
    h_low = h_in.astype(jnp.bfloat16)
    carried_low = carried.astype(jnp.bfloat16)
    offset = jnp.exp(decay_sum)[:, :, None] * ein("thn,hpn->thp", output_heads, h_low)
    grad_sum = jnp.sum(grad_f * offset, axis=2)
    out_heads_grad = ein("thp,hpn->thn", scaled_grad, h_low)
    grad_weighted = ein("shn,hpn->shp", input_heads, carried_low)
    in_heads_grad = ein("shp,hpn->shn", weighted, carried_low)
    back = jnp.sum(grad_weighted * scaled.astype(jnp.float32), axis=2) * to_end
    end_term = jnp.exp(decay_sum[-1]) * jnp.sum(h_in * carried, axis=(1, 2))
    last_row = (lax.broadcasted_iota(jnp.int32, (length, 1), 0) == length - 1).astype(jnp.float32)
    grad_sum = grad_sum - back + last_row * (jnp.sum(back, axis=0) + end_term)[None, :]
    spread = decay_sum.T[:, :, None] - decay_sum.T[:, None, :]
    decay = jnp.where(lower[None] > 0, jnp.exp(jnp.minimum(spread, 0.0)), 0.0)
    score = ein("tgn,sgn->gts", output_map, input_map)
    mix = jnp.repeat(score, ratio, axis=0) * decay
    grad_mix = ein("thp,shp->hts", d_rows, scaled)
    grad_scaled = grad_weighted * to_end[:, :, None] + ein(
        "hts,thp->shp", mix.astype(jnp.bfloat16), d_rows
    )
    product = grad_mix * mix
    grad_sum = grad_sum + (jnp.sum(product, axis=2) - jnp.sum(product, axis=1)).T
    grad_score = jnp.sum((grad_mix * decay).reshape(groups, ratio, length, length), axis=1).astype(
        jnp.bfloat16
    )
    grad_outmap = ein("gts,sgn->tgn", grad_score, input_map) + jnp.sum(
        out_heads_grad.reshape(length, groups, ratio, width_state), axis=2
    )
    grad_in = ein("gts,tgn->sgn", grad_score, output_map) + jnp.sum(
        in_heads_grad.reshape(length, groups, ratio, width_state), axis=2
    )
    grad_log = jnp.dot(lower.T, grad_sum, precision=lax.Precision.HIGHEST)
    descent_increment = grad_log * rate + jnp.sum(grad_scaled * signal_f, axis=2)
    grad_signal = skip_gain[None, :, None] * grad_f + grad_scaled * step[:, :, None]
    grad_dt = descent_increment * jax.nn.sigmoid(dt_rows + dt_bias)
    decay_log_gradient = jnp.sum(grad_log * step, axis=0) * rate
    grad_act = jnp.concatenate(
        [
            grad_signal.reshape(length, heads * HDIM),
            grad_in.reshape(length, groups * width_state),
            grad_outmap.reshape(length, groups * width_state),
        ],
        axis=1,
    )
    return (grad_act, grad_dt, decay_log_gradient, jnp.sum(grad_dt, axis=0), grad_skip)


def link(earlier, later):
    return (earlier[0] + later[0], jnp.exp(later[0])[:, None, None] * earlier[1] + later[1])


def link_blocks(lower_pair, upper_pair):
    zero_rate = jnp.zeros_like(lower_pair[0])
    zero_state = jnp.zeros_like(lower_pair[1])
    below = prefix(lower_pair, "ctx", link, (zero_rate, zero_state), False)
    beyond = prefix(upper_pair, "ctx", link, (zero_rate, zero_state), True)
    total = jax.tree.map(
        lambda part: broadcast(part, "ctx", lax.axis_size("ctx") - 1), link(below, lower_pair)
    )
    return jnp.stack([below[1], link(total, beyond)[1]])


def conv_back(grad_pre, wide_grad, kernel_taps, padded, at_end, length):
    rim = kernel_taps.shape[0] - 1
    after = jnp.stack(
        [jnp.where(at_end, grad_pre[1, :rim], wide_grad[3 * rim : 4 * rim]), wide_grad[0:rim]]
    )
    padded_next = jnp.concatenate([grad_pre, after], axis=1)
    grad_raw = jnp.zeros(grad_pre.shape, jnp.float32)
    for tap in range(rim + 1):
        grad_raw = (
            grad_raw
            + kernel_taps[tap][None, None, :] * padded_next[:, rim - tap : rim - tap + length]
        )
    tap_grads = jnp.stack(
        [jnp.sum(grad_pre * padded[:, tap : tap + length], axis=(0, 1)) for tap in range(rim + 1)]
    )
    return (grad_raw, tap_grads, jnp.sum(grad_pre, axis=(0, 1)))


def first_rows(grad_pre, rim):
    return jnp.concatenate([grad_pre[0, :rim], grad_pre[1, :rim]], axis=0)


def shards_chain(
    sig_raw,
    map_raw,
    step_size_logits,
    d_out,
    sig_taps,
    map_taps,
    sig_bias,
    map_bias,
    a_log,
    dt_bias,
    skip_gain,
):
    all_map_taps, all_map_bias = (
        lax.all_gather(map_taps, "fsdp", axis=1, tiled=True),
        lax.all_gather(map_bias, "fsdp", axis=0, tiled=True),
    )
    kernel_taps = jnp.concatenate([sig_taps, all_map_taps], axis=1)
    kernel_bias = jnp.concatenate([sig_bias, all_map_bias], axis=0)
    kernel = kernel_taps.shape[0]
    rim = kernel - 1
    length = sig_raw.shape[0] // 2
    sig_width = sig_raw.shape[1]
    map_width = map_raw.shape[1]
    width = sig_width + map_width
    heads_here = step_size_logits.shape[1]
    ratio = HEADS // GROUPS
    group_count = max(1, heads_here // ratio)
    first_group = lax.axis_index("fsdp") * heads_here // ratio
    fsdp_count = lax.axis_size("fsdp")
    owned = map_width // fsdp_count
    map_start = lax.axis_index("fsdp") * owned
    raw_rows = jnp.concatenate([sig_raw, map_raw], axis=1).reshape(2, length, width)
    tails = jnp.concatenate([raw_rows[1, length - rim :], raw_rows[0, length - rim :]], axis=0)
    wide = extended(tails, (("ctx", 0),), rim)
    at_end = lax.axis_index("ctx") == lax.axis_size("ctx") - 1
    before = jnp.stack(
        [wide[0:rim], jnp.where(at_end, raw_rows[0, length - rim :], wide[3 * rim : 4 * rim])]
    )
    padded = jnp.concatenate([before, raw_rows], axis=1).astype(jnp.float32)
    preact = kernel_bias[None, None, :] + jnp.zeros((2, length, width), jnp.float32)
    for tap in range(kernel):
        preact = preact + kernel_taps[tap][None, None, :] * padded[:, tap : tap + length]
    activated = jax.nn.silu(preact).astype(jnp.bfloat16)
    maps_all = activated[:, :, sig_width:].reshape(2, length, 2, GROUPS, STATE)
    maps_mine = lax.dynamic_slice_in_dim(maps_all, first_group, group_count, 3)
    local_act = jnp.concatenate(
        [activated[:, :, :sig_width], maps_mine.reshape(2, length, 2 * group_count * STATE)], axis=2
    )
    dt_rows = step_size_logits.reshape(2, length, heads_here)
    grad_rows = d_out.reshape(2, length, heads_here, HDIM)

    def parts_of(act_block, dt_block):
        return block_parts(act_block, dt_block, a_log, dt_bias, group_count)

    parts = jax.vmap(parts_of)(local_act, dt_rows)
    scaled_grad, state_grad = jax.vmap(entry_grad)(parts, grad_rows)
    ends = parts[8][:, -1]
    h_ins = link_blocks((ends[0], parts[12][0]), (ends[1], parts[12][1]))
    carried_pair = link_blocks((ends[1], state_grad[1]), (ends[0], state_grad[0]))
    carried = jnp.stack([carried_pair[1], carried_pair[0]])
    grad_act, grad_dt, decay_log_gradient, grad_dtb, grad_skip = jax.vmap(
        block_grads, in_axes=(0, 0, 0, 0, 0, None, 0, None)
    )(parts, grad_rows, scaled_grad, h_ins, carried, skip_gain, dt_rows, dt_bias)
    slope = silu_slope(preact)
    grad_pre_sig = grad_act[:, :, :sig_width] * slope[:, :, :sig_width]
    grad_mine = grad_act[:, :, sig_width:].reshape(2, length, 2, group_count, STATE)
    zero_index = jnp.zeros((), jnp.int32)
    placed = lax.dynamic_update_slice(
        jnp.zeros((2, length, 2, GROUPS, STATE), jnp.float32),
        grad_mine,
        (zero_index, zero_index, zero_index, first_group, zero_index),
    )
    map_term = placed.reshape(2, length, map_width)
    map_owned = lax.psum_scatter(map_term, "fsdp", scatter_dimension=2, tiled=True)
    map_slope = lax.dynamic_slice_in_dim(slope[:, :, sig_width:], map_start, owned, 2)
    grad_pre = jnp.concatenate([grad_pre_sig, map_owned * map_slope], axis=2)
    own_taps = jnp.concatenate([sig_taps, map_taps], axis=1)
    own_padded = jnp.concatenate(
        [
            padded[:, :, :sig_width],
            lax.dynamic_slice_in_dim(padded[:, :, sig_width:], map_start, owned, 2),
        ],
        axis=2,
    )
    wide_grad = extended(first_rows(grad_pre, rim), (("ctx", 0),), rim)
    grad_raw, tap_grads, bias_grads = conv_back(
        grad_pre, wide_grad, own_taps, own_padded, at_end, length
    )
    map_raw_grad = grad_raw[:, :, sig_width:]
    map_tap_grad = tap_grads[:, sig_width:]
    map_bias_grad = bias_grads[sig_width:]
    sig_raw_grad = grad_raw[:, :, :sig_width]
    sig_tap_grad = tap_grads[:, :sig_width]
    sig_bias_grad = bias_grads[:sig_width]
    reduced = lax.psum(
        (
            sig_tap_grad,
            map_tap_grad,
            sig_bias_grad,
            map_bias_grad,
            jnp.sum(decay_log_gradient, axis=0),
            jnp.sum(grad_dtb, axis=0),
            jnp.sum(grad_skip, axis=0),
        ),
        "ctx",
    )
    scale = 1.0 / math.sqrt(float(lax.axis_size("ctx") * 2 * length))
    final = jax.tree.map(lambda grad_part: grad_part * scale, reduced)
    return (
        sig_raw_grad.reshape(2 * length, sig_width),
        map_raw_grad.reshape(2 * length, owned),
        grad_dt.reshape(2 * length, heads_here),
        final[0],
        final[1],
        final[2],
        final[3],
        final[4],
        final[5],
        final[6],
    )


TILE = 128
HALF = 64
NT = (((1,), (1,)), ((), ()))
TN = (((0,), (0,)), ((), ()))
NN = (((1,), (0,)), ((), ()))
BF = jnp.bfloat16
F32 = jnp.float32


def mm(a, b, dims=NN):
    return lax.dot_general(a, b, dims, preferred_element_type=F32)


def mm_f32(a, b, dims=NN):
    return lax.dot_general(a, b, dims, precision=lax.Precision.HIGHEST, preferred_element_type=F32)


def split3(x):
    hi = x.astype(BF)
    rest = x - hi.astype(F32)
    mid = rest.astype(BF)
    return hi, mid, (rest - mid.astype(F32)).astype(BF)


def ids(shape, dim):
    return lax.broadcasted_iota(jnp.int32, shape, dim)


def lanes_of(j):
    return slice(j * TILE, (j + 1) * TILE)


def place():
    ctx_place = lax.axis_index("ctx")
    quad = lax.div(ctx_place, 4)
    return quad, lax.rem(ctx_place, 4), lax.axis_index("fsdp")


def at_tile(start, width=TILE):
    return pl.ds(pl.multiple_of(start, TILE), width)


def pack_kernel(map_ref, dt_ref, dy_ref, mtaps_ref, mbias_ref, *rest):
    u_refs, tap_ref, (dt_in, sems) = rest[:4], rest[4], rest[5:]
    quad, r, f = place()
    copies = []
    dt_copy = pltpu.make_async_copy(dt_ref, dt_in, sems.at[20])
    dt_copy.start()

    def send(source, target):
        copy = pltpu.make_async_copy(source, target, sems.at[len(copies)])
        copy.start()
        copies.append(copy)

    half = map_ref.shape[1] // 2
    for k in (1, 2, 3, 0):
        dest = lax.bitwise_xor(r, k)
        cols = at_tile(dest * 4 * TILE, 4 * TILE)
        send(dy_ref.at[:, cols], u_refs[k].at[0:TILE, :])
        group = (2 * f + lax.div(dest, 2)) * TILE
        for j in range(2):
            for e in range(2):
                send(
                    map_ref.at[e * HALF : (e + 1) * HALF, at_tile(group + j * half)],
                    u_refs[k].at[TILE : TILE + HALF, lanes_of(2 * j + e)],
                )
    tap_ref[0:4, :] = mtaps_ref[...]
    tap_ref[4:5, :] = mbias_ref[...]
    tap_ref[5:8, :] = jnp.zeros_like(tap_ref[5:8, :])
    dt_copy.wait()
    zero = jnp.zeros((8, TILE), F32)
    for k in range(4):
        dest = lax.bitwise_xor(r, k)
        hi, mid, lo = split3(dt_in[pl.ds(pl.multiple_of(8 * dest, 8), 8), :])
        top = jnp.concatenate([hi.astype(F32), mid.astype(F32)], axis=0)
        low = jnp.concatenate([lo.astype(F32), zero], axis=0)
        u_refs[k][TILE + HALF : TILE + HALF + 16, :] = jnp.concatenate(
            [top, low, jnp.zeros((16, 2 * TILE), F32)], axis=1
        ).astype(BF)
    for copy in copies:
        copy.wait()


def pack_sig_kernel(sig_ref, *rest):
    v_refs, sems = rest[:4], rest[4]
    r = place()[1]
    copies = []
    for k in (1, 2, 3, 0):
        dest = lax.bitwise_xor(r, k)
        copy = pltpu.make_async_copy(
            sig_ref.at[:, at_tile(dest * 4 * TILE, 4 * TILE)], v_refs[k], sems.at[k]
        )
        copy.start()
        copies.append(copy)
    for copy in copies:
        copy.wait()


def sig_tap_rows(j, taps_ref, bias_ref):
    at = at_tile((4 * place()[1] + j) * TILE)
    return [taps_ref[k : k + 1, at] for k in range(4)], bias_ref[0:1, at]


def map_tap_rows(j, mine_ref):
    return [mine_ref[8 * j + k : 8 * j + k + 1, :] for k in range(4)], mine_ref[
        8 * j + 4 : 8 * j + 5, :
    ]


def sigmoid(v):
    return 0.5 * jnp.tanh(0.5 * v) + 0.5


def rolled(block, k):
    return block[8:] if k == 3 else pltpu.roll(block, 3 - k, 0)[8:]


def columns(*rows8):
    total = 8 * len(rows8)
    full = jnp.concatenate(list(rows8) + [jnp.zeros((TILE - total, TILE), F32)], axis=0)
    return jnp.transpose(full)


def head_row(ref, r):
    row8 = ids((8, TILE), 0)
    out = jnp.zeros((8, TILE), F32)
    for h in range(8):
        out = jnp.where(row8 == h, ref[8 * r + h], out)
    return out


def conv(block, taps, bias):
    pre = bias + taps[0] * rolled(block, 0)
    for k in range(1, 4):
        pre = pre + taps[k] * rolled(block, k)
    return pre


def boundary_chunk(i, high):
    return high if i == 0 else jnp.logical_not(high)


def patched(ref, lanes, patch, patch_lanes, i, high):
    rows = slice(i * TILE, (i + 1) * TILE)
    if i % 2 == 1:
        return ref[rows, lanes]
    first = jnp.where(
        boundary_chunk(i, high), patch[:, patch_lanes], ref[i * TILE : i * TILE + 16, lanes]
    )
    return jnp.concatenate([first, ref[i * TILE + 16 : (i + 1) * TILE, lanes]], axis=0)


def grads_kernel(
    u0,
    u1,
    u2,
    u3,
    one_taps,
    two_taps,
    alog_ref,
    dtb_ref,
    mid_ref,
    dp,
    xm,
    actm,
    prem,
    sgrad_s,
    step_e,
    toend_e,
    exp_e,
    t_s,
    step_r,
    ds_r,
    sig_r,
    mine_ref,
    dt_src,
):
    quad, r, f = place()
    high = quad == 1
    half_lane = ids((TILE, TILE), 1) < HALF
    lane8 = ids((8, TILE), 1)
    group = 2 * f + lax.div(r, 2)
    at = at_tile(lax.rem(group, 4) * TILE)
    for j in range(2):
        mine_ref[8 * j : 8 * j + 8, :] = jnp.where(
            lax.rem(f, 2) == j, one_taps[:, at], two_taps[:, at]
        )
    for k, u in enumerate((u0, u1, u2, u3)):
        s = lax.bitwise_xor(r, k)
        for e, start in ((0, HALF * s), (1, HALF * (3 - s))):
            for j in range(2):
                xm[e, pl.ds(pl.multiple_of(8 + start, 8), HALF), lanes_of(j)] = u[
                    TILE : TILE + HALF, lanes_of(2 * j + e)
                ].astype(F32)
            dp[pl.ds(pl.multiple_of(2 * TILE * e + start, HALF), HALF), :] = u[
                e * HALF : (e + 1) * HALF, :
            ]
        packed = u[TILE + HALF : TILE + HALF + 16, 0 : 2 * TILE].astype(F32)
        dt_src[s] = packed[0:8, 0:TILE] + packed[8:16, 0:TILE] + packed[0:8, TILE : 2 * TILE]
    xm[0, 0:8, :] = jnp.zeros((8, 2 * TILE), F32)
    xm[1, 0:8, :] = jnp.where(high, xm[0, 2 * TILE : 2 * TILE + 8, :], 0.0)

    rate8 = -jnp.exp(head_row(alog_ref, r))
    bias8 = head_row(dtb_ref, r)
    for i in range(4):
        if i < 2:
            a, b = dt_src[2 * i], pltpu.roll(dt_src[2 * i + 1], HALF, 1)
        else:
            a, b = pltpu.roll(dt_src[7 - 2 * i], HALF, 1), dt_src[6 - 2 * i]
        logits = jnp.where(lane8 < HALF, a, b) + bias8
        small = jnp.exp(-jnp.abs(logits))
        step = jnp.maximum(logits, 0.0) + jnp.log1p(small)
        at8 = slice(8 * i, 8 * i + 8)
        step_r[at8, :] = step
        sig_r[at8, :] = jnp.where(logits >= 0, 1.0, small) / (1.0 + small)
        ds_r[at8, :] = step * rate8
    upto = (ids((TILE, TILE), 0) <= ids((TILE, TILE), 1)).astype(F32)
    ds_r[...] = mm_f32(ds_r[...], upto)

    ends = []
    for i in range(4):
        rows = slice(i * TILE, (i + 1) * TILE)
        base = (i % 2) * TILE
        for j in range(2):
            lanes = lanes_of(j)
            taps, bias = map_tap_rows(j, mine_ref)
            pre = conv(xm[i // 2, base : base + TILE + 8, lanes], taps, bias)
            actm[rows, lanes] = (pre * sigmoid(pre)).astype(BF)
            prem[rows, lanes] = pre
        cols = columns(step_r[8 * i : 8 * i + 8, :], ds_r[8 * i : 8 * i + 8, :])
        end, masked = [], []
        for j in range(4):
            lanes = lanes_of(j)
            step = jnp.where(half_lane, cols[:, 2 * j : 2 * j + 1], cols[:, 2 * j + 1 : 2 * j + 2])
            ds = jnp.where(
                half_lane, cols[:, 8 + 2 * j : 9 + 2 * j], cols[:, 9 + 2 * j : 10 + 2 * j]
            )
            last = ds[TILE - 1 : TILE, :]
            grow = jnp.exp(ds)
            step_e[rows, lanes] = step
            toend_e[rows, lanes] = jnp.exp(last - ds)
            exp_e[rows, lanes] = grow
            end.append(jnp.exp(last))
            grown = (dp[rows, lanes].astype(F32) * grow).astype(BF)
            sgrad_s[rows, lanes] = grown
            if i % 2 == 0:
                unknown = jnp.logical_and(boundary_chunk(i, high), ids((16, TILE), 0) < 3)
                first = jnp.where(unknown, 0.0, grown[0:16].astype(F32)).astype(BF)
                grown = jnp.concatenate([first, grown[16:]], axis=0)
            masked.append(grown)
        ends.append(jnp.concatenate(end, axis=1))
        t_s[i] = mm(actm[rows, lanes_of(1)], jnp.concatenate(masked, axis=1), TN)
    g_a = t_s[0] + ends[0] * t_s[1]
    g_b = t_s[2] + ends[2] * t_s[3]
    mid_ref[...] = jnp.where(high, g_a + ends[0] * ends[1] * g_b, g_b).astype(BF)


def edge_kernel(v0, v1, v2, v3, xm, out_ref):
    quad, r, f = place()
    high = quad == 1
    wanted = lax.bitwise_xor(r, jnp.where(high, 0, 3))
    found = jnp.zeros((16, 4 * TILE), F32)
    for k, v in enumerate((v0, v1, v2, v3)):
        rows = jnp.where(high, v[TILE - 16 : TILE, :], v[HALF - 16 : HALF, :]).astype(F32)
        found = found + jnp.where(wanted == k, rows, 0.0)
    out_ref[:, 0 : 4 * TILE] = found.astype(BF)
    last = slice(8 + 2 * TILE - 16, 8 + 2 * TILE)
    out_ref[:, 4 * TILE : 6 * TILE] = jnp.where(high, xm[1, last, :], xm[0, last, :]).astype(BF)


def first_kernel(
    v0, v1, v2, v3, step_e, toend_e, taps_ref, bias_ref, xs, acts, pres, scaled_s, weighted_s
):
    quad, r, f = place()
    high = quad == 1
    for k, v in enumerate((v0, v1, v2, v3)):
        s = lax.bitwise_xor(r, k)
        for e, start in ((0, HALF * s), (1, HALF * (3 - s))):
            xs[e, pl.ds(pl.multiple_of(8 + start, 8), HALF), :] = v[
                e * HALF : (e + 1) * HALF, :
            ].astype(F32)
    xs[0, 0:8, :] = jnp.zeros((8, 4 * TILE), F32)
    xs[1, 0:8, :] = jnp.where(high, xs[0, 2 * TILE : 2 * TILE + 8, :], 0.0)
    for i in range(4):
        rows = slice(i * TILE, (i + 1) * TILE)
        base = (i % 2) * TILE
        for j in range(4):
            lanes = lanes_of(j)
            taps, bias = sig_tap_rows(j, taps_ref, bias_ref)
            pre = conv(xs[i // 2, base : base + TILE + 8, lanes], taps, bias)
            value = (pre * sigmoid(pre)).astype(BF)
            acts[rows, lanes] = value
            pres[rows, lanes] = pre
            scaled = (value.astype(F32) * step_e[rows, lanes]).astype(BF)
            scaled_s[rows, lanes] = scaled
            weighted_s[rows, lanes] = (scaled.astype(F32) * toend_e[rows, lanes]).astype(BF)


def states_kernel(
    halo_ref,
    xs,
    xm,
    actm,
    weighted_s,
    sgrad_s,
    step_e,
    toend_e,
    exp_e,
    taps_ref,
    bias_ref,
    mine_ref,
    mid_ref,
    s_s,
    delta_ref,
    edge_ref,
    act_p,
    pre_p,
    scaled_p,
    weighted_p,
):
    quad, r, f = place()
    high = quad == 1
    edge = halo_ref[...].astype(F32)[8:16]
    edge_ref[...] = edge
    segment = jnp.where(high, 0, 1)
    rows16 = pl.ds(pl.multiple_of(2 * TILE * segment, 16), 16)
    for j in range(6):
        lanes = lanes_of(j)
        if j < 4:
            taps, bias = sig_tap_rows(j, taps_ref, bias_ref)
            first = xs[segment, 8:24, lanes]
        else:
            taps, bias = map_tap_rows(j - 4, mine_ref)
            first = xm[segment, 8:24, lanes_of(j - 4)]
        pre = conv(jnp.concatenate([edge[:, lanes], first], axis=0), taps, bias)
        value = (pre * sigmoid(pre)).astype(BF)
        act_p[:, lanes] = value
        pre_p[:, lanes] = pre
        if j < 4:
            scaled = (value.astype(F32) * step_e[rows16, lanes]).astype(BF)
            scaled_p[:, lanes] = scaled
            weighted_p[:, lanes] = (scaled.astype(F32) * toend_e[rows16, lanes]).astype(BF)
    every = slice(0, 4 * TILE)
    for i in range(4):
        s_s[i] = mm(
            patched(actm, lanes_of(0), act_p, lanes_of(4), i, high),
            patched(weighted_s, every, weighted_p, every, i, high),
            TN,
        )
    ends = end_rows_of(exp_e)
    f_a = ends[1] * s_s[0] + s_s[1]
    f_b = ends[3] * s_s[2] + s_s[3]
    d_b = ends[2] * ends[3]
    mid_ref[0:TILE, :] = jnp.where(high, d_b * f_a + f_b, f_a).astype(BF)
    grown = sgrad_s[rows16, :].astype(F32)
    out_rows = act_p[:, lanes_of(5)].astype(F32)
    known = jnp.where(ids((16, TILE), 0) < 3, out_rows, 0.0).astype(BF)
    delta_ref[...] = mm(known, grown.astype(BF), TN)
    hi, mid, lo = [part.astype(F32) for part in split3(ends[0] * ends[1] * d_b)]
    pieces = [hi, mid, lo, grown[0:1], grown[1:2], grown[2:3]]
    for k in range(3):
        pieces.append(
            jnp.concatenate([out_rows[k : k + 1], jnp.zeros((1, 3 * TILE), F32)], axis=1)
        )
    pieces.append(jnp.zeros((7, 4 * TILE), F32))
    mid_ref[TILE : TILE + 16, :] = jnp.concatenate(pieces, axis=0).astype(BF)


def slope_of(pre):
    sig = sigmoid(pre)
    return sig * (1.0 + pre * (1.0 - sig))


def head_sums(*quantities):
    found = []
    head = ids((8, 4 * TILE), 1) // HALF
    pick = (ids((8, 4 * TILE), 0) == head).astype(BF)
    for tiles in quantities:
        x = jnp.concatenate(tiles, axis=1)
        hi = x.astype(BF)
        lo = (x - hi.astype(F32)).astype(BF)
        found.append(mm(pick, hi, NT) + mm(pick, lo, NT))
    return found


def skip_rows(skip_ref, r):
    lane_row = ids((1, TILE), 1)
    found = []
    for j in range(4):
        at = 8 * r + 2 * j
        found.append(jnp.where(lane_row < HALF, skip_ref[at], skip_ref[at + 1]))
    return found


def second_kernel(
    dp,
    acts,
    actm,
    pres,
    prem,
    scaled_s,
    step_e,
    toend_e,
    ds_r,
    act_p,
    pre_p,
    scaled_p,
    skip_ref,
    base_ref,
    coef_ref,
    mslope_ref,
    gmap_ref,
    gsum_ref,
    stepsum_ref,
    skip_acc,
):
    quad, r, f = place()
    high = quad == 1
    skip_row = skip_rows(skip_ref, r)
    skip_acc[...] = jnp.zeros_like(skip_acc)
    half_lane = ids((TILE, TILE), 1) < HALF
    row8 = ids((8, TILE), 0)
    col_q = ids((TILE, TILE), 1)
    seen = ids((TILE, TILE), 0) <= col_q
    for i in range(4):
        rows = slice(i * TILE, (i + 1) * TILE)
        in_map = patched(actm, lanes_of(0), act_p, lanes_of(4), i, high)
        out_map = patched(actm, lanes_of(1), act_p, lanes_of(5), i, high)
        score = mm(in_map, out_map, NT)
        ds8 = ds_r[8 * i : 8 * i + 8, :]
        cols = columns(ds8)
        grad_score = jnp.zeros((TILE, TILE), F32)
        gsum = jnp.zeros((8, TILE), F32)
        rcol = jnp.zeros((TILE, TILE), F32)
        products = []
        for j in range(4):
            sc = patched(scaled_s, lanes_of(j), scaled_p, lanes_of(j), i, high)
            dy = dp[rows, lanes_of(j)]
            diag = jnp.zeros((TILE, TILE), F32)
            for e in range(2):
                h = 2 * j + e
                part = half_lane if e == 0 else jnp.logical_not(half_lane)
                gm = mm(jnp.where(part, sc, jnp.zeros_like(sc)), dy, NT)
                spread = ds8[h : h + 1, :] - cols[:, h : h + 1]
                decay = jnp.exp(jnp.where(seen, spread, -1e30))
                gd = gm * decay
                grad_score = grad_score + gd
                both = gd * score
                rcol = jnp.where(col_q == h, jnp.sum(both, axis=1, keepdims=True), rcol)
                gsum = gsum + jnp.where(row8 == h, jnp.sum(both, axis=0, keepdims=True), 0.0)
                mix = (score * decay).astype(BF)
                diag = diag + mm(mix, jnp.where(part, dy, jnp.zeros_like(dy)))
            lanes = lanes_of(j)
            sigf = patched(acts, lanes, act_p, lanes, i, high).astype(F32)
            dyf = dy.astype(F32)
            step = step_e[rows, lanes]
            slope = slope_of(patched(pres, lanes, pre_p, lanes, i, high))
            base_ref[rows, lanes] = (skip_row[j] * dyf + diag * step) * slope
            coef_ref[rows, lanes] = toend_e[rows, lanes] * step * slope
            products.append(diag * sigf)
            skip_acc[:, lanes] += eights(dyf * sigf)
        stepsum_ref[8 * i : 8 * i + 8, :] = head_sums(products)[0]
        for j in range(2):
            mslope_ref[rows, lanes_of(j)] = slope_of(
                patched(prem, lanes_of(j), pre_p, lanes_of(4 + j), i, high)
            )
        gs = grad_score.astype(BF)
        gmap_ref[rows, lanes_of(0)] = mm(gs, out_map)
        gmap_ref[rows, lanes_of(1)] = mm(gs, in_map, TN)
        gsum_ref[8 * i : 8 * i + 8, :] = gsum - jnp.transpose(rcol)[0:8, :]


def eights(x):
    return jnp.sum(x.reshape(x.shape[0] // 8, 8, x.shape[1]), axis=0)


def end_rows_of(exp_e):
    return [exp_e[(i + 1) * TILE - 8 : (i + 1) * TILE, :][7:8, :] for i in range(4)]


def taps_back(gp, i, lanes, taps):
    base = (i % 2) * TILE
    raw = taps[3] * gp[i // 2, base : base + TILE, lanes]
    for k in range(3):
        start = base + 3 - k
        raw = raw + taps[k] * gp[i // 2, start : start + TILE, lanes]
    return raw


def fill_pads(gp, high):
    first = gp[1, 0:8, :]
    gp[0, 2 * TILE : 2 * TILE + 8, :] = jnp.where(high, first, jnp.zeros_like(first))
    gp[1, 2 * TILE : 2 * TILE + 8, :] = jnp.zeros_like(first)


def spill_of(first, taps):
    grads = jnp.concatenate([jnp.zeros((8, TILE), F32), first], axis=0)
    spill = jnp.zeros((8, TILE), F32)
    for k in range(3):
        spill = spill + taps[k] * pltpu.roll(grads, 5 + k, 0)[8:]
    return spill


def tap_sums(here, x, edge_ref, i, lanes, edge_lanes, high, sums):
    base = (i % 2) * TILE
    if i % 2 == 1:
        windows = [x[i // 2, base + 5 + k : base + 5 + k + TILE, lanes] for k in range(4)]
    else:
        first = x[i // 2, 0:8, lanes] + jnp.where(
            boundary_chunk(i, high), edge_ref[:, edge_lanes], 0.0
        )
        block = jnp.concatenate([first, x[i // 2, 8 : TILE + 8, lanes]], axis=0)
        windows = [rolled(block, k) for k in range(4)]
    for k in range(4):
        sums[k] = sums[k] + eights(here * windows[k])
    sums[4] = sums[4] + eights(here)


def maps_kernel(
    midg_ref,
    midf_ref,
    s_s,
    t_s,
    delta_ref,
    exp_e,
    mslope_ref,
    weighted_s,
    weighted_p,
    sgrad_s,
    gmap_ref,
    xm,
    edge_ref,
    mine_ref,
    one_ref,
    two_ref,
    hlow_ref,
    clow_ref,
    endrow_ref,
    h_s,
    c_s,
    gm,
):
    quad, r, f = place()
    high = quad == 1
    even = lax.rem(f, 2) == 0
    ends = end_rows_of(exp_e)
    f_in = midf_ref[0:TILE, :].astype(F32)
    extra = midf_ref[TILE : TILE + 16, :].astype(F32)
    row16 = ids((16, 4 * TILE), 0)
    across = jnp.sum(jnp.where(row16 < 3, extra, 0.0), axis=0, keepdims=True)
    left_out = jnp.logical_and(row16 >= 3, row16 < 6)
    grown = jnp.where(left_out, extra, 0.0).astype(BF)
    out_rows = jnp.where(left_out[:, 0:TILE], pltpu.roll(extra[:, 0:TILE], 13, 0), 0.0).astype(BF)
    g_in = midg_ref[...].astype(F32) + mm(out_rows, grown, TN)
    t2 = t_s[2] + jnp.where(high, 0.0, delta_ref[...])
    f_a = ends[1] * s_s[0] + s_s[1]
    h_s[0] = jnp.where(high, f_in, 0.0)
    h_s[1] = ends[0] * h_s[0] + s_s[0]
    h_s[2] = jnp.where(high, ends[1] * h_s[1] + s_s[1], across * f_a + f_in)
    h_s[3] = ends[2] * h_s[2] + s_s[2]
    g_b = t2 + ends[2] * t_s[3]
    c_s[3] = jnp.where(high, g_in, 0.0)
    c_s[2] = t_s[3] + ends[3] * c_s[3]
    c_s[1] = jnp.where(high, t2 + ends[2] * c_s[2], g_in + across * g_b)
    c_s[0] = t_s[1] + ends[1] * c_s[1]
    taps_of = [map_tap_rows(j, mine_ref)[0] for j in range(2)]
    sums = [[jnp.zeros((8, TILE), F32) for _ in range(5)] for _ in range(2)]
    end_rows = []
    every = slice(0, 4 * TILE)
    for i in range(4):
        rows = slice(i * TILE, (i + 1) * TILE)
        base = (i % 2) * TILE
        hlow_ref[i] = h_s[i].astype(BF)
        clow_ref[i] = c_s[i].astype(BF)
        end_rows.append(jnp.sum(h_s[i] * c_s[i], axis=0, keepdims=True) * ends[i])
        grads = (
            mm(patched(weighted_s, every, weighted_p, every, i, high), clow_ref[i], NT) + gmap_ref[rows, lanes_of(0)],
            mm(sgrad_s[rows, :], hlow_ref[i], NT) + gmap_ref[rows, lanes_of(1)],
        )
        for j in range(2):
            here = grads[j] * mslope_ref[rows, lanes_of(j)]
            gm[i // 2, base : base + TILE, lanes_of(j)] = here
            tap_sums(here, xm, edge_ref, i, lanes_of(j), lanes_of(4 + j), high, sums[j])
    fill_pads(gm, high)
    for i in range(4):
        rows = slice(i * TILE, (i + 1) * TILE)
        raws = [taps_back(gm, i, lanes_of(j), taps_of[j]) for j in range(2)]
        one_ref[rows, :] = jnp.where(even, raws[0], raws[1]).astype(BF)
        two_ref[rows, :] = jnp.where(even, raws[1], raws[0]).astype(BF)
    first = jnp.where(high, gm[0, 0:8, :], gm[1, 0:8, :])
    endrow_ref[...] = jnp.concatenate(end_rows + [jnp.zeros((4, 4 * TILE), F32)], axis=0)
    row8 = ids((8, TILE), 0)
    tails = []
    for j in range(2):
        five = jnp.zeros((8, TILE), F32)
        for t in range(5):
            five = jnp.where(row8 == t, jnp.sum(sums[j][t], axis=0, keepdims=True), five)
        hi, lo, _ = split3(five)
        zero8 = jnp.zeros((8, TILE), F32)
        tails.append(
            jnp.concatenate(
                [spill_of(first[:, lanes_of(j)], taps_of[j]), zero8, hi.astype(F32), lo.astype(F32)], axis=0
            )
        )
    one_ref[4 * TILE : 4 * TILE + 32, :] = jnp.where(even, tails[0], tails[1]).astype(BF)
    two_ref[4 * TILE : 4 * TILE + 32, :] = jnp.where(even, tails[1], tails[0]).astype(BF)


def third_kernel(
    hlow_ref,
    clow_ref,
    endrow_ref,
    xs,
    dp,
    acts,
    actm,
    edge_ref,
    act_p,
    toend_e,
    exp_e,
    step_r,
    sig_r,
    base_ref,
    coef_ref,
    gsum_ref,
    stepsum_ref,
    skip_acc,
    taps_ref,
    alog_ref,
    gp,
    blk,
    spill_ref,
    params_ref,
):
    quad, r, f = place()
    high = quad == 1
    row8 = ids((8, TILE), 0)
    lane8 = ids((8, TILE), 1)
    rate8 = -jnp.exp(head_row(alog_ref, r))
    row_q = ids((TILE, TILE), 0)
    col_q = ids((TILE, TILE), 1)
    tail_sums = jnp.concatenate(
        [(row_q >= col_q).astype(F32), (row_q < col_q).astype(F32)], axis=0
    )
    sums = [[jnp.zeros((8, TILE), F32) for _ in range(5)] for _ in range(4)]
    alog_acc = jnp.zeros((8, TILE), F32)
    ddt_acc = jnp.zeros((8, TILE), F32)
    for i in range(4):
        rows = slice(i * TILE, (i + 1) * TILE)
        at8 = slice(8 * i, 8 * i + 8)
        base = (i % 2) * TILE
        off = mm(patched(actm, lanes_of(1), act_p, lanes_of(5), i, high), hlow_ref[i])
        gw = mm(patched(actm, lanes_of(0), act_p, lanes_of(4), i, high), clow_ref[i])
        end_row = endrow_ref[i : i + 1, :]
        gsum = gsum_ref[at8, :]
        end_sum = jnp.zeros((8, TILE), F32)
        offs, backs = [], []
        for j in range(4):
            lanes = lanes_of(j)
            sigf = patched(acts, lanes, act_p, lanes, i, high).astype(F32)
            offs.append(dp[rows, lanes].astype(F32) * exp_e[rows, lanes] * off[:, lanes])
            backs.append(gw[:, lanes] * toend_e[rows, lanes] * sigf)
            end_sum = end_sum + jnp.where(row8 == 2 * j + lane8 // HALF, end_row[:, lanes], 0.0)
            here = base_ref[rows, lanes] + gw[:, lanes] * coef_ref[rows, lanes]
            gp[i // 2, base : base + TILE, lanes] = here
            tap_sums(here, xs, edge_ref, i, lanes, lanes, high, sums[j])
        offsum, backsum = head_sums(offs, backs)
        gsum = gsum + offsum
        stepsum = stepsum_ref[at8, :] + backsum
        back = backsum * step_r[at8, :]
        grad_log = mm_f32(jnp.concatenate([gsum, back], axis=1), tail_sums) + jnp.sum(
            end_sum, axis=1, keepdims=True
        )
        ddt = (grad_log * rate8 + stepsum) * sig_r[at8, :]
        blk[2 * i] = ddt
        blk[2 * i + 1] = pltpu.roll(ddt, HALF, 1)
        ddt_acc = ddt_acc + ddt
        alog_acc = alog_acc + grad_log * step_r[at8, :]
    fill_pads(gp, high)
    rows = []
    for j in range(4):
        taps = [taps_ref[k : k + 1, at_tile((4 * r + j) * TILE)] for k in range(4)]
        first = jnp.where(high, gp[0, 0:8, lanes_of(j)], gp[1, 0:8, lanes_of(j)])
        spill_ref[:, lanes_of(j)] = spill_of(first, taps)
        for t in range(5):
            rows.append(jnp.sum(sums[j][t], axis=0, keepdims=True))
    alog = jnp.sum(alog_acc * rate8, axis=1, keepdims=True)
    ddtb = jnp.sum(ddt_acc, axis=1, keepdims=True)
    skips = jnp.zeros((8, TILE), F32)
    for j in range(4):
        total = jnp.sum(skip_acc[:, lanes_of(j)], axis=0, keepdims=True)
        skips = skips + jnp.where(row8 == 2 * j + lane8 // HALF, total, 0.0)
    skips = jnp.sum(skips, axis=1, keepdims=True)
    three = jnp.where(lane8 == 0, alog, jnp.where(lane8 == 1, ddtb, skips))
    flat = columns(jnp.where(lane8 < 3, three, 0.0))
    trio = flat[0:1] + pltpu.roll(flat[0:8], 32, 1)[1:2] + pltpu.roll(flat[0:8], 64, 1)[2:3]
    trio = pltpu.roll(jnp.broadcast_to(trio, (8, TILE)), 8 * r, 1)[0:1]
    params_ref[...] = jnp.concatenate(rows + [trio, jnp.zeros((3, TILE), F32)], axis=0)


def split_params(params):
    hi, lo, _ = split3(params)
    return jnp.concatenate([hi[0:16], hi[16:32], lo[0:16], lo[16:32]], axis=1)


def whole_params(value):
    value = value.astype(F32)
    return jnp.concatenate(
        [
            value[:, lanes_of(0)] + value[:, lanes_of(2)],
            value[:, lanes_of(1)] + value[:, lanes_of(3)],
        ],
        axis=0,
    )


def cross_kernel(scale, params_ref, spill_ref, one_ref, two_ref, cross_ref):
    tails = [ref[4 * TILE : 4 * TILE + 32, :].astype(F32) for ref in (one_ref, two_ref)]
    fives = [tail[16:24] + tail[24:32] for tail in tails]
    params = jnp.concatenate(
        [
            params_ref[0:20],
            fives[0][0:5],
            fives[1][0:5],
            params_ref[20:21],
            jnp.zeros((1, TILE), F32),
        ],
        axis=0,
    )
    maps = jnp.concatenate([tails[0][0:8], tails[1][0:8], jnp.zeros((8, 2 * TILE), F32)], axis=1)
    cross_ref[0:16, :] = jnp.concatenate([spill_ref[...], maps], axis=0).astype(BF)
    cross_ref[16:32, :] = split_params(params * scale)


def send_kernel(gp, taps_ref, y0, y1, y2, y3, dx):
    quad, r, f = place()
    for j in range(4):
        lanes = lanes_of(j)
        taps = [taps_ref[k : k + 1, at_tile((4 * r + j) * TILE)] for k in range(4)]
        for i in range(4):
            dx[i * TILE : (i + 1) * TILE, lanes] = taps_back(gp, i, lanes, taps).astype(BF)
    for k, y in enumerate((y0, y1, y2, y3)):
        s = lax.bitwise_xor(r, k)
        for e, at in ((0, HALF * s), (1, 2 * TILE + HALF * (3 - s))):
            y[e * HALF : (e + 1) * HALF, :] = dx[pl.ds(pl.multiple_of(at, HALF), HALF), :]


def merge_kernel(own_ref, other_ref, one_ref, two_ref, blk, w0, w1, w2, w3):
    quad, r, f = place()
    lane8 = ids((8, TILE), 1)
    param_rows = split_params(
        whole_params(own_ref[16:32, :]) + whole_params(other_ref[16:32, :])
    )
    spill = other_ref[0:16, :].astype(F32)
    for k, w in enumerate((w0, w1, w2, w3)):
        s = lax.bitwise_xor(r, k)
        for e, at in ((0, HALF * s), (1, 2 * TILE + HALF * (3 - s))):
            rows = pl.ds(pl.multiple_of(at, HALF), HALF)
            w[0:HALF, lanes_of(e)] = one_ref[rows, :]
            w[0:HALF, lanes_of(2 + e)] = two_ref[rows, :]
        here = jnp.where(lane8 < HALF, blk[s], pltpu.roll(blk[7 - s], HALF, 1))
        hi, mid, _ = split3(here)
        w[HALF : HALF + 16, :] = jnp.concatenate(
            [
                jnp.concatenate([hi.astype(F32), spill[0:8, 0 : 2 * TILE], spill[8:16, 0:TILE]], axis=1),
                jnp.concatenate(
                    [
                        mid.astype(F32),
                        spill[0:8, 2 * TILE : 4 * TILE],
                        spill[8:16, TILE : 2 * TILE],
                    ],
                    axis=1,
                ),
            ],
            axis=0,
        ).astype(BF)
        w[HALF + 16 : HALF + 32, :] = param_rows


def last_kernel(
    y0, y1, y2, y3, w0, w1, w2, w3, dsig_ref, dmap_ref, ddt_ref, taps_ref, mtaps_ref, bias_ref, mbias_ref, *trio_refs
):
    quad, r, f = place()
    ys = (y0, y1, y2, y3)
    ws = (w0, w1, w2, w3)
    third = jnp.logical_and(quad == 0, r == 3)
    fourth = jnp.logical_and(quad == 1, r == 0)
    params = []
    trio = jnp.zeros((1, TILE), F32)
    for k, y in enumerate(ys):
        s = lax.bitwise_xor(r, k)
        cols = at_tile(s * 4 * TILE, 4 * TILE)
        dsig_ref[:, cols] = y[0:TILE, :].astype(F32)
        extra = ws[k][HALF : HALF + 16, :].astype(F32)
        spill = jnp.concatenate(
            [extra[0:8, TILE : 3 * TILE], extra[8:16, TILE : 3 * TILE]], axis=1
        )
        dsig_ref[HALF - 8 : HALF, cols] += jnp.where(third, spill, 0.0)
        dsig_ref[TILE - 8 : TILE, cols] += jnp.where(fourth, spill, 0.0)
        ddt_ref[pl.ds(pl.multiple_of(8 * s, 8), 8), :] = extra[0:8, 0:TILE] + extra[8:16, 0:TILE]
        param = whole_params(ws[k][HALF + 16 : HALF + 32, :])
        params.append(param)
        for j in range(4):
            lanes = at_tile((4 * s + j) * TILE)
            taps_ref[0:4, lanes] = param[5 * j : 5 * j + 4]
            bias_ref[0:1, lanes] = param[5 * j + 4 : 5 * j + 5]
        trio = trio + param[30:31]
    trio = jnp.broadcast_to(trio, (8, TILE))
    for t, ref in enumerate(trio_refs):
        moved = trio if t == 0 else pltpu.roll(trio, TILE - 32 * t, 1)
        ref[...] = moved[0:1, 0:32]
    own = lax.div(r, 2)
    swap = f >= 2
    for pair in range(2):
        group = own if pair == 0 else 1 - own
        a, b = 2 * pair, 2 * pair + 1
        for j in range(2):
            where = jnp.where(swap, 1 - j, j)
            lanes = at_tile((2 * where + group) * TILE)
            for e in range(2):
                dmap_ref[e * HALF : (e + 1) * HALF, lanes] = ws[a][
                    0:HALF, lanes_of(2 * j + e)
                ].astype(F32) + ws[b][0:HALF, lanes_of(2 * j + e)].astype(F32)
            spill = jnp.zeros((8, TILE), F32)
            for w in (ws[a], ws[b]):
                extra = w[HALF : HALF + 16, 3 * TILE : 4 * TILE].astype(F32)
                spill = spill + extra[8 * j : 8 * j + 8]
            dmap_ref[HALF - 8 : HALF, lanes] += jnp.where(third, spill, 0.0)
            dmap_ref[TILE - 8 : TILE, lanes] += jnp.where(fourth, spill, 0.0)
            five = params[a][20 + 5 * j : 25 + 5 * j] + params[b][20 + 5 * j : 25 + 5 * j]
            mtaps_ref[0:4, lanes] = five[0:4]
            mbias_ref[0:1, lanes] = five[4:5]


ROUTE_ONE = [(0, 0), (2, 1), (1, 2), (3, 3)]
ROUTE_TWO = [(0, 2), (2, 3), (1, 0), (3, 1)]


def back(route):
    return [(target, source) for source, target in route]


def shards_quad(
    sig_raw,
    map_raw,
    step_size_logits,
    d_out,
    sig_taps,
    map_taps,
    sig_bias,
    map_bias,
    a_log,
    dt_bias,
    skip_gain,
):
    ctx = lax.axis_size("ctx")
    rows, sig_width = sig_raw.shape
    vmem = pl.BlockSpec(memory_space=pltpu.VMEM)
    smem = pl.BlockSpec(memory_space=pltpu.SMEM)
    hbm = pl.BlockSpec(memory_space=pltpu.HBM)

    def call(kernel, out_shape, in_specs, out_specs, scratch, mib, cost):
        return pl.pallas_call(
            kernel,
            out_shape=out_shape,
            in_specs=in_specs,
            out_specs=out_specs,
            scratch_shapes=scratch,
            compiler_params=pltpu.CompilerParams(vmem_limit_bytes=mib * 1024 * 1024),
            cost_estimate=pl.CostEstimate(flops=cost, bytes_accessed=cost // 100, transcendentals=0),
        )

    def shape(*dims, kind=F32):
        return jax.ShapeDtypeStruct(dims, kind)

    inside = [[(c, c ^ k) for c in range(ctx)] for k in range(4)]
    over = [(c, c ^ 4) for c in range(ctx)]
    total = 4 * TILE
    wide, narrow = 6 * TILE, 4 * TILE
    owned = map_taps.shape[1]
    sig_bias_row = sig_bias[None, :]
    *packed, map_params = call(
        pack_kernel,
        (shape(TILE + HALF + 16, narrow, kind=BF),) * 4 + (shape(8, owned),),
        [hbm, hbm, hbm, vmem, vmem],
        (vmem,) * 5,
        [pltpu.VMEM((32, TILE), F32), pltpu.SemaphoreType.DMA((21,))],
        60,
        10**6,
    )(map_raw, step_size_logits.T, d_out, map_taps, map_bias[None, :])
    us = [packed[0]] + [lax.ppermute(packed[k], "ctx", inside[k]) for k in (1, 2, 3)]
    map_one = lax.ppermute(map_params, "fsdp", back(ROUTE_ONE))
    map_two = lax.ppermute(map_params, "fsdp", back(ROUTE_TWO))
    packed = call(
        pack_sig_kernel,
        (shape(TILE, narrow, kind=BF),) * 4,
        [hbm],
        (vmem,) * 4,
        [pltpu.SemaphoreType.DMA((4,))],
        60,
        10**6,
    )(sig_raw)
    vs = [packed[0]] + [lax.ppermute(packed[k], "ctx", inside[k]) for k in (1, 2, 3)]
    midg, dp, xm, actm, prem, sgrad, step_e, toend_e, exp_e, t_s, step_r, ds_r, sig_r, mine = call(
        grads_kernel,
        (
            shape(TILE, narrow, kind=BF),
            shape(total, narrow, kind=BF),
            shape(2, 2 * TILE + 8, 2 * TILE),
            shape(total, 2 * TILE, kind=BF),
            shape(total, 2 * TILE),
            shape(total, narrow, kind=BF),
            shape(total, narrow),
            shape(total, narrow),
            shape(total, narrow),
            shape(4, TILE, narrow),
            shape(32, TILE),
            shape(32, TILE),
            shape(32, TILE),
            shape(16, TILE),
        ),
        [vmem] * 6 + [smem] * 2,
        (vmem,) * 14,
        [pltpu.VMEM((4, 8, TILE), F32)],
        24,
        2 * 10**9,
    )(*us, map_one, map_two, a_log, dt_bias)
    midg = lax.ppermute(midg, "ctx", over)
    halo = call(edge_kernel, shape(16, wide, kind=BF), [vmem] * 5, vmem, [], 16, 10**6)(*vs, xm)
    halo = lax.ppermute(halo, "ctx", over)
    xs, acts, pres, scaled, weighted = call(
        first_kernel,
        (
            shape(2, 2 * TILE + 8, narrow),
            shape(total, narrow, kind=BF),
            shape(total, narrow),
            shape(total, narrow, kind=BF),
            shape(total, narrow, kind=BF),
        ),
        [vmem] * 8,
        (vmem,) * 5,
        [],
        24,
        2 * 10**9,
    )(*vs, step_e, toend_e, sig_taps, sig_bias_row)
    midf, s_s, delta, edge, act_p, pre_p, scaled_p, weighted_p = call(
        states_kernel,
        (
            shape(TILE + 16, narrow, kind=BF),
            shape(4, TILE, narrow),
            shape(TILE, narrow),
            shape(8, wide),
            shape(16, wide, kind=BF),
            shape(16, wide),
            shape(16, narrow, kind=BF),
            shape(16, narrow, kind=BF),
        ),
        [vmem] * 12,
        (vmem,) * 8,
        [],
        24,
        10**9,
    )(halo, xs, xm, actm, weighted, sgrad, step_e, toend_e, exp_e, sig_taps, sig_bias_row, mine)
    midf = lax.ppermute(midf, "ctx", over)
    base, coef, mslope, gmap, gsum, stepsum, skips = call(
        second_kernel,
        (
            shape(total, narrow),
            shape(total, narrow),
            shape(total, 2 * TILE),
            shape(total, 2 * TILE),
            shape(32, TILE),
            shape(32, TILE),
            shape(8, narrow),
        ),
        [vmem] * 12 + [smem],
        (vmem,) * 7,
        [],
        24,
        5 * 10**9,
    )(
        dp,
        acts,
        actm,
        pres,
        prem,
        scaled,
        step_e,
        toend_e,
        ds_r,
        act_p,
        pre_p,
        scaled_p,
        skip_gain,
    )
    one, two, hlow, clow, endrow = call(
        maps_kernel,
        (
            shape(total + 32, TILE, kind=BF),
            shape(total + 32, TILE, kind=BF),
            shape(4, TILE, narrow, kind=BF),
            shape(4, TILE, narrow, kind=BF),
            shape(8, narrow),
        ),
        [vmem] * 14,
        (vmem,) * 5,
        [
            pltpu.VMEM((4, TILE, narrow), F32),
            pltpu.VMEM((4, TILE, narrow), F32),
            pltpu.VMEM((2, 2 * TILE + 8, 2 * TILE), F32),
        ],
        24,
        2 * 10**9,
    )(
        midg,
        midf,
        s_s,
        t_s,
        delta,
        exp_e,
        mslope,
        weighted,
        weighted_p,
        sgrad,
        gmap,
        xm,
        edge,
        mine,
    )
    one = lax.ppermute(one, "fsdp", ROUTE_ONE)
    two = lax.ppermute(two, "fsdp", ROUTE_TWO)
    gp, blk, spill, params = call(
        third_kernel,
        (
            shape(2, 2 * TILE + 8, narrow),
            shape(8, 8, TILE),
            shape(8, narrow),
            shape(24, TILE),
        ),
        [vmem] * 19 + [smem],
        (vmem,) * 4,
        [],
        24,
        3 * 10**9,
    )(
        hlow,
        clow,
        endrow,
        xs,
        dp,
        acts,
        actm,
        edge,
        act_p,
        toend_e,
        exp_e,
        step_r,
        sig_r,
        base,
        coef,
        gsum,
        stepsum,
        skips,
        sig_taps,
        a_log,
    )
    scale = 1.0 / math.sqrt(float(ctx * rows))
    cross = call(
        functools.partial(cross_kernel, scale),
        shape(32, narrow, kind=BF),
        [vmem] * 4,
        vmem,
        [],
        16,
        10**6,
    )(params, spill, one, two)
    other = lax.ppermute(cross, "ctx", over)
    ys = call(
        send_kernel,
        (shape(TILE, narrow, kind=BF),) * 4,
        [vmem] * 2,
        (vmem,) * 4,
        [pltpu.VMEM((total, narrow), BF)],
        16,
        10**9,
    )(gp, sig_taps)
    ys = [ys[0]] + [lax.ppermute(ys[k], "ctx", inside[k]) for k in (1, 2, 3)]
    ws = call(
        merge_kernel,
        (shape(HALF + 32, narrow, kind=BF),) * 4,
        [vmem] * 5,
        (vmem,) * 4,
        [],
        16,
        10**6,
    )(cross, other, one, two, blk)
    ws = [ws[0]] + [lax.ppermute(ws[k], "ctx", inside[k]) for k in (1, 2, 3)]
    d_sig, d_map, d_dt, taps, map_taps_grad, bias, map_bias_grad, *trio = call(
        last_kernel,
        (
            shape(rows, sig_width),
            shape(rows, owned),
            shape(32, TILE),
            shape(4, sig_width),
            shape(4, owned),
            shape(1, sig_width),
            shape(1, owned),
        )
        + (shape(1, 32),) * 3,
        [vmem] * 8,
        (vmem,) * 10,
        [],
        16,
        10**6,
    )(*ys, *ws)
    return (
        d_sig,
        d_map,
        d_dt.T,
        taps,
        map_taps_grad,
        bias[0],
        map_bias_grad[0],
        *(t[0] for t in trio),
    )


def shards(*args):
    sig_raw, map_raw, step_size_logits = args[:3]
    ctx = lax.axis_size("ctx")
    fsdp = lax.axis_size("fsdp")
    fits = (
        ctx == 8
        and fsdp == 4
        and sig_raw.shape == (TILE, 2048)
        and map_raw.shape == (TILE, 2 * GROUPS * STATE)
        and step_size_logits.shape[1] == 32
    )
    return shards_quad(*args) if fits else shards_chain(*args)


def solution(mesh):
    return jax.shard_map(
        shards,
        mesh=mesh,
        in_specs=(
            P("ctx", "fsdp"),
            P("ctx", None),
            P("ctx", "fsdp"),
            P("ctx", "fsdp"),
            P(None, "fsdp"),
            P(None, "fsdp"),
            P("fsdp"),
            P("fsdp"),
            P("fsdp"),
            P("fsdp"),
            P("fsdp"),
        ),
        out_specs=(
            P("ctx", "fsdp"),
            P("ctx", "fsdp"),
            P("ctx", "fsdp"),
            P(None, "fsdp"),
            P(None, "fsdp"),
            P("fsdp"),
            P("fsdp"),
            P("fsdp"),
            P("fsdp"),
            P("fsdp"),
        ),
        check_vma=False,
    )
```

```python
import functools
import math

import jax
import jax.numpy as jnp
from jax import lax
from jax.experimental import pallas as pl
from jax.experimental.pallas import tpu as pltpu
from jax.sharding import PartitionSpec as P

HEADS = 128
HDIM = 64
STATE = 128
GROUPS = 8


def prefix(part, axis, combine, identity, reverse):
    count = lax.axis_size(axis)
    place = lax.axis_index(axis)
    ahead = count - 1 - place if reverse else place
    gathered = jax.tree.map(lambda a: lax.all_gather(a, axis), part)
    state = jax.tree.map(lambda a, e: jnp.zeros_like(a) + jnp.asarray(e, a.dtype), part, identity)

    def one(lap, state):
        source = count - 1 - lap if reverse else lap
        return combine(
            state, jax.tree.map(lambda a: lax.dynamic_index_in_dim(a, source, 0, False), gathered)
        )

    return lax.fori_loop(0, ahead, one, state)


def broadcast(x, axis, root):
    mine = lax.axis_index(axis) == root
    return lax.psum(jnp.where(mine, x, jnp.zeros_like(x)), axis)


def extended(block, sides, width):
    for axis, dim in sides:
        count = lax.axis_size(axis)
        forward = [(i, i + 1) for i in range(count - 1)]
        backward = [(target, source) for source, target in forward]
        low = lax.ppermute(
            lax.slice_in_dim(block, block.shape[dim] - width, None, axis=dim), axis, forward
        )
        high = lax.ppermute(lax.slice_in_dim(block, 0, width, axis=dim), axis, backward)
        block = jnp.concatenate([low, block, high], axis=dim)
    return block


def ein(form, left, right):
    return jnp.einsum(form, left, right, preferred_element_type=jnp.float32)


def silu_slope(value):
    sig = jax.nn.sigmoid(value)
    return sig * (1.0 + value * (1.0 - sig))


def block_parts(activated, dt_rows, a_log, dt_bias, groups):
    length = activated.shape[0]
    heads = dt_rows.shape[1]
    inner = heads * HDIM
    shared = groups * STATE
    ratio = heads // groups
    signal = activated[:, :inner].reshape(length, heads, HDIM)
    input_map = activated[:, inner : inner + shared].reshape(length, groups, STATE)
    output_map = activated[:, inner + shared :].reshape(length, groups, STATE)
    input_heads = jnp.repeat(input_map, ratio, axis=1)
    output_heads = jnp.repeat(output_map, ratio, axis=1)
    step = jax.nn.softplus(dt_rows + dt_bias)
    rate = -jnp.exp(a_log)
    row_ids = lax.broadcasted_iota(jnp.int32, (length, length), 0)
    col_ids = lax.broadcasted_iota(jnp.int32, (length, length), 1)
    lower = (row_ids >= col_ids).astype(jnp.float32)
    decay_sum = jnp.dot(lower, step * rate, precision=lax.Precision.HIGHEST)
    to_end = jnp.exp(decay_sum[-1][None, :] - decay_sum)
    scaled = (signal.astype(jnp.float32) * step[:, :, None]).astype(jnp.bfloat16)
    weighted = (scaled.astype(jnp.float32) * to_end[:, :, None]).astype(jnp.bfloat16)
    local = ein("qhp,qhn->hpn", weighted, input_heads)
    return (
        signal,
        input_map,
        output_map,
        input_heads,
        output_heads,
        step,
        rate,
        lower,
        decay_sum,
        scaled,
        to_end,
        weighted,
        local,
    )


def entry_grad(parts, d_rows):
    decay_sum = parts[8]
    output_heads = parts[4]
    scaled_grad = (d_rows.astype(jnp.float32) * jnp.exp(decay_sum)[:, :, None]).astype(jnp.bfloat16)
    return (scaled_grad, ein("thp,thn->hpn", scaled_grad, output_heads))


def block_grads(parts, d_rows, scaled_grad, h_in, carried, skip_gain, dt_rows, dt_bias):
    (
        signal,
        input_map,
        output_map,
        input_heads,
        output_heads,
        step,
        rate,
        lower,
        decay_sum,
        scaled,
        to_end,
        weighted,
        local,
    ) = parts
    length = d_rows.shape[0]
    heads = d_rows.shape[1]
    groups = input_map.shape[1]
    width_state = input_map.shape[2]
    ratio = heads // groups
    grad_f = d_rows.astype(jnp.float32)
    signal_f = signal.astype(jnp.float32)
    grad_skip = jnp.sum(grad_f * signal_f, axis=(0, 2))
    h_low = h_in.astype(jnp.bfloat16)
    carried_low = carried.astype(jnp.bfloat16)
    offset = jnp.exp(decay_sum)[:, :, None] * ein("thn,hpn->thp", output_heads, h_low)
    grad_sum = jnp.sum(grad_f * offset, axis=2)
    out_heads_grad = ein("thp,hpn->thn", scaled_grad, h_low)
    grad_weighted = ein("shn,hpn->shp", input_heads, carried_low)
    in_heads_grad = ein("shp,hpn->shn", weighted, carried_low)
    back = jnp.sum(grad_weighted * scaled.astype(jnp.float32), axis=2) * to_end
    end_term = jnp.exp(decay_sum[-1]) * jnp.sum(h_in * carried, axis=(1, 2))
    last_row = (lax.broadcasted_iota(jnp.int32, (length, 1), 0) == length - 1).astype(jnp.float32)
    grad_sum = grad_sum - back + last_row * (jnp.sum(back, axis=0) + end_term)[None, :]
    spread = decay_sum.T[:, :, None] - decay_sum.T[:, None, :]
    decay = jnp.where(lower[None] > 0, jnp.exp(jnp.minimum(spread, 0.0)), 0.0)
    score = ein("tgn,sgn->gts", output_map, input_map)
    mix = jnp.repeat(score, ratio, axis=0) * decay
    grad_mix = ein("thp,shp->hts", d_rows, scaled)
    grad_scaled = grad_weighted * to_end[:, :, None] + ein(
        "hts,thp->shp", mix.astype(jnp.bfloat16), d_rows
    )
    product = grad_mix * mix
    grad_sum = grad_sum + (jnp.sum(product, axis=2) - jnp.sum(product, axis=1)).T
    grad_score = jnp.sum((grad_mix * decay).reshape(groups, ratio, length, length), axis=1).astype(
        jnp.bfloat16
    )
    grad_outmap = ein("gts,sgn->tgn", grad_score, input_map) + jnp.sum(
        out_heads_grad.reshape(length, groups, ratio, width_state), axis=2
    )
    grad_in = ein("gts,tgn->sgn", grad_score, output_map) + jnp.sum(
        in_heads_grad.reshape(length, groups, ratio, width_state), axis=2
    )
    grad_log = jnp.dot(lower.T, grad_sum, precision=lax.Precision.HIGHEST)
    descent_increment = grad_log * rate + jnp.sum(grad_scaled * signal_f, axis=2)
    grad_signal = skip_gain[None, :, None] * grad_f + grad_scaled * step[:, :, None]
    grad_dt = descent_increment * jax.nn.sigmoid(dt_rows + dt_bias)
    decay_log_gradient = jnp.sum(grad_log * step, axis=0) * rate
    grad_act = jnp.concatenate(
        [
            grad_signal.reshape(length, heads * HDIM),
            grad_in.reshape(length, groups * width_state),
            grad_outmap.reshape(length, groups * width_state),
        ],
        axis=1,
    )
    return (grad_act, grad_dt, decay_log_gradient, jnp.sum(grad_dt, axis=0), grad_skip)


def link(earlier, later):
    return (earlier[0] + later[0], jnp.exp(later[0])[:, None, None] * earlier[1] + later[1])


def link_blocks(lower_pair, upper_pair):
    zero_rate = jnp.zeros_like(lower_pair[0])
    zero_state = jnp.zeros_like(lower_pair[1])
    below = prefix(lower_pair, "ctx", link, (zero_rate, zero_state), False)
    beyond = prefix(upper_pair, "ctx", link, (zero_rate, zero_state), True)
    total = jax.tree.map(
        lambda part: broadcast(part, "ctx", lax.axis_size("ctx") - 1), link(below, lower_pair)
    )
    return jnp.stack([below[1], link(total, beyond)[1]])


def conv_back(grad_pre, wide_grad, kernel_taps, padded, at_end, length):
    rim = kernel_taps.shape[0] - 1
    after = jnp.stack(
        [jnp.where(at_end, grad_pre[1, :rim], wide_grad[3 * rim : 4 * rim]), wide_grad[0:rim]]
    )
    padded_next = jnp.concatenate([grad_pre, after], axis=1)
    grad_raw = jnp.zeros(grad_pre.shape, jnp.float32)
    for tap in range(rim + 1):
        grad_raw = (
            grad_raw
            + kernel_taps[tap][None, None, :] * padded_next[:, rim - tap : rim - tap + length]
        )
    tap_grads = jnp.stack(
        [jnp.sum(grad_pre * padded[:, tap : tap + length], axis=(0, 1)) for tap in range(rim + 1)]
    )
    return (grad_raw, tap_grads, jnp.sum(grad_pre, axis=(0, 1)))


def first_rows(grad_pre, rim):
    return jnp.concatenate([grad_pre[0, :rim], grad_pre[1, :rim]], axis=0)


def shards_chain(
    sig_raw,
    map_raw,
    step_size_logits,
    d_out,
    sig_taps,
    map_taps,
    sig_bias,
    map_bias,
    a_log,
    dt_bias,
    skip_gain,
):
    all_map_taps, all_map_bias = (
        lax.all_gather(map_taps, "fsdp", axis=1, tiled=True),
        lax.all_gather(map_bias, "fsdp", axis=0, tiled=True),
    )
    kernel_taps = jnp.concatenate([sig_taps, all_map_taps], axis=1)
    kernel_bias = jnp.concatenate([sig_bias, all_map_bias], axis=0)
    kernel = kernel_taps.shape[0]
    rim = kernel - 1
    length = sig_raw.shape[0] // 2
    sig_width = sig_raw.shape[1]
    map_width = map_raw.shape[1]
    width = sig_width + map_width
    heads_here = step_size_logits.shape[1]
    ratio = HEADS // GROUPS
    group_count = max(1, heads_here // ratio)
    first_group = lax.axis_index("fsdp") * heads_here // ratio
    fsdp_count = lax.axis_size("fsdp")
    owned = map_width // fsdp_count
    map_start = lax.axis_index("fsdp") * owned
    raw_rows = jnp.concatenate([sig_raw, map_raw], axis=1).reshape(2, length, width)
    tails = jnp.concatenate([raw_rows[1, length - rim :], raw_rows[0, length - rim :]], axis=0)
    wide = extended(tails, (("ctx", 0),), rim)
    at_end = lax.axis_index("ctx") == lax.axis_size("ctx") - 1
    before = jnp.stack(
        [wide[0:rim], jnp.where(at_end, raw_rows[0, length - rim :], wide[3 * rim : 4 * rim])]
    )
    padded = jnp.concatenate([before, raw_rows], axis=1).astype(jnp.float32)
    preact = kernel_bias[None, None, :] + jnp.zeros((2, length, width), jnp.float32)
    for tap in range(kernel):
        preact = preact + kernel_taps[tap][None, None, :] * padded[:, tap : tap + length]
    activated = jax.nn.silu(preact).astype(jnp.bfloat16)
    maps_all = activated[:, :, sig_width:].reshape(2, length, 2, GROUPS, STATE)
    maps_mine = lax.dynamic_slice_in_dim(maps_all, first_group, group_count, 3)
    local_act = jnp.concatenate(
        [activated[:, :, :sig_width], maps_mine.reshape(2, length, 2 * group_count * STATE)], axis=2
    )
    dt_rows = step_size_logits.reshape(2, length, heads_here)
    grad_rows = d_out.reshape(2, length, heads_here, HDIM)

    def parts_of(act_block, dt_block):
        return block_parts(act_block, dt_block, a_log, dt_bias, group_count)

    parts = jax.vmap(parts_of)(local_act, dt_rows)
    scaled_grad, state_grad = jax.vmap(entry_grad)(parts, grad_rows)
    ends = parts[8][:, -1]
    h_ins = link_blocks((ends[0], parts[12][0]), (ends[1], parts[12][1]))
    carried_pair = link_blocks((ends[1], state_grad[1]), (ends[0], state_grad[0]))
    carried = jnp.stack([carried_pair[1], carried_pair[0]])
    grad_act, grad_dt, decay_log_gradient, grad_dtb, grad_skip = jax.vmap(
        block_grads, in_axes=(0, 0, 0, 0, 0, None, 0, None)
    )(parts, grad_rows, scaled_grad, h_ins, carried, skip_gain, dt_rows, dt_bias)
    slope = silu_slope(preact)
    grad_pre_sig = grad_act[:, :, :sig_width] * slope[:, :, :sig_width]
    grad_mine = grad_act[:, :, sig_width:].reshape(2, length, 2, group_count, STATE)
    zero_index = jnp.zeros((), jnp.int32)
    placed = lax.dynamic_update_slice(
        jnp.zeros((2, length, 2, GROUPS, STATE), jnp.float32),
        grad_mine,
        (zero_index, zero_index, zero_index, first_group, zero_index),
    )
    map_term = placed.reshape(2, length, map_width)
    map_owned = lax.psum_scatter(map_term, "fsdp", scatter_dimension=2, tiled=True)
    map_slope = lax.dynamic_slice_in_dim(slope[:, :, sig_width:], map_start, owned, 2)
    grad_pre = jnp.concatenate([grad_pre_sig, map_owned * map_slope], axis=2)
    own_taps = jnp.concatenate([sig_taps, map_taps], axis=1)
    own_padded = jnp.concatenate(
        [
            padded[:, :, :sig_width],
            lax.dynamic_slice_in_dim(padded[:, :, sig_width:], map_start, owned, 2),
        ],
        axis=2,
    )
    wide_grad = extended(first_rows(grad_pre, rim), (("ctx", 0),), rim)
    grad_raw, tap_grads, bias_grads = conv_back(
        grad_pre, wide_grad, own_taps, own_padded, at_end, length
    )
    map_raw_grad = grad_raw[:, :, sig_width:]
    map_tap_grad = tap_grads[:, sig_width:]
    map_bias_grad = bias_grads[sig_width:]
    sig_raw_grad = grad_raw[:, :, :sig_width]
    sig_tap_grad = tap_grads[:, :sig_width]
    sig_bias_grad = bias_grads[:sig_width]
    reduced = lax.psum(
        (
            sig_tap_grad,
            map_tap_grad,
            sig_bias_grad,
            map_bias_grad,
            jnp.sum(decay_log_gradient, axis=0),
            jnp.sum(grad_dtb, axis=0),
            jnp.sum(grad_skip, axis=0),
        ),
        "ctx",
    )
    scale = 1.0 / math.sqrt(float(lax.axis_size("ctx") * 2 * length))
    final = jax.tree.map(lambda grad_part: grad_part * scale, reduced)
    return (
        sig_raw_grad.reshape(2 * length, sig_width),
        map_raw_grad.reshape(2 * length, owned),
        grad_dt.reshape(2 * length, heads_here),
        final[0],
        final[1],
        final[2],
        final[3],
        final[4],
        final[5],
        final[6],
    )


TILE = 128
HALF = 64
NT = (((1,), (1,)), ((), ()))
TN = (((0,), (0,)), ((), ()))
NN = (((1,), (0,)), ((), ()))
BF = jnp.bfloat16
F32 = jnp.float32


def mm(a, b, dims=NN):
    return lax.dot_general(a, b, dims, preferred_element_type=F32)


def mm_f32(a, b, dims=NN):
    return lax.dot_general(a, b, dims, precision=lax.Precision.HIGHEST, preferred_element_type=F32)


def split3(x):
    hi = x.astype(BF)
    rest = x - hi.astype(F32)
    mid = rest.astype(BF)
    return hi, mid, (rest - mid.astype(F32)).astype(BF)


def ids(shape, dim):
    return lax.broadcasted_iota(jnp.int32, shape, dim)


def lanes_of(j):
    return slice(j * TILE, (j + 1) * TILE)


def place():
    ctx_place = lax.axis_index("ctx")
    quad = lax.div(ctx_place, 4)
    return quad, lax.rem(ctx_place, 4), lax.axis_index("fsdp")


def at_tile(start, width=TILE):
    return pl.ds(pl.multiple_of(start, TILE), width)


def pack_kernel(sig_ref, map_ref, dt_ref, dy_ref, mtaps_ref, mbias_ref, *rest):
    u_refs, tap_ref, (dt_in, sig_in, sems) = rest[:4], rest[4], rest[5:]
    quad, r, f = place()
    copies = []
    dt_copy = pltpu.make_async_copy(dt_ref, dt_in, sems.at[20])
    dt_copy.start()
    ends = pl.ds(pl.multiple_of(jnp.where(quad == 0, HALF - 16, TILE - 16), 16), 16)
    sig_copy = pltpu.make_async_copy(sig_ref.at[ends, :], sig_in, sems.at[21])
    sig_copy.start()

    def send(source, target):
        copy = pltpu.make_async_copy(source, target, sems.at[len(copies)])
        copy.start()
        copies.append(copy)

    half = map_ref.shape[1] // 2
    for k in (1, 2, 3, 0):
        dest = lax.bitwise_xor(r, k)
        cols = at_tile(dest * 4 * TILE, 4 * TILE)
        send(dy_ref.at[:, cols], u_refs[k].at[0:TILE, :])
        group = (2 * f + lax.div(dest, 2)) * TILE
        for j in range(2):
            for e in range(2):
                send(
                    map_ref.at[e * HALF : (e + 1) * HALF, at_tile(group + j * half)],
                    u_refs[k].at[TILE : TILE + HALF, lanes_of(2 * j + e)],
                )
    tap_ref[0:4, :] = mtaps_ref[...]
    tap_ref[4:5, :] = mbias_ref[...]
    tap_ref[5:8, :] = jnp.zeros_like(tap_ref[5:8, :])
    dt_copy.wait()
    sig_copy.wait()
    for k in range(4):
        dest = lax.bitwise_xor(r, k)
        hi, mid, lo = split3(dt_in[pl.ds(pl.multiple_of(8 * dest, 8), 8), :])
        edge = sig_in[:, at_tile(dest * 4 * TILE, 4 * TILE)].astype(F32)[8:16]
        top = jnp.concatenate([hi.astype(F32), lo.astype(F32), edge[:, 0 : 2 * TILE]], axis=1)
        low = jnp.concatenate(
            [mid.astype(F32), edge[:, 2 * TILE : 4 * TILE], jnp.zeros((8, TILE), F32)], axis=1
        )
        u_refs[k][TILE + HALF : TILE + HALF + 16, :] = jnp.concatenate([top, low], axis=0).astype(BF)
    for copy in copies:
        copy.wait()


def pack_sig_kernel(sig_ref, *rest):
    v_refs, sems = rest[:4], rest[4]
    r = place()[1]
    copies = []
    for k in (1, 2, 3, 0):
        dest = lax.bitwise_xor(r, k)
        copy = pltpu.make_async_copy(
            sig_ref.at[:, at_tile(dest * 4 * TILE, 4 * TILE)], v_refs[k], sems.at[k]
        )
        copy.start()
        copies.append(copy)
    for copy in copies:
        copy.wait()


def own_kernel(u_ref, v_ref, u_out, v_out):
    u_out[...] = u_ref[...]
    v_out[...] = v_ref[...]


def sig_tap_rows(j, taps_ref, bias_ref):
    at = at_tile((4 * place()[1] + j) * TILE)
    return [taps_ref[k : k + 1, at] for k in range(4)], bias_ref[0:1, at]


def map_tap_rows(j, mine_ref):
    return [mine_ref[8 * j + k : 8 * j + k + 1, :] for k in range(4)], mine_ref[
        8 * j + 4 : 8 * j + 5, :
    ]


def sigmoid(v):
    return 0.5 * jnp.tanh(0.5 * v) + 0.5


def rolled(block, k):
    return block[8:] if k == 3 else pltpu.roll(block, 3 - k, 0)[8:]


def columns(*rows8):
    total = 8 * len(rows8)
    full = jnp.concatenate(list(rows8) + [jnp.zeros((TILE - total, TILE), F32)], axis=0)
    return jnp.transpose(full)


def head_row(ref, r):
    row8 = ids((8, TILE), 0)
    out = jnp.zeros((8, TILE), F32)
    for h in range(8):
        out = jnp.where(row8 == h, ref[8 * r + h], out)
    return out


def conv(block, taps, bias):
    pre = bias + taps[0] * rolled(block, 0)
    for k in range(1, 4):
        pre = pre + taps[k] * rolled(block, k)
    return pre


def boundary_chunk(i, high):
    return high if i == 0 else jnp.logical_not(high)


def patched(ref, lanes, patch, patch_lanes, i, high):
    rows = slice(i * TILE, (i + 1) * TILE)
    if i % 2 == 1:
        return ref[rows, lanes]
    first = jnp.where(
        boundary_chunk(i, high), patch[:, patch_lanes], ref[i * TILE : i * TILE + 16, lanes]
    )
    return jnp.concatenate([first, ref[i * TILE + 16 : (i + 1) * TILE, lanes]], axis=0)


def grads_kernel(
    u0,
    u3,
    u2,
    u1,
    one_taps,
    two_taps,
    alog_ref,
    dtb_ref,
    mid_ref,
    dp,
    xm,
    actm,
    prem,
    sgrad_s,
    step_e,
    toend_e,
    exp_e,
    t_s,
    step_r,
    ds_r,
    sig_r,
    mine_ref,
    halo_ref,
    dt_src,
):
    quad, r, f = place()
    high = quad == 1
    lane8 = ids((8, TILE), 1)
    group = 2 * f + lax.div(r, 2)
    at = at_tile(lax.rem(group, 4) * TILE)
    for j in range(2):
        mine_ref[8 * j : 8 * j + 8, :] = jnp.where(
            lax.rem(f, 2) == j, one_taps[:, at], two_taps[:, at]
        )
    edge = jnp.zeros((8, 4 * TILE), F32)
    for k, u in enumerate((u0, u1, u2, u3)):
        s = lax.bitwise_xor(r, k)
        for e, start in ((0, HALF * s), (1, HALF * (3 - s))):
            for j in range(2):
                xm[e, pl.ds(pl.multiple_of(8 + start, 8), HALF), lanes_of(j)] = u[
                    TILE : TILE + HALF, lanes_of(2 * j + e)
                ].astype(F32)
            dp[pl.ds(pl.multiple_of(2 * TILE * e + start, HALF), HALF), :] = u[
                e * HALF : (e + 1) * HALF, :
            ]
        packed = u[TILE + HALF : TILE + HALF + 16, :].astype(F32)
        dt_src[s] = packed[0:8, 0:TILE] + packed[8:16, 0:TILE] + packed[0:8, TILE : 2 * TILE]
        last = jnp.concatenate(
            [packed[0:8, 2 * TILE : 4 * TILE], packed[8:16, TILE : 3 * TILE]], axis=1
        )
        edge = edge + jnp.where(s == jnp.where(high, 0, 3), last, 0.0)
    last = slice(2 * TILE, 2 * TILE + 8)
    edge = jnp.concatenate([edge, jnp.where(high, xm[1, last, :], xm[0, last, :])], axis=1)
    halo_ref[...] = jnp.concatenate([jnp.zeros_like(edge), edge], axis=0).astype(BF)
    xm[0, 0:8, :] = jnp.zeros((8, 2 * TILE), F32)
    xm[1, 0:8, :] = jnp.where(high, xm[0, 2 * TILE : 2 * TILE + 8, :], 0.0)

    rate8 = -jnp.exp(head_row(alog_ref, r))
    bias8 = head_row(dtb_ref, r)
    for i in range(4):
        if i < 2:
            a, b = dt_src[2 * i], pltpu.roll(dt_src[2 * i + 1], HALF, 1)
        else:
            a, b = pltpu.roll(dt_src[7 - 2 * i], HALF, 1), dt_src[6 - 2 * i]
        logits = jnp.where(lane8 < HALF, a, b) + bias8
        small = jnp.exp(-jnp.abs(logits))
        step = jnp.maximum(logits, 0.0) + jnp.log1p(small)
        at8 = slice(8 * i, 8 * i + 8)
        step_r[at8, :] = step
        sig_r[at8, :] = jnp.where(logits >= 0, 1.0, small) / (1.0 + small)
        ds_r[at8, :] = step * rate8
    upto = (ids((TILE, TILE), 0) <= ids((TILE, TILE), 1)).astype(F32)
    ds_r[...] = mm_f32(ds_r[...], upto)

    row48 = jnp.bitwise_and(ids((48, 8 * TILE), 0), 15)
    expand = (row48 == ids((48, 8 * TILE), 1) // HALF).astype(BF)
    ends = []
    for i in range(4):
        rows = slice(i * TILE, (i + 1) * TILE)
        base = (i % 2) * TILE
        for j in range(2):
            lanes = lanes_of(j)
            taps, bias = map_tap_rows(j, mine_ref)
            pre = conv(xm[i // 2, base : base + TILE + 8, lanes], taps, bias)
            actm[rows, lanes] = (pre * sigmoid(pre)).astype(BF)
            prem[rows, lanes] = pre
        parts = split3(
            jnp.concatenate([step_r[8 * i : 8 * i + 8, :], ds_r[8 * i : 8 * i + 8, :]], axis=0)
        )
        spread = mm(jnp.concatenate(parts, axis=0), expand, TN)
        end, masked = [], []
        for j in range(4):
            lanes = lanes_of(j)
            step = spread[:, lanes]
            ds = spread[:, lanes_of(4 + j)]
            last = ds[TILE - 1 : TILE, :]
            grow = jnp.exp(ds)
            step_e[rows, lanes] = step
            toend_e[rows, lanes] = jnp.exp(last - ds)
            exp_e[rows, lanes] = grow
            end.append(jnp.exp(last))
            grown = (dp[rows, lanes].astype(F32) * grow).astype(BF)
            sgrad_s[rows, lanes] = grown
            if i % 2 == 0:
                unknown = jnp.logical_and(boundary_chunk(i, high), ids((16, TILE), 0) < 3)
                first = jnp.where(unknown, 0.0, grown[0:16].astype(F32)).astype(BF)
                grown = jnp.concatenate([first, grown[16:]], axis=0)
            masked.append(grown)
        ends.append(jnp.concatenate(end, axis=1))
        t_s[i] = mm(actm[rows, lanes_of(1)], jnp.concatenate(masked, axis=1), TN)
    g_a = t_s[0] + ends[0] * t_s[1]
    g_b = t_s[2] + ends[2] * t_s[3]
    mid_ref[...] = jnp.where(high, g_a + ends[0] * ends[1] * g_b, g_b).astype(BF)


def first_kernel(
    v0, v3, v2, v1, step_e, toend_e, taps_ref, bias_ref, xs, acts, pres, scaled_s, weighted_s
):
    quad, r, f = place()
    high = quad == 1
    for k, v in enumerate((v0, v1, v2, v3)):
        s = lax.bitwise_xor(r, k)
        for e, start in ((0, HALF * s), (1, HALF * (3 - s))):
            xs[e, pl.ds(pl.multiple_of(8 + start, 8), HALF), :] = v[
                e * HALF : (e + 1) * HALF, :
            ].astype(F32)
    xs[0, 0:8, :] = jnp.zeros((8, 4 * TILE), F32)
    xs[1, 0:8, :] = jnp.where(high, xs[0, 2 * TILE : 2 * TILE + 8, :], 0.0)
    for i in range(4):
        rows = slice(i * TILE, (i + 1) * TILE)
        base = (i % 2) * TILE
        for j in range(4):
            lanes = lanes_of(j)
            taps, bias = sig_tap_rows(j, taps_ref, bias_ref)
            pre = conv(xs[i // 2, base : base + TILE + 8, lanes], taps, bias)
            value = (pre * sigmoid(pre)).astype(BF)
            acts[rows, lanes] = value
            pres[rows, lanes] = pre
            scaled = (value.astype(F32) * step_e[rows, lanes]).astype(BF)
            scaled_s[rows, lanes] = scaled
            weighted_s[rows, lanes] = (scaled.astype(F32) * toend_e[rows, lanes]).astype(BF)


def states_kernel(
    halo_ref,
    xs,
    xm,
    actm,
    weighted_s,
    sgrad_s,
    step_e,
    toend_e,
    exp_e,
    taps_ref,
    bias_ref,
    mine_ref,
    mid_ref,
    s_s,
    delta_ref,
    edge_ref,
    act_p,
    pre_p,
    scaled_p,
    weighted_p,
):
    quad, r, f = place()
    high = quad == 1
    edge = halo_ref[...].astype(F32)[8:16]
    edge_ref[...] = edge
    segment = jnp.where(high, 0, 1)
    rows16 = pl.ds(pl.multiple_of(2 * TILE * segment, 16), 16)
    for j in range(6):
        lanes = lanes_of(j)
        if j < 4:
            taps, bias = sig_tap_rows(j, taps_ref, bias_ref)
            first = xs[segment, 8:24, lanes]
        else:
            taps, bias = map_tap_rows(j - 4, mine_ref)
            first = xm[segment, 8:24, lanes_of(j - 4)]
        pre = conv(jnp.concatenate([edge[:, lanes], first], axis=0), taps, bias)
        value = (pre * sigmoid(pre)).astype(BF)
        act_p[:, lanes] = value
        pre_p[:, lanes] = pre
        if j < 4:
            scaled = (value.astype(F32) * step_e[rows16, lanes]).astype(BF)
            scaled_p[:, lanes] = scaled
            weighted_p[:, lanes] = (scaled.astype(F32) * toend_e[rows16, lanes]).astype(BF)
    every = slice(0, 4 * TILE)
    for i in range(4):
        s_s[i] = mm(
            patched(actm, lanes_of(0), act_p, lanes_of(4), i, high),
            patched(weighted_s, every, weighted_p, every, i, high),
            TN,
        )
    ends = end_rows_of(exp_e)
    f_a = ends[1] * s_s[0] + s_s[1]
    f_b = ends[3] * s_s[2] + s_s[3]
    d_b = ends[2] * ends[3]
    mid_ref[0:TILE, :] = jnp.where(high, d_b * f_a + f_b, f_a).astype(BF)
    grown = sgrad_s[rows16, :].astype(F32)
    out_rows = act_p[:, lanes_of(5)].astype(F32)
    known = jnp.where(ids((16, TILE), 0) < 3, out_rows, 0.0).astype(BF)
    delta_ref[...] = mm(known, grown.astype(BF), TN)
    hi, mid, lo = [part.astype(F32) for part in split3(ends[0] * ends[1] * d_b)]
    pieces = [hi, mid, lo, grown[0:1], grown[1:2], grown[2:3]]
    for k in range(3):
        pieces.append(
            jnp.concatenate([out_rows[k : k + 1], jnp.zeros((1, 3 * TILE), F32)], axis=1)
        )
    pieces.append(jnp.zeros((7, 4 * TILE), F32))
    mid_ref[TILE : TILE + 16, :] = jnp.concatenate(pieces, axis=0).astype(BF)


def slope_of(pre):
    sig = sigmoid(pre)
    return sig * (1.0 + pre * (1.0 - sig))


def head_sums(*quantities):
    found = []
    head = ids((8, 4 * TILE), 1) // HALF
    pick = (ids((8, 4 * TILE), 0) == head).astype(BF)
    for tiles in quantities:
        x = jnp.concatenate(tiles, axis=1)
        hi = x.astype(BF)
        lo = (x - hi.astype(F32)).astype(BF)
        found.append(mm(pick, hi, NT) + mm(pick, lo, NT))
    return found


def pair_sums(x, two):
    head = ids((8, 2 * TILE), 1) // HALF + 4 * two
    pick = (ids((8, 2 * TILE), 0) == head).astype(BF)
    hi = x.astype(BF)
    lo = (x - hi.astype(F32)).astype(BF)
    return mm(pick, hi, NT) + mm(pick, lo, NT)


def skip_rows(skip_ref, r):
    lane_row = ids((1, TILE), 1)
    found = []
    for j in range(4):
        at = 8 * r + 2 * j
        found.append(jnp.where(lane_row < HALF, skip_ref[at], skip_ref[at + 1]))
    return found


def second_kernel(
    dp,
    acts,
    actm,
    pres,
    prem,
    scaled_s,
    step_e,
    toend_e,
    ds_r,
    act_p,
    pre_p,
    scaled_p,
    skip_ref,
    base_ref,
    coef_ref,
    mslope_ref,
    gmap_ref,
    gsum_ref,
    stepsum_ref,
    skip_acc,
):
    quad, r, f = place()
    high = quad == 1
    skip_row = skip_rows(skip_ref, r)
    skip_acc[...] = jnp.zeros_like(skip_acc)
    half_lane = ids((TILE, TILE), 1) < HALF
    row8 = ids((8, TILE), 0)
    col_q = ids((TILE, TILE), 1)
    seen = ids((TILE, TILE), 0) <= col_q
    for i in range(4):
        rows = slice(i * TILE, (i + 1) * TILE)
        in_map = patched(actm, lanes_of(0), act_p, lanes_of(4), i, high)
        out_map = patched(actm, lanes_of(1), act_p, lanes_of(5), i, high)
        score = mm(in_map, out_map, NT)
        ds8 = ds_r[8 * i : 8 * i + 8, :]
        cols = columns(ds8)
        grad_score = jnp.zeros((TILE, TILE), F32)
        gsum = jnp.zeros((8, TILE), F32)
        rcol = jnp.zeros((TILE, TILE), F32)
        products = []
        for j in range(4):
            sc = patched(scaled_s, lanes_of(j), scaled_p, lanes_of(j), i, high)
            dy = dp[rows, lanes_of(j)]
            diag = jnp.zeros((TILE, TILE), F32)
            for e in range(2):
                h = 2 * j + e
                part = half_lane if e == 0 else jnp.logical_not(half_lane)
                gm = mm(jnp.where(part, sc, jnp.zeros_like(sc)), dy, NT)
                spread = ds8[h : h + 1, :] - cols[:, h : h + 1]
                decay = jnp.exp(jnp.where(seen, spread, -1e30))
                gd = gm * decay
                grad_score = grad_score + gd
                both = gd * score
                rcol = jnp.where(col_q == h, jnp.sum(both, axis=1, keepdims=True), rcol)
                gsum = gsum + jnp.where(row8 == h, jnp.sum(both, axis=0, keepdims=True), 0.0)
                mix = (score * decay).astype(BF)
                diag = diag + mm(mix, jnp.where(part, dy, jnp.zeros_like(dy)))
            lanes = lanes_of(j)
            sigf = patched(acts, lanes, act_p, lanes, i, high).astype(F32)
            dyf = dy.astype(F32)
            step = step_e[rows, lanes]
            slope = slope_of(patched(pres, lanes, pre_p, lanes, i, high))
            base_ref[rows, lanes] = (skip_row[j] * dyf + diag * step) * slope
            coef_ref[rows, lanes] = toend_e[rows, lanes] * step * slope
            products.append(diag * sigf)
            skip_acc[:, lanes] += eights(dyf * sigf)
        stepsum_ref[8 * i : 8 * i + 8, :] = head_sums(products)[0]
        for j in range(2):
            mslope_ref[rows, lanes_of(j)] = slope_of(
                patched(prem, lanes_of(j), pre_p, lanes_of(4 + j), i, high)
            )
        gs = grad_score.astype(BF)
        gmap_ref[rows, lanes_of(0)] = mm(gs, out_map)
        gmap_ref[rows, lanes_of(1)] = mm(gs, in_map, TN)
        gsum_ref[8 * i : 8 * i + 8, :] = gsum - jnp.transpose(rcol)[0:8, :]


def eights(x):
    return jnp.sum(x.reshape(x.shape[0] // 8, 8, x.shape[1]), axis=0)


def end_rows_of(exp_e):
    return [exp_e[(i + 1) * TILE - 8 : (i + 1) * TILE, :][7:8, :] for i in range(4)]


def taps_back(gp, i, lanes, taps):
    base = (i % 2) * TILE
    raw = taps[3] * gp[i // 2, base : base + TILE, lanes]
    for k in range(3):
        start = base + 3 - k
        raw = raw + taps[k] * gp[i // 2, start : start + TILE, lanes]
    return raw


def fill_pads(gp, high):
    first = gp[1, 0:8, :]
    gp[0, 2 * TILE : 2 * TILE + 8, :] = jnp.where(high, first, jnp.zeros_like(first))
    gp[1, 2 * TILE : 2 * TILE + 8, :] = jnp.zeros_like(first)


def spill_of(first, taps):
    grads = jnp.concatenate([jnp.zeros((8, TILE), F32), first], axis=0)
    spill = jnp.zeros((8, TILE), F32)
    for k in range(3):
        spill = spill + taps[k] * pltpu.roll(grads, 5 + k, 0)[8:]
    return spill


def tap_sums(here, x, edge_ref, i, lanes, edge_lanes, high, sums):
    base = (i % 2) * TILE
    if i % 2 == 1:
        windows = [x[i // 2, base + 5 + k : base + 5 + k + TILE, lanes] for k in range(4)]
    else:
        first = x[i // 2, 0:8, lanes] + jnp.where(
            boundary_chunk(i, high), edge_ref[:, edge_lanes], 0.0
        )
        block = jnp.concatenate([first, x[i // 2, 8 : TILE + 8, lanes]], axis=0)
        windows = [rolled(block, k) for k in range(4)]
    for k in range(4):
        sums[k] = sums[k] + eights(here * windows[k])
    sums[4] = sums[4] + eights(here)


def maps_kernel(
    midg_ref,
    midf_ref,
    s_s,
    t_s,
    delta_ref,
    exp_e,
    mslope_ref,
    weighted_s,
    weighted_p,
    sgrad_s,
    gmap_ref,
    xm,
    edge_ref,
    mine_ref,
    one_ref,
    two_ref,
    hlow_ref,
    clow_ref,
    endrow_ref,
    h_s,
    c_s,
    gm,
):
    quad, r, f = place()
    high = quad == 1
    even = lax.rem(f, 2) == 0
    ends = end_rows_of(exp_e)
    f_in = midf_ref[0:TILE, :].astype(F32)
    extra = midf_ref[TILE : TILE + 16, :].astype(F32)
    row16 = ids((16, 4 * TILE), 0)
    across = jnp.sum(jnp.where(row16 < 3, extra, 0.0), axis=0, keepdims=True)
    left_out = jnp.logical_and(row16 >= 3, row16 < 6)
    grown = jnp.where(left_out, extra, 0.0).astype(BF)
    out_rows = jnp.where(left_out[:, 0:TILE], pltpu.roll(extra[:, 0:TILE], 13, 0), 0.0).astype(BF)
    g_in = midg_ref[...].astype(F32) + mm(out_rows, grown, TN)
    t2 = t_s[2] + jnp.where(high, 0.0, delta_ref[...])
    f_a = ends[1] * s_s[0] + s_s[1]
    h_s[0] = jnp.where(high, f_in, 0.0)
    h_s[1] = ends[0] * h_s[0] + s_s[0]
    h_s[2] = jnp.where(high, ends[1] * h_s[1] + s_s[1], across * f_a + f_in)
    h_s[3] = ends[2] * h_s[2] + s_s[2]
    g_b = t2 + ends[2] * t_s[3]
    c_s[3] = jnp.where(high, g_in, 0.0)
    c_s[2] = t_s[3] + ends[3] * c_s[3]
    c_s[1] = jnp.where(high, t2 + ends[2] * c_s[2], g_in + across * g_b)
    c_s[0] = t_s[1] + ends[1] * c_s[1]
    taps_of = [map_tap_rows(j, mine_ref)[0] for j in range(2)]
    sums = [[jnp.zeros((8, TILE), F32) for _ in range(5)] for _ in range(2)]
    end_rows = []
    every = slice(0, 4 * TILE)
    for i in range(4):
        rows = slice(i * TILE, (i + 1) * TILE)
        base = (i % 2) * TILE
        hlow_ref[i] = h_s[i].astype(BF)
        clow_ref[i] = c_s[i].astype(BF)
        end_rows.append(jnp.sum(h_s[i] * c_s[i], axis=0, keepdims=True) * ends[i])
        grads = (
            mm(patched(weighted_s, every, weighted_p, every, i, high), clow_ref[i], NT) + gmap_ref[rows, lanes_of(0)],
            mm(sgrad_s[rows, :], hlow_ref[i], NT) + gmap_ref[rows, lanes_of(1)],
        )
        for j in range(2):
            here = grads[j] * mslope_ref[rows, lanes_of(j)]
            gm[i // 2, base : base + TILE, lanes_of(j)] = here
            tap_sums(here, xm, edge_ref, i, lanes_of(j), lanes_of(4 + j), high, sums[j])
    fill_pads(gm, high)
    for i in range(4):
        rows = slice(i * TILE, (i + 1) * TILE)
        raws = [taps_back(gm, i, lanes_of(j), taps_of[j]) for j in range(2)]
        one_ref[rows, :] = jnp.where(even, raws[0], raws[1]).astype(BF)
        two_ref[rows, :] = jnp.where(even, raws[1], raws[0]).astype(BF)
    first = jnp.where(high, gm[0, 0:8, :], gm[1, 0:8, :])
    endrow_ref[...] = jnp.concatenate(end_rows + [jnp.zeros((4, 4 * TILE), F32)], axis=0)
    row8 = ids((8, TILE), 0)
    tails = []
    for j in range(2):
        five = jnp.zeros((8, TILE), F32)
        for t in range(5):
            five = jnp.where(row8 == t, jnp.sum(sums[j][t], axis=0, keepdims=True), five)
        hi, lo, _ = split3(five)
        zero8 = jnp.zeros((8, TILE), F32)
        tails.append(
            jnp.concatenate(
                [spill_of(first[:, lanes_of(j)], taps_of[j]), zero8, hi.astype(F32), lo.astype(F32)], axis=0
            )
        )
    one_ref[4 * TILE : 4 * TILE + 32, :] = jnp.where(even, tails[0], tails[1]).astype(BF)
    two_ref[4 * TILE : 4 * TILE + 32, :] = jnp.where(even, tails[1], tails[0]).astype(BF)


def third_kernel(
    hlow_ref,
    clow_ref,
    endrow_ref,
    xs,
    dp,
    acts,
    actm,
    edge_ref,
    act_p,
    toend_e,
    exp_e,
    step_r,
    sig_r,
    base_ref,
    coef_ref,
    gsum_ref,
    stepsum_ref,
    skip_acc,
    taps_ref,
    alog_ref,
    gp,
    blk,
    spill_ref,
    params_ref,
):
    quad, r, f = place()
    high = quad == 1
    row8 = ids((8, TILE), 0)
    lane8 = ids((8, TILE), 1)
    rate8 = -jnp.exp(head_row(alog_ref, r))
    row_q = ids((TILE, TILE), 0)
    col_q = ids((TILE, TILE), 1)
    tail_sums = jnp.concatenate(
        [(row_q >= col_q).astype(F32), (row_q < col_q).astype(F32)], axis=0
    )
    sums = [[jnp.zeros((8, TILE), F32) for _ in range(5)] for _ in range(4)]
    alog_acc = jnp.zeros((8, TILE), F32)
    ddt_acc = jnp.zeros((8, TILE), F32)
    for i in range(4):
        rows = slice(i * TILE, (i + 1) * TILE)
        at8 = slice(8 * i, 8 * i + 8)
        base = (i % 2) * TILE
        off = mm(patched(actm, lanes_of(1), act_p, lanes_of(5), i, high), hlow_ref[i])
        gw = mm(patched(actm, lanes_of(0), act_p, lanes_of(4), i, high), clow_ref[i])
        end_row = endrow_ref[i : i + 1, :]
        gsum = gsum_ref[at8, :]
        end_sum = jnp.zeros((8, TILE), F32)
        offsum = jnp.zeros((8, TILE), F32)
        backsum = jnp.zeros((8, TILE), F32)
        for two in range(2):
            lanes2 = slice(2 * two * TILE, (2 * two + 2) * TILE)
            sigf = jnp.concatenate(
                [
                    patched(acts, lanes_of(j), act_p, lanes_of(j), i, high).astype(F32)
                    for j in (2 * two, 2 * two + 1)
                ],
                axis=1,
            )
            offsum = offsum + pair_sums(
                dp[rows, lanes2].astype(F32) * exp_e[rows, lanes2] * off[:, lanes2], two
            )
            backsum = backsum + pair_sums(gw[:, lanes2] * toend_e[rows, lanes2] * sigf, two)
            for j in (2 * two, 2 * two + 1):
                lanes = lanes_of(j)
                end_sum = end_sum + jnp.where(
                    row8 == 2 * j + lane8 // HALF, end_row[:, lanes], 0.0
                )
                here = base_ref[rows, lanes] + gw[:, lanes] * coef_ref[rows, lanes]
                gp[i // 2, base : base + TILE, lanes] = here
                tap_sums(here, xs, edge_ref, i, lanes, lanes, high, sums[j])
        gsum = gsum + offsum
        stepsum = stepsum_ref[at8, :] + backsum
        back = backsum * step_r[at8, :]
        grad_log = mm_f32(jnp.concatenate([gsum, back], axis=1), tail_sums) + jnp.sum(
            end_sum, axis=1, keepdims=True
        )
        ddt = (grad_log * rate8 + stepsum) * sig_r[at8, :]
        blk[2 * i] = ddt
        blk[2 * i + 1] = pltpu.roll(ddt, HALF, 1)
        ddt_acc = ddt_acc + ddt
        alog_acc = alog_acc + grad_log * step_r[at8, :]
    fill_pads(gp, high)
    rows = []
    for j in range(4):
        taps = [taps_ref[k : k + 1, at_tile((4 * r + j) * TILE)] for k in range(4)]
        first = jnp.where(high, gp[0, 0:8, lanes_of(j)], gp[1, 0:8, lanes_of(j)])
        spill_ref[:, lanes_of(j)] = spill_of(first, taps)
        for t in range(5):
            rows.append(jnp.sum(sums[j][t], axis=0, keepdims=True))
    alog = jnp.sum(alog_acc * rate8, axis=1, keepdims=True)
    ddtb = jnp.sum(ddt_acc, axis=1, keepdims=True)
    skips = jnp.zeros((8, TILE), F32)
    for j in range(4):
        total = jnp.sum(skip_acc[:, lanes_of(j)], axis=0, keepdims=True)
        skips = skips + jnp.where(row8 == 2 * j + lane8 // HALF, total, 0.0)
    skips = jnp.sum(skips, axis=1, keepdims=True)
    three = jnp.where(lane8 == 0, alog, jnp.where(lane8 == 1, ddtb, skips))
    flat = columns(jnp.where(lane8 < 3, three, 0.0))
    trio = flat[0:1] + pltpu.roll(flat[0:8], 32, 1)[1:2] + pltpu.roll(flat[0:8], 64, 1)[2:3]
    trio = pltpu.roll(jnp.broadcast_to(trio, (8, TILE)), 8 * r, 1)[0:1]
    params_ref[...] = jnp.concatenate(rows + [trio, jnp.zeros((3, TILE), F32)], axis=0)


def split_params(params):
    hi, lo, _ = split3(params)
    return jnp.concatenate([hi[0:16], hi[16:32], lo[0:16], lo[16:32]], axis=1)


def whole_params(value):
    value = value.astype(F32)
    return jnp.concatenate(
        [
            value[:, lanes_of(0)] + value[:, lanes_of(2)],
            value[:, lanes_of(1)] + value[:, lanes_of(3)],
        ],
        axis=0,
    )


def cross_kernel(scale, params_ref, spill_ref, one_ref, two_ref, cross_ref):
    tails = [ref[4 * TILE : 4 * TILE + 32, :].astype(F32) for ref in (one_ref, two_ref)]
    fives = [tail[16:24] + tail[24:32] for tail in tails]
    params = jnp.concatenate(
        [
            params_ref[0:20],
            fives[0][0:5],
            fives[1][0:5],
            params_ref[20:21],
            jnp.zeros((1, TILE), F32),
        ],
        axis=0,
    )
    maps = jnp.concatenate([tails[0][0:8], tails[1][0:8], jnp.zeros((8, 2 * TILE), F32)], axis=1)
    cross_ref[0:16, :] = jnp.concatenate([spill_ref[...], maps], axis=0).astype(BF)
    cross_ref[16:32, :] = split_params(params * scale)


def send_kernel(gp, taps_ref, y0, y1, y2, y3, dx):
    quad, r, f = place()
    for j in range(4):
        lanes = lanes_of(j)
        taps = [taps_ref[k : k + 1, at_tile((4 * r + j) * TILE)] for k in range(4)]
        for i in range(4):
            dx[i * TILE : (i + 1) * TILE, lanes] = taps_back(gp, i, lanes, taps).astype(BF)
    for k, y in enumerate((y0, y1, y2, y3)):
        s = lax.bitwise_xor(r, k)
        for e, at in ((0, HALF * s), (1, 2 * TILE + HALF * (3 - s))):
            y[e * HALF : (e + 1) * HALF, :] = dx[pl.ds(pl.multiple_of(at, HALF), HALF), :]


def merge_kernel(own_ref, other_ref, one_ref, two_ref, blk, w0, w1, w2, w3):
    quad, r, f = place()
    lane8 = ids((8, TILE), 1)
    param_rows = split_params(
        whole_params(own_ref[16:32, :]) + whole_params(other_ref[16:32, :])
    )
    spill = other_ref[0:16, :].astype(F32)
    for k, w in enumerate((w0, w1, w2, w3)):
        s = lax.bitwise_xor(r, k)
        for e, at in ((0, HALF * s), (1, 2 * TILE + HALF * (3 - s))):
            rows = pl.ds(pl.multiple_of(at, HALF), HALF)
            w[0:HALF, lanes_of(e)] = one_ref[rows, :]
            w[0:HALF, lanes_of(2 + e)] = two_ref[rows, :]
        here = jnp.where(lane8 < HALF, blk[s], pltpu.roll(blk[7 - s], HALF, 1))
        hi, mid, _ = split3(here)
        w[HALF : HALF + 16, :] = jnp.concatenate(
            [
                jnp.concatenate([hi.astype(F32), spill[0:8, 0 : 2 * TILE], spill[8:16, 0:TILE]], axis=1),
                jnp.concatenate(
                    [
                        mid.astype(F32),
                        spill[0:8, 2 * TILE : 4 * TILE],
                        spill[8:16, TILE : 2 * TILE],
                    ],
                    axis=1,
                ),
            ],
            axis=0,
        ).astype(BF)
        w[HALF + 16 : HALF + 32, :] = param_rows


def last_kernel(
    y0, y3, y2, y1, w0, w3, w2, w1, dsig_ref, dmap_ref, ddt_ref, taps_ref, mtaps_ref, bias_ref, mbias_ref, *trio_refs
):
    quad, r, f = place()
    ys = (y0, y1, y2, y3)
    ws = (w0, w1, w2, w3)
    third = jnp.logical_and(quad == 0, r == 3)
    fourth = jnp.logical_and(quad == 1, r == 0)
    params = []
    trio = jnp.zeros((1, TILE), F32)
    for k, y in enumerate(ys):
        s = lax.bitwise_xor(r, k)
        cols = at_tile(s * 4 * TILE, 4 * TILE)
        dsig_ref[:, cols] = y[0:TILE, :].astype(F32)
        extra = ws[k][HALF : HALF + 16, :].astype(F32)
        spill = jnp.concatenate(
            [extra[0:8, TILE : 3 * TILE], extra[8:16, TILE : 3 * TILE]], axis=1
        )
        dsig_ref[HALF - 8 : HALF, cols] += jnp.where(third, spill, 0.0)
        dsig_ref[TILE - 8 : TILE, cols] += jnp.where(fourth, spill, 0.0)
        ddt_ref[pl.ds(pl.multiple_of(8 * s, 8), 8), :] = extra[0:8, 0:TILE] + extra[8:16, 0:TILE]
        param = whole_params(ws[k][HALF + 16 : HALF + 32, :])
        params.append(param)
        for j in range(4):
            lanes = at_tile((4 * s + j) * TILE)
            taps_ref[0:4, lanes] = param[5 * j : 5 * j + 4]
            bias_ref[0:1, lanes] = param[5 * j + 4 : 5 * j + 5]
        trio = trio + param[30:31]
    trio = jnp.broadcast_to(trio, (8, TILE))
    for t, ref in enumerate(trio_refs):
        moved = trio if t == 0 else pltpu.roll(trio, TILE - 32 * t, 1)
        ref[...] = moved[0:1, 0:32]
    own = lax.div(r, 2)
    swap = f >= 2
    for pair in range(2):
        group = own if pair == 0 else 1 - own
        a, b = 2 * pair, 2 * pair + 1
        for j in range(2):
            where = jnp.where(swap, 1 - j, j)
            lanes = at_tile((2 * where + group) * TILE)
            for e in range(2):
                dmap_ref[e * HALF : (e + 1) * HALF, lanes] = ws[a][
                    0:HALF, lanes_of(2 * j + e)
                ].astype(F32) + ws[b][0:HALF, lanes_of(2 * j + e)].astype(F32)
            spill = jnp.zeros((8, TILE), F32)
            for w in (ws[a], ws[b]):
                extra = w[HALF : HALF + 16, 3 * TILE : 4 * TILE].astype(F32)
                spill = spill + extra[8 * j : 8 * j + 8]
            dmap_ref[HALF - 8 : HALF, lanes] += jnp.where(third, spill, 0.0)
            dmap_ref[TILE - 8 : TILE, lanes] += jnp.where(fourth, spill, 0.0)
            five = params[a][20 + 5 * j : 25 + 5 * j] + params[b][20 + 5 * j : 25 + 5 * j]
            mtaps_ref[0:4, lanes] = five[0:4]
            mbias_ref[0:1, lanes] = five[4:5]


ROUTE_ONE = [(0, 0), (2, 1), (1, 2), (3, 3)]
ROUTE_TWO = [(0, 2), (2, 3), (1, 0), (3, 1)]


def back(route):
    return [(target, source) for source, target in route]


def shards_quad(
    sig_raw,
    map_raw,
    step_size_logits,
    d_out,
    sig_taps,
    map_taps,
    sig_bias,
    map_bias,
    a_log,
    dt_bias,
    skip_gain,
):
    ctx = lax.axis_size("ctx")
    rows, sig_width = sig_raw.shape
    vmem = pl.BlockSpec(memory_space=pltpu.VMEM)
    smem = pl.BlockSpec(memory_space=pltpu.SMEM)
    hbm = pl.BlockSpec(memory_space=pltpu.HBM)

    def call(kernel, out_shape, in_specs, out_specs, scratch, mib, cost):
        return pl.pallas_call(
            kernel,
            out_shape=out_shape,
            in_specs=in_specs,
            out_specs=out_specs,
            scratch_shapes=scratch,
            compiler_params=pltpu.CompilerParams(vmem_limit_bytes=mib * 1024 * 1024),
            cost_estimate=pl.CostEstimate(flops=cost, bytes_accessed=cost // 100, transcendentals=0),
        )

    def shape(*dims, kind=F32):
        return jax.ShapeDtypeStruct(dims, kind)

    inside = [[(c, c ^ k) for c in range(ctx)] for k in range(4)]
    over = [(c, c ^ 4) for c in range(ctx)]
    total = 4 * TILE
    wide, narrow = 6 * TILE, 4 * TILE
    owned = map_taps.shape[1]
    sig_bias_row = sig_bias[None, :]
    *packed, map_params = call(
        pack_kernel,
        (shape(TILE + HALF + 16, narrow, kind=BF),) * 4 + (shape(8, owned),),
        [hbm, hbm, hbm, hbm, vmem, vmem],
        (vmem,) * 5,
        [
            pltpu.VMEM((32, TILE), F32),
            pltpu.VMEM((16, sig_width), BF),
            pltpu.SemaphoreType.DMA((22,)),
        ],
        60,
        10**6,
    )(sig_raw, map_raw, step_size_logits.T, d_out, map_taps, map_bias[None, :])
    us = [packed[0]] + [lax.ppermute(packed[k], "ctx", inside[k]) for k in (1, 2, 3)]
    map_one = lax.ppermute(map_params, "fsdp", back(ROUTE_ONE))
    map_two = lax.ppermute(map_params, "fsdp", back(ROUTE_TWO))
    packed = call(
        pack_sig_kernel,
        (shape(TILE, narrow, kind=BF),) * 4,
        [hbm],
        (vmem,) * 4,
        [pltpu.SemaphoreType.DMA((4,))],
        60,
        10**6,
    )(sig_raw)
    own_u, own_v = call(
        own_kernel,
        (shape(TILE + HALF + 16, narrow, kind=BF), shape(TILE, narrow, kind=BF)),
        [vmem] * 2,
        (vmem,) * 2,
        [],
        16,
        10**6,
    )(us[0], packed[0])
    us[0] = own_u
    vs = [own_v] + [lax.ppermute(packed[k], "ctx", inside[k]) for k in (1, 2, 3)]
    midg, dp, xm, actm, prem, sgrad, step_e, toend_e, exp_e, t_s, step_r, ds_r, sig_r, *small = call(
        grads_kernel,
        (
            shape(TILE, narrow, kind=BF),
            shape(total, narrow, kind=BF),
            shape(2, 2 * TILE + 8, 2 * TILE),
            shape(total, 2 * TILE, kind=BF),
            shape(total, 2 * TILE),
            shape(total, narrow, kind=BF),
            shape(total, narrow),
            shape(total, narrow),
            shape(total, narrow),
            shape(4, TILE, narrow),
            shape(32, TILE),
            shape(32, TILE),
            shape(32, TILE),
            shape(16, TILE),
            shape(16, wide, kind=BF),
        ),
        [vmem] * 6 + [smem] * 2,
        (vmem,) * 15,
        [pltpu.VMEM((4, 8, TILE), F32)],
        24,
        2 * 10**9,
    )(us[0], us[3], us[2], us[1], map_one, map_two, a_log, dt_bias)
    mine, halo = small
    halo = lax.ppermute(halo, "ctx", over)
    midg = lax.ppermute(midg, "ctx", over)
    xs, acts, pres, scaled, weighted = call(
        first_kernel,
        (
            shape(2, 2 * TILE + 8, narrow),
            shape(total, narrow, kind=BF),
            shape(total, narrow),
            shape(total, narrow, kind=BF),
            shape(total, narrow, kind=BF),
        ),
        [vmem] * 8,
        (vmem,) * 5,
        [],
        24,
        2 * 10**9,
    )(vs[0], vs[3], vs[2], vs[1], step_e, toend_e, sig_taps, sig_bias_row)
    midf, s_s, delta, edge, act_p, pre_p, scaled_p, weighted_p = call(
        states_kernel,
        (
            shape(TILE + 16, narrow, kind=BF),
            shape(4, TILE, narrow),
            shape(TILE, narrow),
            shape(8, wide),
            shape(16, wide, kind=BF),
            shape(16, wide),
            shape(16, narrow, kind=BF),
            shape(16, narrow, kind=BF),
        ),
        [vmem] * 12,
        (vmem,) * 8,
        [],
        24,
        10**9,
    )(halo, xs, xm, actm, weighted, sgrad, step_e, toend_e, exp_e, sig_taps, sig_bias_row, mine)
    midf = lax.ppermute(midf, "ctx", over)
    base, coef, mslope, gmap, gsum, stepsum, skips = call(
        second_kernel,
        (
            shape(total, narrow),
            shape(total, narrow),
            shape(total, 2 * TILE),
            shape(total, 2 * TILE),
            shape(32, TILE),
            shape(32, TILE),
            shape(8, narrow),
        ),
        [vmem] * 12 + [smem],
        (vmem,) * 7,
        [],
        24,
        5 * 10**9,
    )(
        dp,
        acts,
        actm,
        pres,
        prem,
        scaled,
        step_e,
        toend_e,
        ds_r,
        act_p,
        pre_p,
        scaled_p,
        skip_gain,
    )
    one, two, hlow, clow, endrow = call(
        maps_kernel,
        (
            shape(total + 32, TILE, kind=BF),
            shape(total + 32, TILE, kind=BF),
            shape(4, TILE, narrow, kind=BF),
            shape(4, TILE, narrow, kind=BF),
            shape(8, narrow),
        ),
        [vmem] * 14,
        (vmem,) * 5,
        [
            pltpu.VMEM((4, TILE, narrow), F32),
            pltpu.VMEM((4, TILE, narrow), F32),
            pltpu.VMEM((2, 2 * TILE + 8, 2 * TILE), F32),
        ],
        24,
        2 * 10**9,
    )(
        midg,
        midf,
        s_s,
        t_s,
        delta,
        exp_e,
        mslope,
        weighted,
        weighted_p,
        sgrad,
        gmap,
        xm,
        edge,
        mine,
    )
    one = lax.ppermute(one, "fsdp", ROUTE_ONE)
    two = lax.ppermute(two, "fsdp", ROUTE_TWO)
    gp, blk, spill, params = call(
        third_kernel,
        (
            shape(2, 2 * TILE + 8, narrow),
            shape(8, 8, TILE),
            shape(8, narrow),
            shape(24, TILE),
        ),
        [vmem] * 19 + [smem],
        (vmem,) * 4,
        [],
        24,
        3 * 10**9,
    )(
        hlow,
        clow,
        endrow,
        xs,
        dp,
        acts,
        actm,
        edge,
        act_p,
        toend_e,
        exp_e,
        step_r,
        sig_r,
        base,
        coef,
        gsum,
        stepsum,
        skips,
        sig_taps,
        a_log,
    )
    scale = 1.0 / math.sqrt(float(ctx * rows))
    cross = call(
        functools.partial(cross_kernel, scale),
        shape(32, narrow, kind=BF),
        [vmem] * 4,
        vmem,
        [],
        16,
        10**6,
    )(params, spill, one, two)
    other = lax.ppermute(cross, "ctx", over)
    ys = call(
        send_kernel,
        (shape(TILE, narrow, kind=BF),) * 4,
        [vmem] * 2,
        (vmem,) * 4,
        [pltpu.VMEM((total, narrow), BF)],
        16,
        10**9,
    )(gp, sig_taps)
    ys = [ys[0]] + [lax.ppermute(ys[k], "ctx", inside[k]) for k in (1, 2, 3)]
    ws = call(
        merge_kernel,
        (shape(HALF + 32, narrow, kind=BF),) * 4,
        [vmem] * 5,
        (vmem,) * 4,
        [],
        16,
        10**6,
    )(cross, other, one, two, blk)
    ws = [ws[0]] + [lax.ppermute(ws[k], "ctx", inside[k]) for k in (1, 2, 3)]
    d_sig, d_map, d_dt, taps, map_taps_grad, bias, map_bias_grad, *trio = call(
        last_kernel,
        (
            shape(rows, sig_width),
            shape(rows, owned),
            shape(32, TILE),
            shape(4, sig_width),
            shape(4, owned),
            shape(1, sig_width),
            shape(1, owned),
        )
        + (shape(1, 32),) * 3,
        [vmem] * 8,
        (vmem,) * 10,
        [],
        16,
        10**6,
    )(ys[0], ys[3], ys[2], ys[1], ws[0], ws[3], ws[2], ws[1])
    return (
        d_sig,
        d_map,
        d_dt.T,
        taps,
        map_taps_grad,
        bias[0],
        map_bias_grad[0],
        *(t[0] for t in trio),
    )


def shards(*args):
    sig_raw, map_raw, step_size_logits = args[:3]
    ctx = lax.axis_size("ctx")
    fsdp = lax.axis_size("fsdp")
    fits = (
        ctx == 8
        and fsdp == 4
        and sig_raw.shape == (TILE, 2048)
        and map_raw.shape == (TILE, 2 * GROUPS * STATE)
        and step_size_logits.shape[1] == 32
    )
    return shards_quad(*args) if fits else shards_chain(*args)


def solution(mesh):
    return jax.shard_map(
        shards,
        mesh=mesh,
        in_specs=(
            P("ctx", "fsdp"),
            P("ctx", None),
            P("ctx", "fsdp"),
            P("ctx", "fsdp"),
            P(None, "fsdp"),
            P(None, "fsdp"),
            P("fsdp"),
            P("fsdp"),
            P("fsdp"),
            P("fsdp"),
            P("fsdp"),
        ),
        out_specs=(
            P("ctx", "fsdp"),
            P("ctx", "fsdp"),
            P("ctx", "fsdp"),
            P(None, "fsdp"),
            P(None, "fsdp"),
            P("fsdp"),
            P("fsdp"),
            P("fsdp"),
            P("fsdp"),
            P("fsdp"),
        ),
        check_vma=False,
    )
```

```python
import functools
import math

import jax
import jax.numpy as jnp
from jax import lax
from jax.experimental import pallas as pl
from jax.experimental.pallas import tpu as pltpu
from jax.sharding import PartitionSpec as P

HEADS = 128
HDIM = 64
STATE = 128
GROUPS = 8


def prefix(part, axis, combine, identity, reverse):
    count = lax.axis_size(axis)
    place = lax.axis_index(axis)
    ahead = count - 1 - place if reverse else place
    gathered = jax.tree.map(lambda a: lax.all_gather(a, axis), part)
    state = jax.tree.map(lambda a, e: jnp.zeros_like(a) + jnp.asarray(e, a.dtype), part, identity)

    def one(lap, state):
        source = count - 1 - lap if reverse else lap
        return combine(
            state, jax.tree.map(lambda a: lax.dynamic_index_in_dim(a, source, 0, False), gathered)
        )

    return lax.fori_loop(0, ahead, one, state)


def broadcast(x, axis, root):
    mine = lax.axis_index(axis) == root
    return lax.psum(jnp.where(mine, x, jnp.zeros_like(x)), axis)


def extended(block, sides, width):
    for axis, dim in sides:
        count = lax.axis_size(axis)
        forward = [(i, i + 1) for i in range(count - 1)]
        backward = [(target, source) for source, target in forward]
        low = lax.ppermute(
            lax.slice_in_dim(block, block.shape[dim] - width, None, axis=dim), axis, forward
        )
        high = lax.ppermute(lax.slice_in_dim(block, 0, width, axis=dim), axis, backward)
        block = jnp.concatenate([low, block, high], axis=dim)
    return block


def ein(form, left, right):
    return jnp.einsum(form, left, right, preferred_element_type=jnp.float32)


def silu_slope(value):
    sig = jax.nn.sigmoid(value)
    return sig * (1.0 + value * (1.0 - sig))


def block_parts(activated, dt_rows, a_log, dt_bias, groups):
    length = activated.shape[0]
    heads = dt_rows.shape[1]
    inner = heads * HDIM
    shared = groups * STATE
    ratio = heads // groups
    signal = activated[:, :inner].reshape(length, heads, HDIM)
    input_map = activated[:, inner : inner + shared].reshape(length, groups, STATE)
    output_map = activated[:, inner + shared :].reshape(length, groups, STATE)
    input_heads = jnp.repeat(input_map, ratio, axis=1)
    output_heads = jnp.repeat(output_map, ratio, axis=1)
    step = jax.nn.softplus(dt_rows + dt_bias)
    rate = -jnp.exp(a_log)
    row_ids = lax.broadcasted_iota(jnp.int32, (length, length), 0)
    col_ids = lax.broadcasted_iota(jnp.int32, (length, length), 1)
    lower = (row_ids >= col_ids).astype(jnp.float32)
    decay_sum = jnp.dot(lower, step * rate, precision=lax.Precision.HIGHEST)
    to_end = jnp.exp(decay_sum[-1][None, :] - decay_sum)
    scaled = (signal.astype(jnp.float32) * step[:, :, None]).astype(jnp.bfloat16)
    weighted = (scaled.astype(jnp.float32) * to_end[:, :, None]).astype(jnp.bfloat16)
    local = ein("qhp,qhn->hpn", weighted, input_heads)
    return (
        signal,
        input_map,
        output_map,
        input_heads,
        output_heads,
        step,
        rate,
        lower,
        decay_sum,
        scaled,
        to_end,
        weighted,
        local,
    )


def entry_grad(parts, d_rows):
    decay_sum = parts[8]
    output_heads = parts[4]
    scaled_grad = (d_rows.astype(jnp.float32) * jnp.exp(decay_sum)[:, :, None]).astype(jnp.bfloat16)
    return (scaled_grad, ein("thp,thn->hpn", scaled_grad, output_heads))


def block_grads(parts, d_rows, scaled_grad, h_in, carried, skip_gain, dt_rows, dt_bias):
    (
        signal,
        input_map,
        output_map,
        input_heads,
        output_heads,
        step,
        rate,
        lower,
        decay_sum,
        scaled,
        to_end,
        weighted,
        local,
    ) = parts
    length = d_rows.shape[0]
    heads = d_rows.shape[1]
    groups = input_map.shape[1]
    width_state = input_map.shape[2]
    ratio = heads // groups
    grad_f = d_rows.astype(jnp.float32)
    signal_f = signal.astype(jnp.float32)
    grad_skip = jnp.sum(grad_f * signal_f, axis=(0, 2))
    h_low = h_in.astype(jnp.bfloat16)
    carried_low = carried.astype(jnp.bfloat16)
    offset = jnp.exp(decay_sum)[:, :, None] * ein("thn,hpn->thp", output_heads, h_low)
    grad_sum = jnp.sum(grad_f * offset, axis=2)
    out_heads_grad = ein("thp,hpn->thn", scaled_grad, h_low)
    grad_weighted = ein("shn,hpn->shp", input_heads, carried_low)
    in_heads_grad = ein("shp,hpn->shn", weighted, carried_low)
    back = jnp.sum(grad_weighted * scaled.astype(jnp.float32), axis=2) * to_end
    end_term = jnp.exp(decay_sum[-1]) * jnp.sum(h_in * carried, axis=(1, 2))
    last_row = (lax.broadcasted_iota(jnp.int32, (length, 1), 0) == length - 1).astype(jnp.float32)
    grad_sum = grad_sum - back + last_row * (jnp.sum(back, axis=0) + end_term)[None, :]
    spread = decay_sum.T[:, :, None] - decay_sum.T[:, None, :]
    decay = jnp.where(lower[None] > 0, jnp.exp(jnp.minimum(spread, 0.0)), 0.0)
    score = ein("tgn,sgn->gts", output_map, input_map)
    mix = jnp.repeat(score, ratio, axis=0) * decay
    grad_mix = ein("thp,shp->hts", d_rows, scaled)
    grad_scaled = grad_weighted * to_end[:, :, None] + ein(
        "hts,thp->shp", mix.astype(jnp.bfloat16), d_rows
    )
    product = grad_mix * mix
    grad_sum = grad_sum + (jnp.sum(product, axis=2) - jnp.sum(product, axis=1)).T
    grad_score = jnp.sum((grad_mix * decay).reshape(groups, ratio, length, length), axis=1).astype(
        jnp.bfloat16
    )
    grad_outmap = ein("gts,sgn->tgn", grad_score, input_map) + jnp.sum(
        out_heads_grad.reshape(length, groups, ratio, width_state), axis=2
    )
    grad_in = ein("gts,tgn->sgn", grad_score, output_map) + jnp.sum(
        in_heads_grad.reshape(length, groups, ratio, width_state), axis=2
    )
    grad_log = jnp.dot(lower.T, grad_sum, precision=lax.Precision.HIGHEST)
    descent_increment = grad_log * rate + jnp.sum(grad_scaled * signal_f, axis=2)
    grad_signal = skip_gain[None, :, None] * grad_f + grad_scaled * step[:, :, None]
    grad_dt = descent_increment * jax.nn.sigmoid(dt_rows + dt_bias)
    decay_log_gradient = jnp.sum(grad_log * step, axis=0) * rate
    grad_act = jnp.concatenate(
        [
            grad_signal.reshape(length, heads * HDIM),
            grad_in.reshape(length, groups * width_state),
            grad_outmap.reshape(length, groups * width_state),
        ],
        axis=1,
    )
    return (grad_act, grad_dt, decay_log_gradient, jnp.sum(grad_dt, axis=0), grad_skip)


def link(earlier, later):
    return (earlier[0] + later[0], jnp.exp(later[0])[:, None, None] * earlier[1] + later[1])


def link_blocks(lower_pair, upper_pair):
    zero_rate = jnp.zeros_like(lower_pair[0])
    zero_state = jnp.zeros_like(lower_pair[1])
    below = prefix(lower_pair, "ctx", link, (zero_rate, zero_state), False)
    beyond = prefix(upper_pair, "ctx", link, (zero_rate, zero_state), True)
    total = jax.tree.map(
        lambda part: broadcast(part, "ctx", lax.axis_size("ctx") - 1), link(below, lower_pair)
    )
    return jnp.stack([below[1], link(total, beyond)[1]])


def conv_back(grad_pre, wide_grad, kernel_taps, padded, at_end, length):
    rim = kernel_taps.shape[0] - 1
    after = jnp.stack(
        [jnp.where(at_end, grad_pre[1, :rim], wide_grad[3 * rim : 4 * rim]), wide_grad[0:rim]]
    )
    padded_next = jnp.concatenate([grad_pre, after], axis=1)
    grad_raw = jnp.zeros(grad_pre.shape, jnp.float32)
    for tap in range(rim + 1):
        grad_raw = (
            grad_raw
            + kernel_taps[tap][None, None, :] * padded_next[:, rim - tap : rim - tap + length]
        )
    tap_grads = jnp.stack(
        [jnp.sum(grad_pre * padded[:, tap : tap + length], axis=(0, 1)) for tap in range(rim + 1)]
    )
    return (grad_raw, tap_grads, jnp.sum(grad_pre, axis=(0, 1)))


def first_rows(grad_pre, rim):
    return jnp.concatenate([grad_pre[0, :rim], grad_pre[1, :rim]], axis=0)


def shards_chain(
    sig_raw,
    map_raw,
    step_size_logits,
    d_out,
    sig_taps,
    map_taps,
    sig_bias,
    map_bias,
    a_log,
    dt_bias,
    skip_gain,
):
    all_map_taps, all_map_bias = (
        lax.all_gather(map_taps, "fsdp", axis=1, tiled=True),
        lax.all_gather(map_bias, "fsdp", axis=0, tiled=True),
    )
    kernel_taps = jnp.concatenate([sig_taps, all_map_taps], axis=1)
    kernel_bias = jnp.concatenate([sig_bias, all_map_bias], axis=0)
    kernel = kernel_taps.shape[0]
    rim = kernel - 1
    length = sig_raw.shape[0] // 2
    sig_width = sig_raw.shape[1]
    map_width = map_raw.shape[1]
    width = sig_width + map_width
    heads_here = step_size_logits.shape[1]
    ratio = HEADS // GROUPS
    group_count = max(1, heads_here // ratio)
    first_group = lax.axis_index("fsdp") * heads_here // ratio
    fsdp_count = lax.axis_size("fsdp")
    owned = map_width // fsdp_count
    map_start = lax.axis_index("fsdp") * owned
    raw_rows = jnp.concatenate([sig_raw, map_raw], axis=1).reshape(2, length, width)
    tails = jnp.concatenate([raw_rows[1, length - rim :], raw_rows[0, length - rim :]], axis=0)
    wide = extended(tails, (("ctx", 0),), rim)
    at_end = lax.axis_index("ctx") == lax.axis_size("ctx") - 1
    before = jnp.stack(
        [wide[0:rim], jnp.where(at_end, raw_rows[0, length - rim :], wide[3 * rim : 4 * rim])]
    )
    padded = jnp.concatenate([before, raw_rows], axis=1).astype(jnp.float32)
    preact = kernel_bias[None, None, :] + jnp.zeros((2, length, width), jnp.float32)
    for tap in range(kernel):
        preact = preact + kernel_taps[tap][None, None, :] * padded[:, tap : tap + length]
    activated = jax.nn.silu(preact).astype(jnp.bfloat16)
    maps_all = activated[:, :, sig_width:].reshape(2, length, 2, GROUPS, STATE)
    maps_mine = lax.dynamic_slice_in_dim(maps_all, first_group, group_count, 3)
    local_act = jnp.concatenate(
        [activated[:, :, :sig_width], maps_mine.reshape(2, length, 2 * group_count * STATE)], axis=2
    )
    dt_rows = step_size_logits.reshape(2, length, heads_here)
    grad_rows = d_out.reshape(2, length, heads_here, HDIM)

    def parts_of(act_block, dt_block):
        return block_parts(act_block, dt_block, a_log, dt_bias, group_count)

    parts = jax.vmap(parts_of)(local_act, dt_rows)
    scaled_grad, state_grad = jax.vmap(entry_grad)(parts, grad_rows)
    ends = parts[8][:, -1]
    h_ins = link_blocks((ends[0], parts[12][0]), (ends[1], parts[12][1]))
    carried_pair = link_blocks((ends[1], state_grad[1]), (ends[0], state_grad[0]))
    carried = jnp.stack([carried_pair[1], carried_pair[0]])
    grad_act, grad_dt, decay_log_gradient, grad_dtb, grad_skip = jax.vmap(
        block_grads, in_axes=(0, 0, 0, 0, 0, None, 0, None)
    )(parts, grad_rows, scaled_grad, h_ins, carried, skip_gain, dt_rows, dt_bias)
    slope = silu_slope(preact)
    grad_pre_sig = grad_act[:, :, :sig_width] * slope[:, :, :sig_width]
    grad_mine = grad_act[:, :, sig_width:].reshape(2, length, 2, group_count, STATE)
    zero_index = jnp.zeros((), jnp.int32)
    placed = lax.dynamic_update_slice(
        jnp.zeros((2, length, 2, GROUPS, STATE), jnp.float32),
        grad_mine,
        (zero_index, zero_index, zero_index, first_group, zero_index),
    )
    map_term = placed.reshape(2, length, map_width)
    map_owned = lax.psum_scatter(map_term, "fsdp", scatter_dimension=2, tiled=True)
    map_slope = lax.dynamic_slice_in_dim(slope[:, :, sig_width:], map_start, owned, 2)
    grad_pre = jnp.concatenate([grad_pre_sig, map_owned * map_slope], axis=2)
    own_taps = jnp.concatenate([sig_taps, map_taps], axis=1)
    own_padded = jnp.concatenate(
        [
            padded[:, :, :sig_width],
            lax.dynamic_slice_in_dim(padded[:, :, sig_width:], map_start, owned, 2),
        ],
        axis=2,
    )
    wide_grad = extended(first_rows(grad_pre, rim), (("ctx", 0),), rim)
    grad_raw, tap_grads, bias_grads = conv_back(
        grad_pre, wide_grad, own_taps, own_padded, at_end, length
    )
    map_raw_grad = grad_raw[:, :, sig_width:]
    map_tap_grad = tap_grads[:, sig_width:]
    map_bias_grad = bias_grads[sig_width:]
    sig_raw_grad = grad_raw[:, :, :sig_width]
    sig_tap_grad = tap_grads[:, :sig_width]
    sig_bias_grad = bias_grads[:sig_width]
    reduced = lax.psum(
        (
            sig_tap_grad,
            map_tap_grad,
            sig_bias_grad,
            map_bias_grad,
            jnp.sum(decay_log_gradient, axis=0),
            jnp.sum(grad_dtb, axis=0),
            jnp.sum(grad_skip, axis=0),
        ),
        "ctx",
    )
    scale = 1.0 / math.sqrt(float(lax.axis_size("ctx") * 2 * length))
    final = jax.tree.map(lambda grad_part: grad_part * scale, reduced)
    return (
        sig_raw_grad.reshape(2 * length, sig_width),
        map_raw_grad.reshape(2 * length, owned),
        grad_dt.reshape(2 * length, heads_here),
        final[0],
        final[1],
        final[2],
        final[3],
        final[4],
        final[5],
        final[6],
    )


TILE = 128
HALF = 64
NT = (((1,), (1,)), ((), ()))
TN = (((0,), (0,)), ((), ()))
NN = (((1,), (0,)), ((), ()))
BF = jnp.bfloat16
F32 = jnp.float32


def mm(a, b, dims=NN):
    return lax.dot_general(a, b, dims, preferred_element_type=F32)


def mm_f32(a, b, dims=NN):
    return lax.dot_general(a, b, dims, precision=lax.Precision.HIGHEST, preferred_element_type=F32)


def split3(x):
    hi = x.astype(BF)
    rest = x - hi.astype(F32)
    mid = rest.astype(BF)
    return hi, mid, (rest - mid.astype(F32)).astype(BF)


def ids(shape, dim):
    return lax.broadcasted_iota(jnp.int32, shape, dim)


def lanes_of(j):
    return slice(j * TILE, (j + 1) * TILE)


def place():
    ctx_place = lax.axis_index("ctx")
    quad = lax.div(ctx_place, 4)
    return quad, lax.rem(ctx_place, 4), lax.axis_index("fsdp")


def at_tile(start, width=TILE):
    return pl.ds(pl.multiple_of(start, TILE), width)


def pack_kernel(sig_ref, map_ref, dt_ref, dy_ref, mtaps_ref, mbias_ref, *rest):
    u_refs, tap_ref, (dt_in, sig_in, map_in, sems) = rest[:4], rest[4], rest[5:]
    quad, r, f = place()
    copies = []
    dt_copy = pltpu.make_async_copy(dt_ref, dt_in, sems.at[20])
    dt_copy.start()
    ends = pl.ds(pl.multiple_of(jnp.where(quad == 0, HALF - 16, TILE - 16), 16), 16)
    sig_copy = pltpu.make_async_copy(sig_ref.at[ends, :], sig_in, sems.at[21])
    sig_copy.start()
    map_copy = pltpu.make_async_copy(
        map_ref.at[ends, 0 : map_ref.shape[1] // 2], map_in, sems.at[22]
    )
    map_copy.start()

    def send(source, target):
        copy = pltpu.make_async_copy(source, target, sems.at[len(copies)])
        copy.start()
        copies.append(copy)

    half = map_ref.shape[1] // 2
    for k in (1, 2, 3, 0):
        dest = lax.bitwise_xor(r, k)
        cols = at_tile(dest * 4 * TILE, 4 * TILE)
        send(dy_ref.at[:, cols], u_refs[k].at[0:TILE, :])
        group = (2 * f + lax.div(dest, 2)) * TILE
        for e in range(4):
            send(
                map_ref.at[e * HALF // 2 : (e + 1) * HALF // 2, at_tile(group + half)],
                u_refs[k].at[TILE : TILE + HALF // 2, lanes_of(e)],
            )
    tap_ref[0:4, :] = mtaps_ref[...]
    tap_ref[4:5, :] = mbias_ref[...]
    tap_ref[5:8, :] = jnp.zeros_like(tap_ref[5:8, :])
    dt_copy.wait()
    sig_copy.wait()
    map_copy.wait()
    for k in range(4):
        dest = lax.bitwise_xor(r, k)
        hi, mid, lo = split3(dt_in[pl.ds(pl.multiple_of(8 * dest, 8), 8), :])
        edge = sig_in[:, at_tile(dest * 4 * TILE, 4 * TILE)].astype(F32)[8:16]
        group = (2 * f + lax.div(dest, 2)) * TILE
        edge_in = map_in[:, at_tile(group)].astype(F32)[8:16]
        top = jnp.concatenate([hi.astype(F32), lo.astype(F32), edge[:, 0 : 2 * TILE]], axis=1)
        low = jnp.concatenate(
            [mid.astype(F32), edge[:, 2 * TILE : 4 * TILE], edge_in], axis=1
        )
        u_refs[k][TILE + HALF // 2 : TILE + HALF // 2 + 16, :] = jnp.concatenate([top, low], axis=0).astype(BF)
    for copy in copies:
        copy.wait()


def pack_sig_kernel(sig_ref, map_ref, *rest):
    v_refs, sems = rest[:4], rest[4]
    quad, r, f = place()
    copies = []

    def send(source, target):
        copy = pltpu.make_async_copy(source, target, sems.at[len(copies)])
        copy.start()
        copies.append(copy)

    for k in (1, 2, 3, 0):
        dest = lax.bitwise_xor(r, k)
        send(sig_ref.at[:, at_tile(dest * 4 * TILE, 4 * TILE)], v_refs[k].at[0:TILE, :])
        group = (2 * f + lax.div(dest, 2)) * TILE
        for e in range(4):
            send(
                map_ref.at[e * HALF // 2 : (e + 1) * HALF // 2, at_tile(group)],
                v_refs[k].at[TILE : TILE + HALF // 2, lanes_of(e)],
            )
    for copy in copies:
        copy.wait()


def own_kernel(u_ref, v_ref, u_out, v_out):
    u_out[...] = u_ref[...]
    v_out[...] = v_ref[...]


def sig_tap_rows(j, taps_ref, bias_ref):
    at = at_tile((4 * place()[1] + j) * TILE)
    return [taps_ref[k : k + 1, at] for k in range(4)], bias_ref[0:1, at]


def map_tap_rows(j, mine_ref):
    return [mine_ref[8 * j + k : 8 * j + k + 1, :] for k in range(4)], mine_ref[
        8 * j + 4 : 8 * j + 5, :
    ]


def sigmoid(v):
    return 0.5 * jnp.tanh(0.5 * v) + 0.5


def rolled(block, k):
    return block[8:] if k == 3 else pltpu.roll(block, 3 - k, 0)[8:]


def columns(*rows8):
    total = 8 * len(rows8)
    full = jnp.concatenate(list(rows8) + [jnp.zeros((TILE - total, TILE), F32)], axis=0)
    return jnp.transpose(full)


def head_row(ref, r):
    row8 = ids((8, TILE), 0)
    out = jnp.zeros((8, TILE), F32)
    for h in range(8):
        out = jnp.where(row8 == h, ref[8 * r + h], out)
    return out


def conv(block, taps, bias):
    pre = bias + taps[0] * rolled(block, 0)
    for k in range(1, 4):
        pre = pre + taps[k] * rolled(block, k)
    return pre


def boundary_chunk(i, high):
    return high if i == 0 else jnp.logical_not(high)


def patched(ref, lanes, patch, patch_lanes, i, high):
    rows = slice(i * TILE, (i + 1) * TILE)
    if i % 2 == 1:
        return ref[rows, lanes]
    first = jnp.where(
        boundary_chunk(i, high), patch[:, patch_lanes], ref[i * TILE : i * TILE + 16, lanes]
    )
    return jnp.concatenate([first, ref[i * TILE + 16 : (i + 1) * TILE, lanes]], axis=0)


def map_rows(x, segment, start, block):
    for p in range(2):
        at = pl.ds(pl.multiple_of(8 + start + p * HALF // 2, 8), HALF // 2)
        x[segment, at, :] = block[
            TILE : TILE + HALF // 2, lanes_of(2 * segment + p)
        ].astype(F32)


def own_halo(x, high):
    first = x[0, 2 * TILE : 2 * TILE + 8, :]
    x[0, 0:8, :] = jnp.zeros_like(first)
    x[1, 0:8, :] = jnp.where(high, first, jnp.zeros_like(first))


def grads_kernel(
    u0,
    u3,
    u2,
    u1,
    one_taps,
    two_taps,
    alog_ref,
    dtb_ref,
    mid_ref,
    dp,
    xo,
    act_out,
    pre_out,
    sgrad_s,
    step_e,
    toend_e,
    exp_e,
    t_s,
    step_r,
    ds_r,
    sig_r,
    mine_ref,
    halo_ref,
    dt_src,
):
    quad, r, f = place()
    high = quad == 1
    lane8 = ids((8, TILE), 1)
    group = 2 * f + lax.div(r, 2)
    at = at_tile(lax.rem(group, 4) * TILE)
    for j in range(2):
        mine_ref[8 * j : 8 * j + 8, :] = jnp.where(
            lax.rem(f, 2) == j, one_taps[:, at], two_taps[:, at]
        )
    edge = jnp.zeros((8, 5 * TILE), F32)
    for k, u in enumerate((u0, u1, u2, u3)):
        s = lax.bitwise_xor(r, k)
        for e, start in ((0, HALF * s), (1, HALF * (3 - s))):
            map_rows(xo, e, start, u)
            dp[pl.ds(pl.multiple_of(2 * TILE * e + start, HALF), HALF), :] = u[
                e * HALF : (e + 1) * HALF, :
            ]
        packed = u[TILE + HALF // 2 : TILE + HALF // 2 + 16, :].astype(F32)
        dt_src[s] = packed[0:8, 0:TILE] + packed[8:16, 0:TILE] + packed[0:8, TILE : 2 * TILE]
        last = jnp.concatenate(
            [packed[0:8, 2 * TILE : 4 * TILE], packed[8:16, TILE : 4 * TILE]], axis=1
        )
        edge = edge + jnp.where(s == jnp.where(high, 0, 3), last, 0.0)
    last = slice(2 * TILE, 2 * TILE + 8)
    edge = jnp.concatenate([edge, jnp.where(high, xo[1, last, :], xo[0, last, :])], axis=1)
    own_halo(xo, high)

    rate8 = -jnp.exp(head_row(alog_ref, r))
    bias8 = head_row(dtb_ref, r)
    for i in range(4):
        if i < 2:
            a, b = dt_src[2 * i], pltpu.roll(dt_src[2 * i + 1], HALF, 1)
        else:
            a, b = pltpu.roll(dt_src[7 - 2 * i], HALF, 1), dt_src[6 - 2 * i]
        logits = jnp.where(lane8 < HALF, a, b) + bias8
        small = jnp.exp(-jnp.abs(logits))
        step = jnp.maximum(logits, 0.0) + jnp.log1p(small)
        at8 = slice(8 * i, 8 * i + 8)
        step_r[at8, :] = step
        sig_r[at8, :] = jnp.where(logits >= 0, 1.0, small) / (1.0 + small)
        ds_r[at8, :] = step * rate8
    upto = (ids((TILE, TILE), 0) <= ids((TILE, TILE), 1)).astype(F32)
    ds_r[...] = mm_f32(ds_r[...], upto)

    row48 = jnp.bitwise_and(ids((48, 8 * TILE), 0), 15)
    expand = (row48 == ids((48, 8 * TILE), 1) // HALF).astype(BF)
    ends = []
    for i in range(4):
        rows = slice(i * TILE, (i + 1) * TILE)
        base = (i % 2) * TILE
        taps, bias = map_tap_rows(1, mine_ref)
        pre = conv(xo[i // 2, base : base + TILE + 8, :], taps, bias)
        act_out[rows, :] = (pre * sigmoid(pre)).astype(BF)
        pre_out[rows, :] = pre
        parts = split3(
            jnp.concatenate([step_r[8 * i : 8 * i + 8, :], ds_r[8 * i : 8 * i + 8, :]], axis=0)
        )
        spread = mm(jnp.concatenate(parts, axis=0), expand, TN)
        end, masked = [], []
        for j in range(4):
            lanes = lanes_of(j)
            step = spread[:, lanes]
            ds = spread[:, lanes_of(4 + j)]
            last = ds[TILE - 1 : TILE, :]
            grow = jnp.exp(ds)
            step_e[rows, lanes] = step
            toend_e[rows, lanes] = jnp.exp(last - ds)
            exp_e[rows, lanes] = grow
            end.append(jnp.exp(last))
            grown = (dp[rows, lanes].astype(F32) * grow).astype(BF)
            sgrad_s[rows, lanes] = grown
            if i % 2 == 0:
                unknown = jnp.logical_and(boundary_chunk(i, high), ids((16, TILE), 0) < 3)
                first = jnp.where(unknown, 0.0, grown[0:16].astype(F32)).astype(BF)
                grown = jnp.concatenate([first, grown[16:]], axis=0)
            masked.append(grown)
        ends.append(jnp.concatenate(end, axis=1))
        t_s[i] = mm(act_out[rows, :], jnp.concatenate(masked, axis=1), TN)
    g_a = t_s[0] + ends[0] * t_s[1]
    g_b = t_s[2] + ends[2] * t_s[3]
    mid_ref[...] = jnp.where(high, g_a + ends[0] * ends[1] * g_b, g_b).astype(BF)
    across = [part.astype(F32) for part in split3(ends[0] * ends[1] * ends[2] * ends[3])]
    raw = jnp.where(high, xo[0, 8:16, :], xo[1, 8:16, :])
    grown = jnp.where(high, sgrad_s[0:16, :], sgrad_s[2 * TILE : 2 * TILE + 16, :]).astype(F32)
    pieces = []
    for k in range(3):
        pieces.append(
            jnp.concatenate([across[k], jnp.zeros((1, TILE), F32), raw[k : k + 1]], axis=1)
        )
    for k in range(3):
        pieces.append(jnp.concatenate([grown[k : k + 1], jnp.zeros((1, 2 * TILE), F32)], axis=1))
    pieces += [jnp.zeros((2, 6 * TILE), F32), edge]
    halo_ref[...] = jnp.concatenate(pieces, axis=0).astype(BF)


def first_kernel(
    v0, v3, v2, v1, step_e, toend_e, taps_ref, bias_ref, mine_ref, xs, acts, pres, scaled_s, weighted_s, xi, act_in, pre_in
):
    quad, r, f = place()
    high = quad == 1
    for k, v in enumerate((v0, v1, v2, v3)):
        s = lax.bitwise_xor(r, k)
        for e, start in ((0, HALF * s), (1, HALF * (3 - s))):
            xs[e, pl.ds(pl.multiple_of(8 + start, 8), HALF), :] = v[
                e * HALF : (e + 1) * HALF, :
            ].astype(F32)
            map_rows(xi, e, start, v)
    own_halo(xs, high)
    own_halo(xi, high)
    for i in range(4):
        rows = slice(i * TILE, (i + 1) * TILE)
        base = (i % 2) * TILE
        taps, bias = map_tap_rows(0, mine_ref)
        pre = conv(xi[i // 2, base : base + TILE + 8, :], taps, bias)
        act_in[rows, :] = (pre * sigmoid(pre)).astype(BF)
        pre_in[rows, :] = pre
        for j in range(4):
            lanes = lanes_of(j)
            taps, bias = sig_tap_rows(j, taps_ref, bias_ref)
            pre = conv(xs[i // 2, base : base + TILE + 8, lanes], taps, bias)
            value = (pre * sigmoid(pre)).astype(BF)
            acts[rows, lanes] = value
            pres[rows, lanes] = pre
            scaled = (value.astype(F32) * step_e[rows, lanes]).astype(BF)
            scaled_s[rows, lanes] = scaled
            weighted_s[rows, lanes] = (scaled.astype(F32) * toend_e[rows, lanes]).astype(BF)


def states_kernel(
    halo_ref,
    xs,
    xi,
    xo,
    act_in,
    weighted_s,
    sgrad_s,
    step_e,
    toend_e,
    exp_e,
    taps_ref,
    bias_ref,
    mine_ref,
    mid_ref,
    s_s,
    delta_ref,
    edge_ref,
    act_p,
    pre_p,
    scaled_p,
    weighted_p,
):
    quad, r, f = place()
    high = quad == 1
    edge = halo_ref[...].astype(F32)[8:16]
    edge_ref[...] = edge
    segment = jnp.where(high, 0, 1)
    rows16 = pl.ds(pl.multiple_of(2 * TILE * segment, 16), 16)
    for j in range(6):
        lanes = lanes_of(j)
        if j < 4:
            taps, bias = sig_tap_rows(j, taps_ref, bias_ref)
            first = xs[segment, 8:24, lanes]
        else:
            taps, bias = map_tap_rows(j - 4, mine_ref)
            first = xi[segment, 8:24, :] if j == 4 else xo[segment, 8:24, :]
        pre = conv(jnp.concatenate([edge[:, lanes], first], axis=0), taps, bias)
        value = (pre * sigmoid(pre)).astype(BF)
        act_p[:, lanes] = value
        pre_p[:, lanes] = pre
        if j < 4:
            scaled = (value.astype(F32) * step_e[rows16, lanes]).astype(BF)
            scaled_p[:, lanes] = scaled
            weighted_p[:, lanes] = (scaled.astype(F32) * toend_e[rows16, lanes]).astype(BF)
    every = slice(0, 4 * TILE)
    for i in range(4):
        s_s[i] = mm(
            patched(act_in, lanes_of(0), act_p, lanes_of(4), i, high),
            patched(weighted_s, every, weighted_p, every, i, high),
            TN,
        )
    ends = end_rows_of(exp_e)
    f_a = ends[1] * s_s[0] + s_s[1]
    f_b = ends[3] * s_s[2] + s_s[3]
    d_b = ends[2] * ends[3]
    mid_ref[...] = jnp.where(high, d_b * f_a + f_b, f_a).astype(BF)
    grown = sgrad_s[rows16, :].astype(F32)
    out_rows = act_p[:, lanes_of(5)].astype(F32)
    known = jnp.where(ids((16, TILE), 0) < 3, out_rows, 0.0).astype(BF)
    delta_ref[...] = mm(known, grown.astype(BF), TN)


def slope_of(pre):
    sig = sigmoid(pre)
    return sig * (1.0 + pre * (1.0 - sig))


def head_sums(*quantities):
    found = []
    head = ids((8, 4 * TILE), 1) // HALF
    pick = (ids((8, 4 * TILE), 0) == head).astype(BF)
    for tiles in quantities:
        x = jnp.concatenate(tiles, axis=1)
        hi = x.astype(BF)
        lo = (x - hi.astype(F32)).astype(BF)
        found.append(mm(pick, hi, NT) + mm(pick, lo, NT))
    return found


def pair_sums(x, two):
    head = ids((8, 2 * TILE), 1) // HALF + 4 * two
    pick = (ids((8, 2 * TILE), 0) == head).astype(BF)
    hi = x.astype(BF)
    lo = (x - hi.astype(F32)).astype(BF)
    return mm(pick, hi, NT) + mm(pick, lo, NT)


def skip_rows(skip_ref, r):
    lane_row = ids((1, TILE), 1)
    found = []
    for j in range(4):
        at = 8 * r + 2 * j
        found.append(jnp.where(lane_row < HALF, skip_ref[at], skip_ref[at + 1]))
    return found


def second_kernel(
    dp,
    acts,
    act_in,
    act_out,
    pres,
    pre_in,
    pre_out,
    scaled_s,
    step_e,
    toend_e,
    ds_r,
    act_p,
    pre_p,
    scaled_p,
    halo_ref,
    xo,
    mine_ref,
    skip_ref,
    base_ref,
    coef_ref,
    mslope_ref,
    gmap_ref,
    gsum_ref,
    stepsum_ref,
    skip_acc,
    left_ref,
):
    quad, r, f = place()
    high = quad == 1
    skip_row = skip_rows(skip_ref, r)
    skip_acc[...] = jnp.zeros_like(skip_acc)
    got = halo_ref[...].astype(F32)
    ends_at = slice(2 * TILE, 2 * TILE + 8)
    before = jnp.where(high, xo[1, ends_at, :], xo[0, ends_at, :])
    taps, bias = map_tap_rows(1, mine_ref)
    pre = conv(jnp.concatenate([before, got[0:8, lanes_of(5)]], axis=0), taps, bias)
    three = ids((8, TILE), 0) < 3
    out_rows = jnp.where(three, pre * sigmoid(pre), 0.0)
    out_rows = jnp.concatenate([out_rows, jnp.zeros((8, TILE), F32)], axis=0).astype(BF)
    grown = pltpu.roll(got[:, 0 : 4 * TILE], 13, 0)
    grown = jnp.where(ids((16, 4 * TILE), 0) < 3, grown, 0.0).astype(BF)
    left_ref[...] = mm(out_rows, grown, TN)
    half_lane = ids((TILE, TILE), 1) < HALF
    row8 = ids((8, TILE), 0)
    col_q = ids((TILE, TILE), 1)
    seen = ids((TILE, TILE), 0) <= col_q
    for i in range(4):
        rows = slice(i * TILE, (i + 1) * TILE)
        in_map = patched(act_in, lanes_of(0), act_p, lanes_of(4), i, high)
        out_map = patched(act_out, lanes_of(0), act_p, lanes_of(5), i, high)
        score = mm(in_map, out_map, NT)
        ds8 = ds_r[8 * i : 8 * i + 8, :]
        cols = columns(ds8)
        grad_score = jnp.zeros((TILE, TILE), F32)
        gsum = jnp.zeros((8, TILE), F32)
        rcol = jnp.zeros((TILE, TILE), F32)
        products = []
        for j in range(4):
            sc = patched(scaled_s, lanes_of(j), scaled_p, lanes_of(j), i, high)
            dy = dp[rows, lanes_of(j)]
            diag = jnp.zeros((TILE, TILE), F32)
            for e in range(2):
                h = 2 * j + e
                part = half_lane if e == 0 else jnp.logical_not(half_lane)
                gm = mm(jnp.where(part, sc, jnp.zeros_like(sc)), dy, NT)
                spread = ds8[h : h + 1, :] - cols[:, h : h + 1]
                decay = jnp.exp(jnp.where(seen, spread, -1e30))
                gd = gm * decay
                grad_score = grad_score + gd
                both = gd * score
                rcol = jnp.where(col_q == h, jnp.sum(both, axis=1, keepdims=True), rcol)
                gsum = gsum + jnp.where(row8 == h, jnp.sum(both, axis=0, keepdims=True), 0.0)
                mix = (score * decay).astype(BF)
                diag = diag + mm(mix, jnp.where(part, dy, jnp.zeros_like(dy)))
            lanes = lanes_of(j)
            sigf = patched(acts, lanes, act_p, lanes, i, high).astype(F32)
            dyf = dy.astype(F32)
            step = step_e[rows, lanes]
            slope = slope_of(patched(pres, lanes, pre_p, lanes, i, high))
            base_ref[rows, lanes] = (skip_row[j] * dyf + diag * step) * slope
            coef_ref[rows, lanes] = toend_e[rows, lanes] * step * slope
            products.append(diag * sigf)
            skip_acc[:, lanes] += eights(dyf * sigf)
        stepsum_ref[8 * i : 8 * i + 8, :] = head_sums(products)[0]
        for j, pre_ref in enumerate((pre_in, pre_out)):
            mslope_ref[rows, lanes_of(j)] = slope_of(
                patched(pre_ref, lanes_of(0), pre_p, lanes_of(4 + j), i, high)
            )
        gs = grad_score.astype(BF)
        gmap_ref[rows, lanes_of(0)] = mm(gs, out_map)
        gmap_ref[rows, lanes_of(1)] = mm(gs, in_map, TN)
        gsum_ref[8 * i : 8 * i + 8, :] = gsum - jnp.transpose(rcol)[0:8, :]


def eights(x):
    return jnp.sum(x.reshape(x.shape[0] // 8, 8, x.shape[1]), axis=0)


def end_rows_of(exp_e):
    return [exp_e[(i + 1) * TILE - 8 : (i + 1) * TILE, :][7:8, :] for i in range(4)]


def taps_back(gp, i, lanes, taps):
    base = (i % 2) * TILE
    raw = taps[3] * gp[i // 2, base : base + TILE, lanes]
    for k in range(3):
        start = base + 3 - k
        raw = raw + taps[k] * gp[i // 2, start : start + TILE, lanes]
    return raw


def fill_pads(gp, high):
    first = gp[1, 0:8, :]
    gp[0, 2 * TILE : 2 * TILE + 8, :] = jnp.where(high, first, jnp.zeros_like(first))
    gp[1, 2 * TILE : 2 * TILE + 8, :] = jnp.zeros_like(first)


def spill_of(first, taps):
    grads = jnp.concatenate([jnp.zeros((8, TILE), F32), first], axis=0)
    spill = jnp.zeros((8, TILE), F32)
    for k in range(3):
        spill = spill + taps[k] * pltpu.roll(grads, 5 + k, 0)[8:]
    return spill


def tap_sums(here, x, edge_ref, i, lanes, edge_lanes, high, sums):
    base = (i % 2) * TILE
    if i % 2 == 1:
        windows = [x[i // 2, base + 5 + k : base + 5 + k + TILE, lanes] for k in range(4)]
    else:
        first = x[i // 2, 0:8, lanes] + jnp.where(
            boundary_chunk(i, high), edge_ref[:, edge_lanes], 0.0
        )
        block = jnp.concatenate([first, x[i // 2, 8 : TILE + 8, lanes]], axis=0)
        windows = [rolled(block, k) for k in range(4)]
    for k in range(4):
        sums[k] = sums[k] + eights(here * windows[k])
    sums[4] = sums[4] + eights(here)


def maps_kernel(
    midg_ref,
    midf_ref,
    halo_ref,
    left_ref,
    s_s,
    t_s,
    delta_ref,
    exp_e,
    mslope_ref,
    weighted_s,
    weighted_p,
    sgrad_s,
    gmap_ref,
    xi,
    xo,
    edge_ref,
    mine_ref,
    one_ref,
    two_ref,
    hlow_ref,
    clow_ref,
    endrow_ref,
    h_s,
    c_s,
    gm,
):
    quad, r, f = place()
    high = quad == 1
    even = lax.rem(f, 2) == 0
    ends = end_rows_of(exp_e)
    f_in = midf_ref[...].astype(F32)
    got = halo_ref[:, 0 : 4 * TILE].astype(F32)
    across = got[0:1] + got[1:2] + got[2:3]
    g_in = midg_ref[...].astype(F32) + left_ref[...]
    t2 = t_s[2] + jnp.where(high, 0.0, delta_ref[...])
    f_a = ends[1] * s_s[0] + s_s[1]
    h_s[0] = jnp.where(high, f_in, 0.0)
    h_s[1] = ends[0] * h_s[0] + s_s[0]
    h_s[2] = jnp.where(high, ends[1] * h_s[1] + s_s[1], across * f_a + f_in)
    h_s[3] = ends[2] * h_s[2] + s_s[2]
    g_b = t2 + ends[2] * t_s[3]
    c_s[3] = jnp.where(high, g_in, 0.0)
    c_s[2] = t_s[3] + ends[3] * c_s[3]
    c_s[1] = jnp.where(high, t2 + ends[2] * c_s[2], g_in + across * g_b)
    c_s[0] = t_s[1] + ends[1] * c_s[1]
    taps_of = [map_tap_rows(j, mine_ref)[0] for j in range(2)]
    sums = [[jnp.zeros((8, TILE), F32) for _ in range(5)] for _ in range(2)]
    end_rows = []
    every = slice(0, 4 * TILE)
    for i in range(4):
        rows = slice(i * TILE, (i + 1) * TILE)
        base = (i % 2) * TILE
        hlow_ref[i] = h_s[i].astype(BF)
        clow_ref[i] = c_s[i].astype(BF)
        end_rows.append(jnp.sum(h_s[i] * c_s[i], axis=0, keepdims=True) * ends[i])
        grads = (
            mm(patched(weighted_s, every, weighted_p, every, i, high), clow_ref[i], NT) + gmap_ref[rows, lanes_of(0)],
            mm(sgrad_s[rows, :], hlow_ref[i], NT) + gmap_ref[rows, lanes_of(1)],
        )
        for j in range(2):
            here = grads[j] * mslope_ref[rows, lanes_of(j)]
            gm[i // 2, base : base + TILE, lanes_of(j)] = here
            tap_sums(
                here, (xi, xo)[j], edge_ref, i, lanes_of(0), lanes_of(4 + j), high, sums[j]
            )
    fill_pads(gm, high)
    for i in range(4):
        rows = slice(i * TILE, (i + 1) * TILE)
        raws = [taps_back(gm, i, lanes_of(j), taps_of[j]) for j in range(2)]
        one_ref[rows, :] = jnp.where(even, raws[0], raws[1]).astype(BF)
        two_ref[rows, :] = jnp.where(even, raws[1], raws[0]).astype(BF)
    first = jnp.where(high, gm[0, 0:8, :], gm[1, 0:8, :])
    endrow_ref[...] = jnp.concatenate(end_rows + [jnp.zeros((4, 4 * TILE), F32)], axis=0)
    row8 = ids((8, TILE), 0)
    tails = []
    for j in range(2):
        five = jnp.zeros((8, TILE), F32)
        for t in range(5):
            five = jnp.where(row8 == t, jnp.sum(sums[j][t], axis=0, keepdims=True), five)
        hi, lo, _ = split3(five)
        zero8 = jnp.zeros((8, TILE), F32)
        tails.append(
            jnp.concatenate(
                [spill_of(first[:, lanes_of(j)], taps_of[j]), zero8, hi.astype(F32), lo.astype(F32)], axis=0
            )
        )
    one_ref[4 * TILE : 4 * TILE + 32, :] = jnp.where(even, tails[0], tails[1]).astype(BF)
    two_ref[4 * TILE : 4 * TILE + 32, :] = jnp.where(even, tails[1], tails[0]).astype(BF)


def third_kernel(
    hlow_ref,
    clow_ref,
    endrow_ref,
    xs,
    dp,
    acts,
    act_in,
    act_out,
    edge_ref,
    act_p,
    toend_e,
    exp_e,
    step_r,
    sig_r,
    base_ref,
    coef_ref,
    gsum_ref,
    stepsum_ref,
    skip_acc,
    taps_ref,
    alog_ref,
    gp,
    blk,
    spill_ref,
    params_ref,
):
    quad, r, f = place()
    high = quad == 1
    row8 = ids((8, TILE), 0)
    lane8 = ids((8, TILE), 1)
    rate8 = -jnp.exp(head_row(alog_ref, r))
    row_q = ids((TILE, TILE), 0)
    col_q = ids((TILE, TILE), 1)
    tail_sums = jnp.concatenate(
        [(row_q >= col_q).astype(F32), (row_q < col_q).astype(F32)], axis=0
    )
    sums = [[jnp.zeros((8, TILE), F32) for _ in range(5)] for _ in range(4)]
    alog_acc = jnp.zeros((8, TILE), F32)
    ddt_acc = jnp.zeros((8, TILE), F32)
    for i in range(4):
        rows = slice(i * TILE, (i + 1) * TILE)
        at8 = slice(8 * i, 8 * i + 8)
        base = (i % 2) * TILE
        off = mm(patched(act_out, lanes_of(0), act_p, lanes_of(5), i, high), hlow_ref[i])
        gw = mm(patched(act_in, lanes_of(0), act_p, lanes_of(4), i, high), clow_ref[i])
        end_row = endrow_ref[i : i + 1, :]
        gsum = gsum_ref[at8, :]
        end_sum = jnp.zeros((8, TILE), F32)
        offsum = jnp.zeros((8, TILE), F32)
        backsum = jnp.zeros((8, TILE), F32)
        for two in range(2):
            lanes2 = slice(2 * two * TILE, (2 * two + 2) * TILE)
            sigf = jnp.concatenate(
                [
                    patched(acts, lanes_of(j), act_p, lanes_of(j), i, high).astype(F32)
                    for j in (2 * two, 2 * two + 1)
                ],
                axis=1,
            )
            offsum = offsum + pair_sums(
                dp[rows, lanes2].astype(F32) * exp_e[rows, lanes2] * off[:, lanes2], two
            )
            backsum = backsum + pair_sums(gw[:, lanes2] * toend_e[rows, lanes2] * sigf, two)
            for j in (2 * two, 2 * two + 1):
                lanes = lanes_of(j)
                end_sum = end_sum + jnp.where(
                    row8 == 2 * j + lane8 // HALF, end_row[:, lanes], 0.0
                )
                here = base_ref[rows, lanes] + gw[:, lanes] * coef_ref[rows, lanes]
                gp[i // 2, base : base + TILE, lanes] = here
                tap_sums(here, xs, edge_ref, i, lanes, lanes, high, sums[j])
        gsum = gsum + offsum
        stepsum = stepsum_ref[at8, :] + backsum
        back = backsum * step_r[at8, :]
        grad_log = mm_f32(jnp.concatenate([gsum, back], axis=1), tail_sums) + jnp.sum(
            end_sum, axis=1, keepdims=True
        )
        ddt = (grad_log * rate8 + stepsum) * sig_r[at8, :]
        blk[2 * i] = ddt
        blk[2 * i + 1] = pltpu.roll(ddt, HALF, 1)
        ddt_acc = ddt_acc + ddt
        alog_acc = alog_acc + grad_log * step_r[at8, :]
    fill_pads(gp, high)
    rows = []
    for j in range(4):
        taps = [taps_ref[k : k + 1, at_tile((4 * r + j) * TILE)] for k in range(4)]
        first = jnp.where(high, gp[0, 0:8, lanes_of(j)], gp[1, 0:8, lanes_of(j)])
        spill_ref[:, lanes_of(j)] = spill_of(first, taps)
        for t in range(5):
            rows.append(jnp.sum(sums[j][t], axis=0, keepdims=True))
    alog = jnp.sum(alog_acc * rate8, axis=1, keepdims=True)
    ddtb = jnp.sum(ddt_acc, axis=1, keepdims=True)
    skips = jnp.zeros((8, TILE), F32)
    for j in range(4):
        total = jnp.sum(skip_acc[:, lanes_of(j)], axis=0, keepdims=True)
        skips = skips + jnp.where(row8 == 2 * j + lane8 // HALF, total, 0.0)
    skips = jnp.sum(skips, axis=1, keepdims=True)
    three = jnp.where(lane8 == 0, alog, jnp.where(lane8 == 1, ddtb, skips))
    flat = columns(jnp.where(lane8 < 3, three, 0.0))
    trio = flat[0:1] + pltpu.roll(flat[0:8], 32, 1)[1:2] + pltpu.roll(flat[0:8], 64, 1)[2:3]
    trio = pltpu.roll(jnp.broadcast_to(trio, (8, TILE)), 8 * r, 1)[0:1]
    params_ref[...] = jnp.concatenate(rows + [trio, jnp.zeros((3, TILE), F32)], axis=0)


def split_params(params):
    hi, lo, _ = split3(params)
    return jnp.concatenate([hi[0:16], hi[16:32], lo[0:16], lo[16:32]], axis=1)


def whole_params(value):
    value = value.astype(F32)
    return jnp.concatenate(
        [
            value[:, lanes_of(0)] + value[:, lanes_of(2)],
            value[:, lanes_of(1)] + value[:, lanes_of(3)],
        ],
        axis=0,
    )


def cross_kernel(scale, params_ref, spill_ref, one_ref, two_ref, cross_ref):
    tails = [ref[4 * TILE : 4 * TILE + 32, :].astype(F32) for ref in (one_ref, two_ref)]
    fives = [tail[16:24] + tail[24:32] for tail in tails]
    params = jnp.concatenate(
        [
            params_ref[0:20],
            fives[0][0:5],
            fives[1][0:5],
            params_ref[20:21],
            jnp.zeros((1, TILE), F32),
        ],
        axis=0,
    )
    maps = jnp.concatenate([tails[0][0:8], tails[1][0:8], jnp.zeros((8, 2 * TILE), F32)], axis=1)
    cross_ref[0:16, :] = jnp.concatenate([spill_ref[...], maps], axis=0).astype(BF)
    cross_ref[16:32, :] = split_params(params * scale)


def send_kernel(gp, taps_ref, y0, y1, y2, y3, dx):
    quad, r, f = place()
    for j in range(4):
        lanes = lanes_of(j)
        taps = [taps_ref[k : k + 1, at_tile((4 * r + j) * TILE)] for k in range(4)]
        for i in range(4):
            dx[i * TILE : (i + 1) * TILE, lanes] = taps_back(gp, i, lanes, taps).astype(BF)
    for k, y in enumerate((y0, y1, y2, y3)):
        s = lax.bitwise_xor(r, k)
        for e, at in ((0, HALF * s), (1, 2 * TILE + HALF * (3 - s))):
            y[e * HALF : (e + 1) * HALF, :] = dx[pl.ds(pl.multiple_of(at, HALF), HALF), :]


def merge_kernel(own_ref, other_ref, one_ref, two_ref, blk, w0, w1, w2, w3):
    quad, r, f = place()
    lane8 = ids((8, TILE), 1)
    param_rows = split_params(
        whole_params(own_ref[16:32, :]) + whole_params(other_ref[16:32, :])
    )
    spill = other_ref[0:16, :].astype(F32)
    for k, w in enumerate((w0, w1, w2, w3)):
        s = lax.bitwise_xor(r, k)
        for e, at in ((0, HALF * s), (1, 2 * TILE + HALF * (3 - s))):
            rows = pl.ds(pl.multiple_of(at, HALF), HALF)
            w[0:HALF, lanes_of(e)] = one_ref[rows, :]
            w[0:HALF, lanes_of(2 + e)] = two_ref[rows, :]
        here = jnp.where(lane8 < HALF, blk[s], pltpu.roll(blk[7 - s], HALF, 1))
        hi, mid, _ = split3(here)
        w[HALF : HALF + 16, :] = jnp.concatenate(
            [
                jnp.concatenate([hi.astype(F32), spill[0:8, 0 : 2 * TILE], spill[8:16, 0:TILE]], axis=1),
                jnp.concatenate(
                    [
                        mid.astype(F32),
                        spill[0:8, 2 * TILE : 4 * TILE],
                        spill[8:16, TILE : 2 * TILE],
                    ],
                    axis=1,
                ),
            ],
            axis=0,
        ).astype(BF)
        w[HALF + 16 : HALF + 32, :] = param_rows


def last_kernel(
    y0, y3, y2, y1, w0, w3, w2, w1, dsig_ref, dmap_ref, ddt_ref, taps_ref, mtaps_ref, bias_ref, mbias_ref, *trio_refs
):
    quad, r, f = place()
    ys = (y0, y1, y2, y3)
    ws = (w0, w1, w2, w3)
    third = jnp.logical_and(quad == 0, r == 3)
    fourth = jnp.logical_and(quad == 1, r == 0)
    params = []
    trio = jnp.zeros((1, TILE), F32)
    for k, y in enumerate(ys):
        s = lax.bitwise_xor(r, k)
        cols = at_tile(s * 4 * TILE, 4 * TILE)
        dsig_ref[:, cols] = y[0:TILE, :].astype(F32)
        extra = ws[k][HALF : HALF + 16, :].astype(F32)
        spill = jnp.concatenate(
            [extra[0:8, TILE : 3 * TILE], extra[8:16, TILE : 3 * TILE]], axis=1
        )
        dsig_ref[HALF - 8 : HALF, cols] += jnp.where(third, spill, 0.0)
        dsig_ref[TILE - 8 : TILE, cols] += jnp.where(fourth, spill, 0.0)
        ddt_ref[pl.ds(pl.multiple_of(8 * s, 8), 8), :] = extra[0:8, 0:TILE] + extra[8:16, 0:TILE]
        param = whole_params(ws[k][HALF + 16 : HALF + 32, :])
        params.append(param)
        for j in range(4):
            lanes = at_tile((4 * s + j) * TILE)
            taps_ref[0:4, lanes] = param[5 * j : 5 * j + 4]
            bias_ref[0:1, lanes] = param[5 * j + 4 : 5 * j + 5]
        trio = trio + param[30:31]
    trio = jnp.broadcast_to(trio, (8, TILE))
    for t, ref in enumerate(trio_refs):
        moved = trio if t == 0 else pltpu.roll(trio, TILE - 32 * t, 1)
        ref[...] = moved[0:1, 0:32]
    own = lax.div(r, 2)
    swap = f >= 2
    for pair in range(2):
        group = own if pair == 0 else 1 - own
        a, b = 2 * pair, 2 * pair + 1
        for j in range(2):
            where = jnp.where(swap, 1 - j, j)
            lanes = at_tile((2 * where + group) * TILE)
            for e in range(2):
                dmap_ref[e * HALF : (e + 1) * HALF, lanes] = ws[a][
                    0:HALF, lanes_of(2 * j + e)
                ].astype(F32) + ws[b][0:HALF, lanes_of(2 * j + e)].astype(F32)
            spill = jnp.zeros((8, TILE), F32)
            for w in (ws[a], ws[b]):
                extra = w[HALF : HALF + 16, 3 * TILE : 4 * TILE].astype(F32)
                spill = spill + extra[8 * j : 8 * j + 8]
            dmap_ref[HALF - 8 : HALF, lanes] += jnp.where(third, spill, 0.0)
            dmap_ref[TILE - 8 : TILE, lanes] += jnp.where(fourth, spill, 0.0)
            five = params[a][20 + 5 * j : 25 + 5 * j] + params[b][20 + 5 * j : 25 + 5 * j]
            mtaps_ref[0:4, lanes] = five[0:4]
            mbias_ref[0:1, lanes] = five[4:5]


ROUTE_ONE = [(0, 0), (2, 1), (1, 2), (3, 3)]
ROUTE_TWO = [(0, 2), (2, 3), (1, 0), (3, 1)]


def back(route):
    return [(target, source) for source, target in route]


def shards_quad(
    sig_raw,
    map_raw,
    step_size_logits,
    d_out,
    sig_taps,
    map_taps,
    sig_bias,
    map_bias,
    a_log,
    dt_bias,
    skip_gain,
):
    ctx = lax.axis_size("ctx")
    rows, sig_width = sig_raw.shape
    vmem = pl.BlockSpec(memory_space=pltpu.VMEM)
    smem = pl.BlockSpec(memory_space=pltpu.SMEM)
    hbm = pl.BlockSpec(memory_space=pltpu.HBM)

    def call(kernel, out_shape, in_specs, out_specs, scratch, mib, cost):
        return pl.pallas_call(
            kernel,
            out_shape=out_shape,
            in_specs=in_specs,
            out_specs=out_specs,
            scratch_shapes=scratch,
            compiler_params=pltpu.CompilerParams(vmem_limit_bytes=mib * 1024 * 1024),
            cost_estimate=pl.CostEstimate(flops=cost, bytes_accessed=cost // 100, transcendentals=0),
        )

    def shape(*dims, kind=F32):
        return jax.ShapeDtypeStruct(dims, kind)

    inside = [[(c, c ^ k) for c in range(ctx)] for k in range(4)]
    over = [(c, c ^ 4) for c in range(ctx)]
    total = 4 * TILE
    wide, narrow = 6 * TILE, 4 * TILE
    owned = map_taps.shape[1]
    sig_bias_row = sig_bias[None, :]
    *packed, map_params = call(
        pack_kernel,
        (shape(TILE + HALF // 2 + 16, narrow, kind=BF),) * 4 + (shape(8, owned),),
        [hbm, hbm, hbm, hbm, vmem, vmem],
        (vmem,) * 5,
        [
            pltpu.VMEM((32, TILE), F32),
            pltpu.VMEM((16, sig_width), BF),
            pltpu.VMEM((16, map_raw.shape[1] // 2), BF),
            pltpu.SemaphoreType.DMA((23,)),
        ],
        60,
        10**6,
    )(sig_raw, map_raw, step_size_logits.T, d_out, map_taps, map_bias[None, :])
    us = [packed[0]] + [lax.ppermute(packed[k], "ctx", inside[k]) for k in (1, 2, 3)]
    map_one = lax.ppermute(map_params, "fsdp", back(ROUTE_ONE))
    map_two = lax.ppermute(map_params, "fsdp", back(ROUTE_TWO))
    packed = call(
        pack_sig_kernel,
        (shape(TILE + HALF // 2, narrow, kind=BF),) * 4,
        [hbm, hbm],
        (vmem,) * 4,
        [pltpu.SemaphoreType.DMA((20,))],
        60,
        10**6,
    )(sig_raw, map_raw)
    own_u, own_v = call(
        own_kernel,
        (
            shape(TILE + HALF // 2 + 16, narrow, kind=BF),
            shape(TILE + HALF // 2, narrow, kind=BF),
        ),
        [vmem] * 2,
        (vmem,) * 2,
        [],
        16,
        10**6,
    )(us[0], packed[0])
    us[0] = own_u
    vs = [own_v] + [lax.ppermute(packed[k], "ctx", inside[k]) for k in (1, 2, 3)]
    midg, dp, xo, act_out, pre_out, sgrad, step_e, toend_e, exp_e, t_s, step_r, ds_r, sig_r, *small = call(
        grads_kernel,
        (
            shape(TILE, narrow, kind=BF),
            shape(total, narrow, kind=BF),
            shape(2, 2 * TILE + 8, TILE),
            shape(total, TILE, kind=BF),
            shape(total, TILE),
            shape(total, narrow, kind=BF),
            shape(total, narrow),
            shape(total, narrow),
            shape(total, narrow),
            shape(4, TILE, narrow),
            shape(32, TILE),
            shape(32, TILE),
            shape(32, TILE),
            shape(16, TILE),
            shape(16, wide, kind=BF),
        ),
        [vmem] * 6 + [smem] * 2,
        (vmem,) * 15,
        [pltpu.VMEM((4, 8, TILE), F32)],
        24,
        2 * 10**9,
    )(us[0], us[3], us[2], us[1], map_one, map_two, a_log, dt_bias)
    mine, halo = small
    halo = lax.ppermute(halo, "ctx", over)
    midg = lax.ppermute(midg, "ctx", over)
    xs, acts, pres, scaled, weighted, xi, act_in, pre_in = call(
        first_kernel,
        (
            shape(2, 2 * TILE + 8, narrow),
            shape(total, narrow, kind=BF),
            shape(total, narrow),
            shape(total, narrow, kind=BF),
            shape(total, narrow, kind=BF),
            shape(2, 2 * TILE + 8, TILE),
            shape(total, TILE, kind=BF),
            shape(total, TILE),
        ),
        [vmem] * 9,
        (vmem,) * 8,
        [],
        24,
        2 * 10**9,
    )(vs[0], vs[3], vs[2], vs[1], step_e, toend_e, sig_taps, sig_bias_row, mine)
    midf, s_s, delta, edge, act_p, pre_p, scaled_p, weighted_p = call(
        states_kernel,
        (
            shape(TILE, narrow, kind=BF),
            shape(4, TILE, narrow),
            shape(TILE, narrow),
            shape(8, wide),
            shape(16, wide, kind=BF),
            shape(16, wide),
            shape(16, narrow, kind=BF),
            shape(16, narrow, kind=BF),
        ),
        [vmem] * 13,
        (vmem,) * 8,
        [],
        24,
        10**9,
    )(halo, xs, xi, xo, act_in, weighted, sgrad, step_e, toend_e, exp_e, sig_taps, sig_bias_row, mine)
    midf = lax.ppermute(midf, "ctx", over)
    base, coef, mslope, gmap, gsum, stepsum, skips, left = call(
        second_kernel,
        (
            shape(total, narrow),
            shape(total, narrow),
            shape(total, 2 * TILE),
            shape(total, 2 * TILE),
            shape(32, TILE),
            shape(32, TILE),
            shape(8, narrow),
            shape(TILE, narrow),
        ),
        [vmem] * 17 + [smem],
        (vmem,) * 8,
        [],
        24,
        5 * 10**9,
    )(
        dp,
        acts,
        act_in,
        act_out,
        pres,
        pre_in,
        pre_out,
        scaled,
        step_e,
        toend_e,
        ds_r,
        act_p,
        pre_p,
        scaled_p,
        halo,
        xo,
        mine,
        skip_gain,
    )
    one, two, hlow, clow, endrow = call(
        maps_kernel,
        (
            shape(total + 32, TILE, kind=BF),
            shape(total + 32, TILE, kind=BF),
            shape(4, TILE, narrow, kind=BF),
            shape(4, TILE, narrow, kind=BF),
            shape(8, narrow),
        ),
        [vmem] * 17,
        (vmem,) * 5,
        [
            pltpu.VMEM((4, TILE, narrow), F32),
            pltpu.VMEM((4, TILE, narrow), F32),
            pltpu.VMEM((2, 2 * TILE + 8, 2 * TILE), F32),
        ],
        24,
        2 * 10**9,
    )(
        midg,
        midf,
        halo,
        left,
        s_s,
        t_s,
        delta,
        exp_e,
        mslope,
        weighted,
        weighted_p,
        sgrad,
        gmap,
        xi,
        xo,
        edge,
        mine,
    )
    one = lax.ppermute(one, "fsdp", ROUTE_ONE)
    two = lax.ppermute(two, "fsdp", ROUTE_TWO)
    gp, blk, spill, params = call(
        third_kernel,
        (
            shape(2, 2 * TILE + 8, narrow),
            shape(8, 8, TILE),
            shape(8, narrow),
            shape(24, TILE),
        ),
        [vmem] * 20 + [smem],
        (vmem,) * 4,
        [],
        24,
        3 * 10**9,
    )(
        hlow,
        clow,
        endrow,
        xs,
        dp,
        acts,
        act_in,
        act_out,
        edge,
        act_p,
        toend_e,
        exp_e,
        step_r,
        sig_r,
        base,
        coef,
        gsum,
        stepsum,
        skips,
        sig_taps,
        a_log,
    )
    scale = 1.0 / math.sqrt(float(ctx * rows))
    cross = call(
        functools.partial(cross_kernel, scale),
        shape(32, narrow, kind=BF),
        [vmem] * 4,
        vmem,
        [],
        16,
        10**6,
    )(params, spill, one, two)
    other = lax.ppermute(cross, "ctx", over)
    ys = call(
        send_kernel,
        (shape(TILE, narrow, kind=BF),) * 4,
        [vmem] * 2,
        (vmem,) * 4,
        [pltpu.VMEM((total, narrow), BF)],
        16,
        10**9,
    )(gp, sig_taps)
    ys = [ys[0]] + [lax.ppermute(ys[k], "ctx", inside[k]) for k in (1, 2, 3)]
    ws = call(
        merge_kernel,
        (shape(HALF + 32, narrow, kind=BF),) * 4,
        [vmem] * 5,
        (vmem,) * 4,
        [],
        16,
        10**6,
    )(cross, other, one, two, blk)
    ws = [ws[0]] + [lax.ppermute(ws[k], "ctx", inside[k]) for k in (1, 2, 3)]
    d_sig, d_map, d_dt, taps, map_taps_grad, bias, map_bias_grad, *trio = call(
        last_kernel,
        (
            shape(rows, sig_width),
            shape(rows, owned),
            shape(32, TILE),
            shape(4, sig_width),
            shape(4, owned),
            shape(1, sig_width),
            shape(1, owned),
        )
        + (shape(1, 32),) * 3,
        [vmem] * 8,
        (vmem,) * 10,
        [],
        16,
        10**6,
    )(ys[0], ys[3], ys[2], ys[1], ws[0], ws[3], ws[2], ws[1])
    return (
        d_sig,
        d_map,
        d_dt.T,
        taps,
        map_taps_grad,
        bias[0],
        map_bias_grad[0],
        *(t[0] for t in trio),
    )


def shards(*args):
    sig_raw, map_raw, step_size_logits = args[:3]
    ctx = lax.axis_size("ctx")
    fsdp = lax.axis_size("fsdp")
    fits = (
        ctx == 8
        and fsdp == 4
        and sig_raw.shape == (TILE, 2048)
        and map_raw.shape == (TILE, 2 * GROUPS * STATE)
        and step_size_logits.shape[1] == 32
    )
    return shards_quad(*args) if fits else shards_chain(*args)


def solution(mesh):
    return jax.shard_map(
        shards,
        mesh=mesh,
        in_specs=(
            P("ctx", "fsdp"),
            P("ctx", None),
            P("ctx", "fsdp"),
            P("ctx", "fsdp"),
            P(None, "fsdp"),
            P(None, "fsdp"),
            P("fsdp"),
            P("fsdp"),
            P("fsdp"),
            P("fsdp"),
            P("fsdp"),
        ),
        out_specs=(
            P("ctx", "fsdp"),
            P("ctx", "fsdp"),
            P("ctx", "fsdp"),
            P(None, "fsdp"),
            P(None, "fsdp"),
            P("fsdp"),
            P("fsdp"),
            P("fsdp"),
            P("fsdp"),
            P("fsdp"),
        ),
        check_vma=False,
    )
```

```python
import functools
import math

import jax
import jax.numpy as jnp
from jax import lax
from jax.experimental import pallas as pl
from jax.experimental.pallas import tpu as pltpu
from jax.sharding import PartitionSpec as P

HEADS = 128
HDIM = 64
STATE = 128
GROUPS = 8


def prefix(part, axis, combine, identity, reverse):
    count = lax.axis_size(axis)
    place = lax.axis_index(axis)
    ahead = count - 1 - place if reverse else place
    gathered = jax.tree.map(lambda a: lax.all_gather(a, axis), part)
    state = jax.tree.map(lambda a, e: jnp.zeros_like(a) + jnp.asarray(e, a.dtype), part, identity)

    def one(lap, state):
        source = count - 1 - lap if reverse else lap
        return combine(
            state, jax.tree.map(lambda a: lax.dynamic_index_in_dim(a, source, 0, False), gathered)
        )

    return lax.fori_loop(0, ahead, one, state)


def broadcast(x, axis, root):
    mine = lax.axis_index(axis) == root
    return lax.psum(jnp.where(mine, x, jnp.zeros_like(x)), axis)


def extended(block, sides, width):
    for axis, dim in sides:
        count = lax.axis_size(axis)
        forward = [(i, i + 1) for i in range(count - 1)]
        backward = [(target, source) for source, target in forward]
        low = lax.ppermute(
            lax.slice_in_dim(block, block.shape[dim] - width, None, axis=dim), axis, forward
        )
        high = lax.ppermute(lax.slice_in_dim(block, 0, width, axis=dim), axis, backward)
        block = jnp.concatenate([low, block, high], axis=dim)
    return block


def ein(form, left, right):
    return jnp.einsum(form, left, right, preferred_element_type=jnp.float32)


def silu_slope(value):
    sig = jax.nn.sigmoid(value)
    return sig * (1.0 + value * (1.0 - sig))


def block_parts(activated, dt_rows, a_log, dt_bias, groups):
    length = activated.shape[0]
    heads = dt_rows.shape[1]
    inner = heads * HDIM
    shared = groups * STATE
    ratio = heads // groups
    signal = activated[:, :inner].reshape(length, heads, HDIM)
    input_map = activated[:, inner : inner + shared].reshape(length, groups, STATE)
    output_map = activated[:, inner + shared :].reshape(length, groups, STATE)
    input_heads = jnp.repeat(input_map, ratio, axis=1)
    output_heads = jnp.repeat(output_map, ratio, axis=1)
    step = jax.nn.softplus(dt_rows + dt_bias)
    rate = -jnp.exp(a_log)
    row_ids = lax.broadcasted_iota(jnp.int32, (length, length), 0)
    col_ids = lax.broadcasted_iota(jnp.int32, (length, length), 1)
    lower = (row_ids >= col_ids).astype(jnp.float32)
    decay_sum = jnp.dot(lower, step * rate, precision=lax.Precision.HIGHEST)
    to_end = jnp.exp(decay_sum[-1][None, :] - decay_sum)
    scaled = (signal.astype(jnp.float32) * step[:, :, None]).astype(jnp.bfloat16)
    weighted = (scaled.astype(jnp.float32) * to_end[:, :, None]).astype(jnp.bfloat16)
    local = ein("qhp,qhn->hpn", weighted, input_heads)
    return (
        signal,
        input_map,
        output_map,
        input_heads,
        output_heads,
        step,
        rate,
        lower,
        decay_sum,
        scaled,
        to_end,
        weighted,
        local,
    )


def entry_grad(parts, d_rows):
    decay_sum = parts[8]
    output_heads = parts[4]
    scaled_grad = (d_rows.astype(jnp.float32) * jnp.exp(decay_sum)[:, :, None]).astype(jnp.bfloat16)
    return (scaled_grad, ein("thp,thn->hpn", scaled_grad, output_heads))


def block_grads(parts, d_rows, scaled_grad, h_in, carried, skip_gain, dt_rows, dt_bias):
    (
        signal,
        input_map,
        output_map,
        input_heads,
        output_heads,
        step,
        rate,
        lower,
        decay_sum,
        scaled,
        to_end,
        weighted,
        local,
    ) = parts
    length = d_rows.shape[0]
    heads = d_rows.shape[1]
    groups = input_map.shape[1]
    width_state = input_map.shape[2]
    ratio = heads // groups
    grad_f = d_rows.astype(jnp.float32)
    signal_f = signal.astype(jnp.float32)
    grad_skip = jnp.sum(grad_f * signal_f, axis=(0, 2))
    h_low = h_in.astype(jnp.bfloat16)
    carried_low = carried.astype(jnp.bfloat16)
    offset = jnp.exp(decay_sum)[:, :, None] * ein("thn,hpn->thp", output_heads, h_low)
    grad_sum = jnp.sum(grad_f * offset, axis=2)
    out_heads_grad = ein("thp,hpn->thn", scaled_grad, h_low)
    grad_weighted = ein("shn,hpn->shp", input_heads, carried_low)
    in_heads_grad = ein("shp,hpn->shn", weighted, carried_low)
    back = jnp.sum(grad_weighted * scaled.astype(jnp.float32), axis=2) * to_end
    end_term = jnp.exp(decay_sum[-1]) * jnp.sum(h_in * carried, axis=(1, 2))
    last_row = (lax.broadcasted_iota(jnp.int32, (length, 1), 0) == length - 1).astype(jnp.float32)
    grad_sum = grad_sum - back + last_row * (jnp.sum(back, axis=0) + end_term)[None, :]
    spread = decay_sum.T[:, :, None] - decay_sum.T[:, None, :]
    decay = jnp.where(lower[None] > 0, jnp.exp(jnp.minimum(spread, 0.0)), 0.0)
    score = ein("tgn,sgn->gts", output_map, input_map)
    mix = jnp.repeat(score, ratio, axis=0) * decay
    grad_mix = ein("thp,shp->hts", d_rows, scaled)
    grad_scaled = grad_weighted * to_end[:, :, None] + ein(
        "hts,thp->shp", mix.astype(jnp.bfloat16), d_rows
    )
    product = grad_mix * mix
    grad_sum = grad_sum + (jnp.sum(product, axis=2) - jnp.sum(product, axis=1)).T
    grad_score = jnp.sum((grad_mix * decay).reshape(groups, ratio, length, length), axis=1).astype(
        jnp.bfloat16
    )
    grad_outmap = ein("gts,sgn->tgn", grad_score, input_map) + jnp.sum(
        out_heads_grad.reshape(length, groups, ratio, width_state), axis=2
    )
    grad_in = ein("gts,tgn->sgn", grad_score, output_map) + jnp.sum(
        in_heads_grad.reshape(length, groups, ratio, width_state), axis=2
    )
    grad_log = jnp.dot(lower.T, grad_sum, precision=lax.Precision.HIGHEST)
    descent_increment = grad_log * rate + jnp.sum(grad_scaled * signal_f, axis=2)
    grad_signal = skip_gain[None, :, None] * grad_f + grad_scaled * step[:, :, None]
    grad_dt = descent_increment * jax.nn.sigmoid(dt_rows + dt_bias)
    decay_log_gradient = jnp.sum(grad_log * step, axis=0) * rate
    grad_act = jnp.concatenate(
        [
            grad_signal.reshape(length, heads * HDIM),
            grad_in.reshape(length, groups * width_state),
            grad_outmap.reshape(length, groups * width_state),
        ],
        axis=1,
    )
    return (grad_act, grad_dt, decay_log_gradient, jnp.sum(grad_dt, axis=0), grad_skip)


def link(earlier, later):
    return (earlier[0] + later[0], jnp.exp(later[0])[:, None, None] * earlier[1] + later[1])


def link_blocks(lower_pair, upper_pair):
    zero_rate = jnp.zeros_like(lower_pair[0])
    zero_state = jnp.zeros_like(lower_pair[1])
    below = prefix(lower_pair, "ctx", link, (zero_rate, zero_state), False)
    beyond = prefix(upper_pair, "ctx", link, (zero_rate, zero_state), True)
    total = jax.tree.map(
        lambda part: broadcast(part, "ctx", lax.axis_size("ctx") - 1), link(below, lower_pair)
    )
    return jnp.stack([below[1], link(total, beyond)[1]])


def conv_back(grad_pre, wide_grad, kernel_taps, padded, at_end, length):
    rim = kernel_taps.shape[0] - 1
    after = jnp.stack(
        [jnp.where(at_end, grad_pre[1, :rim], wide_grad[3 * rim : 4 * rim]), wide_grad[0:rim]]
    )
    padded_next = jnp.concatenate([grad_pre, after], axis=1)
    grad_raw = jnp.zeros(grad_pre.shape, jnp.float32)
    for tap in range(rim + 1):
        grad_raw = (
            grad_raw
            + kernel_taps[tap][None, None, :] * padded_next[:, rim - tap : rim - tap + length]
        )
    tap_grads = jnp.stack(
        [jnp.sum(grad_pre * padded[:, tap : tap + length], axis=(0, 1)) for tap in range(rim + 1)]
    )
    return (grad_raw, tap_grads, jnp.sum(grad_pre, axis=(0, 1)))


def first_rows(grad_pre, rim):
    return jnp.concatenate([grad_pre[0, :rim], grad_pre[1, :rim]], axis=0)


def shards_chain(
    sig_raw,
    map_raw,
    step_size_logits,
    d_out,
    sig_taps,
    map_taps,
    sig_bias,
    map_bias,
    a_log,
    dt_bias,
    skip_gain,
):
    all_map_taps, all_map_bias = (
        lax.all_gather(map_taps, "fsdp", axis=1, tiled=True),
        lax.all_gather(map_bias, "fsdp", axis=0, tiled=True),
    )
    kernel_taps = jnp.concatenate([sig_taps, all_map_taps], axis=1)
    kernel_bias = jnp.concatenate([sig_bias, all_map_bias], axis=0)
    kernel = kernel_taps.shape[0]
    rim = kernel - 1
    length = sig_raw.shape[0] // 2
    sig_width = sig_raw.shape[1]
    map_width = map_raw.shape[1]
    width = sig_width + map_width
    heads_here = step_size_logits.shape[1]
    ratio = HEADS // GROUPS
    group_count = max(1, heads_here // ratio)
    first_group = lax.axis_index("fsdp") * heads_here // ratio
    fsdp_count = lax.axis_size("fsdp")
    owned = map_width // fsdp_count
    map_start = lax.axis_index("fsdp") * owned
    raw_rows = jnp.concatenate([sig_raw, map_raw], axis=1).reshape(2, length, width)
    tails = jnp.concatenate([raw_rows[1, length - rim :], raw_rows[0, length - rim :]], axis=0)
    wide = extended(tails, (("ctx", 0),), rim)
    at_end = lax.axis_index("ctx") == lax.axis_size("ctx") - 1
    before = jnp.stack(
        [wide[0:rim], jnp.where(at_end, raw_rows[0, length - rim :], wide[3 * rim : 4 * rim])]
    )
    padded = jnp.concatenate([before, raw_rows], axis=1).astype(jnp.float32)
    preact = kernel_bias[None, None, :] + jnp.zeros((2, length, width), jnp.float32)
    for tap in range(kernel):
        preact = preact + kernel_taps[tap][None, None, :] * padded[:, tap : tap + length]
    activated = jax.nn.silu(preact).astype(jnp.bfloat16)
    maps_all = activated[:, :, sig_width:].reshape(2, length, 2, GROUPS, STATE)
    maps_mine = lax.dynamic_slice_in_dim(maps_all, first_group, group_count, 3)
    local_act = jnp.concatenate(
        [activated[:, :, :sig_width], maps_mine.reshape(2, length, 2 * group_count * STATE)], axis=2
    )
    dt_rows = step_size_logits.reshape(2, length, heads_here)
    grad_rows = d_out.reshape(2, length, heads_here, HDIM)

    def parts_of(act_block, dt_block):
        return block_parts(act_block, dt_block, a_log, dt_bias, group_count)

    parts = jax.vmap(parts_of)(local_act, dt_rows)
    scaled_grad, state_grad = jax.vmap(entry_grad)(parts, grad_rows)
    ends = parts[8][:, -1]
    h_ins = link_blocks((ends[0], parts[12][0]), (ends[1], parts[12][1]))
    carried_pair = link_blocks((ends[1], state_grad[1]), (ends[0], state_grad[0]))
    carried = jnp.stack([carried_pair[1], carried_pair[0]])
    grad_act, grad_dt, decay_log_gradient, grad_dtb, grad_skip = jax.vmap(
        block_grads, in_axes=(0, 0, 0, 0, 0, None, 0, None)
    )(parts, grad_rows, scaled_grad, h_ins, carried, skip_gain, dt_rows, dt_bias)
    slope = silu_slope(preact)
    grad_pre_sig = grad_act[:, :, :sig_width] * slope[:, :, :sig_width]
    grad_mine = grad_act[:, :, sig_width:].reshape(2, length, 2, group_count, STATE)
    zero_index = jnp.zeros((), jnp.int32)
    placed = lax.dynamic_update_slice(
        jnp.zeros((2, length, 2, GROUPS, STATE), jnp.float32),
        grad_mine,
        (zero_index, zero_index, zero_index, first_group, zero_index),
    )
    map_term = placed.reshape(2, length, map_width)
    map_owned = lax.psum_scatter(map_term, "fsdp", scatter_dimension=2, tiled=True)
    map_slope = lax.dynamic_slice_in_dim(slope[:, :, sig_width:], map_start, owned, 2)
    grad_pre = jnp.concatenate([grad_pre_sig, map_owned * map_slope], axis=2)
    own_taps = jnp.concatenate([sig_taps, map_taps], axis=1)
    own_padded = jnp.concatenate(
        [
            padded[:, :, :sig_width],
            lax.dynamic_slice_in_dim(padded[:, :, sig_width:], map_start, owned, 2),
        ],
        axis=2,
    )
    wide_grad = extended(first_rows(grad_pre, rim), (("ctx", 0),), rim)
    grad_raw, tap_grads, bias_grads = conv_back(
        grad_pre, wide_grad, own_taps, own_padded, at_end, length
    )
    map_raw_grad = grad_raw[:, :, sig_width:]
    map_tap_grad = tap_grads[:, sig_width:]
    map_bias_grad = bias_grads[sig_width:]
    sig_raw_grad = grad_raw[:, :, :sig_width]
    sig_tap_grad = tap_grads[:, :sig_width]
    sig_bias_grad = bias_grads[:sig_width]
    reduced = lax.psum(
        (
            sig_tap_grad,
            map_tap_grad,
            sig_bias_grad,
            map_bias_grad,
            jnp.sum(decay_log_gradient, axis=0),
            jnp.sum(grad_dtb, axis=0),
            jnp.sum(grad_skip, axis=0),
        ),
        "ctx",
    )
    scale = 1.0 / math.sqrt(float(lax.axis_size("ctx") * 2 * length))
    final = jax.tree.map(lambda grad_part: grad_part * scale, reduced)
    return (
        sig_raw_grad.reshape(2 * length, sig_width),
        map_raw_grad.reshape(2 * length, owned),
        grad_dt.reshape(2 * length, heads_here),
        final[0],
        final[1],
        final[2],
        final[3],
        final[4],
        final[5],
        final[6],
    )


TILE = 128
HALF = 64
NT = (((1,), (1,)), ((), ()))
TN = (((0,), (0,)), ((), ()))
NN = (((1,), (0,)), ((), ()))
BF = jnp.bfloat16
F32 = jnp.float32


def mm(a, b, dims=NN):
    return lax.dot_general(a, b, dims, preferred_element_type=F32)


def mm_f32(a, b, dims=NN):
    return lax.dot_general(a, b, dims, precision=lax.Precision.HIGHEST, preferred_element_type=F32)


def split3(x):
    hi = x.astype(BF)
    rest = x - hi.astype(F32)
    mid = rest.astype(BF)
    return hi, mid, (rest - mid.astype(F32)).astype(BF)


def ids(shape, dim):
    return lax.broadcasted_iota(jnp.int32, shape, dim)


def lanes_of(j):
    return slice(j * TILE, (j + 1) * TILE)


def place():
    ctx_place = lax.axis_index("ctx")
    quad = lax.div(ctx_place, 4)
    return quad, lax.rem(ctx_place, 4), lax.axis_index("fsdp")


def at_tile(start, width=TILE):
    return pl.ds(pl.multiple_of(start, TILE), width)


def pack_kernel(sig_ref, map_ref, dt_ref, dy_ref, mtaps_ref, mbias_ref, *rest):
    u_refs, tap_ref, (dt_in, sig_in, map_in, sems) = rest[:4], rest[4], rest[5:]
    quad, r, f = place()
    copies = []
    dt_copy = pltpu.make_async_copy(dt_ref, dt_in, sems.at[20])
    dt_copy.start()
    ends = pl.ds(pl.multiple_of(jnp.where(quad == 0, HALF - 16, TILE - 16), 16), 16)
    sig_copy = pltpu.make_async_copy(sig_ref.at[ends, :], sig_in, sems.at[21])
    sig_copy.start()
    map_copy = pltpu.make_async_copy(
        map_ref.at[ends, 0 : map_ref.shape[1] // 2], map_in, sems.at[22]
    )
    map_copy.start()

    def send(source, target):
        copy = pltpu.make_async_copy(source, target, sems.at[len(copies)])
        copy.start()
        copies.append(copy)

    half = map_ref.shape[1] // 2
    for k in (1, 2, 3, 0):
        dest = lax.bitwise_xor(r, k)
        cols = at_tile(dest * 4 * TILE, 4 * TILE)
        send(dy_ref.at[:, cols], u_refs[k].at[0:TILE, :])
        group = (2 * f + lax.div(dest, 2)) * TILE
        for e in range(4):
            send(
                map_ref.at[e * HALF // 2 : (e + 1) * HALF // 2, at_tile(group + half)],
                u_refs[k].at[TILE : TILE + HALF // 2, lanes_of(e)],
            )
    tap_ref[0:4, :] = mtaps_ref[...]
    tap_ref[4:5, :] = mbias_ref[...]
    tap_ref[5:8, :] = jnp.zeros_like(tap_ref[5:8, :])
    dt_copy.wait()
    sig_copy.wait()
    map_copy.wait()
    for k in range(4):
        dest = lax.bitwise_xor(r, k)
        hi, mid, lo = split3(dt_in[pl.ds(pl.multiple_of(8 * dest, 8), 8), :])
        edge = sig_in[:, at_tile(dest * 4 * TILE, 4 * TILE)].astype(F32)[8:16]
        group = (2 * f + lax.div(dest, 2)) * TILE
        edge_in = map_in[:, at_tile(group)].astype(F32)[8:16]
        top = jnp.concatenate([hi.astype(F32), lo.astype(F32), edge[:, 0 : 2 * TILE]], axis=1)
        low = jnp.concatenate(
            [mid.astype(F32), edge[:, 2 * TILE : 4 * TILE], edge_in], axis=1
        )
        u_refs[k][TILE + HALF // 2 : TILE + HALF // 2 + 16, :] = jnp.concatenate([top, low], axis=0).astype(BF)
    for copy in copies:
        copy.wait()


def pack_sig_kernel(sig_ref, map_ref, *rest):
    v_refs, sems = rest[:4], rest[4]
    quad, r, f = place()
    copies = []

    def send(source, target):
        copy = pltpu.make_async_copy(source, target, sems.at[len(copies)])
        copy.start()
        copies.append(copy)

    for k in (1, 2, 3, 0):
        dest = lax.bitwise_xor(r, k)
        send(sig_ref.at[:, at_tile(dest * 4 * TILE, 4 * TILE)], v_refs[k].at[0:TILE, :])
        group = (2 * f + lax.div(dest, 2)) * TILE
        for e in range(4):
            send(
                map_ref.at[e * HALF // 2 : (e + 1) * HALF // 2, at_tile(group)],
                v_refs[k].at[TILE : TILE + HALF // 2, lanes_of(e)],
            )
    for copy in copies:
        copy.wait()


def own_kernel(ref, out):
    out[...] = ref[...]


def own_later_kernel(ref, after, out):
    out[...] = ref[...]


def sig_tap_rows(j, taps_ref, bias_ref):
    at = at_tile((4 * place()[1] + j) * TILE)
    return [taps_ref[k : k + 1, at] for k in range(4)], bias_ref[0:1, at]


def map_tap_rows(j, mine_ref):
    return [mine_ref[8 * j + k : 8 * j + k + 1, :] for k in range(4)], mine_ref[
        8 * j + 4 : 8 * j + 5, :
    ]


def sigmoid(v):
    return 0.5 * jnp.tanh(0.5 * v) + 0.5


def rolled(block, k):
    return block[8:] if k == 3 else pltpu.roll(block, 3 - k, 0)[8:]


def columns(*rows8):
    total = 8 * len(rows8)
    full = jnp.concatenate(list(rows8) + [jnp.zeros((TILE - total, TILE), F32)], axis=0)
    return jnp.transpose(full)


def head_row(ref, r):
    row8 = ids((8, TILE), 0)
    out = jnp.zeros((8, TILE), F32)
    for h in range(8):
        out = jnp.where(row8 == h, ref[8 * r + h], out)
    return out


def conv(block, taps, bias):
    pre = bias + taps[0] * rolled(block, 0)
    for k in range(1, 4):
        pre = pre + taps[k] * rolled(block, k)
    return pre


def boundary_chunk(i, high):
    return high if i == 0 else jnp.logical_not(high)


def patched(ref, lanes, patch, patch_lanes, i, high):
    rows = slice(i * TILE, (i + 1) * TILE)
    if i % 2 == 1:
        return ref[rows, lanes]
    first = jnp.where(
        boundary_chunk(i, high), patch[:, patch_lanes], ref[i * TILE : i * TILE + 16, lanes]
    )
    return jnp.concatenate([first, ref[i * TILE + 16 : (i + 1) * TILE, lanes]], axis=0)


def map_rows(x, segment, start, block):
    for p in range(2):
        at = pl.ds(pl.multiple_of(8 + start + p * HALF // 2, 8), HALF // 2)
        x[segment, at, :] = block[
            TILE : TILE + HALF // 2, lanes_of(2 * segment + p)
        ].astype(F32)


def own_halo(x, high):
    first = x[0, 2 * TILE : 2 * TILE + 8, :]
    x[0, 0:8, :] = jnp.zeros_like(first)
    x[1, 0:8, :] = jnp.where(high, first, jnp.zeros_like(first))


def grads_kernel(
    u0,
    u3,
    u2,
    u1,
    own_taps,
    one_taps,
    two_taps,
    alog_ref,
    dtb_ref,
    mid_ref,
    dp,
    xo,
    act_out,
    pre_out,
    sgrad_s,
    step_e,
    toend_e,
    exp_e,
    t_s,
    step_r,
    ds_r,
    sig_r,
    mine_ref,
    halo_ref,
    dt_src,
):
    quad, r, f = place()
    high = quad == 1
    lane8 = ids((8, TILE), 1)
    group = 2 * f + lax.div(r, 2)
    at = at_tile(lax.rem(group, 4) * TILE)
    for j in range(2):
        mine_ref[8 * j : 8 * j + 8, :] = jnp.where(
            lax.rem(f, 2) == j,
            jnp.where(keeps_own(), own_taps[:, at], one_taps[:, at]),
            two_taps[:, at],
        )
    edge = jnp.zeros((8, 5 * TILE), F32)
    for k, u in enumerate((u0, u1, u2, u3)):
        s = lax.bitwise_xor(r, k)
        for e, start in ((0, HALF * s), (1, HALF * (3 - s))):
            map_rows(xo, e, start, u)
            dp[pl.ds(pl.multiple_of(2 * TILE * e + start, HALF), HALF), :] = u[
                e * HALF : (e + 1) * HALF, :
            ]
        packed = u[TILE + HALF // 2 : TILE + HALF // 2 + 16, :].astype(F32)
        dt_src[s] = packed[0:8, 0:TILE] + packed[8:16, 0:TILE] + packed[0:8, TILE : 2 * TILE]
        last = jnp.concatenate(
            [packed[0:8, 2 * TILE : 4 * TILE], packed[8:16, TILE : 4 * TILE]], axis=1
        )
        edge = edge + jnp.where(s == jnp.where(high, 0, 3), last, 0.0)
    last = slice(2 * TILE, 2 * TILE + 8)
    edge = jnp.concatenate([edge, jnp.where(high, xo[1, last, :], xo[0, last, :])], axis=1)
    own_halo(xo, high)

    rate8 = -jnp.exp(head_row(alog_ref, r))
    bias8 = head_row(dtb_ref, r)
    for i in range(4):
        if i < 2:
            a, b = dt_src[2 * i], pltpu.roll(dt_src[2 * i + 1], HALF, 1)
        else:
            a, b = pltpu.roll(dt_src[7 - 2 * i], HALF, 1), dt_src[6 - 2 * i]
        logits = jnp.where(lane8 < HALF, a, b) + bias8
        small = jnp.exp(-jnp.abs(logits))
        step = jnp.maximum(logits, 0.0) + jnp.log1p(small)
        at8 = slice(8 * i, 8 * i + 8)
        step_r[at8, :] = step
        sig_r[at8, :] = jnp.where(logits >= 0, 1.0, small) / (1.0 + small)
        ds_r[at8, :] = step * rate8
    upto = (ids((TILE, TILE), 0) <= ids((TILE, TILE), 1)).astype(F32)
    ds_r[...] = mm_f32(ds_r[...], upto)

    row48 = jnp.bitwise_and(ids((48, 8 * TILE), 0), 15)
    expand = (row48 == ids((48, 8 * TILE), 1) // HALF).astype(BF)
    ends = []
    for i in range(4):
        rows = slice(i * TILE, (i + 1) * TILE)
        base = (i % 2) * TILE
        taps, bias = map_tap_rows(1, mine_ref)
        pre = conv(xo[i // 2, base : base + TILE + 8, :], taps, bias)
        act_out[rows, :] = (pre * sigmoid(pre)).astype(BF)
        pre_out[rows, :] = pre
        parts = split3(
            jnp.concatenate([step_r[8 * i : 8 * i + 8, :], ds_r[8 * i : 8 * i + 8, :]], axis=0)
        )
        spread = mm(jnp.concatenate(parts, axis=0), expand, TN)
        end, masked = [], []
        for j in range(4):
            lanes = lanes_of(j)
            step = spread[:, lanes]
            ds = spread[:, lanes_of(4 + j)]
            last = ds[TILE - 1 : TILE, :]
            grow = jnp.exp(ds)
            step_e[rows, lanes] = step
            toend_e[rows, lanes] = jnp.exp(last - ds)
            exp_e[rows, lanes] = grow
            end.append(jnp.exp(last))
            grown = (dp[rows, lanes].astype(F32) * grow).astype(BF)
            sgrad_s[rows, lanes] = grown
            if i % 2 == 0:
                unknown = jnp.logical_and(boundary_chunk(i, high), ids((16, TILE), 0) < 3)
                first = jnp.where(unknown, 0.0, grown[0:16].astype(F32)).astype(BF)
                grown = jnp.concatenate([first, grown[16:]], axis=0)
            masked.append(grown)
        ends.append(jnp.concatenate(end, axis=1))
        t_s[i] = mm(act_out[rows, :], jnp.concatenate(masked, axis=1), TN)
    g_a = t_s[0] + ends[0] * t_s[1]
    g_b = t_s[2] + ends[2] * t_s[3]
    mid_ref[...] = jnp.where(high, g_a + ends[0] * ends[1] * g_b, g_b).astype(BF)
    across = [part.astype(F32) for part in split3(ends[0] * ends[1] * ends[2] * ends[3])]
    raw = jnp.where(high, xo[0, 8:16, :], xo[1, 8:16, :])
    grown = jnp.where(high, sgrad_s[0:16, :], sgrad_s[2 * TILE : 2 * TILE + 16, :]).astype(F32)
    pieces = []
    for k in range(3):
        pieces.append(
            jnp.concatenate([across[k], jnp.zeros((1, TILE), F32), raw[k : k + 1]], axis=1)
        )
    for k in range(3):
        pieces.append(jnp.concatenate([grown[k : k + 1], jnp.zeros((1, 2 * TILE), F32)], axis=1))
    pieces += [jnp.zeros((2, 6 * TILE), F32), edge]
    halo_ref[...] = jnp.concatenate(pieces, axis=0).astype(BF)


def first_kernel(
    v0, v1, v3, v2, step_e, toend_e, taps_ref, bias_ref, mine_ref, xs, acts, pres, scaled_s, weighted_s, xi, act_in, pre_in
):
    quad, r, f = place()
    high = quad == 1
    for k, v in enumerate((v0, v1, v2, v3)):
        s = lax.bitwise_xor(r, k)
        for e, start in ((0, HALF * s), (1, HALF * (3 - s))):
            xs[e, pl.ds(pl.multiple_of(8 + start, 8), HALF), :] = v[
                e * HALF : (e + 1) * HALF, :
            ].astype(F32)
            map_rows(xi, e, start, v)
    own_halo(xs, high)
    own_halo(xi, high)
    for i in range(4):
        rows = slice(i * TILE, (i + 1) * TILE)
        base = (i % 2) * TILE
        taps, bias = map_tap_rows(0, mine_ref)
        pre = conv(xi[i // 2, base : base + TILE + 8, :], taps, bias)
        act_in[rows, :] = (pre * sigmoid(pre)).astype(BF)
        pre_in[rows, :] = pre
        for j in range(4):
            lanes = lanes_of(j)
            taps, bias = sig_tap_rows(j, taps_ref, bias_ref)
            pre = conv(xs[i // 2, base : base + TILE + 8, lanes], taps, bias)
            value = (pre * sigmoid(pre)).astype(BF)
            acts[rows, lanes] = value
            pres[rows, lanes] = pre
            scaled = (value.astype(F32) * step_e[rows, lanes]).astype(BF)
            scaled_s[rows, lanes] = scaled
            weighted_s[rows, lanes] = (scaled.astype(F32) * toend_e[rows, lanes]).astype(BF)


def states_kernel(
    halo_ref,
    xs,
    xi,
    xo,
    act_in,
    weighted_s,
    sgrad_s,
    step_e,
    toend_e,
    exp_e,
    taps_ref,
    bias_ref,
    mine_ref,
    mid_ref,
    s_s,
    delta_ref,
    edge_ref,
    act_p,
    pre_p,
    scaled_p,
    weighted_p,
):
    quad, r, f = place()
    high = quad == 1
    edge = halo_ref[...].astype(F32)[8:16]
    edge_ref[...] = edge
    segment = jnp.where(high, 0, 1)
    rows16 = pl.ds(pl.multiple_of(2 * TILE * segment, 16), 16)
    for j in range(6):
        lanes = lanes_of(j)
        if j < 4:
            taps, bias = sig_tap_rows(j, taps_ref, bias_ref)
            first = xs[segment, 8:24, lanes]
        else:
            taps, bias = map_tap_rows(j - 4, mine_ref)
            first = xi[segment, 8:24, :] if j == 4 else xo[segment, 8:24, :]
        pre = conv(jnp.concatenate([edge[:, lanes], first], axis=0), taps, bias)
        value = (pre * sigmoid(pre)).astype(BF)
        act_p[:, lanes] = value
        pre_p[:, lanes] = pre
        if j < 4:
            scaled = (value.astype(F32) * step_e[rows16, lanes]).astype(BF)
            scaled_p[:, lanes] = scaled
            weighted_p[:, lanes] = (scaled.astype(F32) * toend_e[rows16, lanes]).astype(BF)
    every = slice(0, 4 * TILE)
    for i in range(4):
        s_s[i] = mm(
            patched(act_in, lanes_of(0), act_p, lanes_of(4), i, high),
            patched(weighted_s, every, weighted_p, every, i, high),
            TN,
        )
    ends = end_rows_of(exp_e)
    f_a = ends[1] * s_s[0] + s_s[1]
    f_b = ends[3] * s_s[2] + s_s[3]
    d_b = ends[2] * ends[3]
    mid_ref[...] = jnp.where(high, d_b * f_a + f_b, f_a).astype(BF)
    grown = sgrad_s[rows16, :].astype(F32)
    out_rows = act_p[:, lanes_of(5)].astype(F32)
    known = jnp.where(ids((16, TILE), 0) < 3, out_rows, 0.0).astype(BF)
    delta_ref[...] = mm(known, grown.astype(BF), TN)


def slope_of(pre):
    sig = sigmoid(pre)
    return sig * (1.0 + pre * (1.0 - sig))


def head_sums(*quantities):
    found = []
    head = ids((8, 4 * TILE), 1) // HALF
    pick = (ids((8, 4 * TILE), 0) == head).astype(BF)
    for tiles in quantities:
        x = jnp.concatenate(tiles, axis=1)
        hi = x.astype(BF)
        lo = (x - hi.astype(F32)).astype(BF)
        found.append(mm(pick, hi, NT) + mm(pick, lo, NT))
    return found


def pair_sums(x, two):
    head = ids((8, 2 * TILE), 1) // HALF + 4 * two
    pick = (ids((8, 2 * TILE), 0) == head).astype(BF)
    hi = x.astype(BF)
    lo = (x - hi.astype(F32)).astype(BF)
    return mm(pick, hi, NT) + mm(pick, lo, NT)


def skip_rows(skip_ref, r):
    lane_row = ids((1, TILE), 1)
    found = []
    for j in range(4):
        at = 8 * r + 2 * j
        found.append(jnp.where(lane_row < HALF, skip_ref[at], skip_ref[at + 1]))
    return found


def second_kernel(
    dp,
    acts,
    act_in,
    act_out,
    pres,
    pre_in,
    pre_out,
    scaled_s,
    step_e,
    toend_e,
    ds_r,
    act_p,
    pre_p,
    scaled_p,
    halo_ref,
    xo,
    mine_ref,
    skip_ref,
    base_ref,
    coef_ref,
    mslope_ref,
    gmap_ref,
    gsum_ref,
    stepsum_ref,
    skip_acc,
    left_ref,
):
    quad, r, f = place()
    high = quad == 1
    skip_row = skip_rows(skip_ref, r)
    skip_acc[...] = jnp.zeros_like(skip_acc)
    got = halo_ref[...].astype(F32)
    ends_at = slice(2 * TILE, 2 * TILE + 8)
    before = jnp.where(high, xo[1, ends_at, :], xo[0, ends_at, :])
    taps, bias = map_tap_rows(1, mine_ref)
    pre = conv(jnp.concatenate([before, got[0:8, lanes_of(5)]], axis=0), taps, bias)
    three = ids((8, TILE), 0) < 3
    out_rows = jnp.where(three, pre * sigmoid(pre), 0.0)
    out_rows = jnp.concatenate([out_rows, jnp.zeros((8, TILE), F32)], axis=0).astype(BF)
    grown = pltpu.roll(got[:, 0 : 4 * TILE], 13, 0)
    grown = jnp.where(ids((16, 4 * TILE), 0) < 3, grown, 0.0).astype(BF)
    left_ref[...] = mm(out_rows, grown, TN)
    half_lane = ids((TILE, TILE), 1) < HALF
    row8 = ids((8, TILE), 0)
    col_q = ids((TILE, TILE), 1)
    seen = ids((TILE, TILE), 0) <= col_q
    for i in range(4):
        rows = slice(i * TILE, (i + 1) * TILE)
        in_map = patched(act_in, lanes_of(0), act_p, lanes_of(4), i, high)
        out_map = patched(act_out, lanes_of(0), act_p, lanes_of(5), i, high)
        score = mm(in_map, out_map, NT)
        ds8 = ds_r[8 * i : 8 * i + 8, :]
        cols = columns(ds8)
        grad_score = jnp.zeros((TILE, TILE), F32)
        gsum = jnp.zeros((8, TILE), F32)
        rcol = jnp.zeros((TILE, TILE), F32)
        products = []
        for j in range(4):
            sc = patched(scaled_s, lanes_of(j), scaled_p, lanes_of(j), i, high)
            dy = dp[rows, lanes_of(j)]
            diag = jnp.zeros((TILE, TILE), F32)
            for e in range(2):
                h = 2 * j + e
                part = half_lane if e == 0 else jnp.logical_not(half_lane)
                gm = mm(jnp.where(part, sc, jnp.zeros_like(sc)), dy, NT)
                spread = ds8[h : h + 1, :] - cols[:, h : h + 1]
                decay = jnp.exp(jnp.where(seen, spread, -1e30))
                gd = gm * decay
                grad_score = grad_score + gd
                both = gd * score
                rcol = jnp.where(col_q == h, jnp.sum(both, axis=1, keepdims=True), rcol)
                gsum = gsum + jnp.where(row8 == h, jnp.sum(both, axis=0, keepdims=True), 0.0)
                mix = (score * decay).astype(BF)
                diag = diag + mm(mix, jnp.where(part, dy, jnp.zeros_like(dy)))
            lanes = lanes_of(j)
            sigf = patched(acts, lanes, act_p, lanes, i, high).astype(F32)
            dyf = dy.astype(F32)
            step = step_e[rows, lanes]
            slope = slope_of(patched(pres, lanes, pre_p, lanes, i, high))
            base_ref[rows, lanes] = (skip_row[j] * dyf + diag * step) * slope
            coef_ref[rows, lanes] = toend_e[rows, lanes] * step * slope
            products.append(diag * sigf)
            skip_acc[:, lanes] += eights(dyf * sigf)
        stepsum_ref[8 * i : 8 * i + 8, :] = head_sums(products)[0]
        for j, pre_ref in enumerate((pre_in, pre_out)):
            mslope_ref[rows, lanes_of(j)] = slope_of(
                patched(pre_ref, lanes_of(0), pre_p, lanes_of(4 + j), i, high)
            )
        gs = grad_score.astype(BF)
        gmap_ref[rows, lanes_of(0)] = mm(gs, out_map)
        gmap_ref[rows, lanes_of(1)] = mm(gs, in_map, TN)
        gsum_ref[8 * i : 8 * i + 8, :] = gsum - jnp.transpose(rcol)[0:8, :]


def eights(x):
    return jnp.sum(x.reshape(x.shape[0] // 8, 8, x.shape[1]), axis=0)


def end_rows_of(exp_e):
    return [exp_e[(i + 1) * TILE - 8 : (i + 1) * TILE, :][7:8, :] for i in range(4)]


def taps_back(gp, i, lanes, taps):
    base = (i % 2) * TILE
    raw = taps[3] * gp[i // 2, base : base + TILE, lanes]
    for k in range(3):
        start = base + 3 - k
        raw = raw + taps[k] * gp[i // 2, start : start + TILE, lanes]
    return raw


def fill_pads(gp, high):
    first = gp[1, 0:8, :]
    gp[0, 2 * TILE : 2 * TILE + 8, :] = jnp.where(high, first, jnp.zeros_like(first))
    gp[1, 2 * TILE : 2 * TILE + 8, :] = jnp.zeros_like(first)


def spill_of(first, taps):
    grads = jnp.concatenate([jnp.zeros((8, TILE), F32), first], axis=0)
    spill = jnp.zeros((8, TILE), F32)
    for k in range(3):
        spill = spill + taps[k] * pltpu.roll(grads, 5 + k, 0)[8:]
    return spill


def tap_sums(here, x, edge_ref, i, lanes, edge_lanes, high, sums):
    base = (i % 2) * TILE
    if i % 2 == 1:
        windows = [x[i // 2, base + 5 + k : base + 5 + k + TILE, lanes] for k in range(4)]
    else:
        first = x[i // 2, 0:8, lanes] + jnp.where(
            boundary_chunk(i, high), edge_ref[:, edge_lanes], 0.0
        )
        block = jnp.concatenate([first, x[i // 2, 8 : TILE + 8, lanes]], axis=0)
        windows = [rolled(block, k) for k in range(4)]
    for k in range(4):
        sums[k] = sums[k] + eights(here * windows[k])
    sums[4] = sums[4] + eights(here)


def maps_kernel(
    midg_ref,
    midf_ref,
    halo_ref,
    left_ref,
    s_s,
    t_s,
    delta_ref,
    exp_e,
    mslope_ref,
    weighted_s,
    weighted_p,
    sgrad_s,
    gmap_ref,
    xi,
    xo,
    edge_ref,
    mine_ref,
    one_ref,
    two_ref,
    hlow_ref,
    clow_ref,
    endrow_ref,
    h_s,
    c_s,
    gm,
):
    quad, r, f = place()
    high = quad == 1
    even = lax.rem(f, 2) == 0
    ends = end_rows_of(exp_e)
    f_in = midf_ref[...].astype(F32)
    got = halo_ref[:, 0 : 4 * TILE].astype(F32)
    across = got[0:1] + got[1:2] + got[2:3]
    g_in = midg_ref[...].astype(F32) + left_ref[...]
    t2 = t_s[2] + jnp.where(high, 0.0, delta_ref[...])
    f_a = ends[1] * s_s[0] + s_s[1]
    h_s[0] = jnp.where(high, f_in, 0.0)
    h_s[1] = ends[0] * h_s[0] + s_s[0]
    h_s[2] = jnp.where(high, ends[1] * h_s[1] + s_s[1], across * f_a + f_in)
    h_s[3] = ends[2] * h_s[2] + s_s[2]
    g_b = t2 + ends[2] * t_s[3]
    c_s[3] = jnp.where(high, g_in, 0.0)
    c_s[2] = t_s[3] + ends[3] * c_s[3]
    c_s[1] = jnp.where(high, t2 + ends[2] * c_s[2], g_in + across * g_b)
    c_s[0] = t_s[1] + ends[1] * c_s[1]
    taps_of = [map_tap_rows(j, mine_ref)[0] for j in range(2)]
    sums = [[jnp.zeros((8, TILE), F32) for _ in range(5)] for _ in range(2)]
    end_rows = []
    every = slice(0, 4 * TILE)
    for i in range(4):
        rows = slice(i * TILE, (i + 1) * TILE)
        base = (i % 2) * TILE
        hlow_ref[i] = h_s[i].astype(BF)
        clow_ref[i] = c_s[i].astype(BF)
        end_rows.append(jnp.sum(h_s[i] * c_s[i], axis=0, keepdims=True) * ends[i])
        grads = (
            mm(patched(weighted_s, every, weighted_p, every, i, high), clow_ref[i], NT) + gmap_ref[rows, lanes_of(0)],
            mm(sgrad_s[rows, :], hlow_ref[i], NT) + gmap_ref[rows, lanes_of(1)],
        )
        for j in range(2):
            here = grads[j] * mslope_ref[rows, lanes_of(j)]
            gm[i // 2, base : base + TILE, lanes_of(j)] = here
            tap_sums(
                here, (xi, xo)[j], edge_ref, i, lanes_of(0), lanes_of(4 + j), high, sums[j]
            )
    fill_pads(gm, high)
    for i in range(4):
        rows = slice(i * TILE, (i + 1) * TILE)
        raws = [taps_back(gm, i, lanes_of(j), taps_of[j]) for j in range(2)]
        one_ref[rows, :] = jnp.where(even, raws[0], raws[1]).astype(BF)
        two_ref[rows, :] = jnp.where(even, raws[1], raws[0]).astype(BF)
    first = jnp.where(high, gm[0, 0:8, :], gm[1, 0:8, :])
    endrow_ref[...] = jnp.concatenate(end_rows + [jnp.zeros((4, 4 * TILE), F32)], axis=0)
    row8 = ids((8, TILE), 0)
    tails = []
    for j in range(2):
        five = jnp.zeros((8, TILE), F32)
        for t in range(5):
            five = jnp.where(row8 == t, jnp.sum(sums[j][t], axis=0, keepdims=True), five)
        hi, lo, _ = split3(five)
        zero8 = jnp.zeros((8, TILE), F32)
        tails.append(
            jnp.concatenate(
                [spill_of(first[:, lanes_of(j)], taps_of[j]), zero8, hi.astype(F32), lo.astype(F32)], axis=0
            )
        )
    one_ref[4 * TILE : 4 * TILE + 32, :] = jnp.where(even, tails[0], tails[1]).astype(BF)
    two_ref[4 * TILE : 4 * TILE + 32, :] = jnp.where(even, tails[1], tails[0]).astype(BF)


def third_kernel(
    hlow_ref,
    clow_ref,
    endrow_ref,
    xs,
    dp,
    acts,
    act_in,
    act_out,
    edge_ref,
    act_p,
    toend_e,
    exp_e,
    step_r,
    sig_r,
    base_ref,
    coef_ref,
    gsum_ref,
    stepsum_ref,
    skip_acc,
    taps_ref,
    alog_ref,
    gp,
    blk,
    spill_ref,
    params_ref,
):
    quad, r, f = place()
    high = quad == 1
    row8 = ids((8, TILE), 0)
    lane8 = ids((8, TILE), 1)
    rate8 = -jnp.exp(head_row(alog_ref, r))
    row_q = ids((TILE, TILE), 0)
    col_q = ids((TILE, TILE), 1)
    tail_sums = jnp.concatenate(
        [(row_q >= col_q).astype(F32), (row_q < col_q).astype(F32)], axis=0
    )
    sums = [[jnp.zeros((8, TILE), F32) for _ in range(5)] for _ in range(4)]
    alog_acc = jnp.zeros((8, TILE), F32)
    ddt_acc = jnp.zeros((8, TILE), F32)
    for i in range(4):
        rows = slice(i * TILE, (i + 1) * TILE)
        at8 = slice(8 * i, 8 * i + 8)
        base = (i % 2) * TILE
        off = mm(patched(act_out, lanes_of(0), act_p, lanes_of(5), i, high), hlow_ref[i])
        gw = mm(patched(act_in, lanes_of(0), act_p, lanes_of(4), i, high), clow_ref[i])
        end_row = endrow_ref[i : i + 1, :]
        gsum = gsum_ref[at8, :]
        end_sum = jnp.zeros((8, TILE), F32)
        offsum = jnp.zeros((8, TILE), F32)
        backsum = jnp.zeros((8, TILE), F32)
        for two in range(2):
            lanes2 = slice(2 * two * TILE, (2 * two + 2) * TILE)
            sigf = jnp.concatenate(
                [
                    patched(acts, lanes_of(j), act_p, lanes_of(j), i, high).astype(F32)
                    for j in (2 * two, 2 * two + 1)
                ],
                axis=1,
            )
            offsum = offsum + pair_sums(
                dp[rows, lanes2].astype(F32) * exp_e[rows, lanes2] * off[:, lanes2], two
            )
            backsum = backsum + pair_sums(gw[:, lanes2] * toend_e[rows, lanes2] * sigf, two)
            for j in (2 * two, 2 * two + 1):
                lanes = lanes_of(j)
                end_sum = end_sum + jnp.where(
                    row8 == 2 * j + lane8 // HALF, end_row[:, lanes], 0.0
                )
                here = base_ref[rows, lanes] + gw[:, lanes] * coef_ref[rows, lanes]
                gp[i // 2, base : base + TILE, lanes] = here
                tap_sums(here, xs, edge_ref, i, lanes, lanes, high, sums[j])
        gsum = gsum + offsum
        stepsum = stepsum_ref[at8, :] + backsum
        back = backsum * step_r[at8, :]
        grad_log = mm_f32(jnp.concatenate([gsum, back], axis=1), tail_sums) + jnp.sum(
            end_sum, axis=1, keepdims=True
        )
        ddt = (grad_log * rate8 + stepsum) * sig_r[at8, :]
        blk[2 * i] = ddt
        blk[2 * i + 1] = pltpu.roll(ddt, HALF, 1)
        ddt_acc = ddt_acc + ddt
        alog_acc = alog_acc + grad_log * step_r[at8, :]
    fill_pads(gp, high)
    rows = []
    for j in range(4):
        taps = [taps_ref[k : k + 1, at_tile((4 * r + j) * TILE)] for k in range(4)]
        first = jnp.where(high, gp[0, 0:8, lanes_of(j)], gp[1, 0:8, lanes_of(j)])
        spill_ref[:, lanes_of(j)] = spill_of(first, taps)
        for t in range(5):
            rows.append(jnp.sum(sums[j][t], axis=0, keepdims=True))
    alog = jnp.sum(alog_acc * rate8, axis=1, keepdims=True)
    ddtb = jnp.sum(ddt_acc, axis=1, keepdims=True)
    skips = jnp.zeros((8, TILE), F32)
    for j in range(4):
        total = jnp.sum(skip_acc[:, lanes_of(j)], axis=0, keepdims=True)
        skips = skips + jnp.where(row8 == 2 * j + lane8 // HALF, total, 0.0)
    skips = jnp.sum(skips, axis=1, keepdims=True)
    three = jnp.where(lane8 == 0, alog, jnp.where(lane8 == 1, ddtb, skips))
    flat = columns(jnp.where(lane8 < 3, three, 0.0))
    trio = flat[0:1] + pltpu.roll(flat[0:8], 32, 1)[1:2] + pltpu.roll(flat[0:8], 64, 1)[2:3]
    trio = pltpu.roll(jnp.broadcast_to(trio, (8, TILE)), 8 * r, 1)[0:1]
    params_ref[...] = jnp.concatenate(rows + [trio, jnp.zeros((3, TILE), F32)], axis=0)


def split_params(params):
    hi, lo, _ = split3(params)
    return jnp.concatenate([hi[0:16], hi[16:32], lo[0:16], lo[16:32]], axis=1)


def whole_params(value):
    value = value.astype(F32)
    return jnp.concatenate(
        [
            value[:, lanes_of(0)] + value[:, lanes_of(2)],
            value[:, lanes_of(1)] + value[:, lanes_of(3)],
        ],
        axis=0,
    )


def keeps_own():
    f = place()[2]
    return jnp.logical_or(f == 0, f == 3)


def cross_kernel(scale, params_ref, spill_ref, own_ref, one_ref, two_ref, cross_ref):
    tails = [ref[4 * TILE : 4 * TILE + 32, :].astype(F32) for ref in (own_ref, one_ref, two_ref)]
    tails = [jnp.where(keeps_own(), tails[0], tails[1]), tails[2]]
    fives = [tail[16:24] + tail[24:32] for tail in tails]
    params = jnp.concatenate(
        [
            params_ref[0:20],
            fives[0][0:5],
            fives[1][0:5],
            params_ref[20:21],
            jnp.zeros((1, TILE), F32),
        ],
        axis=0,
    )
    maps = jnp.concatenate([tails[0][0:8], tails[1][0:8], jnp.zeros((8, 2 * TILE), F32)], axis=1)
    cross_ref[0:16, :] = jnp.concatenate([spill_ref[...], maps], axis=0).astype(BF)
    cross_ref[16:32, :] = split_params(params * scale)


def send_kernel(gp, taps_ref, y0, y1, y2, y3, dx):
    quad, r, f = place()
    for j in range(4):
        lanes = lanes_of(j)
        taps = [taps_ref[k : k + 1, at_tile((4 * r + j) * TILE)] for k in range(4)]
        for i in range(4):
            dx[i * TILE : (i + 1) * TILE, lanes] = taps_back(gp, i, lanes, taps).astype(BF)
    for k, y in enumerate((y0, y1, y2, y3)):
        s = lax.bitwise_xor(r, k)
        for e, at in ((0, HALF * s), (1, 2 * TILE + HALF * (3 - s))):
            y[e * HALF : (e + 1) * HALF, :] = dx[pl.ds(pl.multiple_of(at, HALF), HALF), :]


def merge_kernel(own_ref, other_ref, kept_ref, one_ref, two_ref, blk, w0, w1, w2, w3):
    quad, r, f = place()
    lane8 = ids((8, TILE), 1)
    param_rows = split_params(
        whole_params(own_ref[16:32, :]) + whole_params(other_ref[16:32, :])
    )
    spill = other_ref[0:16, :].astype(F32)
    for k, w in enumerate((w0, w1, w2, w3)):
        s = lax.bitwise_xor(r, k)
        for e, at in ((0, HALF * s), (1, 2 * TILE + HALF * (3 - s))):
            rows = pl.ds(pl.multiple_of(at, HALF), HALF)
            w[0:HALF, lanes_of(e)] = jnp.where(keeps_own(), kept_ref[rows, :], one_ref[rows, :])
            w[0:HALF, lanes_of(2 + e)] = two_ref[rows, :]
        here = jnp.where(lane8 < HALF, blk[s], pltpu.roll(blk[7 - s], HALF, 1))
        hi, mid, _ = split3(here)
        w[HALF : HALF + 16, :] = jnp.concatenate(
            [
                jnp.concatenate([hi.astype(F32), spill[0:8, 0 : 2 * TILE], spill[8:16, 0:TILE]], axis=1),
                jnp.concatenate(
                    [
                        mid.astype(F32),
                        spill[0:8, 2 * TILE : 4 * TILE],
                        spill[8:16, TILE : 2 * TILE],
                    ],
                    axis=1,
                ),
            ],
            axis=0,
        ).astype(BF)
        w[HALF + 16 : HALF + 32, :] = param_rows


def last_kernel(
    y0, y3, y2, y1, w0, w3, w2, w1, dsig_ref, dmap_ref, ddt_ref, taps_ref, mtaps_ref, bias_ref, mbias_ref, *trio_refs
):
    quad, r, f = place()
    ys = (y0, y1, y2, y3)
    ws = (w0, w1, w2, w3)
    third = jnp.logical_and(quad == 0, r == 3)
    fourth = jnp.logical_and(quad == 1, r == 0)
    params = []
    trio = jnp.zeros((1, TILE), F32)
    for k, y in enumerate(ys):
        s = lax.bitwise_xor(r, k)
        cols = at_tile(s * 4 * TILE, 4 * TILE)
        dsig_ref[:, cols] = y[0:TILE, :].astype(F32)
        extra = ws[k][HALF : HALF + 16, :].astype(F32)
        spill = jnp.concatenate(
            [extra[0:8, TILE : 3 * TILE], extra[8:16, TILE : 3 * TILE]], axis=1
        )
        dsig_ref[HALF - 8 : HALF, cols] += jnp.where(third, spill, 0.0)
        dsig_ref[TILE - 8 : TILE, cols] += jnp.where(fourth, spill, 0.0)
        ddt_ref[pl.ds(pl.multiple_of(8 * s, 8), 8), :] = extra[0:8, 0:TILE] + extra[8:16, 0:TILE]
        param = whole_params(ws[k][HALF + 16 : HALF + 32, :])
        params.append(param)
        for j in range(4):
            lanes = at_tile((4 * s + j) * TILE)
            taps_ref[0:4, lanes] = param[5 * j : 5 * j + 4]
            bias_ref[0:1, lanes] = param[5 * j + 4 : 5 * j + 5]
        trio = trio + param[30:31]
    trio = jnp.broadcast_to(trio, (8, TILE))
    for t, ref in enumerate(trio_refs):
        moved = trio if t == 0 else pltpu.roll(trio, TILE - 32 * t, 1)
        ref[...] = moved[0:1, 0:32]
    own = lax.div(r, 2)
    swap = f >= 2
    for pair in range(2):
        group = own if pair == 0 else 1 - own
        a, b = 2 * pair, 2 * pair + 1
        for j in range(2):
            where = jnp.where(swap, 1 - j, j)
            lanes = at_tile((2 * where + group) * TILE)
            for e in range(2):
                dmap_ref[e * HALF : (e + 1) * HALF, lanes] = ws[a][
                    0:HALF, lanes_of(2 * j + e)
                ].astype(F32) + ws[b][0:HALF, lanes_of(2 * j + e)].astype(F32)
            spill = jnp.zeros((8, TILE), F32)
            for w in (ws[a], ws[b]):
                extra = w[HALF : HALF + 16, 3 * TILE : 4 * TILE].astype(F32)
                spill = spill + extra[8 * j : 8 * j + 8]
            dmap_ref[HALF - 8 : HALF, lanes] += jnp.where(third, spill, 0.0)
            dmap_ref[TILE - 8 : TILE, lanes] += jnp.where(fourth, spill, 0.0)
            five = params[a][20 + 5 * j : 25 + 5 * j] + params[b][20 + 5 * j : 25 + 5 * j]
            mtaps_ref[0:4, lanes] = five[0:4]
            mbias_ref[0:1, lanes] = five[4:5]


ROUTE_ONE = [(2, 1), (1, 2)]
ROUTE_TWO = [(0, 2), (2, 3), (1, 0), (3, 1)]


def back(route):
    return [(target, source) for source, target in route]


def shards_quad(
    sig_raw,
    map_raw,
    step_size_logits,
    d_out,
    sig_taps,
    map_taps,
    sig_bias,
    map_bias,
    a_log,
    dt_bias,
    skip_gain,
):
    ctx = lax.axis_size("ctx")
    rows, sig_width = sig_raw.shape
    vmem = pl.BlockSpec(memory_space=pltpu.VMEM)
    smem = pl.BlockSpec(memory_space=pltpu.SMEM)
    hbm = pl.BlockSpec(memory_space=pltpu.HBM)

    def call(kernel, out_shape, in_specs, out_specs, scratch, mib, cost):
        return pl.pallas_call(
            kernel,
            out_shape=out_shape,
            in_specs=in_specs,
            out_specs=out_specs,
            scratch_shapes=scratch,
            compiler_params=pltpu.CompilerParams(vmem_limit_bytes=mib * 1024 * 1024),
            cost_estimate=pl.CostEstimate(flops=cost, bytes_accessed=cost // 100, transcendentals=0),
        )

    def shape(*dims, kind=F32):
        return jax.ShapeDtypeStruct(dims, kind)

    inside = [[(c, c ^ k) for c in range(ctx)] for k in range(4)]
    over = [(c, c ^ 4) for c in range(ctx)]
    total = 4 * TILE
    wide, narrow = 6 * TILE, 4 * TILE
    owned = map_taps.shape[1]
    sig_bias_row = sig_bias[None, :]
    *packed, map_params = call(
        pack_kernel,
        (shape(TILE + HALF // 2 + 16, narrow, kind=BF),) * 4 + (shape(8, owned),),
        [hbm, hbm, hbm, hbm, vmem, vmem],
        (vmem,) * 5,
        [
            pltpu.VMEM((32, TILE), F32),
            pltpu.VMEM((16, sig_width), BF),
            pltpu.VMEM((16, map_raw.shape[1] // 2), BF),
            pltpu.SemaphoreType.DMA((23,)),
        ],
        60,
        10**6,
    )(sig_raw, map_raw, step_size_logits.T, d_out, map_taps, map_bias[None, :])
    us = [packed[0]] + [lax.ppermute(packed[k], "ctx", inside[k]) for k in (1, 2, 3)]
    map_one = lax.ppermute(map_params, "fsdp", back(ROUTE_ONE))
    map_two = lax.ppermute(map_params, "fsdp", back(ROUTE_TWO))
    packed = call(
        pack_sig_kernel,
        (shape(TILE + HALF // 2, narrow, kind=BF),) * 4,
        [hbm, hbm],
        (vmem,) * 4,
        [pltpu.SemaphoreType.DMA((20,))],
        60,
        10**6,
    )(sig_raw, map_raw)
    us[0] = call(
        own_kernel, shape(TILE + HALF // 2 + 16, narrow, kind=BF), [vmem], vmem, [], 16, 10**6
    )(us[0])
    vs = [None] + [lax.ppermute(packed[k], "ctx", inside[k]) for k in (1, 2, 3)]
    midg, dp, xo, act_out, pre_out, sgrad, step_e, toend_e, exp_e, t_s, step_r, ds_r, sig_r, *small = call(
        grads_kernel,
        (
            shape(TILE, narrow, kind=BF),
            shape(total, narrow, kind=BF),
            shape(2, 2 * TILE + 8, TILE),
            shape(total, TILE, kind=BF),
            shape(total, TILE),
            shape(total, narrow, kind=BF),
            shape(total, narrow),
            shape(total, narrow),
            shape(total, narrow),
            shape(4, TILE, narrow),
            shape(32, TILE),
            shape(32, TILE),
            shape(32, TILE),
            shape(16, TILE),
            shape(16, wide, kind=BF),
        ),
        [vmem] * 7 + [smem] * 2,
        (vmem,) * 15,
        [pltpu.VMEM((4, 8, TILE), F32)],
        24,
        2 * 10**9,
    )(us[0], us[3], us[2], us[1], map_params, map_one, map_two, a_log, dt_bias)
    mine, halo = small
    halo = lax.ppermute(halo, "ctx", over)
    midg = lax.ppermute(midg, "ctx", over)
    vs[0] = call(
        own_later_kernel,
        shape(TILE + HALF // 2, narrow, kind=BF),
        [vmem] * 2,
        vmem,
        [],
        16,
        10**6,
    )(packed[0], mine)
    xs, acts, pres, scaled, weighted, xi, act_in, pre_in = call(
        first_kernel,
        (
            shape(2, 2 * TILE + 8, narrow),
            shape(total, narrow, kind=BF),
            shape(total, narrow),
            shape(total, narrow, kind=BF),
            shape(total, narrow, kind=BF),
            shape(2, 2 * TILE + 8, TILE),
            shape(total, TILE, kind=BF),
            shape(total, TILE),
        ),
        [vmem] * 9,
        (vmem,) * 8,
        [],
        24,
        2 * 10**9,
    )(vs[0], vs[1], vs[3], vs[2], step_e, toend_e, sig_taps, sig_bias_row, mine)
    midf, s_s, delta, edge, act_p, pre_p, scaled_p, weighted_p = call(
        states_kernel,
        (
            shape(TILE, narrow, kind=BF),
            shape(4, TILE, narrow),
            shape(TILE, narrow),
            shape(8, wide),
            shape(16, wide, kind=BF),
            shape(16, wide),
            shape(16, narrow, kind=BF),
            shape(16, narrow, kind=BF),
        ),
        [vmem] * 13,
        (vmem,) * 8,
        [],
        24,
        10**9,
    )(halo, xs, xi, xo, act_in, weighted, sgrad, step_e, toend_e, exp_e, sig_taps, sig_bias_row, mine)
    midf = lax.ppermute(midf, "ctx", over)
    base, coef, mslope, gmap, gsum, stepsum, skips, left = call(
        second_kernel,
        (
            shape(total, narrow),
            shape(total, narrow),
            shape(total, 2 * TILE),
            shape(total, 2 * TILE),
            shape(32, TILE),
            shape(32, TILE),
            shape(8, narrow),
            shape(TILE, narrow),
        ),
        [vmem] * 17 + [smem],
        (vmem,) * 8,
        [],
        24,
        5 * 10**9,
    )(
        dp,
        acts,
        act_in,
        act_out,
        pres,
        pre_in,
        pre_out,
        scaled,
        step_e,
        toend_e,
        ds_r,
        act_p,
        pre_p,
        scaled_p,
        halo,
        xo,
        mine,
        skip_gain,
    )
    one, two, hlow, clow, endrow = call(
        maps_kernel,
        (
            shape(total + 32, TILE, kind=BF),
            shape(total + 32, TILE, kind=BF),
            shape(4, TILE, narrow, kind=BF),
            shape(4, TILE, narrow, kind=BF),
            shape(8, narrow),
        ),
        [vmem] * 17,
        (vmem,) * 5,
        [
            pltpu.VMEM((4, TILE, narrow), F32),
            pltpu.VMEM((4, TILE, narrow), F32),
            pltpu.VMEM((2, 2 * TILE + 8, 2 * TILE), F32),
        ],
        24,
        2 * 10**9,
    )(
        midg,
        midf,
        halo,
        left,
        s_s,
        t_s,
        delta,
        exp_e,
        mslope,
        weighted,
        weighted_p,
        sgrad,
        gmap,
        xi,
        xo,
        edge,
        mine,
    )
    kept = one
    one = lax.ppermute(one, "fsdp", ROUTE_ONE)
    two = lax.ppermute(two, "fsdp", ROUTE_TWO)
    gp, blk, spill, params = call(
        third_kernel,
        (
            shape(2, 2 * TILE + 8, narrow),
            shape(8, 8, TILE),
            shape(8, narrow),
            shape(24, TILE),
        ),
        [vmem] * 20 + [smem],
        (vmem,) * 4,
        [],
        24,
        3 * 10**9,
    )(
        hlow,
        clow,
        endrow,
        xs,
        dp,
        acts,
        act_in,
        act_out,
        edge,
        act_p,
        toend_e,
        exp_e,
        step_r,
        sig_r,
        base,
        coef,
        gsum,
        stepsum,
        skips,
        sig_taps,
        a_log,
    )
    scale = 1.0 / math.sqrt(float(ctx * rows))
    cross = call(
        functools.partial(cross_kernel, scale),
        shape(32, narrow, kind=BF),
        [vmem] * 5,
        vmem,
        [],
        16,
        10**6,
    )(params, spill, kept, one, two)
    other = lax.ppermute(cross, "ctx", over)
    ys = call(
        send_kernel,
        (shape(TILE, narrow, kind=BF),) * 4,
        [vmem] * 2,
        (vmem,) * 4,
        [pltpu.VMEM((total, narrow), BF)],
        16,
        10**9,
    )(gp, sig_taps)
    ys = [ys[0]] + [lax.ppermute(ys[k], "ctx", inside[k]) for k in (1, 2, 3)]
    ws = call(
        merge_kernel,
        (shape(HALF + 32, narrow, kind=BF),) * 4,
        [vmem] * 6,
        (vmem,) * 4,
        [],
        16,
        10**6,
    )(cross, other, kept, one, two, blk)
    ws = [ws[0]] + [lax.ppermute(ws[k], "ctx", inside[k]) for k in (1, 2, 3)]
    d_sig, d_map, d_dt, taps, map_taps_grad, bias, map_bias_grad, *trio = call(
        last_kernel,
        (
            shape(rows, sig_width),
            shape(rows, owned),
            shape(32, TILE),
            shape(4, sig_width),
            shape(4, owned),
            shape(1, sig_width),
            shape(1, owned),
        )
        + (shape(1, 32),) * 3,
        [vmem] * 8,
        (vmem,) * 10,
        [],
        16,
        10**6,
    )(ys[0], ys[3], ys[2], ys[1], ws[0], ws[3], ws[2], ws[1])
    return (
        d_sig,
        d_map,
        d_dt.T,
        taps,
        map_taps_grad,
        bias[0],
        map_bias_grad[0],
        *(t[0] for t in trio),
    )


def shards(*args):
    sig_raw, map_raw, step_size_logits = args[:3]
    ctx = lax.axis_size("ctx")
    fsdp = lax.axis_size("fsdp")
    fits = (
        ctx == 8
        and fsdp == 4
        and sig_raw.shape == (TILE, 2048)
        and map_raw.shape == (TILE, 2 * GROUPS * STATE)
        and step_size_logits.shape[1] == 32
    )
    return shards_quad(*args) if fits else shards_chain(*args)


def solution(mesh):
    return jax.shard_map(
        shards,
        mesh=mesh,
        in_specs=(
            P("ctx", "fsdp"),
            P("ctx", None),
            P("ctx", "fsdp"),
            P("ctx", "fsdp"),
            P(None, "fsdp"),
            P(None, "fsdp"),
            P("fsdp"),
            P("fsdp"),
            P("fsdp"),
            P("fsdp"),
            P("fsdp"),
        ),
        out_specs=(
            P("ctx", "fsdp"),
            P("ctx", "fsdp"),
            P("ctx", "fsdp"),
            P(None, "fsdp"),
            P(None, "fsdp"),
            P("fsdp"),
            P("fsdp"),
            P("fsdp"),
            P("fsdp"),
            P("fsdp"),
        ),
        check_vma=False,
    )
```

```python
import functools
import math

import jax
import jax.numpy as jnp
from jax import lax
from jax.experimental import pallas as pl
from jax.experimental.pallas import tpu as pltpu
from jax.sharding import PartitionSpec as P

HEADS = 128
HDIM = 64
STATE = 128
GROUPS = 8


def prefix(part, axis, combine, identity, reverse):
    count = lax.axis_size(axis)
    place = lax.axis_index(axis)
    ahead = count - 1 - place if reverse else place
    gathered = jax.tree.map(lambda a: lax.all_gather(a, axis), part)
    state = jax.tree.map(lambda a, e: jnp.zeros_like(a) + jnp.asarray(e, a.dtype), part, identity)

    def one(lap, state):
        source = count - 1 - lap if reverse else lap
        return combine(
            state, jax.tree.map(lambda a: lax.dynamic_index_in_dim(a, source, 0, False), gathered)
        )

    return lax.fori_loop(0, ahead, one, state)


def broadcast(x, axis, root):
    mine = lax.axis_index(axis) == root
    return lax.psum(jnp.where(mine, x, jnp.zeros_like(x)), axis)


def extended(block, sides, width):
    for axis, dim in sides:
        count = lax.axis_size(axis)
        forward = [(i, i + 1) for i in range(count - 1)]
        backward = [(target, source) for source, target in forward]
        low = lax.ppermute(
            lax.slice_in_dim(block, block.shape[dim] - width, None, axis=dim), axis, forward
        )
        high = lax.ppermute(lax.slice_in_dim(block, 0, width, axis=dim), axis, backward)
        block = jnp.concatenate([low, block, high], axis=dim)
    return block


def ein(form, left, right):
    return jnp.einsum(form, left, right, preferred_element_type=jnp.float32)


def silu_slope(value):
    sig = jax.nn.sigmoid(value)
    return sig * (1.0 + value * (1.0 - sig))


def block_parts(activated, dt_rows, a_log, dt_bias, groups):
    length = activated.shape[0]
    heads = dt_rows.shape[1]
    inner = heads * HDIM
    shared = groups * STATE
    ratio = heads // groups
    signal = activated[:, :inner].reshape(length, heads, HDIM)
    input_map = activated[:, inner : inner + shared].reshape(length, groups, STATE)
    output_map = activated[:, inner + shared :].reshape(length, groups, STATE)
    input_heads = jnp.repeat(input_map, ratio, axis=1)
    output_heads = jnp.repeat(output_map, ratio, axis=1)
    step = jax.nn.softplus(dt_rows + dt_bias)
    rate = -jnp.exp(a_log)
    row_ids = lax.broadcasted_iota(jnp.int32, (length, length), 0)
    col_ids = lax.broadcasted_iota(jnp.int32, (length, length), 1)
    lower = (row_ids >= col_ids).astype(jnp.float32)
    decay_sum = jnp.dot(lower, step * rate, precision=lax.Precision.HIGHEST)
    to_end = jnp.exp(decay_sum[-1][None, :] - decay_sum)
    scaled = (signal.astype(jnp.float32) * step[:, :, None]).astype(jnp.bfloat16)
    weighted = (scaled.astype(jnp.float32) * to_end[:, :, None]).astype(jnp.bfloat16)
    local = ein("qhp,qhn->hpn", weighted, input_heads)
    return (
        signal,
        input_map,
        output_map,
        input_heads,
        output_heads,
        step,
        rate,
        lower,
        decay_sum,
        scaled,
        to_end,
        weighted,
        local,
    )


def entry_grad(parts, d_rows):
    decay_sum = parts[8]
    output_heads = parts[4]
    scaled_grad = (d_rows.astype(jnp.float32) * jnp.exp(decay_sum)[:, :, None]).astype(jnp.bfloat16)
    return (scaled_grad, ein("thp,thn->hpn", scaled_grad, output_heads))


def block_grads(parts, d_rows, scaled_grad, h_in, carried, skip_gain, dt_rows, dt_bias):
    (
        signal,
        input_map,
        output_map,
        input_heads,
        output_heads,
        step,
        rate,
        lower,
        decay_sum,
        scaled,
        to_end,
        weighted,
        local,
    ) = parts
    length = d_rows.shape[0]
    heads = d_rows.shape[1]
    groups = input_map.shape[1]
    width_state = input_map.shape[2]
    ratio = heads // groups
    grad_f = d_rows.astype(jnp.float32)
    signal_f = signal.astype(jnp.float32)
    grad_skip = jnp.sum(grad_f * signal_f, axis=(0, 2))
    h_low = h_in.astype(jnp.bfloat16)
    carried_low = carried.astype(jnp.bfloat16)
    offset = jnp.exp(decay_sum)[:, :, None] * ein("thn,hpn->thp", output_heads, h_low)
    grad_sum = jnp.sum(grad_f * offset, axis=2)
    out_heads_grad = ein("thp,hpn->thn", scaled_grad, h_low)
    grad_weighted = ein("shn,hpn->shp", input_heads, carried_low)
    in_heads_grad = ein("shp,hpn->shn", weighted, carried_low)
    back = jnp.sum(grad_weighted * scaled.astype(jnp.float32), axis=2) * to_end
    end_term = jnp.exp(decay_sum[-1]) * jnp.sum(h_in * carried, axis=(1, 2))
    last_row = (lax.broadcasted_iota(jnp.int32, (length, 1), 0) == length - 1).astype(jnp.float32)
    grad_sum = grad_sum - back + last_row * (jnp.sum(back, axis=0) + end_term)[None, :]
    spread = decay_sum.T[:, :, None] - decay_sum.T[:, None, :]
    decay = jnp.where(lower[None] > 0, jnp.exp(jnp.minimum(spread, 0.0)), 0.0)
    score = ein("tgn,sgn->gts", output_map, input_map)
    mix = jnp.repeat(score, ratio, axis=0) * decay
    grad_mix = ein("thp,shp->hts", d_rows, scaled)
    grad_scaled = grad_weighted * to_end[:, :, None] + ein(
        "hts,thp->shp", mix.astype(jnp.bfloat16), d_rows
    )
    product = grad_mix * mix
    grad_sum = grad_sum + (jnp.sum(product, axis=2) - jnp.sum(product, axis=1)).T
    grad_score = jnp.sum((grad_mix * decay).reshape(groups, ratio, length, length), axis=1).astype(
        jnp.bfloat16
    )
    grad_outmap = ein("gts,sgn->tgn", grad_score, input_map) + jnp.sum(
        out_heads_grad.reshape(length, groups, ratio, width_state), axis=2
    )
    grad_in = ein("gts,tgn->sgn", grad_score, output_map) + jnp.sum(
        in_heads_grad.reshape(length, groups, ratio, width_state), axis=2
    )
    grad_log = jnp.dot(lower.T, grad_sum, precision=lax.Precision.HIGHEST)
    descent_increment = grad_log * rate + jnp.sum(grad_scaled * signal_f, axis=2)
    grad_signal = skip_gain[None, :, None] * grad_f + grad_scaled * step[:, :, None]
    grad_dt = descent_increment * jax.nn.sigmoid(dt_rows + dt_bias)
    decay_log_gradient = jnp.sum(grad_log * step, axis=0) * rate
    grad_act = jnp.concatenate(
        [
            grad_signal.reshape(length, heads * HDIM),
            grad_in.reshape(length, groups * width_state),
            grad_outmap.reshape(length, groups * width_state),
        ],
        axis=1,
    )
    return (grad_act, grad_dt, decay_log_gradient, jnp.sum(grad_dt, axis=0), grad_skip)


def link(earlier, later):
    return (earlier[0] + later[0], jnp.exp(later[0])[:, None, None] * earlier[1] + later[1])


def link_blocks(lower_pair, upper_pair):
    zero_rate = jnp.zeros_like(lower_pair[0])
    zero_state = jnp.zeros_like(lower_pair[1])
    below = prefix(lower_pair, "ctx", link, (zero_rate, zero_state), False)
    beyond = prefix(upper_pair, "ctx", link, (zero_rate, zero_state), True)
    total = jax.tree.map(
        lambda part: broadcast(part, "ctx", lax.axis_size("ctx") - 1), link(below, lower_pair)
    )
    return jnp.stack([below[1], link(total, beyond)[1]])


def conv_back(grad_pre, wide_grad, kernel_taps, padded, at_end, length):
    rim = kernel_taps.shape[0] - 1
    after = jnp.stack(
        [jnp.where(at_end, grad_pre[1, :rim], wide_grad[3 * rim : 4 * rim]), wide_grad[0:rim]]
    )
    padded_next = jnp.concatenate([grad_pre, after], axis=1)
    grad_raw = jnp.zeros(grad_pre.shape, jnp.float32)
    for tap in range(rim + 1):
        grad_raw = (
            grad_raw
            + kernel_taps[tap][None, None, :] * padded_next[:, rim - tap : rim - tap + length]
        )
    tap_grads = jnp.stack(
        [jnp.sum(grad_pre * padded[:, tap : tap + length], axis=(0, 1)) for tap in range(rim + 1)]
    )
    return (grad_raw, tap_grads, jnp.sum(grad_pre, axis=(0, 1)))


def first_rows(grad_pre, rim):
    return jnp.concatenate([grad_pre[0, :rim], grad_pre[1, :rim]], axis=0)


def shards_chain(
    sig_raw,
    map_raw,
    step_size_logits,
    d_out,
    sig_taps,
    map_taps,
    sig_bias,
    map_bias,
    a_log,
    dt_bias,
    skip_gain,
):
    all_map_taps, all_map_bias = (
        lax.all_gather(map_taps, "fsdp", axis=1, tiled=True),
        lax.all_gather(map_bias, "fsdp", axis=0, tiled=True),
    )
    kernel_taps = jnp.concatenate([sig_taps, all_map_taps], axis=1)
    kernel_bias = jnp.concatenate([sig_bias, all_map_bias], axis=0)
    kernel = kernel_taps.shape[0]
    rim = kernel - 1
    length = sig_raw.shape[0] // 2
    sig_width = sig_raw.shape[1]
    map_width = map_raw.shape[1]
    width = sig_width + map_width
    heads_here = step_size_logits.shape[1]
    ratio = HEADS // GROUPS
    group_count = max(1, heads_here // ratio)
    first_group = lax.axis_index("fsdp") * heads_here // ratio
    fsdp_count = lax.axis_size("fsdp")
    owned = map_width // fsdp_count
    map_start = lax.axis_index("fsdp") * owned
    raw_rows = jnp.concatenate([sig_raw, map_raw], axis=1).reshape(2, length, width)
    tails = jnp.concatenate([raw_rows[1, length - rim :], raw_rows[0, length - rim :]], axis=0)
    wide = extended(tails, (("ctx", 0),), rim)
    at_end = lax.axis_index("ctx") == lax.axis_size("ctx") - 1
    before = jnp.stack(
        [wide[0:rim], jnp.where(at_end, raw_rows[0, length - rim :], wide[3 * rim : 4 * rim])]
    )
    padded = jnp.concatenate([before, raw_rows], axis=1).astype(jnp.float32)
    preact = kernel_bias[None, None, :] + jnp.zeros((2, length, width), jnp.float32)
    for tap in range(kernel):
        preact = preact + kernel_taps[tap][None, None, :] * padded[:, tap : tap + length]
    activated = jax.nn.silu(preact).astype(jnp.bfloat16)
    maps_all = activated[:, :, sig_width:].reshape(2, length, 2, GROUPS, STATE)
    maps_mine = lax.dynamic_slice_in_dim(maps_all, first_group, group_count, 3)
    local_act = jnp.concatenate(
        [activated[:, :, :sig_width], maps_mine.reshape(2, length, 2 * group_count * STATE)], axis=2
    )
    dt_rows = step_size_logits.reshape(2, length, heads_here)
    grad_rows = d_out.reshape(2, length, heads_here, HDIM)

    def parts_of(act_block, dt_block):
        return block_parts(act_block, dt_block, a_log, dt_bias, group_count)

    parts = jax.vmap(parts_of)(local_act, dt_rows)
    scaled_grad, state_grad = jax.vmap(entry_grad)(parts, grad_rows)
    ends = parts[8][:, -1]
    h_ins = link_blocks((ends[0], parts[12][0]), (ends[1], parts[12][1]))
    carried_pair = link_blocks((ends[1], state_grad[1]), (ends[0], state_grad[0]))
    carried = jnp.stack([carried_pair[1], carried_pair[0]])
    grad_act, grad_dt, decay_log_gradient, grad_dtb, grad_skip = jax.vmap(
        block_grads, in_axes=(0, 0, 0, 0, 0, None, 0, None)
    )(parts, grad_rows, scaled_grad, h_ins, carried, skip_gain, dt_rows, dt_bias)
    slope = silu_slope(preact)
    grad_pre_sig = grad_act[:, :, :sig_width] * slope[:, :, :sig_width]
    grad_mine = grad_act[:, :, sig_width:].reshape(2, length, 2, group_count, STATE)
    zero_index = jnp.zeros((), jnp.int32)
    placed = lax.dynamic_update_slice(
        jnp.zeros((2, length, 2, GROUPS, STATE), jnp.float32),
        grad_mine,
        (zero_index, zero_index, zero_index, first_group, zero_index),
    )
    map_term = placed.reshape(2, length, map_width)
    map_owned = lax.psum_scatter(map_term, "fsdp", scatter_dimension=2, tiled=True)
    map_slope = lax.dynamic_slice_in_dim(slope[:, :, sig_width:], map_start, owned, 2)
    grad_pre = jnp.concatenate([grad_pre_sig, map_owned * map_slope], axis=2)
    own_taps = jnp.concatenate([sig_taps, map_taps], axis=1)
    own_padded = jnp.concatenate(
        [
            padded[:, :, :sig_width],
            lax.dynamic_slice_in_dim(padded[:, :, sig_width:], map_start, owned, 2),
        ],
        axis=2,
    )
    wide_grad = extended(first_rows(grad_pre, rim), (("ctx", 0),), rim)
    grad_raw, tap_grads, bias_grads = conv_back(
        grad_pre, wide_grad, own_taps, own_padded, at_end, length
    )
    map_raw_grad = grad_raw[:, :, sig_width:]
    map_tap_grad = tap_grads[:, sig_width:]
    map_bias_grad = bias_grads[sig_width:]
    sig_raw_grad = grad_raw[:, :, :sig_width]
    sig_tap_grad = tap_grads[:, :sig_width]
    sig_bias_grad = bias_grads[:sig_width]
    reduced = lax.psum(
        (
            sig_tap_grad,
            map_tap_grad,
            sig_bias_grad,
            map_bias_grad,
            jnp.sum(decay_log_gradient, axis=0),
            jnp.sum(grad_dtb, axis=0),
            jnp.sum(grad_skip, axis=0),
        ),
        "ctx",
    )
    scale = 1.0 / math.sqrt(float(lax.axis_size("ctx") * 2 * length))
    final = jax.tree.map(lambda grad_part: grad_part * scale, reduced)
    return (
        sig_raw_grad.reshape(2 * length, sig_width),
        map_raw_grad.reshape(2 * length, owned),
        grad_dt.reshape(2 * length, heads_here),
        final[0],
        final[1],
        final[2],
        final[3],
        final[4],
        final[5],
        final[6],
    )


TILE = 128
HALF = 64
NT = (((1,), (1,)), ((), ()))
TN = (((0,), (0,)), ((), ()))
NN = (((1,), (0,)), ((), ()))
BF = jnp.bfloat16
F32 = jnp.float32


def mm(a, b, dims=NN):
    return lax.dot_general(a, b, dims, preferred_element_type=F32)


def mm_f32(a, b, dims=NN):
    return lax.dot_general(a, b, dims, precision=lax.Precision.HIGHEST, preferred_element_type=F32)


def split3(x):
    hi = x.astype(BF)
    rest = x - hi.astype(F32)
    mid = rest.astype(BF)
    return hi, mid, (rest - mid.astype(F32)).astype(BF)


def ids(shape, dim):
    return lax.broadcasted_iota(jnp.int32, shape, dim)


def lanes_of(j):
    return slice(j * TILE, (j + 1) * TILE)


def place():
    ctx_place = lax.axis_index("ctx")
    quad = lax.div(ctx_place, 4)
    return quad, lax.rem(ctx_place, 4), lax.axis_index("fsdp")


def at_tile(start, width=TILE):
    return pl.ds(pl.multiple_of(start, TILE), width)


def pack_kernel(sig_ref, map_ref, dt_ref, dy_ref, *rest):
    u_refs, (dt_in, sig_in, map_in, sems) = rest[:4], rest[4:]
    quad, r, f = place()
    copies = []
    dt_copy = pltpu.make_async_copy(dt_ref, dt_in, sems.at[20])
    dt_copy.start()
    ends = pl.ds(pl.multiple_of(jnp.where(quad == 0, HALF - 16, TILE - 16), 16), 16)
    sig_copy = pltpu.make_async_copy(sig_ref.at[ends, :], sig_in, sems.at[21])
    sig_copy.start()
    map_copy = pltpu.make_async_copy(
        map_ref.at[ends, 0 : map_ref.shape[1] // 2], map_in, sems.at[22]
    )
    map_copy.start()

    def send(source, target):
        copy = pltpu.make_async_copy(source, target, sems.at[len(copies)])
        copy.start()
        copies.append(copy)

    half = map_ref.shape[1] // 2
    for k in (1, 2, 3, 0):
        dest = lax.bitwise_xor(r, k)
        cols = at_tile(dest * 4 * TILE, 4 * TILE)
        send(dy_ref.at[:, cols], u_refs[k].at[0:TILE, :])
        group = (2 * f + lax.div(dest, 2)) * TILE
        for e in range(4):
            send(
                map_ref.at[e * HALF // 2 : (e + 1) * HALF // 2, at_tile(group + half)],
                u_refs[k].at[TILE : TILE + HALF // 2, lanes_of(e)],
            )
    dt_copy.wait()
    sig_copy.wait()
    map_copy.wait()
    for k in range(4):
        dest = lax.bitwise_xor(r, k)
        hi, mid, lo = split3(dt_in[pl.ds(pl.multiple_of(8 * dest, 8), 8), :])
        edge = sig_in[:, at_tile(dest * 4 * TILE, 4 * TILE)].astype(F32)[8:16]
        group = (2 * f + lax.div(dest, 2)) * TILE
        edge_in = map_in[:, at_tile(group)].astype(F32)[8:16]
        top = jnp.concatenate([hi.astype(F32), lo.astype(F32), edge[:, 0 : 2 * TILE]], axis=1)
        low = jnp.concatenate(
            [mid.astype(F32), edge[:, 2 * TILE : 4 * TILE], edge_in], axis=1
        )
        u_refs[k][TILE + HALF // 2 : TILE + HALF // 2 + 16, :] = jnp.concatenate([top, low], axis=0).astype(BF)
    for copy in copies:
        copy.wait()


def pack_sig_kernel(sig_ref, map_ref, *rest):
    v_refs, sems = rest[:4], rest[4]
    quad, r, f = place()
    copies = []

    def send(source, target):
        copy = pltpu.make_async_copy(source, target, sems.at[len(copies)])
        copy.start()
        copies.append(copy)

    for k in (1, 2, 3, 0):
        dest = lax.bitwise_xor(r, k)
        send(sig_ref.at[:, at_tile(dest * 4 * TILE, 4 * TILE)], v_refs[k].at[0:TILE, :])
        group = (2 * f + lax.div(dest, 2)) * TILE
        for e in range(4):
            send(
                map_ref.at[e * HALF // 2 : (e + 1) * HALF // 2, at_tile(group)],
                v_refs[k].at[TILE : TILE + HALF // 2, lanes_of(e)],
            )
    for copy in copies:
        copy.wait()


def own_kernel(ref, out):
    out[...] = ref[...]


def own_later_kernel(ref, after, out):
    out[...] = ref[...]


def sig_tap_rows(j, taps_ref, bias_ref):
    at = at_tile((4 * place()[1] + j) * TILE)
    return [taps_ref[k : k + 1, at] for k in range(4)], bias_ref[0:1, at]


def map_tap_rows(j, mine_ref):
    return [mine_ref[8 * j + k : 8 * j + k + 1, :] for k in range(4)], mine_ref[
        8 * j + 4 : 8 * j + 5, :
    ]


def sigmoid(v):
    return 0.5 * jnp.tanh(0.5 * v) + 0.5


def rolled(block, k):
    return block[8:] if k == 3 else pltpu.roll(block, 3 - k, 0)[8:]


def columns(*rows8):
    total = 8 * len(rows8)
    full = jnp.concatenate(list(rows8) + [jnp.zeros((TILE - total, TILE), F32)], axis=0)
    return jnp.transpose(full)


def head_row(ref, r):
    row8 = ids((8, TILE), 0)
    out = jnp.zeros((8, TILE), F32)
    for h in range(8):
        out = jnp.where(row8 == h, ref[8 * r + h], out)
    return out


def conv(block, taps, bias):
    pre = bias + taps[0] * rolled(block, 0)
    for k in range(1, 4):
        pre = pre + taps[k] * rolled(block, k)
    return pre


def boundary_chunk(i, high):
    return high if i == 0 else jnp.logical_not(high)


def patched(ref, lanes, patch, patch_lanes, i, high):
    rows = slice(i * TILE, (i + 1) * TILE)
    if i % 2 == 1:
        return ref[rows, lanes]
    first = jnp.where(
        boundary_chunk(i, high), patch[:, patch_lanes], ref[i * TILE : i * TILE + 16, lanes]
    )
    return jnp.concatenate([first, ref[i * TILE + 16 : (i + 1) * TILE, lanes]], axis=0)


def map_rows(x, segment, start, block):
    for p in range(2):
        at = pl.ds(pl.multiple_of(8 + start + p * HALF // 2, 8), HALF // 2)
        x[segment, at, :] = block[
            TILE : TILE + HALF // 2, lanes_of(2 * segment + p)
        ].astype(F32)


def own_halo(x, high):
    first = x[0, 2 * TILE : 2 * TILE + 8, :]
    x[0, 0:8, :] = jnp.zeros_like(first)
    x[1, 0:8, :] = jnp.where(high, first, jnp.zeros_like(first))


def grads_kernel(
    u0,
    u3,
    u2,
    u1,
    own_taps,
    one_taps,
    two_taps,
    alog_ref,
    dtb_ref,
    mid_ref,
    dp,
    xo,
    act_out,
    pre_out,
    sgrad_s,
    step_e,
    toend_e,
    exp_e,
    t_s,
    step_r,
    ds_r,
    sig_r,
    mine_ref,
    halo_ref,
    dt_src,
):
    quad, r, f = place()
    high = quad == 1
    lane8 = ids((8, TILE), 1)
    group = 2 * f + lax.div(r, 2)
    at = at_tile(lax.rem(group, 4) * TILE)
    for j in range(2):
        mine_ref[8 * j : 8 * j + 8, :] = jnp.where(
            lax.rem(f, 2) == j,
            jnp.where(keeps_own(), own_taps[:, at], one_taps[:, at]),
            two_taps[:, at],
        )
    edge = jnp.zeros((8, 5 * TILE), F32)
    for k, u in enumerate((u0, u1, u2, u3)):
        s = lax.bitwise_xor(r, k)
        for e, start in ((0, HALF * s), (1, HALF * (3 - s))):
            map_rows(xo, e, start, u)
            dp[pl.ds(pl.multiple_of(2 * TILE * e + start, HALF), HALF), :] = u[
                e * HALF : (e + 1) * HALF, :
            ]
        packed = u[TILE + HALF // 2 : TILE + HALF // 2 + 16, :].astype(F32)
        dt_src[s] = packed[0:8, 0:TILE] + packed[8:16, 0:TILE] + packed[0:8, TILE : 2 * TILE]
        last = jnp.concatenate(
            [packed[0:8, 2 * TILE : 4 * TILE], packed[8:16, TILE : 4 * TILE]], axis=1
        )
        edge = edge + jnp.where(s == jnp.where(high, 0, 3), last, 0.0)
    last = slice(2 * TILE, 2 * TILE + 8)
    edge = jnp.concatenate([edge, jnp.where(high, xo[1, last, :], xo[0, last, :])], axis=1)
    own_halo(xo, high)

    rate8 = -jnp.exp(head_row(alog_ref, r))
    bias8 = head_row(dtb_ref, r)
    for i in range(4):
        if i < 2:
            a, b = dt_src[2 * i], pltpu.roll(dt_src[2 * i + 1], HALF, 1)
        else:
            a, b = pltpu.roll(dt_src[7 - 2 * i], HALF, 1), dt_src[6 - 2 * i]
        logits = jnp.where(lane8 < HALF, a, b) + bias8
        small = jnp.exp(-jnp.abs(logits))
        step = jnp.maximum(logits, 0.0) + jnp.log1p(small)
        at8 = slice(8 * i, 8 * i + 8)
        step_r[at8, :] = step
        sig_r[at8, :] = jnp.where(logits >= 0, 1.0, small) / (1.0 + small)
        ds_r[at8, :] = step * rate8
    upto = (ids((TILE, TILE), 0) <= ids((TILE, TILE), 1)).astype(F32)
    ds_r[...] = mm_f32(ds_r[...], upto)

    row48 = jnp.bitwise_and(ids((48, 8 * TILE), 0), 15)
    expand = (row48 == ids((48, 8 * TILE), 1) // HALF).astype(BF)
    ends = []
    for i in range(4):
        rows = slice(i * TILE, (i + 1) * TILE)
        base = (i % 2) * TILE
        taps, bias = map_tap_rows(1, mine_ref)
        pre = conv(xo[i // 2, base : base + TILE + 8, :], taps, bias)
        act_out[rows, :] = (pre * sigmoid(pre)).astype(BF)
        pre_out[rows, :] = pre
        parts = split3(
            jnp.concatenate([step_r[8 * i : 8 * i + 8, :], ds_r[8 * i : 8 * i + 8, :]], axis=0)
        )
        spread = mm(jnp.concatenate(parts, axis=0), expand, TN)
        end, masked = [], []
        for j in range(4):
            lanes = lanes_of(j)
            step = spread[:, lanes]
            ds = spread[:, lanes_of(4 + j)]
            last = ds[TILE - 1 : TILE, :]
            grow = jnp.exp(ds)
            step_e[rows, lanes] = step
            toend_e[rows, lanes] = jnp.exp(last - ds)
            exp_e[rows, lanes] = grow
            end.append(jnp.exp(last))
            grown = (dp[rows, lanes].astype(F32) * grow).astype(BF)
            sgrad_s[rows, lanes] = grown
            if i % 2 == 0:
                unknown = jnp.logical_and(boundary_chunk(i, high), ids((16, TILE), 0) < 3)
                first = jnp.where(unknown, 0.0, grown[0:16].astype(F32)).astype(BF)
                grown = jnp.concatenate([first, grown[16:]], axis=0)
            masked.append(grown)
        ends.append(jnp.concatenate(end, axis=1))
        t_s[i] = mm(act_out[rows, :], jnp.concatenate(masked, axis=1), TN)
    g_a = t_s[0] + ends[0] * t_s[1]
    g_b = t_s[2] + ends[2] * t_s[3]
    mid_ref[...] = jnp.where(high, g_a + ends[0] * ends[1] * g_b, g_b).astype(BF)
    across = [part.astype(F32) for part in split3(ends[0] * ends[1] * ends[2] * ends[3])]
    raw = jnp.where(high, xo[0, 8:16, :], xo[1, 8:16, :])
    grown = jnp.where(high, sgrad_s[0:16, :], sgrad_s[2 * TILE : 2 * TILE + 16, :]).astype(F32)
    pieces = []
    for k in range(3):
        pieces.append(
            jnp.concatenate([across[k], jnp.zeros((1, TILE), F32), raw[k : k + 1]], axis=1)
        )
    for k in range(3):
        pieces.append(jnp.concatenate([grown[k : k + 1], jnp.zeros((1, 2 * TILE), F32)], axis=1))
    pieces += [jnp.zeros((2, 6 * TILE), F32), edge]
    halo_ref[...] = jnp.concatenate(pieces, axis=0).astype(BF)


def first_kernel(
    v0, v1, v3, v2, step_e, toend_e, taps_ref, bias_ref, mine_ref, xs, acts, pres, scaled_s, weighted_s, xi, act_in, pre_in
):
    quad, r, f = place()
    high = quad == 1
    for k, v in enumerate((v0, v1, v2, v3)):
        s = lax.bitwise_xor(r, k)
        for e, start in ((0, HALF * s), (1, HALF * (3 - s))):
            xs[e, pl.ds(pl.multiple_of(8 + start, 8), HALF), :] = v[
                e * HALF : (e + 1) * HALF, :
            ].astype(F32)
            map_rows(xi, e, start, v)
    own_halo(xs, high)
    own_halo(xi, high)
    for i in range(4):
        rows = slice(i * TILE, (i + 1) * TILE)
        base = (i % 2) * TILE
        taps, bias = map_tap_rows(0, mine_ref)
        pre = conv(xi[i // 2, base : base + TILE + 8, :], taps, bias)
        act_in[rows, :] = (pre * sigmoid(pre)).astype(BF)
        pre_in[rows, :] = pre
        for j in range(4):
            lanes = lanes_of(j)
            taps, bias = sig_tap_rows(j, taps_ref, bias_ref)
            pre = conv(xs[i // 2, base : base + TILE + 8, lanes], taps, bias)
            value = (pre * sigmoid(pre)).astype(BF)
            acts[rows, lanes] = value
            pres[rows, lanes] = pre
            scaled = (value.astype(F32) * step_e[rows, lanes]).astype(BF)
            scaled_s[rows, lanes] = scaled
            weighted_s[rows, lanes] = (scaled.astype(F32) * toend_e[rows, lanes]).astype(BF)


def states_kernel(
    halo_ref,
    xs,
    xi,
    xo,
    act_in,
    weighted_s,
    sgrad_s,
    step_e,
    toend_e,
    exp_e,
    taps_ref,
    bias_ref,
    mine_ref,
    mid_ref,
    s_s,
    delta_ref,
    edge_ref,
    act_p,
    pre_p,
    scaled_p,
    weighted_p,
):
    quad, r, f = place()
    high = quad == 1
    edge = halo_ref[...].astype(F32)[8:16]
    edge_ref[...] = edge
    segment = jnp.where(high, 0, 1)
    rows16 = pl.ds(pl.multiple_of(2 * TILE * segment, 16), 16)
    for j in range(6):
        lanes = lanes_of(j)
        if j < 4:
            taps, bias = sig_tap_rows(j, taps_ref, bias_ref)
            first = xs[segment, 8:24, lanes]
        else:
            taps, bias = map_tap_rows(j - 4, mine_ref)
            first = xi[segment, 8:24, :] if j == 4 else xo[segment, 8:24, :]
        pre = conv(jnp.concatenate([edge[:, lanes], first], axis=0), taps, bias)
        value = (pre * sigmoid(pre)).astype(BF)
        act_p[:, lanes] = value
        pre_p[:, lanes] = pre
        if j < 4:
            scaled = (value.astype(F32) * step_e[rows16, lanes]).astype(BF)
            scaled_p[:, lanes] = scaled
            weighted_p[:, lanes] = (scaled.astype(F32) * toend_e[rows16, lanes]).astype(BF)
    every = slice(0, 4 * TILE)
    for i in range(4):
        s_s[i] = mm(
            patched(act_in, lanes_of(0), act_p, lanes_of(4), i, high),
            patched(weighted_s, every, weighted_p, every, i, high),
            TN,
        )
    ends = end_rows_of(exp_e)
    f_a = ends[1] * s_s[0] + s_s[1]
    f_b = ends[3] * s_s[2] + s_s[3]
    d_b = ends[2] * ends[3]
    mid_ref[...] = jnp.where(high, d_b * f_a + f_b, f_a).astype(BF)
    grown = sgrad_s[rows16, :].astype(F32)
    out_rows = act_p[:, lanes_of(5)].astype(F32)
    known = jnp.where(ids((16, TILE), 0) < 3, out_rows, 0.0).astype(BF)
    delta_ref[...] = mm(known, grown.astype(BF), TN)


def slope_of(pre):
    sig = sigmoid(pre)
    return sig * (1.0 + pre * (1.0 - sig))


def head_sums(*quantities):
    found = []
    head = ids((8, 4 * TILE), 1) // HALF
    pick = (ids((8, 4 * TILE), 0) == head).astype(BF)
    for tiles in quantities:
        x = jnp.concatenate(tiles, axis=1)
        hi = x.astype(BF)
        lo = (x - hi.astype(F32)).astype(BF)
        found.append(mm(pick, hi, NT) + mm(pick, lo, NT))
    return found


def pair_sums(x, two):
    head = ids((8, 2 * TILE), 1) // HALF + 4 * two
    pick = (ids((8, 2 * TILE), 0) == head).astype(BF)
    hi = x.astype(BF)
    lo = (x - hi.astype(F32)).astype(BF)
    return mm(pick, hi, NT) + mm(pick, lo, NT)


def skip_rows(skip_ref, r):
    lane_row = ids((1, TILE), 1)
    found = []
    for j in range(4):
        at = 8 * r + 2 * j
        found.append(jnp.where(lane_row < HALF, skip_ref[at], skip_ref[at + 1]))
    return found


def second_kernel(
    dp,
    acts,
    act_in,
    act_out,
    pres,
    pre_in,
    pre_out,
    scaled_s,
    step_e,
    toend_e,
    ds_r,
    act_p,
    pre_p,
    scaled_p,
    halo_ref,
    xo,
    mine_ref,
    skip_ref,
    base_ref,
    coef_ref,
    mslope_ref,
    gmap_ref,
    gsum_ref,
    stepsum_ref,
    skip_acc,
    left_ref,
):
    quad, r, f = place()
    high = quad == 1
    skip_row = skip_rows(skip_ref, r)
    skip_acc[...] = jnp.zeros_like(skip_acc)
    got = halo_ref[...].astype(F32)
    ends_at = slice(2 * TILE, 2 * TILE + 8)
    before = jnp.where(high, xo[1, ends_at, :], xo[0, ends_at, :])
    taps, bias = map_tap_rows(1, mine_ref)
    pre = conv(jnp.concatenate([before, got[0:8, lanes_of(5)]], axis=0), taps, bias)
    three = ids((8, TILE), 0) < 3
    out_rows = jnp.where(three, pre * sigmoid(pre), 0.0)
    out_rows = jnp.concatenate([out_rows, jnp.zeros((8, TILE), F32)], axis=0).astype(BF)
    grown = pltpu.roll(got[:, 0 : 4 * TILE], 13, 0)
    grown = jnp.where(ids((16, 4 * TILE), 0) < 3, grown, 0.0).astype(BF)
    left_ref[...] = mm(out_rows, grown, TN)
    half_lane = ids((TILE, TILE), 1) < HALF
    row8 = ids((8, TILE), 0)
    col_q = ids((TILE, TILE), 1)
    seen = ids((TILE, TILE), 0) <= col_q
    for i in range(4):
        rows = slice(i * TILE, (i + 1) * TILE)
        in_map = patched(act_in, lanes_of(0), act_p, lanes_of(4), i, high)
        out_map = patched(act_out, lanes_of(0), act_p, lanes_of(5), i, high)
        score = mm(in_map, out_map, NT)
        ds8 = ds_r[8 * i : 8 * i + 8, :]
        cols = columns(ds8)
        grad_score = jnp.zeros((TILE, TILE), F32)
        gsum = jnp.zeros((8, TILE), F32)
        rcol = jnp.zeros((TILE, TILE), F32)
        products = []
        for j in range(4):
            sc = patched(scaled_s, lanes_of(j), scaled_p, lanes_of(j), i, high)
            dy = dp[rows, lanes_of(j)]
            diag = jnp.zeros((TILE, TILE), F32)
            for e in range(2):
                h = 2 * j + e
                part = half_lane if e == 0 else jnp.logical_not(half_lane)
                gm = mm(jnp.where(part, sc, jnp.zeros_like(sc)), dy, NT)
                spread = ds8[h : h + 1, :] - cols[:, h : h + 1]
                decay = jnp.exp(jnp.where(seen, spread, -1e30))
                gd = gm * decay
                grad_score = grad_score + gd
                both = gd * score
                rcol = jnp.where(col_q == h, jnp.sum(both, axis=1, keepdims=True), rcol)
                gsum = gsum + jnp.where(row8 == h, jnp.sum(both, axis=0, keepdims=True), 0.0)
                mix = (score * decay).astype(BF)
                diag = diag + mm(mix, jnp.where(part, dy, jnp.zeros_like(dy)))
            lanes = lanes_of(j)
            sigf = patched(acts, lanes, act_p, lanes, i, high).astype(F32)
            dyf = dy.astype(F32)
            step = step_e[rows, lanes]
            slope = slope_of(patched(pres, lanes, pre_p, lanes, i, high))
            base_ref[rows, lanes] = (skip_row[j] * dyf + diag * step) * slope
            coef_ref[rows, lanes] = toend_e[rows, lanes] * step * slope
            products.append(diag * sigf)
            skip_acc[:, lanes] += eights(dyf * sigf)
        stepsum_ref[8 * i : 8 * i + 8, :] = head_sums(products)[0]
        for j, pre_ref in enumerate((pre_in, pre_out)):
            mslope_ref[rows, lanes_of(j)] = slope_of(
                patched(pre_ref, lanes_of(0), pre_p, lanes_of(4 + j), i, high)
            )
        gs = grad_score.astype(BF)
        gmap_ref[rows, lanes_of(0)] = mm(gs, out_map)
        gmap_ref[rows, lanes_of(1)] = mm(gs, in_map, TN)
        gsum_ref[8 * i : 8 * i + 8, :] = gsum - jnp.transpose(rcol)[0:8, :]


def eights(x):
    return jnp.sum(x.reshape(x.shape[0] // 8, 8, x.shape[1]), axis=0)


def end_rows_of(exp_e):
    return [exp_e[(i + 1) * TILE - 8 : (i + 1) * TILE, :][7:8, :] for i in range(4)]


def taps_back(gp, i, lanes, taps):
    base = (i % 2) * TILE
    raw = taps[3] * gp[i // 2, base : base + TILE, lanes]
    for k in range(3):
        start = base + 3 - k
        raw = raw + taps[k] * gp[i // 2, start : start + TILE, lanes]
    return raw


def fill_pads(gp, high):
    first = gp[1, 0:8, :]
    gp[0, 2 * TILE : 2 * TILE + 8, :] = jnp.where(high, first, jnp.zeros_like(first))
    gp[1, 2 * TILE : 2 * TILE + 8, :] = jnp.zeros_like(first)


def spill_of(first, taps):
    grads = jnp.concatenate([jnp.zeros((8, TILE), F32), first], axis=0)
    spill = jnp.zeros((8, TILE), F32)
    for k in range(3):
        spill = spill + taps[k] * pltpu.roll(grads, 5 + k, 0)[8:]
    return spill


def tap_sums(here, x, edge_ref, i, lanes, edge_lanes, high, sums):
    base = (i % 2) * TILE
    if i % 2 == 1:
        windows = [x[i // 2, base + 5 + k : base + 5 + k + TILE, lanes] for k in range(4)]
    else:
        first = x[i // 2, 0:8, lanes] + jnp.where(
            boundary_chunk(i, high), edge_ref[:, edge_lanes], 0.0
        )
        block = jnp.concatenate([first, x[i // 2, 8 : TILE + 8, lanes]], axis=0)
        windows = [rolled(block, k) for k in range(4)]
    for k in range(4):
        sums[k] = sums[k] + eights(here * windows[k])
    sums[4] = sums[4] + eights(here)


def maps_kernel(
    midg_ref,
    midf_ref,
    halo_ref,
    left_ref,
    s_s,
    t_s,
    delta_ref,
    exp_e,
    mslope_ref,
    weighted_s,
    weighted_p,
    sgrad_s,
    gmap_ref,
    xi,
    xo,
    edge_ref,
    mine_ref,
    one_ref,
    two_ref,
    hlow_ref,
    clow_ref,
    endrow_ref,
    h_s,
    c_s,
    gm,
):
    quad, r, f = place()
    high = quad == 1
    even = lax.rem(f, 2) == 0
    ends = end_rows_of(exp_e)
    f_in = midf_ref[...].astype(F32)
    got = halo_ref[:, 0 : 4 * TILE].astype(F32)
    across = got[0:1] + got[1:2] + got[2:3]
    g_in = midg_ref[...].astype(F32) + left_ref[...]
    t2 = t_s[2] + jnp.where(high, 0.0, delta_ref[...])
    f_a = ends[1] * s_s[0] + s_s[1]
    h_s[0] = jnp.where(high, f_in, 0.0)
    h_s[1] = ends[0] * h_s[0] + s_s[0]
    h_s[2] = jnp.where(high, ends[1] * h_s[1] + s_s[1], across * f_a + f_in)
    h_s[3] = ends[2] * h_s[2] + s_s[2]
    g_b = t2 + ends[2] * t_s[3]
    c_s[3] = jnp.where(high, g_in, 0.0)
    c_s[2] = t_s[3] + ends[3] * c_s[3]
    c_s[1] = jnp.where(high, t2 + ends[2] * c_s[2], g_in + across * g_b)
    c_s[0] = t_s[1] + ends[1] * c_s[1]
    taps_of = [map_tap_rows(j, mine_ref)[0] for j in range(2)]
    sums = [[jnp.zeros((8, TILE), F32) for _ in range(5)] for _ in range(2)]
    end_rows = []
    every = slice(0, 4 * TILE)
    for i in range(4):
        rows = slice(i * TILE, (i + 1) * TILE)
        base = (i % 2) * TILE
        hlow_ref[i] = h_s[i].astype(BF)
        clow_ref[i] = c_s[i].astype(BF)
        end_rows.append(jnp.sum(h_s[i] * c_s[i], axis=0, keepdims=True) * ends[i])
        grads = (
            mm(patched(weighted_s, every, weighted_p, every, i, high), clow_ref[i], NT) + gmap_ref[rows, lanes_of(0)],
            mm(sgrad_s[rows, :], hlow_ref[i], NT) + gmap_ref[rows, lanes_of(1)],
        )
        for j in range(2):
            here = grads[j] * mslope_ref[rows, lanes_of(j)]
            gm[i // 2, base : base + TILE, lanes_of(j)] = here
            tap_sums(
                here, (xi, xo)[j], edge_ref, i, lanes_of(0), lanes_of(4 + j), high, sums[j]
            )
    fill_pads(gm, high)
    for i in range(4):
        rows = slice(i * TILE, (i + 1) * TILE)
        raws = [taps_back(gm, i, lanes_of(j), taps_of[j]) for j in range(2)]
        one_ref[rows, :] = jnp.where(even, raws[0], raws[1]).astype(BF)
        two_ref[rows, :] = jnp.where(even, raws[1], raws[0]).astype(BF)
    first = jnp.where(high, gm[0, 0:8, :], gm[1, 0:8, :])
    endrow_ref[...] = jnp.concatenate(end_rows + [jnp.zeros((4, 4 * TILE), F32)], axis=0)
    row8 = ids((8, TILE), 0)
    tails = []
    for j in range(2):
        five = jnp.zeros((8, TILE), F32)
        for t in range(5):
            five = jnp.where(row8 == t, jnp.sum(sums[j][t], axis=0, keepdims=True), five)
        hi, lo, _ = split3(five)
        zero8 = jnp.zeros((8, TILE), F32)
        tails.append(
            jnp.concatenate(
                [spill_of(first[:, lanes_of(j)], taps_of[j]), zero8, hi.astype(F32), lo.astype(F32)], axis=0
            )
        )
    one_ref[4 * TILE : 4 * TILE + 32, :] = jnp.where(even, tails[0], tails[1]).astype(BF)
    two_ref[4 * TILE : 4 * TILE + 32, :] = jnp.where(even, tails[1], tails[0]).astype(BF)


def third_kernel(
    hlow_ref,
    clow_ref,
    endrow_ref,
    xs,
    dp,
    acts,
    act_in,
    act_out,
    edge_ref,
    act_p,
    toend_e,
    exp_e,
    step_r,
    sig_r,
    base_ref,
    coef_ref,
    gsum_ref,
    stepsum_ref,
    skip_acc,
    taps_ref,
    alog_ref,
    gp,
    blk,
    spill_ref,
    params_ref,
):
    quad, r, f = place()
    high = quad == 1
    row8 = ids((8, TILE), 0)
    lane8 = ids((8, TILE), 1)
    rate8 = -jnp.exp(head_row(alog_ref, r))
    row_q = ids((TILE, TILE), 0)
    col_q = ids((TILE, TILE), 1)
    tail_sums = jnp.concatenate(
        [(row_q >= col_q).astype(F32), (row_q < col_q).astype(F32)], axis=0
    )
    sums = [[jnp.zeros((8, TILE), F32) for _ in range(5)] for _ in range(4)]
    alog_acc = jnp.zeros((8, TILE), F32)
    ddt_acc = jnp.zeros((8, TILE), F32)
    for i in range(4):
        rows = slice(i * TILE, (i + 1) * TILE)
        at8 = slice(8 * i, 8 * i + 8)
        base = (i % 2) * TILE
        off = mm(patched(act_out, lanes_of(0), act_p, lanes_of(5), i, high), hlow_ref[i])
        gw = mm(patched(act_in, lanes_of(0), act_p, lanes_of(4), i, high), clow_ref[i])
        end_row = endrow_ref[i : i + 1, :]
        gsum = gsum_ref[at8, :]
        end_sum = jnp.zeros((8, TILE), F32)
        offsum = jnp.zeros((8, TILE), F32)
        backsum = jnp.zeros((8, TILE), F32)
        for two in range(2):
            lanes2 = slice(2 * two * TILE, (2 * two + 2) * TILE)
            sigf = jnp.concatenate(
                [
                    patched(acts, lanes_of(j), act_p, lanes_of(j), i, high).astype(F32)
                    for j in (2 * two, 2 * two + 1)
                ],
                axis=1,
            )
            offsum = offsum + pair_sums(
                dp[rows, lanes2].astype(F32) * exp_e[rows, lanes2] * off[:, lanes2], two
            )
            backsum = backsum + pair_sums(gw[:, lanes2] * toend_e[rows, lanes2] * sigf, two)
            for j in (2 * two, 2 * two + 1):
                lanes = lanes_of(j)
                end_sum = end_sum + jnp.where(
                    row8 == 2 * j + lane8 // HALF, end_row[:, lanes], 0.0
                )
                here = base_ref[rows, lanes] + gw[:, lanes] * coef_ref[rows, lanes]
                gp[i // 2, base : base + TILE, lanes] = here
                tap_sums(here, xs, edge_ref, i, lanes, lanes, high, sums[j])
        gsum = gsum + offsum
        stepsum = stepsum_ref[at8, :] + backsum
        back = backsum * step_r[at8, :]
        grad_log = mm_f32(jnp.concatenate([gsum, back], axis=1), tail_sums) + jnp.sum(
            end_sum, axis=1, keepdims=True
        )
        ddt = (grad_log * rate8 + stepsum) * sig_r[at8, :]
        blk[2 * i] = ddt
        blk[2 * i + 1] = pltpu.roll(ddt, HALF, 1)
        ddt_acc = ddt_acc + ddt
        alog_acc = alog_acc + grad_log * step_r[at8, :]
    fill_pads(gp, high)
    rows = []
    for j in range(4):
        taps = [taps_ref[k : k + 1, at_tile((4 * r + j) * TILE)] for k in range(4)]
        first = jnp.where(high, gp[0, 0:8, lanes_of(j)], gp[1, 0:8, lanes_of(j)])
        spill_ref[:, lanes_of(j)] = spill_of(first, taps)
        for t in range(5):
            rows.append(jnp.sum(sums[j][t], axis=0, keepdims=True))
    alog = jnp.sum(alog_acc * rate8, axis=1, keepdims=True)
    ddtb = jnp.sum(ddt_acc, axis=1, keepdims=True)
    skips = jnp.zeros((8, TILE), F32)
    for j in range(4):
        total = jnp.sum(skip_acc[:, lanes_of(j)], axis=0, keepdims=True)
        skips = skips + jnp.where(row8 == 2 * j + lane8 // HALF, total, 0.0)
    skips = jnp.sum(skips, axis=1, keepdims=True)
    three = jnp.where(lane8 == 0, alog, jnp.where(lane8 == 1, ddtb, skips))
    flat = columns(jnp.where(lane8 < 3, three, 0.0))
    trio = flat[0:1] + pltpu.roll(flat[0:8], 32, 1)[1:2] + pltpu.roll(flat[0:8], 64, 1)[2:3]
    trio = pltpu.roll(jnp.broadcast_to(trio, (8, TILE)), 8 * r, 1)[0:1]
    params_ref[...] = jnp.concatenate(rows + [trio, jnp.zeros((3, TILE), F32)], axis=0)


def split_params(params):
    hi, lo, _ = split3(params)
    return jnp.concatenate([hi[0:16], hi[16:32], lo[0:16], lo[16:32]], axis=1)


def whole_params(value):
    value = value.astype(F32)
    return jnp.concatenate(
        [
            value[:, lanes_of(0)] + value[:, lanes_of(2)],
            value[:, lanes_of(1)] + value[:, lanes_of(3)],
        ],
        axis=0,
    )


def keeps_own():
    f = place()[2]
    return jnp.logical_or(f == 0, f == 3)


def cross_kernel(scale, params_ref, spill_ref, own_ref, one_ref, two_ref, cross_ref):
    tails = [ref[4 * TILE : 4 * TILE + 32, :].astype(F32) for ref in (own_ref, one_ref, two_ref)]
    tails = [jnp.where(keeps_own(), tails[0], tails[1]), tails[2]]
    fives = [tail[16:24] + tail[24:32] for tail in tails]
    params = jnp.concatenate(
        [
            params_ref[0:20],
            fives[0][0:5],
            fives[1][0:5],
            params_ref[20:21],
            jnp.zeros((1, TILE), F32),
        ],
        axis=0,
    )
    maps = jnp.concatenate([tails[0][0:8], tails[1][0:8], jnp.zeros((8, 2 * TILE), F32)], axis=1)
    cross_ref[0:16, :] = jnp.concatenate([spill_ref[...], maps], axis=0).astype(BF)
    cross_ref[16:32, :] = split_params(params * scale)


def send_kernel(gp, taps_ref, y0, y1, y2, y3, dx):
    quad, r, f = place()
    for j in range(4):
        lanes = lanes_of(j)
        taps = [taps_ref[k : k + 1, at_tile((4 * r + j) * TILE)] for k in range(4)]
        for i in range(4):
            dx[i * TILE : (i + 1) * TILE, lanes] = taps_back(gp, i, lanes, taps).astype(BF)
    for k, y in enumerate((y0, y1, y2, y3)):
        s = lax.bitwise_xor(r, k)
        for e, at in ((0, HALF * s), (1, 2 * TILE + HALF * (3 - s))):
            y[e * HALF : (e + 1) * HALF, :] = dx[pl.ds(pl.multiple_of(at, HALF), HALF), :]


def merge_kernel(own_ref, other_ref, kept_ref, one_ref, two_ref, blk, w0, w1, w2, w3):
    quad, r, f = place()
    lane8 = ids((8, TILE), 1)
    param_rows = split_params(
        whole_params(own_ref[16:32, :]) + whole_params(other_ref[16:32, :])
    )
    spill = other_ref[0:16, :].astype(F32)
    for k, w in enumerate((w0, w1, w2, w3)):
        s = lax.bitwise_xor(r, k)
        for e, at in ((0, HALF * s), (1, 2 * TILE + HALF * (3 - s))):
            rows = pl.ds(pl.multiple_of(at, HALF), HALF)
            w[0:HALF, lanes_of(e)] = jnp.where(keeps_own(), kept_ref[rows, :], one_ref[rows, :])
            w[0:HALF, lanes_of(2 + e)] = two_ref[rows, :]
        here = jnp.where(lane8 < HALF, blk[s], pltpu.roll(blk[7 - s], HALF, 1))
        hi, mid, _ = split3(here)
        w[HALF : HALF + 16, :] = jnp.concatenate(
            [
                jnp.concatenate([hi.astype(F32), spill[0:8, 0 : 2 * TILE], spill[8:16, 0:TILE]], axis=1),
                jnp.concatenate(
                    [
                        mid.astype(F32),
                        spill[0:8, 2 * TILE : 4 * TILE],
                        spill[8:16, TILE : 2 * TILE],
                    ],
                    axis=1,
                ),
            ],
            axis=0,
        ).astype(BF)
        w[HALF + 16 : HALF + 32, :] = param_rows


def last_kernel(
    y0, y3, y2, y1, w0, w3, w2, w1, dsig_ref, dmap_ref, ddt_ref, taps_ref, mtaps_ref, bias_ref, mbias_ref, *trio_refs
):
    quad, r, f = place()
    ys = (y0, y1, y2, y3)
    ws = (w0, w1, w2, w3)
    third = jnp.logical_and(quad == 0, r == 3)
    fourth = jnp.logical_and(quad == 1, r == 0)
    params = []
    trio = jnp.zeros((1, TILE), F32)
    for k, y in enumerate(ys):
        s = lax.bitwise_xor(r, k)
        cols = at_tile(s * 4 * TILE, 4 * TILE)
        dsig_ref[:, cols] = y[0:TILE, :].astype(F32)
        extra = ws[k][HALF : HALF + 16, :].astype(F32)
        spill = jnp.concatenate(
            [extra[0:8, TILE : 3 * TILE], extra[8:16, TILE : 3 * TILE]], axis=1
        )
        dsig_ref[HALF - 8 : HALF, cols] += jnp.where(third, spill, 0.0)
        dsig_ref[TILE - 8 : TILE, cols] += jnp.where(fourth, spill, 0.0)
        ddt_ref[pl.ds(pl.multiple_of(8 * s, 8), 8), :] = extra[0:8, 0:TILE] + extra[8:16, 0:TILE]
        param = whole_params(ws[k][HALF + 16 : HALF + 32, :])
        params.append(param)
        for j in range(4):
            lanes = at_tile((4 * s + j) * TILE)
            taps_ref[0:4, lanes] = param[5 * j : 5 * j + 4]
            bias_ref[0:1, lanes] = param[5 * j + 4 : 5 * j + 5]
        trio = trio + param[30:31]
    trio = jnp.broadcast_to(trio, (8, TILE))
    for t, ref in enumerate(trio_refs):
        moved = trio if t == 0 else pltpu.roll(trio, TILE - 32 * t, 1)
        ref[...] = moved[0:1, 0:32]
    own = lax.div(r, 2)
    swap = f >= 2
    for pair in range(2):
        group = own if pair == 0 else 1 - own
        a, b = 2 * pair, 2 * pair + 1
        for j in range(2):
            where = jnp.where(swap, 1 - j, j)
            lanes = at_tile((2 * where + group) * TILE)
            for e in range(2):
                dmap_ref[e * HALF : (e + 1) * HALF, lanes] = ws[a][
                    0:HALF, lanes_of(2 * j + e)
                ].astype(F32) + ws[b][0:HALF, lanes_of(2 * j + e)].astype(F32)
            spill = jnp.zeros((8, TILE), F32)
            for w in (ws[a], ws[b]):
                extra = w[HALF : HALF + 16, 3 * TILE : 4 * TILE].astype(F32)
                spill = spill + extra[8 * j : 8 * j + 8]
            dmap_ref[HALF - 8 : HALF, lanes] += jnp.where(third, spill, 0.0)
            dmap_ref[TILE - 8 : TILE, lanes] += jnp.where(fourth, spill, 0.0)
            five = params[a][20 + 5 * j : 25 + 5 * j] + params[b][20 + 5 * j : 25 + 5 * j]
            mtaps_ref[0:4, lanes] = five[0:4]
            mbias_ref[0:1, lanes] = five[4:5]


ROUTE_ONE = [(2, 1), (1, 2)]
ROUTE_TWO = [(0, 2), (2, 3), (1, 0), (3, 1)]


def back(route):
    return [(target, source) for source, target in route]


def shards_quad(
    sig_raw,
    map_raw,
    step_size_logits,
    d_out,
    sig_taps,
    map_taps,
    sig_bias,
    map_bias,
    a_log,
    dt_bias,
    skip_gain,
):
    ctx = lax.axis_size("ctx")
    rows, sig_width = sig_raw.shape
    vmem = pl.BlockSpec(memory_space=pltpu.VMEM)
    smem = pl.BlockSpec(memory_space=pltpu.SMEM)
    hbm = pl.BlockSpec(memory_space=pltpu.HBM)

    def call(kernel, out_shape, in_specs, out_specs, scratch, mib, cost):
        return pl.pallas_call(
            kernel,
            out_shape=out_shape,
            in_specs=in_specs,
            out_specs=out_specs,
            scratch_shapes=scratch,
            compiler_params=pltpu.CompilerParams(vmem_limit_bytes=int(mib * 1024 * 1024)),
            cost_estimate=pl.CostEstimate(flops=cost, bytes_accessed=cost // 100, transcendentals=0),
        )

    def shape(*dims, kind=F32):
        return jax.ShapeDtypeStruct(dims, kind)

    inside = [[(c, c ^ k) for c in range(ctx)] for k in range(4)]
    over = [(c, c ^ 4) for c in range(ctx)]
    total = 4 * TILE
    wide, narrow = 6 * TILE, 4 * TILE
    owned = map_taps.shape[1]
    sig_bias_row = sig_bias[None, :]
    packed = call(
        pack_kernel,
        (shape(TILE + HALF // 2 + 16, narrow, kind=BF),) * 4,
        [hbm] * 4,
        (vmem,) * 4,
        [
            pltpu.VMEM((32, TILE), F32),
            pltpu.VMEM((16, sig_width), BF),
            pltpu.VMEM((16, map_raw.shape[1] // 2), BF),
            pltpu.SemaphoreType.DMA((23,)),
        ],
        53.2,
        10**6,
    )(sig_raw, map_raw, step_size_logits.T, d_out)
    map_params = jnp.concatenate(
        [map_taps, map_bias[None, :], jnp.zeros((3, owned), F32)], axis=0
    )
    us = [packed[0]] + [lax.ppermute(packed[k], "ctx", inside[k]) for k in (1, 2, 3)]
    map_one = lax.ppermute(map_params, "fsdp", back(ROUTE_ONE))
    map_two = lax.ppermute(map_params, "fsdp", back(ROUTE_TWO))
    packed = call(
        pack_sig_kernel,
        (shape(TILE + HALF // 2, narrow, kind=BF),) * 4,
        [hbm, hbm],
        (vmem,) * 4,
        [pltpu.SemaphoreType.DMA((20,))],
        60,
        10**6,
    )(sig_raw, map_raw)
    us[0] = call(
        own_kernel, shape(TILE + HALF // 2 + 16, narrow, kind=BF), [vmem], vmem, [], 16, 10**6
    )(us[0])
    vs = [None] + [lax.ppermute(packed[k], "ctx", inside[k]) for k in (1, 2, 3)]
    midg, dp, xo, act_out, pre_out, sgrad, step_e, toend_e, exp_e, t_s, step_r, ds_r, sig_r, *small = call(
        grads_kernel,
        (
            shape(TILE, narrow, kind=BF),
            shape(total, narrow, kind=BF),
            shape(2, 2 * TILE + 8, TILE),
            shape(total, TILE, kind=BF),
            shape(total, TILE),
            shape(total, narrow, kind=BF),
            shape(total, narrow),
            shape(total, narrow),
            shape(total, narrow),
            shape(4, TILE, narrow),
            shape(32, TILE),
            shape(32, TILE),
            shape(32, TILE),
            shape(16, TILE),
            shape(16, wide, kind=BF),
        ),
        [vmem] * 7 + [smem] * 2,
        (vmem,) * 15,
        [pltpu.VMEM((4, 8, TILE), F32)],
        24,
        2 * 10**9,
    )(us[0], us[3], us[2], us[1], map_params, map_one, map_two, a_log, dt_bias)
    mine, halo = small
    halo = lax.ppermute(halo, "ctx", over)
    midg = lax.ppermute(midg, "ctx", over)
    vs[0] = call(
        own_later_kernel,
        shape(TILE + HALF // 2, narrow, kind=BF),
        [vmem] * 2,
        vmem,
        [],
        16,
        10**6,
    )(packed[0], mine)
    xs, acts, pres, scaled, weighted, xi, act_in, pre_in = call(
        first_kernel,
        (
            shape(2, 2 * TILE + 8, narrow),
            shape(total, narrow, kind=BF),
            shape(total, narrow),
            shape(total, narrow, kind=BF),
            shape(total, narrow, kind=BF),
            shape(2, 2 * TILE + 8, TILE),
            shape(total, TILE, kind=BF),
            shape(total, TILE),
        ),
        [vmem] * 9,
        (vmem,) * 8,
        [],
        24,
        2 * 10**9,
    )(vs[0], vs[1], vs[3], vs[2], step_e, toend_e, sig_taps, sig_bias_row, mine)
    midf, s_s, delta, edge, act_p, pre_p, scaled_p, weighted_p = call(
        states_kernel,
        (
            shape(TILE, narrow, kind=BF),
            shape(4, TILE, narrow),
            shape(TILE, narrow),
            shape(8, wide),
            shape(16, wide, kind=BF),
            shape(16, wide),
            shape(16, narrow, kind=BF),
            shape(16, narrow, kind=BF),
        ),
        [vmem] * 13,
        (vmem,) * 8,
        [],
        24,
        10**9,
    )(halo, xs, xi, xo, act_in, weighted, sgrad, step_e, toend_e, exp_e, sig_taps, sig_bias_row, mine)
    midf = lax.ppermute(midf, "ctx", over)
    base, coef, mslope, gmap, gsum, stepsum, skips, left = call(
        second_kernel,
        (
            shape(total, narrow),
            shape(total, narrow),
            shape(total, 2 * TILE),
            shape(total, 2 * TILE),
            shape(32, TILE),
            shape(32, TILE),
            shape(8, narrow),
            shape(TILE, narrow),
        ),
        [vmem] * 17 + [smem],
        (vmem,) * 8,
        [],
        24,
        5 * 10**9,
    )(
        dp,
        acts,
        act_in,
        act_out,
        pres,
        pre_in,
        pre_out,
        scaled,
        step_e,
        toend_e,
        ds_r,
        act_p,
        pre_p,
        scaled_p,
        halo,
        xo,
        mine,
        skip_gain,
    )
    one, two, hlow, clow, endrow = call(
        maps_kernel,
        (
            shape(total + 32, TILE, kind=BF),
            shape(total + 32, TILE, kind=BF),
            shape(4, TILE, narrow, kind=BF),
            shape(4, TILE, narrow, kind=BF),
            shape(8, narrow),
        ),
        [vmem] * 17,
        (vmem,) * 5,
        [
            pltpu.VMEM((4, TILE, narrow), F32),
            pltpu.VMEM((4, TILE, narrow), F32),
            pltpu.VMEM((2, 2 * TILE + 8, 2 * TILE), F32),
        ],
        24,
        2 * 10**9,
    )(
        midg,
        midf,
        halo,
        left,
        s_s,
        t_s,
        delta,
        exp_e,
        mslope,
        weighted,
        weighted_p,
        sgrad,
        gmap,
        xi,
        xo,
        edge,
        mine,
    )
    kept = one
    one = lax.ppermute(one, "fsdp", ROUTE_ONE)
    two = lax.ppermute(two, "fsdp", ROUTE_TWO)
    gp, blk, spill, params = call(
        third_kernel,
        (
            shape(2, 2 * TILE + 8, narrow),
            shape(8, 8, TILE),
            shape(8, narrow),
            shape(24, TILE),
        ),
        [vmem] * 20 + [smem],
        (vmem,) * 4,
        [],
        24,
        3 * 10**9,
    )(
        hlow,
        clow,
        endrow,
        xs,
        dp,
        acts,
        act_in,
        act_out,
        edge,
        act_p,
        toend_e,
        exp_e,
        step_r,
        sig_r,
        base,
        coef,
        gsum,
        stepsum,
        skips,
        sig_taps,
        a_log,
    )
    scale = 1.0 / math.sqrt(float(ctx * rows))
    cross = call(
        functools.partial(cross_kernel, scale),
        shape(32, narrow, kind=BF),
        [vmem] * 5,
        vmem,
        [],
        16,
        10**6,
    )(params, spill, kept, one, two)
    other = lax.ppermute(cross, "ctx", over)
    ys = call(
        send_kernel,
        (shape(TILE, narrow, kind=BF),) * 4,
        [vmem] * 2,
        (vmem,) * 4,
        [pltpu.VMEM((total, narrow), BF)],
        16,
        10**9,
    )(gp, sig_taps)
    ys = [ys[0]] + [lax.ppermute(ys[k], "ctx", inside[k]) for k in (1, 2, 3)]
    ws = call(
        merge_kernel,
        (shape(HALF + 32, narrow, kind=BF),) * 4,
        [vmem] * 6,
        (vmem,) * 4,
        [],
        16,
        10**6,
    )(cross, other, kept, one, two, blk)
    ws = [ws[0]] + [lax.ppermute(ws[k], "ctx", inside[k]) for k in (1, 2, 3)]
    d_sig, d_map, d_dt, taps, map_taps_grad, bias, map_bias_grad, *trio = call(
        last_kernel,
        (
            shape(rows, sig_width),
            shape(rows, owned),
            shape(32, TILE),
            shape(4, sig_width),
            shape(4, owned),
            shape(1, sig_width),
            shape(1, owned),
        )
        + (shape(1, 32),) * 3,
        [vmem] * 8,
        (vmem,) * 10,
        [],
        16,
        10**6,
    )(ys[0], ys[3], ys[2], ys[1], ws[0], ws[3], ws[2], ws[1])
    return (
        d_sig,
        d_map,
        d_dt.T,
        taps,
        map_taps_grad,
        bias[0],
        map_bias_grad[0],
        *(t[0] for t in trio),
    )


def shards(*args):
    sig_raw, map_raw, step_size_logits = args[:3]
    ctx = lax.axis_size("ctx")
    fsdp = lax.axis_size("fsdp")
    fits = (
        ctx == 8
        and fsdp == 4
        and sig_raw.shape == (TILE, 2048)
        and map_raw.shape == (TILE, 2 * GROUPS * STATE)
        and step_size_logits.shape[1] == 32
    )
    return shards_quad(*args) if fits else shards_chain(*args)


def solution(mesh):
    return jax.shard_map(
        shards,
        mesh=mesh,
        in_specs=(
            P("ctx", "fsdp"),
            P("ctx", None),
            P("ctx", "fsdp"),
            P("ctx", "fsdp"),
            P(None, "fsdp"),
            P(None, "fsdp"),
            P("fsdp"),
            P("fsdp"),
            P("fsdp"),
            P("fsdp"),
            P("fsdp"),
        ),
        out_specs=(
            P("ctx", "fsdp"),
            P("ctx", "fsdp"),
            P("ctx", "fsdp"),
            P(None, "fsdp"),
            P(None, "fsdp"),
            P("fsdp"),
            P("fsdp"),
            P("fsdp"),
            P("fsdp"),
            P("fsdp"),
        ),
        check_vma=False,
    )
```
